32 devices in a mesh: seq: 4 (over x, core), dp: 8 (over z, y).
Axes of the slice: x: 2, y: 2, z: 4, core: 2. Of those that a mesh axis runs over, the one named last changes fastest.
Arguments:
- tokens: bfloat16 [8, 1024, 1024], P('dp', 'seq'), may hold values from -6 to 6
- cotangent: bfloat16 [8, 1024, 1024], P('dp', 'seq'), may hold values from -6 to 6
- norm1_gain: bfloat16 [1024], P('dp'), may hold values from 0.5 to 1.5
- norm1_bias: bfloat16 [1024], P('dp'), may hold values from -4 to 4
- norm2_gain: bfloat16 [1024], P('dp'), may hold values from 0.5 to 1.5
- norm2_bias: bfloat16 [1024], P('dp'), may hold values from -4 to 4
- qkv_weight: bfloat16 [1024, 3072], P('dp'), may hold values from -0.25 to 0.25
- qkv_bias: bfloat16 [3072], P('dp'), may hold values from -4 to 4
- out_weight: bfloat16 [1024, 1024], P('dp'), may hold values from -1.5 to 1.5
- out_bias: bfloat16 [1024], P('dp'), may hold values from -4 to 4
- up_weight: bfloat16 [1024, 4096], P('dp'), may hold values from -0.1875 to 0.1875
- up_bias: bfloat16 [4096], P('dp'), may hold values from -4 to 4
- down_weight: bfloat16 [4096, 1024], P('dp'), may hold values from -0.09375 to 0.09375
- down_bias: bfloat16 [1024], P('dp'), may hold values from -4 to 4
- segment_ids: int32 [8, 1024], P('dp', 'seq'), may hold values from 0 to 3, as said below
- pad_length: int32 [8], P('dp'), may hold values from 0 to 512, as said below
Outputs:
- block_output: bfloat16 [8, 1024, 1024], P('dp', 'seq')
- input_grad: bfloat16 [8, 1024, 1024], P('dp', 'seq')
- norm1_gain_grad: float32 [1024], P('dp')
- norm1_bias_grad: float32 [1024], P('dp')
- norm2_gain_grad: float32 [1024], P('dp')
- norm2_bias_grad: float32 [1024], P('dp')
- qkv_weight_grad: float32 [1024, 3072], P('dp')
- qkv_bias_grad: float32 [3072], P('dp')
- out_weight_grad: float32 [1024, 1024], P('dp')
- out_bias_grad: float32 [1024], P('dp')
- up_weight_grad: float32 [1024, 4096], P('dp')
- up_bias_grad: float32 [4096], P('dp')
- down_weight_grad: float32 [4096, 1024], P('dp')
- down_bias_grad: float32 [1024], P('dp')
The draws below stay inside these ranges and needn't reach their ends.
Inputs may be any that keep to these rules, and one draw needn't show every extreme that they name: `segment_ids`: within a slot the numbers never fall. When pad_length of the slot is positive, its padded positions form a segment of their own. In every slot one document starts within the first 256 positions and runs to within 256 positions of the slot's unpadded end. `pad_length`: the last slot is padded by exactly 512 positions; of the others one at most is padded, by at most 128.
All inputs are finite; a program needn't handle non-finite values.
Results may differ from the reference program's by a relative error of at most 0.015.
Values may be sent and summed in bfloat16 or wider, within the bound.
A program may use at most 192 MiB of HBM per device.

```python
import jax
import jax.numpy as jnp
from jax import lax

D = 1024
HEADS = 16
HEAD_DIM = 64
ROT = 16
FF = 4096
TOK_DEV = 256
SLOT_LEN = 1024
SLOTS = 8


def slot_pads(key):
    key_pick, key_size = jax.random.split(jax.random.fold_in(key, 7))
    slot_index = jnp.arange(SLOTS, dtype=jnp.int32)
    chosen = jax.random.randint(key_pick, (), 0, SLOTS - 1)
    amount = jax.random.randint(key_size, (), 1, SLOT_LEN // 8 + 1)
    padding = jnp.where(slot_index == chosen, amount, 0)
    return jnp.where(slot_index == SLOTS - 1, SLOT_LEN // 2, padding).astype(jnp.int32)


def draw_pad_length(key, part):
    return slot_pads(key)


def draw_segment_ids(key, part):
    padding = slot_pads(key)
    key = jax.random.fold_in(key, 3)
    key_head, key_tail = jax.random.split(key)
    head_end = jax.random.randint(key_head, (SLOTS, 1), 1, TOK_DEV)
    tail_len = jax.random.randint(key_tail, (SLOTS, 1), 1, TOK_DEV)
    filled = SLOT_LEN - padding[:, None]
    places = jnp.arange(SLOT_LEN, dtype=jnp.int32)[None, :]
    numbers = (places >= head_end).astype(jnp.int32) + (places >= filled - tail_len).astype(jnp.int32) + (places >= filled).astype(jnp.int32)
    return numbers.astype(jnp.int32)


def steps_of(own_key, extent, cuts, least, largest):
    def one(dim, blocks):
        heights = jax.random.uniform(jax.random.fold_in(jax.random.fold_in(own_key, 6), dim), (blocks,), jnp.float32, least / len(cuts), largest / len(cuts))
        return jnp.repeat(jnp.exp(heights), extent[dim] // blocks).reshape((-1,) + (1,) * (len(extent) - dim - 1))

    loudness = one(*cuts[0])
    for cut in cuts[1:]:
        loudness = loudness * one(*cut)
    return loudness


def centred(key, shape, scale, bound, shards=(), kind=jnp.bfloat16):
    drawn = jax.random.normal(key, shape, jnp.float32) * scale
    if len(shards) > 0:
        drawn = steps_of(key, shape, shards, -0.22, 0.18) * drawn
    return jnp.clip(drawn, min=-bound, max=bound).astype(kind)


def setup_inputs(seed: int = 0) -> dict:
    key_list = jax.random.split(jax.random.key(seed), 17)
    return {
        "tokens": centred(key_list[0], (SLOTS, SLOT_LEN, D), 1.0, 6.0, ((0, 8), (1, 4))),
        "cotangent": centred(key_list[1], (SLOTS, SLOT_LEN, D), 1.0, 6.0, ((0, 8), (1, 4))),
        "norm1_gain": jnp.clip(1.0 + 0.1 * jax.random.normal(key_list[2], (D,), jnp.float32), 0.5, 1.5).astype(jnp.bfloat16),
        "norm1_bias": centred(key_list[3], (D,), 0.3, 4.0, ((0, 8),)),
        "norm2_gain": jnp.clip(1.0 + 0.1 * jax.random.normal(key_list[4], (D,), jnp.float32), 0.5, 1.5).astype(jnp.bfloat16),
        "norm2_bias": centred(key_list[5], (D,), 0.3, 4.0, ((0, 8),)),
        "qkv_weight": centred(key_list[6], (D, 3 * D), (D // 2) ** -0.5, 0.25, ((0, 8),)),
        "qkv_bias": centred(key_list[7], (3 * D,), 0.3, 4.0, ((0, 8),)),
        "out_weight": centred(key_list[8], (D, D), (D // 64) ** -0.5, 1.5, ((0, 8),)),
        "out_bias": centred(key_list[9], (D,), 0.3, 4.0, ((0, 8),)),
        "up_weight": centred(key_list[10], (D, FF), D ** -0.5, 0.1875, ((0, 8),)),
        "up_bias": centred(key_list[11], (FF,), 0.3, 4.0, ((0, 8),)),
        "down_weight": centred(key_list[12], (FF, D), FF ** -0.5, 0.09375, ((0, 8),)),
        "down_bias": centred(key_list[13], (D,), 0.3, 4.0, ((0, 8),)),
        "segment_ids": draw_segment_ids(jax.random.fold_in(key_list[16], 71), 0),
        "pad_length": draw_pad_length(jax.random.fold_in(key_list[16], 71), 0),
    }


HIGH = lax.Precision.HIGHEST
EPS = 1e-05
BASE = 10000.0
NEG = -1e+30

@jax.custom_vjp
def low(v):
    return lax.optimization_barrier(v.astype(jnp.bfloat16)).astype(jnp.float32)

@jax.custom_vjp
def low_back(v):
    return v

def low_keep(v):
    return (low(v), None)

def low_pass(kept, grad):
    return (grad,)

def back_keep(v):
    return (v, None)

def back_low(kept, grad):
    return (low(grad),)
low.defvjp(low_keep, low_pass)
low_back.defvjp(back_keep, back_low)

def layer_norm(values, gain_vec, shift_vec):
    center = values - lax.optimization_barrier(jnp.mean(values, axis=-1, keepdims=True))
    spread = lax.optimization_barrier(jnp.mean(center * center, axis=-1, keepdims=True))
    return center * lax.rsqrt(spread + EPS) * gain_vec + shift_vec

def angle_tables(positions):
    frequency = BASE ** (-jnp.arange(0, ROT, 2).astype(jnp.float32) / ROT)
    angles = positions[:, None] * frequency[None, :]
    angles = jnp.concatenate([angles, angles], axis=-1)[:, None, :]
    return (jnp.cos(angles), jnp.sin(angles))

def turn_part(piece_in, cosine, sine_table):
    rotary_part = piece_in[..., :ROT]
    half_rot = ROT // 2
    turned = jnp.concatenate([-rotary_part[..., half_rot:], rotary_part[..., :half_rot]], axis=-1)
    return jnp.concatenate([rotary_part * cosine + turned * sine_table, piece_in[..., ROT:]], axis=-1)

def attend(queries, keys_all, values_all, segments):
    length = queries.shape[0]
    block_rows = min(512, length)
    block_count = length // block_rows
    score_scale = HEAD_DIM ** (-0.5)
    key_pos = jnp.arange(length, dtype=jnp.int32)

    def one_block(block_index):
        row_start = block_index * block_rows
        q_block = lax.dynamic_slice_in_dim(queries, row_start, block_rows, 0)
        q_seg = lax.dynamic_slice_in_dim(segments, row_start, block_rows, 0)
        q_pos = row_start + jnp.arange(block_rows, dtype=jnp.int32)
        scores = jnp.einsum('qhd,khd->hqk', q_block, keys_all, precision=HIGH) * score_scale
        scores = low_back(scores)
        allowed = (key_pos[None, :] <= q_pos[:, None]) & (segments[None, :] == q_seg[:, None])
        scores = jnp.where(allowed[None], scores, NEG)
        row_top = lax.optimization_barrier(jnp.max(scores, axis=-1, keepdims=True))
        raised = jnp.exp(scores - row_top)
        weights_soft = raised / lax.optimization_barrier(jnp.sum(raised, axis=-1, keepdims=True))
        return jnp.einsum('hqk,khd->qhd', low(weights_soft), values_all, precision=HIGH)
    blocks = lax.map(jax.checkpoint(one_block), jnp.arange(block_count, dtype=jnp.int32))
    return blocks.reshape(length, queries.shape[1], queries.shape[2])

def slot_forward(parameters, tokens_slot, segments, padding):
    gain_one, shift_one, gain_two, shift_two, w_mix, b_mix, w_proj, b_proj, w_rise, b_rise, w_fall, b_fall = parameters
    length = tokens_slot.shape[0]
    row_ids = jnp.arange(length, dtype=jnp.int32)
    valid_rows = (row_ids < length - padding).astype(jnp.float32)[:, None]
    cosine, sine_table = angle_tables(row_ids.astype(jnp.float32))
    normed = layer_norm(tokens_slot, gain_one, shift_one)
    projected = low_back(jnp.dot(low(normed), w_mix, precision=HIGH) + b_mix)
    projected = projected.reshape(length, HEADS, 3 * HEAD_DIM)
    queries = low_back(low(turn_part(projected[..., :HEAD_DIM], cosine, sine_table)))
    keys_all = low_back(low(turn_part(projected[..., HEAD_DIM:2 * HEAD_DIM], cosine, sine_table)))
    values_all = low_back(low(projected[..., 2 * HEAD_DIM:]))
    heads_out = low_back(low(attend(queries, keys_all, values_all, segments)))
    attn_rows = heads_out.reshape(length, D) * valid_rows
    attn_out = jnp.dot(attn_rows, w_proj, precision=HIGH) + b_proj
    normed_two = layer_norm(tokens_slot, gain_two, shift_two)
    upward = low_back(jnp.dot(low(normed_two), w_rise, precision=HIGH) + b_rise)
    active = low(jax.nn.gelu(upward, approximate=False))
    mlp_out = jnp.dot(active, w_fall, precision=HIGH) + b_fall
    return tokens_slot + attn_out + mlp_out

def reference(tokens, cotangent, norm1_gain, norm1_bias, norm2_gain, norm2_bias, qkv_weight, qkv_bias, out_weight, out_bias, up_weight, up_bias, down_weight, down_bias, segment_ids, pad_length):
    parameters = tuple((piece.astype(jnp.float32) for piece in (norm1_gain, norm1_bias, norm2_gain, norm2_bias, qkv_weight, qkv_bias, out_weight, out_bias, up_weight, up_bias, down_weight, down_bias)))

    def forward(param_set, inputs):

        def one_slot(slot_items):
            return slot_forward(param_set, slot_items[0], slot_items[1], slot_items[2])
        return lax.map(jax.checkpoint(one_slot), (inputs, segment_ids, pad_length))
    output, pullback = jax.vjp(forward, parameters, tokens.astype(jnp.float32))
    gradients, input_grad = pullback(cotangent.astype(jnp.float32))
    return (output.astype(jnp.bfloat16), input_grad.astype(jnp.bfloat16), gradients[0], gradients[1], gradients[2], gradients[3], gradients[4], gradients[5], gradients[6], gradients[7], gradients[8], gradients[9], gradients[10], gradients[11])
```

```python
import functools

import jax
import jax.numpy as jnp
import numpy as np
from jax import lax
from jax.experimental import pallas as pl
from jax.experimental.pallas import tpu as pltpu
from jax.sharding import PartitionSpec as P

D = 1024
HEADS = 16
HEAD_DIM = 64
ROT = 16
FF = 4096
EPS = 1e-05
BASE = 10000.0
NEG = -1e30
MESH = pl.DeviceIdType.MESH
BF = jnp.bfloat16
F32 = jnp.float32


def ring_pos(dev, size):
    return (dev // 2) * (1 - dev % 2) + (size - 1 - dev // 2) * (dev % 2)


def ring_dev(pos, size):
    high = pos // (size // 2)
    return (1 - high) * 2 * pos + high * (2 * (size - 1 - pos) + 1)


class Place:
    def __init__(self, seq_size, dp_size):
        self.seq_size, self.dp_size = seq_size, dp_size
        self.seq = lax.axis_index("seq")
        self.dp = lax.axis_index("dp")
        self.pos = ring_pos(self.dp, dp_size)
        self.half = dp_size // 2
        self.pairs = seq_size // 2
        self.core = self.seq % 2
        self.pair = self.seq // 2
        self.sibling = self.pair * 2 + 1 - self.core

    def ring(self, offset):
        return ring_dev((self.pos + offset + self.dp_size) % self.dp_size, self.dp_size)

    def dp_peer(self, step):
        return (self.dp + step) % self.dp_size

    def pair_peer(self, step):
        return ((self.pair + step) % self.pairs) * 2 + self.core

    def seq_peer(self, step):
        return (self.seq + step) % self.seq_size

    def greet(self):
        barrier = pltpu.get_barrier_semaphore()
        for step in range(1, self.dp_size):
            pl.semaphore_signal(
                barrier, inc=1, device_id={"dp": self.dp_peer(step)}, device_id_type=MESH
            )
        for step in range(1, self.seq_size):
            pl.semaphore_signal(
                barrier, inc=1, device_id={"seq": self.seq_peer(step)}, device_id_type=MESH
            )
        pl.semaphore_wait(barrier, self.dp_size - 1 + self.seq_size - 1)


def send(src, dst, sems, index, target):
    return pltpu.make_async_remote_copy(
        src_ref=src,
        dst_ref=dst,
        send_sem=sems.at[0, index],
        recv_sem=sems.at[1, index],
        device_id=target,
        device_id_type=MESH,
    )


def halves(ref):
    rows = ref.shape[0]
    columns = ref.shape[1]
    if rows % 32 == 0:
        return ref.at[pl.ds(0, rows // 2)], ref.at[pl.ds(rows // 2, rows // 2)]
    return ref.at[:, pl.ds(0, columns // 2)], ref.at[:, pl.ds(columns // 2, columns // 2)]


class RingGather:
    def __init__(self, place, full, sems):
        self.place, self.full, self.sems = place, full, sems

    def piece(self, offset, step, way):
        block = self.full.at[self.place.ring(offset)]
        return block if step < self.place.half else halves(block)[way]

    def copies(self, step):
        place = self.place
        right = self.piece(-(step - 1), step, 0)
        left = self.piece(step - 1, step, 1)
        index = 2 * (step - 1)
        return (
            send(right, right, self.sems, index, {"dp": place.ring(1)}),
            send(left, left, self.sems, index + 1, {"dp": place.ring(-1)}),
        )

    def arrivals(self, step):
        right = self.piece(-step, step, 0)
        left = self.piece(step, step, 1)
        index = 2 * (step - 1)
        return (
            send(right, right, self.sems, index, {"dp": self.place.ring(1)}),
            send(left, left, self.sems, index + 1, {"dp": self.place.ring(-1)}),
        )

    def tick(self, step):
        if step > 1:
            for copy in self.arrivals(step - 1):
                copy.wait_recv()
        if step <= self.place.half:
            for copy in self.copies(step):
                copy.start()

    def finish(self):
        for step in range(1, self.place.half + 1):
            for copy in self.copies(step):
                copy.wait_send()


class RingReduce:
    def __init__(self, place, parts, arrived, sems):
        self.place, self.parts, self.arrived, self.sems = place, parts, arrived, sems

    def piece(self, ref, step, way):
        return ref if step > 1 else halves(ref)[way]

    def copies(self, step):
        place = self.place
        away = place.half - step + 1
        index = 2 * (step - 1)
        out = []
        for way, (offset, target) in enumerate(((away, 1), (-away, -1))):
            src = self.piece(self.parts.at[place.ring(offset)], step, way)
            dst = self.piece(self.arrived.at[way, step - 1], step, way)
            out.append(send(src, dst, self.sems, index + way, {"dp": place.ring(target)}))
        return out

    def tick(self, step):
        place = self.place
        if step > 1:
            for way, copy in enumerate(self.copies(step - 1)):
                copy.wait_recv()
                away = (place.half - step + 1) * (1 - 2 * way)
                held = self.piece(self.parts.at[place.ring(away)], step - 1, way)
                came = self.piece(self.arrived.at[way, step - 2], step - 1, way)
                held[...] = (held[...].astype(F32) + came[...].astype(F32)).astype(held.dtype)
        if step <= place.half:
            for copy in self.copies(step):
                copy.start()

    def finish(self):
        for step in range(1, self.place.half + 1):
            for copy in self.copies(step):
                copy.wait_send()

    def own(self):
        return self.parts.at[self.place.dp]


class SeqGather:
    def __init__(self, place, full, sems):
        self.place, self.full, self.sems = place, full, sems

    def direct(self, step):
        block = self.full.at[self.place.seq]
        return send(block, block, self.sems, step, {"seq": self.place.pair_peer(step)})

    def arrival(self, step):
        block = self.full.at[self.place.pair_peer(-step)]
        return send(block, block, self.sems, step, {"seq": self.place.pair_peer(step)})

    def across(self, step):
        block = self.full.at[self.place.pair_peer(-step)]
        return send(
            block, block, self.sems, self.place.pairs + step, {"seq": self.place.sibling}
        )

    def across_arrival(self, step):
        place = self.place
        source = ((place.pair - step) % place.pairs) * 2 + 1 - place.core
        block = self.full.at[source]
        return send(block, block, self.sems, place.pairs + step, {"seq": place.sibling})

    def begin(self):
        for step in range(1, self.place.pairs):
            self.direct(step).start()
        self.across(0).start()

    def forward(self):
        for step in range(1, self.place.pairs):
            self.arrival(step).wait_recv()
            self.across(step).start()

    def finish(self):
        for step in range(self.place.pairs):
            self.across_arrival(step).wait_recv()
        for step in range(1, self.place.pairs):
            self.direct(step).wait_send()
        for step in range(self.place.pairs):
            self.across(step).wait_send()


class SeqReduce:
    def __init__(self, place, parts, crossed, arrived, sems):
        self.place, self.parts, self.crossed, self.arrived = place, parts, crossed, arrived
        self.sems = sems

    def over(self, index):
        place = self.place
        return send(
            self.parts.at[index * 2 + 1 - place.core],
            self.crossed.at[index],
            self.sems,
            index,
            {"seq": place.sibling},
        )

    def direct(self, step):
        place = self.place
        return send(
            self.parts.at[place.pair_peer(step)],
            self.arrived.at[step],
            self.sems,
            place.pairs + step,
            {"seq": place.pair_peer(step)},
        )

    def begin(self):
        for index in range(self.place.pairs):
            self.over(index).start()

    def middle(self):
        place = self.place
        for index in range(place.pairs):
            self.over(index).wait_recv()
            held = self.parts.at[index * 2 + place.core]
            held[...] = (held[...].astype(F32) + self.crossed[index].astype(F32)).astype(held.dtype)
        for step in range(1, place.pairs):
            self.direct(step).start()

    def total(self):
        place = self.place
        total = self.parts[place.seq].astype(F32)
        for step in range(1, place.pairs):
            self.direct(step).wait_recv()
            total = total + self.arrived[step].astype(F32)
        return total

    def finish(self):
        for index in range(self.place.pairs):
            self.over(index).wait_send()
        for step in range(1, self.place.pairs):
            self.direct(step).wait_send()


class DpSpread:
    def __init__(self, place, src_of, full, sems):
        self.place, self.src_of, self.full, self.sems = place, src_of, full, sems

    def copy(self, step):
        place = self.place
        peer = place.dp_peer(step)
        return send(self.src_of(peer), self.full.at[place.dp], self.sems, step, {"dp": peer})

    def arrival(self, step):
        place = self.place
        source = place.dp_peer(-step)
        return send(
            self.src_of(source), self.full.at[source], self.sems, step, {"dp": place.dp_peer(step)}
        )

    def begin(self):
        for step in range(1, self.place.dp_size):
            self.copy(step).start()

    def finish(self):
        for step in range(1, self.place.dp_size):
            self.arrival(step).wait_recv()
        for step in range(1, self.place.dp_size):
            self.copy(step).wait_send()


def sems_of(count):
    return pltpu.SemaphoreType.DMA((2, count))


def gather_kernel(seq_size, dp_size, *refs):
    (x_ref, dy_ref, mix_ref, proj_ref, rise_ref, fall_ref, vec_ref, seg_ref) = refs[:8]
    (x_all, dy_all, mix_all, proj_cols, rise_all, fall_all, vec_all, seg_all, proj_all) = refs[8:17]
    (x_sems, dy_sems, mix_sems, proj_sems, rise_sems, fall_sems, vec_sems, seg_sems, swap_sems, own_sems) = refs[17:]
    place = Place(seq_size, dp_size)
    own = [
        pltpu.make_async_copy(src, dst, own_sems.at[i])
        for i, (src, dst) in enumerate(
            (
                (x_ref, x_all.at[place.seq]),
                (dy_ref, dy_all.at[place.seq]),
                (mix_ref, mix_all.at[place.dp]),
                (proj_ref, proj_cols.at[place.dp]),
                (rise_ref, rise_all.at[place.dp]),
                (fall_ref, fall_all.at[place.dp]),
                (vec_ref, vec_all.at[place.dp]),
                (seg_ref, seg_all.at[place.seq]),
            )
        )
    ]
    for copy in own:
        copy.start()
    place.greet()
    for copy in own:
        copy.wait()
    x_move = SeqGather(place, x_all, x_sems)
    dy_move = SeqGather(place, dy_all, dy_sems)
    seg_move = SeqGather(place, seg_all, seg_sems)
    vec_move = DpSpread(place, lambda peer: vec_ref, vec_all, vec_sems)
    mix_move = RingGather(place, mix_all, mix_sems)
    proj_move = RingGather(place, proj_cols, proj_sems)
    rise_move = RingGather(place, rise_all, rise_sems)
    fall_move = RingGather(place, fall_all, fall_sems)
    x_move.begin()
    seg_move.begin()
    vec_move.begin()
    half = place.half
    for step in range(1, half + 1):
        mix_move.tick(step)
        proj_move.tick(step)
    x_move.forward()
    seg_move.forward()
    dy_move.begin()
    mix_move.tick(half + 1)
    proj_move.tick(half + 1)
    rise_move.tick(1)
    fall_move.tick(1)
    rows = proj_cols.shape[0] * proj_cols.shape[1] // seq_size
    each = rows // proj_cols.shape[1]
    swaps = []
    for step in range(1, seq_size):
        peer = place.seq_peer(step)
        swaps.append(
            send(
                proj_cols.at[pl.ds(peer * each, each)],
                proj_all.at[place.seq],
                swap_sems,
                step,
                {"seq": peer},
            )
        )
    for copy in swaps:
        copy.start()
    mine = pltpu.make_async_copy(
        proj_cols.at[pl.ds(place.seq * each, each)], proj_all.at[place.seq], own_sems.at[0]
    )
    mine.start()
    for step in range(2, half + 2):
        rise_move.tick(step)
        fall_move.tick(step)
        if step == 3:
            dy_move.forward()
    mine.wait()
    for step in range(1, seq_size):
        source = place.seq_peer(-step)
        send(
            proj_cols.at[pl.ds(source * each, each)],
            proj_all.at[source],
            swap_sems,
            step,
            {"seq": place.seq_peer(step)},
        ).wait_recv()
    for copy in swaps:
        copy.wait_send()
    for move in (x_move, dy_move, seg_move, vec_move, mix_move, proj_move, rise_move, fall_move):
        move.finish()


def gather_all(seq_size, dp_size, x, dy, mix, proj, rise, fall, vec, seg):
    half = dp_size // 2
    pairs = seq_size // 2

    def lead(count, like):
        return jax.ShapeDtypeStruct((count,) + like.shape, like.dtype)

    each = dp_size // seq_size
    any_spec = pl.BlockSpec(memory_space=pl.ANY)
    return pl.pallas_call(
        functools.partial(gather_kernel, seq_size, dp_size),
        out_shape=(
            lead(seq_size, x),
            lead(seq_size, dy),
            lead(dp_size, mix),
            lead(dp_size, proj),
            lead(dp_size, rise),
            lead(dp_size, fall),
            lead(dp_size, vec),
            lead(seq_size, seg),
            jax.ShapeDtypeStruct((seq_size, each) + proj.shape, proj.dtype),
        ),
        in_specs=[any_spec] * 8,
        out_specs=[any_spec] * 9,
        scratch_shapes=[
            sems_of(2 * pairs),
            sems_of(2 * pairs),
            sems_of(2 * half),
            sems_of(2 * half),
            sems_of(2 * half),
            sems_of(2 * half),
            sems_of(dp_size),
            sems_of(2 * pairs),
            sems_of(seq_size),
            pltpu.SemaphoreType.DMA((8,)),
        ],
        compiler_params=pltpu.CompilerParams(collective_id=0, has_side_effects=True),
    )(x, dy, mix, proj, rise, fall, vec, seg)


def reduce_kernel(seq_size, dp_size, *refs):
    (out_ref, back_ref, mix_ref, proj_ref, rise_ref, fall_ref, vec_ref), refs = refs[:7], refs[7:]
    (out_sum, back_sum, mix_fin, proj_fin, rise_fin, fall_fin, vec_fin), refs = refs[:7], refs[7:]
    (
        out_cross,
        out_came,
        back_cross,
        back_came,
        proj_full,
        mix_came,
        proj_came,
        rise_came,
        fall_came,
        vec_came,
        out_sems,
        back_sems,
        swap_sems,
        mix_sems,
        proj_sems,
        rise_sems,
        fall_sems,
        vec_sems,
        mix_fs,
        proj_fs,
        rise_fs,
        fall_fs,
        vec_fs,
    ) = refs
    place = Place(seq_size, dp_size)
    each = dp_size // seq_size
    half = place.half
    place.greet()

    def mine(index):
        return proj_full.at[pl.ds(index * each, each)]

    def swap(step):
        peer = place.seq_peer(step)
        return send(proj_ref.at[peer], mine(place.seq), swap_sems, step, {"seq": peer})

    def swap_arrival(step):
        source = place.seq_peer(-step)
        target = {"seq": place.seq_peer(step)}
        return send(proj_ref.at[source], mine(source), swap_sems, step, target)

    for step in range(1, seq_size):
        swap(step).start()
    mine(place.seq)[...] = proj_ref[place.seq]
    mix = RingReduce(place, mix_ref, mix_came, mix_sems)
    proj = RingReduce(place, proj_full, proj_came, proj_sems)
    rise = RingReduce(place, rise_ref, rise_came, rise_sems)
    fall = RingReduce(place, fall_ref, fall_came, fall_sems)
    out = SeqReduce(place, out_ref, out_cross, out_came, out_sems)
    back = SeqReduce(place, back_ref, back_cross, back_came, back_sems)
    vec = DpSpread(place, lambda peer: vec_ref.at[peer], vec_came, vec_sems)
    mix.tick(1)
    rise.tick(1)
    out.begin()
    back.begin()
    vec.begin()
    for step in range(1, seq_size):
        swap_arrival(step).wait_recv()
    proj.tick(1)
    fall.tick(1)
    out.middle()
    back.middle()
    for step in range(2, half + 2):
        for move in (mix, rise, proj, fall):
            move.tick(step)
    finals = []
    for move, fin, fin_sems in (
        (mix, mix_fin, mix_fs),
        (rise, rise_fin, rise_fs),
        (proj, proj_fin, proj_fs),
        (fall, fall_fin, fall_fs),
    ):
        fin[place.seq] = move.parts[place.dp]
        gather = SeqGather(place, fin, fin_sems)
        gather.begin()
        finals.append(gather)
    vec_came[place.dp] = vec_ref[place.dp]
    vec.finish()
    vec_fin[place.seq] = jnp.sum(vec_came[...], axis=0)
    gather = SeqGather(place, vec_fin, vec_fs)
    gather.begin()
    finals.append(gather)
    out_sum[...] = out.total()
    back_sum[...] = back.total()
    for gather in finals:
        gather.forward()
    for gather in finals:
        gather.finish()
    for step in range(1, seq_size):
        swap(step).wait_send()
    for move in (mix, rise, proj, fall, out, back):
        move.finish()


def reduce_all(seq_size, dp_size, out, back, mix, proj, rise, fall, vec):
    half = dp_size // 2
    pairs = seq_size // 2
    each = dp_size // seq_size

    def fin(like):
        return jax.ShapeDtypeStruct((seq_size,) + like.shape[1:], like.dtype)

    def came(like):
        return pltpu.VMEM((2, half) + like.shape[1:], like.dtype)

    proj_blocks = jax.ShapeDtypeStruct((dp_size,) + proj.shape[2:], proj.dtype)
    vmem = pl.BlockSpec(memory_space=pltpu.VMEM)
    return pl.pallas_call(
        functools.partial(reduce_kernel, seq_size, dp_size),
        out_shape=(
            jax.ShapeDtypeStruct(out.shape[1:], F32),
            jax.ShapeDtypeStruct(back.shape[1:], F32),
            fin(mix),
            fin(proj_blocks),
            fin(rise),
            fin(fall),
            fin(vec),
        ),
        in_specs=[vmem] * 7,
        out_specs=[vmem] * 7,
        scratch_shapes=[
            pltpu.VMEM((pairs,) + out.shape[1:], BF),
            pltpu.VMEM((pairs,) + out.shape[1:], BF),
            pltpu.VMEM((pairs,) + back.shape[1:], BF),
            pltpu.VMEM((pairs,) + back.shape[1:], BF),
            pltpu.VMEM(proj_blocks.shape, BF),
            came(mix),
            came(proj_blocks),
            came(rise),
            came(fall),
            pltpu.VMEM(vec.shape, F32),
            sems_of(2 * pairs),
            sems_of(2 * pairs),
            sems_of(seq_size),
            sems_of(2 * half),
            sems_of(2 * half),
            sems_of(2 * half),
            sems_of(2 * half),
            sems_of(dp_size),
            sems_of(2 * pairs),
            sems_of(2 * pairs),
            sems_of(2 * pairs),
            sems_of(2 * pairs),
            sems_of(2 * pairs),
        ],
        compiler_params=pltpu.CompilerParams(
            collective_id=1, has_side_effects=True, vmem_limit_bytes=56 * 2**20
        ),
    )(out, back, mix, proj, rise, fall, vec)


def angle_tables(length):
    frequency = BASE ** (-np.arange(0, ROT, 2).astype(np.float32) / np.float32(ROT))
    angles = np.arange(length, dtype=np.float32)[:, None] * frequency.astype(np.float32)[None, :]
    return np.cos(angles).astype(np.float32), np.sin(angles).astype(np.float32)


def turn(piece, cosine, sine, sign):
    half = ROT // 2
    low, high = piece[..., :half], piece[..., half:ROT]
    return jnp.concatenate(
        [low * cosine - sign * high * sine, high * cosine + sign * low * sine, piece[..., ROT:]],
        axis=-1,
    )


TILE = 256

def mm(a, b, dims):
    return lax.dot_general(a, b, ((dims[0], dims[1]), ((), ())), preferred_element_type=F32)

def nn(a, b):
    return mm(a, b, ((1,), (0,)))

def nt(a, b):
    return mm(a, b, ((1,), (1,)))

def tn(a, b):
    return mm(a, b, ((0,), (0,)))

def fold(count, body, init):
    if isinstance(count, int):
        for index in range(count):
            init = body(index, init)
        return init
    return lax.fori_loop(0, count, body, init)

def rows_of(index):
    start = index * TILE
    return pl.ds(start if isinstance(start, int) else pl.multiple_of(start, TILE), TILE)

def attend_block(head, block, refs):
    q_ref, k_ref, v_ref, g_ref, kt_ref, vt_ref, s_ref, p_ref, ht_ref, dqt_ref, dk_ref, dv_ref = refs
    here = rows_of(block)
    span = block + 1
    dims = pl.ds(pl.multiple_of(head * HEAD_DIM, HEAD_DIM), HEAD_DIM)
    query = q_ref[head, here, :]
    grad = g_ref[head, here, :]

    def score(index, top):
        tile = nt(k_ref[head, rows_of(index), :], query)
        if isinstance(index, int) and isinstance(block, int) and index < block:
            keep = tile
        else:
            key = lax.broadcasted_iota(jnp.int32, (TILE, TILE), 0) + (index - block) * TILE
            place = lax.broadcasted_iota(jnp.int32, (TILE, TILE), 1)
            keep = jnp.where(key <= place, tile, NEG)
        s_ref[index] = keep
        return jnp.maximum(top, jnp.max(keep, axis=0, keepdims=True))

    top = fold(span, score, jnp.full((1, TILE), 2 * NEG, F32))

    def raise_(index, total):
        raised = jnp.exp(s_ref[index] - top)
        s_ref[index] = raised
        return total + jnp.sum(raised, axis=0, keepdims=True)

    total = fold(span, raise_, jnp.zeros((1, TILE), F32))
    share = 1.0 / total

    def weigh(index, carried):
        heads, delta = carried
        weights = s_ref[index] * share
        s_ref[index] = weights
        weights_b = weights.astype(BF)
        d_weights = nt(v_ref[head, rows_of(index), :], grad)
        p_ref[index] = d_weights
        dv_ref[head, rows_of(index), :] += nn(weights_b, grad)
        heads = heads + nn(vt_ref[dims, rows_of(index)], weights_b)
        return heads, delta + jnp.sum(weights * d_weights, axis=0, keepdims=True)

    heads, delta = fold(
        span, weigh, (jnp.zeros((HEAD_DIM, TILE), F32), jnp.zeros((1, TILE), F32))
    )
    ht_ref[dims, here] = heads

    def back(index, d_query):
        d_scores = (s_ref[index] * (p_ref[index] - delta)).astype(BF)
        dk_ref[head, rows_of(index), :] += nn(d_scores, query)
        return d_query + nn(kt_ref[dims, rows_of(index)], d_scores)

    dqt_ref[dims, here] = fold(span, back, jnp.zeros((HEAD_DIM, TILE), F32))

def attend(heads_n, length, refs):
    dk_ref, dv_ref = refs[-2:]
    dk_ref[...] = jnp.zeros(dk_ref.shape, F32)
    dv_ref[...] = jnp.zeros(dv_ref.shape, F32)
    blocks = length // TILE

    @pl.loop(0, heads_n)
    def _(head):
        if blocks <= 4:
            for block in range(blocks):
                attend_block(head, block, refs)
        else:
            @pl.loop(0, blocks)
            def _(block):
                attend_block(head, block, refs)

def attend_kernel(H, L, q, k, v, g, kt, vt, ht, dqt, dk, dv, s_ref, p_ref):
    attend(H, L, (q, k, v, g, kt, vt, s_ref, p_ref, ht, dqt, dk, dv))

def attention_call(q, k, v, g, kt, vt):
    H, L, _ = q.shape
    vm = pl.BlockSpec(memory_space=pltpu.VMEM)
    nb = L // TILE
    return pl.pallas_call(functools.partial(attend_kernel, H, L),
        out_shape=(jax.ShapeDtypeStruct((H*64, L), F32), jax.ShapeDtypeStruct((H*64, L), F32), jax.ShapeDtypeStruct((H, L, 128), F32), jax.ShapeDtypeStruct((H, L, 128), F32)),
        in_specs=[vm]*6, out_specs=[vm]*4,
        scratch_shapes=[pltpu.VMEM((nb, TILE, TILE), F32), pltpu.VMEM((nb, TILE, TILE), F32)],
        compiler_params=pltpu.CompilerParams(vmem_limit_bytes=56 * 2**20))(q, k, v, g, kt, vt)

def prep(queries, keys, values, d_heads, segments):
    seg = segments[:, None] == jnp.arange(64)[None, :]
    e = jnp.broadcast_to(seg.astype(BF)[None], queries.shape)
    f = jnp.broadcast_to(jnp.where(seg, 0.0, NEG).astype(BF)[None], queries.shape)
    lane = jnp.arange(64)
    f = jnp.where(lane < 4, f, 0).astype(BF)
    qa = jnp.concatenate([(queries.astype(F32) * 0.125).astype(BF), e], -1)
    ka = jnp.concatenate([keys, f], -1)
    z = jnp.zeros_like(values)
    va = jnp.concatenate([values, z], -1)
    ga = jnp.concatenate([d_heads, z], -1)
    kt = keys.transpose(0, 2, 1).reshape(-1, keys.shape[1])
    vt = values.transpose(0, 2, 1).reshape(-1, keys.shape[1])
    return qa, ka, va, ga, kt, vt

def attention(queries, keys, values, d_heads, segments):
    H, L, _ = queries.shape
    ht, dqt, dk, dv = attention_call(*prep(queries, keys, values, d_heads, segments))

    def back(t):
        return t.reshape(H, 64, L).transpose(0, 2, 1)

    return back(ht).astype(BF), (back(dqt) * 0.125).astype(BF), dk[..., :64].astype(BF), dv[..., :64].astype(BF)


def dot(a, b):
    return jnp.dot(a, b, preferred_element_type=F32)


def dot_t(a, b):
    return lax.dot_general(a, b, (((0,), (0,)), ((), ())), preferred_element_type=F32)


def dot_nt(a, b):
    return lax.dot_general(a, b, (((1,), (1,)), ((), ())), preferred_element_type=F32)


def shards(
    tokens,
    cotangent,
    norm1_gain,
    norm1_bias,
    norm2_gain,
    norm2_bias,
    qkv_weight,
    qkv_bias,
    out_weight,
    out_bias,
    up_weight,
    up_bias,
    down_weight,
    down_bias,
    segment_ids,
    pad_length,
):
    seq_size, dp_size = lax.axis_size("seq"), lax.axis_size("dp")
    seq = lax.axis_index("seq")
    dp = lax.axis_index("dp")
    tok = tokens.shape[1]
    length = tok * seq_size
    heads_n = HEADS // seq_size
    rows = D // dp_size
    wide = heads_n * HEAD_DIM
    units = FF // dp_size // seq_size

    mix = qkv_weight.reshape(rows, seq_size, heads_n, 3, HEAD_DIM)
    mix = lax.dynamic_index_in_dim(mix, seq, 1, keepdims=False)
    mix = mix.transpose(0, 2, 1, 3).reshape(rows, 3 * wide)
    proj = lax.dynamic_slice_in_dim(out_weight, seq * wide, wide, 1)
    rise = up_weight.reshape(rows, dp_size, seq_size, units)
    rise = lax.dynamic_index_in_dim(rise, seq, 2, keepdims=False).reshape(rows, dp_size * units)
    fall = lax.dynamic_slice_in_dim(down_weight, seq * units, units, 0)
    vec = jnp.concatenate(
        [norm1_gain, norm1_bias, norm2_gain, norm2_bias, out_bias, down_bias, qkv_bias, up_bias]
    )
    vec_len = vec.shape[0]
    vec = jnp.pad(vec, (0, 2048 - vec_len)).reshape(16, 128)
    seg = jnp.broadcast_to(segment_ids, (8, tok))
    x_all, dy_all, w_mix, _, w_rise, w_fall, vec_all, seg_all, w_proj = gather_all(
        seq_size, dp_size, tokens[0], cotangent[0], mix, proj, rise, fall, vec, seg
    )
    x = x_all.reshape(length, D).astype(F32)
    dy = dy_all.reshape(length, D)
    w_mix = w_mix.reshape(D, 3 * wide)
    w_rise = w_rise.reshape(D, dp_size * units)
    w_fall = w_fall.reshape(dp_size * units, D)
    w_proj = w_proj.reshape(seq_size, wide, wide).transpose(1, 0, 2).reshape(wide, D)
    segments = seg_all[:, 0, :].reshape(length)
    vec_all = vec_all.reshape(dp_size, 2048)[:, :vec_len].astype(F32)
    g1, s1, g2, s2, b_proj, b_fall = (
        vec_all[:, i * rows : (i + 1) * rows].reshape(D) for i in range(6)
    )
    b_mix = vec_all[:, 6 * rows : 9 * rows].reshape(seq_size, heads_n, 3, HEAD_DIM)
    b_mix = lax.dynamic_index_in_dim(b_mix, seq, 0, keepdims=False)
    b_mix = b_mix.transpose(1, 0, 2).reshape(3 * wide)
    b_rise = vec_all[:, 9 * rows :].reshape(dp_size, seq_size, units)
    b_rise = lax.dynamic_index_in_dim(b_rise, seq, 1, keepdims=False).reshape(dp_size * units)

    center = x - jnp.mean(x, axis=-1, keepdims=True)
    rstd = lax.rsqrt(jnp.mean(center * center, axis=-1, keepdims=True) + EPS)
    n = center * rstd
    normed1 = (n * g1 + s1).astype(BF)
    normed2 = (n * g2 + s2).astype(BF)
    valid = (jnp.arange(length, dtype=jnp.int32) < length - pad_length[0]).astype(F32)[:, None]
    cosine, sine = (jnp.asarray(t) for t in angle_tables(length))

    mixed = dot(normed1, w_mix) + b_mix
    mixed = mixed.reshape(length, 3, heads_n, HEAD_DIM).transpose(1, 2, 0, 3)
    queries = turn(mixed[0], cosine, sine, 1.0).astype(BF)
    keys = turn(mixed[1], cosine, sine, 1.0).astype(BF)
    values = mixed[2].astype(BF)
    d_heads = (dot_nt(dy, w_proj) * valid).astype(BF)
    d_heads = d_heads.reshape(length, heads_n, HEAD_DIM).transpose(1, 0, 2)
    heads, d_q, d_k, d_v = attention(queries, keys, values, d_heads, segments)
    attn_rows = (heads.transpose(1, 0, 2).reshape(length, wide).astype(F32) * valid).astype(BF)
    d_mixed = jnp.stack(
        [
            turn(d_q.astype(F32), cosine, sine, -1.0).astype(BF),
            turn(d_k.astype(F32), cosine, sine, -1.0).astype(BF),
            d_v,
        ]
    )
    d_mixed = d_mixed.transpose(2, 0, 1, 3).reshape(length, 3 * wide)

    upward = dot(normed2, w_rise) + b_rise
    active = jax.nn.gelu(upward, approximate=False).astype(BF)
    slope = 0.5 * (1 + lax.erf(upward * (0.5**0.5))) + upward * jnp.exp(
        -0.5 * upward * upward
    ) * ((2 * np.pi) ** -0.5)
    d_up = (slope * dot_nt(dy, w_fall)).astype(BF)
    out_part = (dot(attn_rows, w_proj) + dot(active, w_fall)).astype(BF)
    d_n1 = dot_nt(d_mixed, w_mix)
    d_n2 = dot_nt(d_up, w_rise)
    back_part = (g1 * d_n1 + g2 * d_n2).astype(BF)

    g_mix = dot_t(normed1, d_mixed).astype(BF).reshape(dp_size, rows, 3 * wide)
    g_proj = dot_t(attn_rows, dy).astype(BF).reshape(dp_size // seq_size, rows, seq_size, wide)
    g_proj = g_proj.transpose(2, 0, 1, 3)
    g_rise = dot_t(normed2, d_up).astype(BF).reshape(dp_size, rows, dp_size * units)
    g_fall = dot_t(active, dy).astype(BF).reshape(dp_size, units, D)
    dyf = dy.astype(F32)
    vec_part = jnp.concatenate(
        [
            t.reshape(dp_size, -1)
            for t in (
                jnp.sum(d_n1 * n, axis=0),
                jnp.sum(d_n1, axis=0),
                jnp.sum(d_n2 * n, axis=0),
                jnp.sum(d_n2, axis=0),
                jnp.sum(dyf, axis=0),
                jnp.sum(d_up.astype(F32), axis=0),
            )
        ]
        + [jnp.broadcast_to(jnp.sum(d_mixed.astype(F32), axis=0)[None], (dp_size, 3 * wide))],
        axis=1,
    )
    part_len = vec_part.shape[1]
    vec_part = jnp.pad(vec_part, ((0, 0), (0, 2048 - part_len))).reshape(dp_size, 16, 128)
    out_sum, back_sum, f_mix, f_proj, f_rise, f_fall, f_vec = reduce_all(
        seq_size,
        dp_size,
        out_part.reshape(seq_size, tok, D),
        back_part.reshape(seq_size, tok, D),
        g_mix,
        g_proj,
        g_rise,
        g_fall,
        vec_part,
    )
    own_x = tokens[0].astype(F32)
    block_output = (own_x + out_sum + b_proj + b_fall).astype(BF)
    own_center = own_x - jnp.mean(own_x, axis=-1, keepdims=True)
    own_rstd = lax.rsqrt(jnp.mean(own_center * own_center, axis=-1, keepdims=True) + EPS)
    own_n = own_center * own_rstd
    back = own_rstd * (
        back_sum
        - jnp.mean(back_sum, axis=-1, keepdims=True)
        - own_n * jnp.mean(back_sum * own_n, axis=-1, keepdims=True)
    )
    input_grad = (cotangent[0].astype(F32) + back).astype(BF)
    f_mix = f_mix.reshape(seq_size, rows, 3, heads_n, HEAD_DIM)
    f_mix = f_mix.transpose(1, 0, 3, 2, 4).reshape(rows, 3 * D).astype(F32)
    f_proj = f_proj.transpose(1, 0, 2).reshape(rows, D).astype(F32)
    f_rise = f_rise.reshape(seq_size, rows, dp_size, units)
    f_rise = f_rise.transpose(1, 2, 0, 3).reshape(rows, FF).astype(F32)
    f_fall = f_fall.reshape(seq_size * units, D).astype(F32)
    f_vec = f_vec.reshape(seq_size, 2048)[:, :part_len]
    norm_sums = jnp.sum(f_vec[:, : 4 * rows], axis=0)
    column = f_vec[0, 4 * rows : 5 * rows]
    f_b_rise = f_vec[:, 5 * rows : 5 * rows + units].reshape(seq_size * units)
    f_b_mix = f_vec[:, 5 * rows + units :].reshape(seq_size, 3, heads_n, HEAD_DIM)
    f_b_mix = f_b_mix.transpose(0, 2, 1, 3).reshape(dp_size, 3 * rows)
    f_b_mix = lax.dynamic_index_in_dim(f_b_mix, dp, 0, keepdims=False)
    return (
        block_output[None],
        input_grad[None],
        norm_sums[:rows],
        norm_sums[rows : 2 * rows],
        norm_sums[2 * rows : 3 * rows],
        norm_sums[3 * rows :],
        f_mix,
        f_b_mix,
        f_proj,
        column,
        f_rise,
        f_b_rise,
        f_fall,
        column,
    )


def solution(mesh):
    rows = P("dp", "seq", None)
    weight = P("dp", None)
    vector = P("dp")
    return jax.shard_map(
        shards,
        mesh=mesh,
        in_specs=(rows, rows)
        + (vector,) * 4
        + (weight, vector) * 4
        + (P("dp", "seq"), vector),
        out_specs=(rows, rows) + (vector,) * 4 + (weight, vector) * 4,
        check_vma=False,
    )
```

```python
import functools

import jax
import jax.numpy as jnp
import numpy as np
from jax import lax
from jax.experimental import pallas as pl
from jax.experimental.pallas import tpu as pltpu
from jax.sharding import PartitionSpec as P

D = 1024
HEADS = 16
HEAD_DIM = 64
ROT = 16
FF = 4096
EPS = 1e-05
BASE = 10000.0
NEG = -1e30
MESH = pl.DeviceIdType.MESH
BF = jnp.bfloat16
F32 = jnp.float32


def ring_pos(dev, size):
    return (dev // 2) * (1 - dev % 2) + (size - 1 - dev // 2) * (dev % 2)


def ring_dev(pos, size):
    high = pos // (size // 2)
    return (1 - high) * 2 * pos + high * (2 * (size - 1 - pos) + 1)


class Place:
    def __init__(self, seq_size, dp_size):
        self.seq_size, self.dp_size = seq_size, dp_size
        self.seq = lax.axis_index("seq")
        self.dp = lax.axis_index("dp")
        self.pos = ring_pos(self.dp, dp_size)
        self.half = dp_size // 2
        self.pairs = seq_size // 2
        self.core = self.seq % 2
        self.pair = self.seq // 2
        self.sibling = self.pair * 2 + 1 - self.core

    def ring(self, offset):
        return ring_dev((self.pos + offset + self.dp_size) % self.dp_size, self.dp_size)

    def dp_peer(self, step):
        return (self.dp + step + self.dp_size) % self.dp_size

    def pair_peer(self, step):
        return ((self.pair + step + self.pairs) % self.pairs) * 2 + self.core

    def across_source(self, step):
        return ((self.pair - step + self.pairs) % self.pairs) * 2 + 1 - self.core

    def seq_peer(self, step):
        return (self.seq + step + self.seq_size) % self.seq_size

    def greet(self):
        barrier = pltpu.get_barrier_semaphore()
        for step in range(1, self.dp_size):
            pl.semaphore_signal(
                barrier, inc=1, device_id={"dp": self.dp_peer(step)}, device_id_type=MESH
            )
        for step in range(1, self.seq_size):
            pl.semaphore_signal(
                barrier, inc=1, device_id={"seq": self.seq_peer(step)}, device_id_type=MESH
            )
        pl.semaphore_wait(barrier, self.dp_size - 1 + self.seq_size - 1)


def send(src, dst, sems, index, target):
    return pltpu.make_async_remote_copy(
        src_ref=src,
        dst_ref=dst,
        send_sem=sems.at[0, index],
        recv_sem=sems.at[1, index],
        device_id=target,
        device_id_type=MESH,
    )


def halves(ref):
    rows = ref.shape[0]
    columns = ref.shape[1]
    if rows % 32 == 0:
        return ref.at[pl.ds(0, rows // 2)], ref.at[pl.ds(rows // 2, rows // 2)]
    return ref.at[:, pl.ds(0, columns // 2)], ref.at[:, pl.ds(columns // 2, columns // 2)]


class RingGather:
    def __init__(self, place, full, sems):
        self.place, self.full, self.sems = place, full, sems

    def piece(self, offset, step, way):
        block = self.full.at[self.place.ring(offset)]
        return block if step < self.place.half else halves(block)[way]

    def copies(self, step):
        place = self.place
        right = self.piece(-(step - 1), step, 0)
        left = self.piece(step - 1, step, 1)
        index = 2 * (step - 1)
        return (
            send(right, right, self.sems, index, {"dp": place.ring(1)}),
            send(left, left, self.sems, index + 1, {"dp": place.ring(-1)}),
        )

    def arrivals(self, step):
        right = self.piece(-step, step, 0)
        left = self.piece(step, step, 1)
        index = 2 * (step - 1)
        return (
            send(right, right, self.sems, index, {"dp": self.place.ring(1)}),
            send(left, left, self.sems, index + 1, {"dp": self.place.ring(-1)}),
        )

    def tick(self, step):
        if step > 1:
            for copy in self.arrivals(step - 1):
                copy.wait_recv()
        if step <= self.place.half:
            for copy in self.copies(step):
                copy.start()

    def finish(self):
        for step in range(1, self.place.half + 1):
            for copy in self.copies(step):
                copy.wait_send()


class RingReduce:
    def __init__(self, place, parts, arrived, sems):
        self.place, self.parts, self.arrived, self.sems = place, parts, arrived, sems

    def piece(self, ref, step, way):
        return ref if step > 1 else halves(ref)[way]

    def copies(self, step):
        place = self.place
        away = place.half - step + 1
        index = 2 * (step - 1)
        out = []
        for way, (offset, target) in enumerate(((away, 1), (-away, -1))):
            src = self.piece(self.parts.at[place.ring(offset)], step, way)
            dst = self.piece(self.arrived.at[way, step - 1], step, way)
            out.append(send(src, dst, self.sems, index + way, {"dp": place.ring(target)}))
        return out

    def tick(self, step):
        place = self.place
        if step > 1:
            for way, copy in enumerate(self.copies(step - 1)):
                copy.wait_recv()
                away = (place.half - step + 1) * (1 - 2 * way)
                held = self.piece(self.parts.at[place.ring(away)], step - 1, way)
                came = self.piece(self.arrived.at[way, step - 2], step - 1, way)
                held[...] = (held[...].astype(F32) + came[...].astype(F32)).astype(held.dtype)
        if step <= place.half:
            for copy in self.copies(step):
                copy.start()

    def finish(self):
        for step in range(1, self.place.half + 1):
            for copy in self.copies(step):
                copy.wait_send()

    def own(self):
        return self.parts.at[self.place.dp]


class SeqGather:
    def __init__(self, place, full, sems):
        self.place, self.full, self.sems = place, full, sems

    def direct(self, step):
        block = self.full.at[self.place.seq]
        return send(block, block, self.sems, step, {"seq": self.place.pair_peer(step)})

    def arrival(self, step):
        block = self.full.at[self.place.pair_peer(-step)]
        return send(block, block, self.sems, step, {"seq": self.place.pair_peer(step)})

    def across(self, step):
        block = self.full.at[self.place.pair_peer(-step)]
        return send(
            block, block, self.sems, self.place.pairs + step, {"seq": self.place.sibling}
        )

    def across_arrival(self, step):
        place = self.place
        block = self.full.at[place.across_source(step)]
        return send(block, block, self.sems, place.pairs + step, {"seq": place.sibling})

    def begin(self):
        for step in range(1, self.place.pairs):
            self.direct(step).start()
        self.across(0).start()

    def forward(self):
        for step in range(1, self.place.pairs):
            self.arrival(step).wait_recv()
            self.across(step).start()

    def across_arrived(self, step):
        self.across_arrival(step).wait_recv()

    def sent(self):
        for step in range(1, self.place.pairs):
            self.direct(step).wait_send()
        for step in range(self.place.pairs):
            self.across(step).wait_send()

    def finish(self):
        for step in range(self.place.pairs):
            self.across_arrived(step)
        self.sent()


class SeqReduce:
    def __init__(self, place, parts, crossed, arrived, sems):
        self.place, self.parts, self.crossed, self.arrived = place, parts, crossed, arrived
        self.sems = sems

    def over(self, index):
        place = self.place
        return send(
            self.parts.at[index * 2 + 1 - place.core],
            self.crossed.at[index],
            self.sems,
            index,
            {"seq": place.sibling},
        )

    def direct(self, step):
        place = self.place
        return send(
            self.parts.at[place.pair_peer(step)],
            self.arrived.at[step],
            self.sems,
            place.pairs + step,
            {"seq": place.pair_peer(step)},
        )

    def begin(self):
        for index in range(self.place.pairs):
            self.over(index).start()

    def middle(self):
        place = self.place
        for index in range(place.pairs):
            self.over(index).wait_recv()
            held = self.parts.at[index * 2 + place.core]
            held[...] = (held[...].astype(F32) + self.crossed[index].astype(F32)).astype(held.dtype)
        for step in range(1, place.pairs):
            self.direct(step).start()

    def total(self):
        place = self.place
        total = self.parts.at[place.seq][...].astype(F32)
        for step in range(1, place.pairs):
            self.direct(step).wait_recv()
            total = total + self.arrived[step].astype(F32)
        return total

    def finish(self):
        for index in range(self.place.pairs):
            self.over(index).wait_send()
        for step in range(1, self.place.pairs):
            self.direct(step).wait_send()


class DpSpread:
    def __init__(self, place, src_of, full, sems):
        self.place, self.src_of, self.full, self.sems = place, src_of, full, sems

    def copy(self, step):
        place = self.place
        peer = place.dp_peer(step)
        return send(self.src_of(peer), self.full.at[place.dp], self.sems, step, {"dp": peer})

    def arrival(self, step):
        place = self.place
        source = place.dp_peer(-step)
        return send(
            self.src_of(source), self.full.at[source], self.sems, step, {"dp": place.dp_peer(step)}
        )

    def begin(self):
        for step in range(1, self.place.dp_size):
            self.copy(step).start()

    def finish(self):
        for step in range(1, self.place.dp_size):
            self.arrival(step).wait_recv()
        for step in range(1, self.place.dp_size):
            self.copy(step).wait_send()


def sems_of(count):
    return pltpu.SemaphoreType.DMA((2, count))


def gather_kernel(seq_size, dp_size, *refs):
    (x_ref, dy_ref, mix_ref, proj_ref, rise_ref, fall_ref, vec_ref, seg_ref) = refs[:8]
    (x_all, dy_all, mix_all, proj_cols, rise_all, fall_all, vec_all, seg_all, proj_all) = refs[8:17]
    (x_sems, dy_sems, mix_sems, proj_sems, rise_sems, fall_sems, vec_sems, seg_sems, swap_sems, own_sems) = refs[17:]
    place = Place(seq_size, dp_size)
    own = [
        pltpu.make_async_copy(src, dst, own_sems.at[i])
        for i, (src, dst) in enumerate(
            (
                (x_ref, x_all.at[place.seq]),
                (dy_ref, dy_all.at[place.seq]),
                (mix_ref, mix_all.at[place.dp]),
                (proj_ref, proj_cols.at[place.dp]),
                (rise_ref, rise_all.at[place.dp]),
                (fall_ref, fall_all.at[place.dp]),
                (vec_ref, vec_all.at[place.dp]),
                (seg_ref, seg_all.at[place.seq]),
            )
        )
    ]
    for copy in own:
        copy.start()
    place.greet()
    for copy in own:
        copy.wait()
    x_move = SeqGather(place, x_all, x_sems)
    dy_move = SeqGather(place, dy_all, dy_sems)
    seg_move = SeqGather(place, seg_all, seg_sems)
    vec_move = DpSpread(place, lambda peer: vec_ref, vec_all, vec_sems)
    mix_move = RingGather(place, mix_all, mix_sems)
    proj_move = RingGather(place, proj_cols, proj_sems)
    rise_move = RingGather(place, rise_all, rise_sems)
    fall_move = RingGather(place, fall_all, fall_sems)
    x_move.begin()
    seg_move.begin()
    vec_move.begin()
    half = place.half
    for step in range(1, half + 1):
        mix_move.tick(step)
        proj_move.tick(step)
    x_move.forward()
    seg_move.forward()
    dy_move.begin()
    mix_move.tick(half + 1)
    proj_move.tick(half + 1)
    rise_move.tick(1)
    fall_move.tick(1)
    rows = proj_cols.shape[0] * proj_cols.shape[1] // seq_size
    each = rows // proj_cols.shape[1]
    swaps = []
    for step in range(1, seq_size):
        peer = place.seq_peer(step)
        swaps.append(
            send(
                proj_cols.at[pl.ds(peer * each, each)],
                proj_all.at[place.seq],
                swap_sems,
                step,
                {"seq": peer},
            )
        )
    for copy in swaps:
        copy.start()
    mine = pltpu.make_async_copy(
        proj_cols.at[pl.ds(place.seq * each, each)], proj_all.at[place.seq], own_sems.at[0]
    )
    mine.start()
    for step in range(2, half + 2):
        rise_move.tick(step)
        fall_move.tick(step)
        if step == 3:
            dy_move.forward()
    mine.wait()
    for step in range(1, seq_size):
        source = place.seq_peer(-step)
        send(
            proj_cols.at[pl.ds(source * each, each)],
            proj_all.at[source],
            swap_sems,
            step,
            {"seq": place.seq_peer(step)},
        ).wait_recv()
    for copy in swaps:
        copy.wait_send()
    for move in (x_move, dy_move, seg_move, vec_move, mix_move, proj_move, rise_move, fall_move):
        move.finish()


def gather_all(seq_size, dp_size, x, dy, mix, proj, rise, fall, vec, seg):
    half = dp_size // 2
    pairs = seq_size // 2

    def lead(count, like):
        return jax.ShapeDtypeStruct((count,) + like.shape, like.dtype)

    each = dp_size // seq_size
    any_spec = pl.BlockSpec(memory_space=pl.ANY)
    return pl.pallas_call(
        functools.partial(gather_kernel, seq_size, dp_size),
        out_shape=(
            lead(seq_size, x),
            lead(seq_size, dy),
            lead(dp_size, mix),
            lead(dp_size, proj),
            lead(dp_size, rise),
            lead(dp_size, fall),
            lead(dp_size, vec),
            lead(seq_size, seg),
            jax.ShapeDtypeStruct((seq_size, each) + proj.shape, proj.dtype),
        ),
        in_specs=[any_spec] * 8,
        out_specs=[any_spec] * 9,
        scratch_shapes=[
            sems_of(2 * pairs),
            sems_of(2 * pairs),
            sems_of(2 * half),
            sems_of(2 * half),
            sems_of(2 * half),
            sems_of(2 * half),
            sems_of(dp_size),
            sems_of(2 * pairs),
            sems_of(seq_size),
            pltpu.SemaphoreType.DMA((8,)),
        ],
        compiler_params=pltpu.CompilerParams(collective_id=0, has_side_effects=True),
    )(x, dy, mix, proj, rise, fall, vec, seg)


def reduce_kernel(seq_size, dp_size, *refs):
    (out_ref, back_ref, mix_ref, proj_ref, rise_ref, fall_ref, vec_ref), refs = refs[:7], refs[7:]
    (out_sum, back_sum, mix_fin, proj_fin, rise_fin, fall_fin, vec_fin), refs = refs[:7], refs[7:]
    (
        out_cross,
        out_came,
        back_cross,
        back_came,
        proj_full,
        mix_came,
        proj_came,
        rise_came,
        fall_came,
        vec_came,
        out_sems,
        back_sems,
        swap_sems,
        mix_sems,
        proj_sems,
        rise_sems,
        fall_sems,
        vec_sems,
        mix_fs,
        proj_fs,
        rise_fs,
        fall_fs,
        vec_fs,
    ) = refs
    place = Place(seq_size, dp_size)
    each = dp_size // seq_size
    half = place.half
    place.greet()

    def mine(index):
        return proj_full.at[pl.ds(index * each, each)]

    def swap(step):
        peer = place.seq_peer(step)
        return send(proj_ref.at[peer], mine(place.seq), swap_sems, step, {"seq": peer})

    def swap_arrival(step):
        source = place.seq_peer(-step)
        target = {"seq": place.seq_peer(step)}
        return send(proj_ref.at[source], mine(source), swap_sems, step, target)

    for step in range(1, seq_size):
        swap(step).start()
    mine(place.seq)[...] = proj_ref[place.seq]
    mix = RingReduce(place, mix_ref, mix_came, mix_sems)
    proj = RingReduce(place, proj_full, proj_came, proj_sems)
    rise = RingReduce(place, rise_ref, rise_came, rise_sems)
    fall = RingReduce(place, fall_ref, fall_came, fall_sems)
    out = SeqReduce(place, out_ref, out_cross, out_came, out_sems)
    back = SeqReduce(place, back_ref, back_cross, back_came, back_sems)
    vec = DpSpread(place, lambda peer: vec_ref.at[peer], vec_came, vec_sems)
    mix.tick(1)
    rise.tick(1)
    out.begin()
    back.begin()
    vec.begin()
    for step in range(1, seq_size):
        swap_arrival(step).wait_recv()
    proj.tick(1)
    fall.tick(1)
    out.middle()
    back.middle()
    for step in range(2, half + 2):
        for move in (mix, rise, proj, fall):
            move.tick(step)
    finals = []
    for move, fin, fin_sems in (
        (mix, mix_fin, mix_fs),
        (rise, rise_fin, rise_fs),
        (proj, proj_fin, proj_fs),
        (fall, fall_fin, fall_fs),
    ):
        fin[place.seq] = move.parts[place.dp]
        gather = SeqGather(place, fin, fin_sems)
        gather.begin()
        finals.append(gather)
    vec_came[place.dp] = vec_ref[place.dp]
    vec.finish()
    vec_fin[place.seq] = jnp.sum(vec_came[...], axis=0)
    gather = SeqGather(place, vec_fin, vec_fs)
    gather.begin()
    finals.append(gather)
    out_sum[...] = out.total()
    back_sum[...] = back.total()
    for gather in finals:
        gather.forward()
    for gather in finals:
        gather.finish()
    for step in range(1, seq_size):
        swap(step).wait_send()
    for move in (mix, rise, proj, fall, out, back):
        move.finish()


def reduce_all(seq_size, dp_size, out, back, mix, proj, rise, fall, vec):
    half = dp_size // 2
    pairs = seq_size // 2
    each = dp_size // seq_size

    def fin(like):
        return jax.ShapeDtypeStruct((seq_size,) + like.shape[1:], like.dtype)

    def came(like):
        return pltpu.VMEM((2, half) + like.shape[1:], like.dtype)

    proj_blocks = jax.ShapeDtypeStruct((dp_size,) + proj.shape[2:], proj.dtype)
    vmem = pl.BlockSpec(memory_space=pltpu.VMEM)
    return pl.pallas_call(
        functools.partial(reduce_kernel, seq_size, dp_size),
        out_shape=(
            jax.ShapeDtypeStruct(out.shape[1:], F32),
            jax.ShapeDtypeStruct(back.shape[1:], F32),
            fin(mix),
            fin(proj_blocks),
            fin(rise),
            fin(fall),
            fin(vec),
        ),
        in_specs=[vmem] * 7,
        out_specs=[vmem] * 7,
        scratch_shapes=[
            pltpu.VMEM((pairs,) + out.shape[1:], BF),
            pltpu.VMEM((pairs,) + out.shape[1:], BF),
            pltpu.VMEM((pairs,) + back.shape[1:], BF),
            pltpu.VMEM((pairs,) + back.shape[1:], BF),
            pltpu.VMEM(proj_blocks.shape, BF),
            came(mix),
            came(proj_blocks),
            came(rise),
            came(fall),
            pltpu.VMEM(vec.shape, F32),
            sems_of(2 * pairs),
            sems_of(2 * pairs),
            sems_of(seq_size),
            sems_of(2 * half),
            sems_of(2 * half),
            sems_of(2 * half),
            sems_of(2 * half),
            sems_of(dp_size),
            sems_of(2 * pairs),
            sems_of(2 * pairs),
            sems_of(2 * pairs),
            sems_of(2 * pairs),
            sems_of(2 * pairs),
        ],
        compiler_params=pltpu.CompilerParams(
            collective_id=1, has_side_effects=True, vmem_limit_bytes=56 * 2**20
        ),
    )(out, back, mix, proj, rise, fall, vec)


def angle_tables(length):
    frequency = BASE ** (-np.arange(0, ROT, 2).astype(np.float32) / np.float32(ROT))
    angles = np.arange(length, dtype=np.float32)[:, None] * frequency.astype(np.float32)[None, :]
    return np.cos(angles).astype(np.float32), np.sin(angles).astype(np.float32)


def turn(piece, cosine, sine, sign):
    half = ROT // 2
    low, high = piece[..., :half], piece[..., half:ROT]
    return jnp.concatenate(
        [low * cosine - sign * high * sine, high * cosine + sign * low * sine, piece[..., ROT:]],
        axis=-1,
    )


TILE = 256

def mm(a, b, dims):
    return lax.dot_general(a, b, ((dims[0], dims[1]), ((), ())), preferred_element_type=F32)

def nn(a, b):
    return mm(a, b, ((1,), (0,)))

def nt(a, b):
    return mm(a, b, ((1,), (1,)))

def tn(a, b):
    return mm(a, b, ((0,), (0,)))

def fold(count, body, init):
    if isinstance(count, int):
        for index in range(count):
            init = body(index, init)
        return init
    return lax.fori_loop(0, count, body, init)

def rows_of(index):
    start = index * TILE
    return pl.ds(start if isinstance(start, int) else pl.multiple_of(start, TILE), TILE)

def attend_block(head, block, refs):
    q_ref, k_ref, v_ref, g_ref, kt_ref, vt_ref, s_ref, p_ref, ht_ref, dqt_ref, dk_ref, dv_ref = refs
    here = rows_of(block)
    span = block + 1
    dims = pl.ds(pl.multiple_of(head * HEAD_DIM, HEAD_DIM), HEAD_DIM)
    query = q_ref[head, here, :]
    grad = g_ref[head, here, :]

    def score(index, top):
        tile = nt(k_ref[head, rows_of(index), :], query)
        if isinstance(index, int) and isinstance(block, int) and index < block:
            keep = tile
        else:
            key = lax.broadcasted_iota(jnp.int32, (TILE, TILE), 0) + (index - block) * TILE
            place = lax.broadcasted_iota(jnp.int32, (TILE, TILE), 1)
            keep = jnp.where(key <= place, tile, NEG)
        s_ref[index] = keep
        return jnp.maximum(top, jnp.max(keep, axis=0, keepdims=True))

    top = fold(span, score, jnp.full((1, TILE), 2 * NEG, F32))

    def raise_(index, total):
        raised = jnp.exp(s_ref[index] - top)
        s_ref[index] = raised
        return total + jnp.sum(raised, axis=0, keepdims=True)

    total = fold(span, raise_, jnp.zeros((1, TILE), F32))
    share = 1.0 / total

    def weigh(index, carried):
        heads, delta = carried
        weights = s_ref[index] * share
        s_ref[index] = weights
        weights_b = weights.astype(BF)
        d_weights = nt(v_ref[head, rows_of(index), :], grad)
        p_ref[index] = d_weights
        dv_ref[head, rows_of(index), :] += nn(weights_b, grad)
        heads = heads + nn(vt_ref[dims, rows_of(index)], weights_b)
        return heads, delta + jnp.sum(weights * d_weights, axis=0, keepdims=True)

    heads, delta = fold(
        span, weigh, (jnp.zeros((HEAD_DIM, TILE), F32), jnp.zeros((1, TILE), F32))
    )
    ht_ref[dims, here] = heads

    def back(index, d_query):
        d_scores = (s_ref[index] * (p_ref[index] - delta)).astype(BF)
        dk_ref[head, rows_of(index), :] += nn(d_scores, query)
        return d_query + nn(kt_ref[dims, rows_of(index)], d_scores)

    dqt_ref[dims, here] = fold(span, back, jnp.zeros((HEAD_DIM, TILE), F32))

def attend(heads_n, length, refs):
    dk_ref, dv_ref = refs[-2:]
    dk_ref[...] = jnp.zeros(dk_ref.shape, F32)
    dv_ref[...] = jnp.zeros(dv_ref.shape, F32)
    blocks = length // TILE

    @pl.loop(0, heads_n)
    def _(head):
        if blocks <= 4:
            for block in range(blocks):
                attend_block(head, block, refs)
        else:
            @pl.loop(0, blocks)
            def _(block):
                attend_block(head, block, refs)

def attend_kernel(H, L, q, k, v, g, kt, vt, ht, dqt, dk, dv, s_ref, p_ref):
    attend(H, L, (q, k, v, g, kt, vt, s_ref, p_ref, ht, dqt, dk, dv))

def attention_call(q, k, v, g, kt, vt):
    H, L, _ = q.shape
    vm = pl.BlockSpec(memory_space=pltpu.VMEM)
    nb = L // TILE
    return pl.pallas_call(functools.partial(attend_kernel, H, L),
        out_shape=(jax.ShapeDtypeStruct((H*64, L), F32), jax.ShapeDtypeStruct((H*64, L), F32), jax.ShapeDtypeStruct((H, L, 128), F32), jax.ShapeDtypeStruct((H, L, 128), F32)),
        in_specs=[vm]*6, out_specs=[vm]*4,
        scratch_shapes=[pltpu.VMEM((nb, TILE, TILE), F32), pltpu.VMEM((nb, TILE, TILE), F32)],
        compiler_params=pltpu.CompilerParams(vmem_limit_bytes=56 * 2**20))(q, k, v, g, kt, vt)

def prep(queries, keys, values, d_heads, segments):
    seg = segments[:, None] == jnp.arange(64)[None, :]
    e = jnp.broadcast_to(seg.astype(BF)[None], queries.shape)
    f = jnp.broadcast_to(jnp.where(seg, 0.0, NEG).astype(BF)[None], queries.shape)
    lane = jnp.arange(64)
    f = jnp.where(lane < 4, f, 0).astype(BF)
    qa = jnp.concatenate([(queries.astype(F32) * 0.125).astype(BF), e], -1)
    ka = jnp.concatenate([keys, f], -1)
    z = jnp.zeros_like(values)
    va = jnp.concatenate([values, z], -1)
    ga = jnp.concatenate([d_heads, z], -1)
    kt = keys.transpose(0, 2, 1).reshape(-1, keys.shape[1])
    vt = values.transpose(0, 2, 1).reshape(-1, keys.shape[1])
    return qa, ka, va, ga, kt, vt

def attention(queries, keys, values, d_heads, segments):
    H, L, _ = queries.shape
    ht, dqt, dk, dv = attention_call(*prep(queries, keys, values, d_heads, segments))

    def back(t):
        return t.reshape(H, 64, L).transpose(0, 2, 1)

    return back(ht).astype(BF), (back(dqt) * 0.125).astype(BF), dk[..., :64].astype(BF), dv[..., :64].astype(BF)


def dot(a, b):
    return jnp.dot(a, b, preferred_element_type=F32)


def dot_t(a, b):
    return lax.dot_general(a, b, (((0,), (0,)), ((), ())), preferred_element_type=F32)


def dot_nt(a, b):
    return lax.dot_general(a, b, (((1,), (1,)), ((), ())), preferred_element_type=F32)


LANES = 128


def resident_fits(seq_size, dp_size, tok):
    return (
        D // dp_size == LANES
        and FF // dp_size // seq_size == LANES
        and HEADS // seq_size == 4
        and tok * seq_size <= 1024
        and tok % TILE == 0
    )


def rows_at(ref, index, count):
    return ref.at[pl.ds(pl.multiple_of(index * count, count), count)]


def columns_at(ref, index, count):
    return ref.at[:, pl.ds(pl.multiple_of(index * count, count), count)]


class Flat:
    def __init__(self, ref, count, by_columns=False):
        self.ref, self.count, self.by_columns = ref, count, by_columns

    @property
    def at(self):
        return self

    def __getitem__(self, index):
        if self.by_columns:
            return columns_at(self.ref, index, self.count)
        return rows_at(self.ref, index, self.count)


def lanes_like(shape):
    return lax.broadcasted_iota(jnp.int32, shape, len(shape) - 1)


def head_part(values, start):
    tile = values[:, start // LANES * LANES : start // LANES * LANES + LANES]
    return tile if start % LANES == 0 else pltpu.roll(tile, HEAD_DIM, 1)


def spin(tile, cosine, sine):
    lane = lanes_like(tile.shape)
    partner = jnp.where(lane < ROT // 2, pltpu.roll(tile, LANES - ROT // 2, 1), pltpu.roll(tile, ROT // 2, 1))
    return tile * cosine + partner * sine


def attend_head(head, block, refs):
    q_ref, k_ref, v_ref, g_ref, kt_ref, vt_ref, s_ref, p_ref, ht_ref, dqt_ref, dk_ref, dv_ref = refs
    here = pl.ds(block * TILE, TILE)
    wide = pl.ds(head * LANES, LANES)
    dims = pl.ds(head * HEAD_DIM, HEAD_DIM)
    query = q_ref[here, wide]
    grad = g_ref[here, wide]
    span = block + 1
    top = jnp.full((1, TILE), 2 * NEG, F32)
    for index in range(span):
        tile = nt(k_ref[pl.ds(index * TILE, TILE), wide], query)
        if index == block:
            key = lax.broadcasted_iota(jnp.int32, (TILE, TILE), 0)
            place = lax.broadcasted_iota(jnp.int32, (TILE, TILE), 1)
            tile = jnp.where(key <= place, tile, NEG)
        s_ref[index] = tile
        top = jnp.maximum(top, jnp.max(tile, axis=0, keepdims=True))
    total = jnp.zeros((1, TILE), F32)
    for index in range(span):
        raised = jnp.exp(s_ref[index] - top)
        s_ref[index] = raised
        total = total + jnp.sum(raised, axis=0, keepdims=True)
    share = 1.0 / total
    delta = jnp.zeros((1, TILE), F32)
    heads = jnp.zeros((HEAD_DIM, TILE), F32)
    for index in range(span):
        there = pl.ds(index * TILE, TILE)
        weights = s_ref[index] * share
        s_ref[index] = weights
        weights_b = weights.astype(BF)
        d_weights = nt(v_ref[there, wide], grad)
        p_ref[index] = d_weights
        d_value = nn(weights_b, grad)
        dv_ref[head, there, :] = d_value if index == block else dv_ref[head, there, :] + d_value
        heads = heads + nn(vt_ref[dims, there], weights_b)
        delta = delta + jnp.sum(weights * d_weights, axis=0, keepdims=True)
    ht_ref[dims, here] = heads
    d_query = jnp.zeros((HEAD_DIM, TILE), F32)
    for index in range(span):
        there = pl.ds(index * TILE, TILE)
        d_scores = (s_ref[index] * (p_ref[index] - delta)).astype(BF)
        d_key = nn(d_scores, query)
        dk_ref[head, there, :] = d_key if index == block else dk_ref[head, there, :] + d_key
        d_query = d_query + nn(kt_ref[dims, there], d_scores)
    dqt_ref[dims, here] = d_query


RESIDENT_NAMES = (
    "x_own",
    "dy_own",
    "w_mix_own",
    "w_proj_own",
    "w_rise_own",
    "w_fall_own",
    "vec_own",
    "hot_own",
    "pad",
    "cos",
    "sin",
    "block_out",
    "input_grad",
    "mix_fin",
    "proj_fin",
    "rise_fin",
    "fall_fin",
    "norm_out",
    "col_out",
    "b_mix_out",
    "b_rise_out",
    "x",
    "dy",
    "hot",
    "w_mix",
    "w_proj_cols",
    "w_proj",
    "w_rise",
    "w_fall",
    "vec_all",
    "rows",
    "normed1",
    "normed2",
    "stat",
    "qk",
    "vg",
    "kt",
    "vt",
    "s",
    "p",
    "ht",
    "dqt",
    "dk",
    "dv",
    "attn",
    "d_mixed",
    "out_part",
    "back_part",
    "g_mix",
    "g_proj",
    "g_proj_cols",
    "g_rise",
    "g_fall",
    "c_mix",
    "c_proj",
    "c_rise",
    "c_fall",
    "out_cross",
    "out_came",
    "back_cross",
    "back_came",
    "rise_stage",
    "sums",
    "vec_part",
    "vec_came",
    "vec_fin",
    "m_x",
    "m_dy",
    "m_hot",
    "m_vec",
    "m_mix",
    "m_proj",
    "m_rise",
    "m_fall",
    "m_swap",
    "m_own",
    "m_swap2",
    "m_rmix",
    "m_rproj",
    "m_rrise",
    "m_rfall",
    "m_out",
    "m_back",
    "m_vec2",
    "m_fmix",
    "m_fproj",
    "m_frise",
    "m_ffall",
    "m_fvec",
)


class Names:
    def __init__(self, refs):
        for name, ref in zip(RESIDENT_NAMES, refs, strict=True):
            setattr(self, name, ref)


def resident_kernel(seq_size, dp_size, *refs):
    r = Names(refs)
    place = Place(seq_size, dp_size)
    half = place.half
    tok = r.x_own.shape[0]
    length = r.x.shape[0]
    wide = r.w_proj.shape[0]
    mixed_wide = 3 * wide
    units = LANES
    each = dp_size // seq_size
    heads_n = wide // HEAD_DIM
    blocks = length // TILE

    own = {}

    def bring(name, src, dst):
        copy = pltpu.make_async_copy(src, dst, r.m_own.at[len(own)])
        copy.start()
        own[name] = copy

    bring("mix", columns_at(r.w_mix_own, place.seq, mixed_wide), rows_at(r.w_mix, place.dp, LANES))
    bring("proj", columns_at(r.w_proj_own, place.seq, wide), rows_at(r.w_proj_cols, place.dp, LANES))
    bring("x", r.x_own, rows_at(r.x, place.seq, tok))
    bring("hot", r.hot_own, rows_at(r.hot, place.seq, tok))
    bring("dy", r.dy_own, rows_at(r.dy, place.seq, tok))
    for index in range(dp_size):
        bring(
            ("rise", index),
            columns_at(r.w_rise_own, index * seq_size + place.seq, units),
            rows_at(r.w_rise, place.dp, LANES).at[:, pl.ds(index * units, units)],
        )
    bring("fall", rows_at(r.w_fall_own, place.seq, units), rows_at(r.w_fall, place.dp, units))
    r.vec_all[place.dp] = r.vec_own[...]

    mix = RingGather(place, Flat(r.w_mix, LANES), r.m_mix)
    proj = RingGather(place, Flat(r.w_proj_cols, LANES), r.m_proj)
    rise = RingGather(place, Flat(r.w_rise, LANES), r.m_rise)
    fall = RingGather(place, Flat(r.w_fall, units), r.m_fall)
    x_move = SeqGather(place, Flat(r.x, tok), r.m_x)
    dy_move = SeqGather(place, Flat(r.dy, tok), r.m_dy)
    hot_move = SeqGather(place, Flat(r.hot, tok), r.m_hot)
    vec_move = DpSpread(place, lambda peer: r.vec_own, r.vec_all, r.m_vec)

    place.greet()
    own["mix"].wait()
    own["proj"].wait()
    mix.tick(1)
    proj.tick(1)
    own["x"].wait()
    x_move.begin()
    own["hot"].wait()
    hot_move.begin()
    vec_move.begin()
    vec_move.finish()
    for index in range(dp_size):
        for row in range(6):
            r.rows[row : row + 1, index * LANES : (index + 1) * LANES] = r.vec_all[index, row : row + 1, :]
        r.rows[6:7, index * LANES : (index + 1) * LANES] = r.vec_all[index, pl.ds(9 + place.seq, 1), :]
    for index in range(each):
        for row in range(3):
            start = (index * 3 + row) * LANES
            r.rows[7:8, start : start + LANES] = r.vec_all[place.seq * each + index, 6 + row : 7 + row, :]

    chunk = 64

    def normalize(block):
        @pl.loop(0, tok // chunk)
        def _(step):
            here = pl.ds(pl.multiple_of(block * tok + step * chunk, chunk), chunk)
            values = r.x[here, :].astype(F32)
            mean = jnp.sum(values, axis=-1, keepdims=True) * (1.0 / D)
            center = values - mean
            rstd = lax.rsqrt(jnp.sum(center * center, axis=-1, keepdims=True) * (1.0 / D) + EPS)
            n = center * rstd
            r.normed1[here, :] = (n * r.rows[0:1, :] + r.rows[1:2, :]).astype(BF)
            r.normed2[here, :] = (n * r.rows[2:3, :] + r.rows[3:4, :]).astype(BF)
            lane = lanes_like((chunk, LANES))
            r.stat[here, :] = jnp.where(lane < HEAD_DIM, mean, rstd)

    def unit_rows(here):
        stat = r.stat[here, :]
        return (r.x[here, :].astype(F32) - stat[:, 0:1]) * stat[:, HEAD_DIM : HEAD_DIM + 1]

    normalize(place.seq)
    own["dy"].wait()
    mix.tick(2)
    proj.tick(2)
    x_move.across_arrived(0)
    normalize(place.sibling)
    mix.tick(3)
    proj.tick(3)
    x_move.forward()
    hot_move.forward()
    dy_move.begin()
    for step in range(1, place.pairs):
        normalize(place.pair_peer(-step))
    mix.tick(4)
    proj.tick(4)
    for index in range(dp_size):
        own["rise", index].wait()
    rise.tick(1)
    for step in range(1, place.pairs):
        x_move.across_arrived(step)
        normalize(place.across_source(step))
    for step in range(place.pairs):
        hot_move.across_arrived(step)
    mix.tick(5)
    proj.tick(5)

    def swap(step):
        peer = place.seq_peer(step)
        return send(
            rows_at(r.w_proj_cols, peer, wide),
            columns_at(r.w_proj, place.seq, wide),
            r.m_swap,
            step,
            {"seq": peer},
        )

    def swap_arrival(step):
        source = place.seq_peer(-step)
        return send(
            rows_at(r.w_proj_cols, source, wide),
            columns_at(r.w_proj, source, wide),
            r.m_swap,
            step,
            {"seq": place.seq_peer(step)},
        )

    for step in range(1, seq_size):
        swap(step).start()
    columns_at(r.w_proj, place.seq, wide)[...] = rows_at(r.w_proj_cols, place.seq, wide)[...]

    def column(ref, kind, head):
        start = kind * heads_n * LANES + head * LANES
        return (slice(None), slice(start, start + LANES))

    @pl.loop(0, blocks)
    def _(block):
        here = pl.ds(pl.multiple_of(block * TILE, TILE), TILE)
        mixed = nn(r.normed1[here, :], r.w_mix[...]) + r.rows[7:8, 0:mixed_wide]
        cosine, sine = r.cos[here, :], r.sin[here, :]
        lane = lanes_like((TILE, LANES))
        hot = r.hot[here, :].astype(F32)
        cold = jnp.where((lane >= HEAD_DIM) & (lane < HEAD_DIM + 4), (1.0 - hot) * NEG, 0.0)
        for head in range(heads_n):
            start = head * 3 * HEAD_DIM
            query = spin(head_part(mixed, start), cosine, sine) * HEAD_DIM**-0.5
            key = spin(head_part(mixed, start + HEAD_DIM), cosine, sine)
            value = head_part(mixed, start + 2 * HEAD_DIM)
            at = pl.ds(head * LANES, LANES)
            at_more = pl.ds((heads_n + head) * LANES, LANES)
            dims = pl.ds(head * HEAD_DIM, HEAD_DIM)
            r.qk[here, at] = jnp.where(lane < HEAD_DIM, query, hot).astype(BF)
            r.qk[here, at_more] = jnp.where(lane < HEAD_DIM, key, cold).astype(BF)
            r.vg[here, at] = jnp.where(lane < HEAD_DIM, value, 0.0).astype(BF)
            r.kt[dims, here] = key.T[:HEAD_DIM, :].astype(BF)
            r.vt[dims, here] = value.T[:HEAD_DIM, :].astype(BF)

    rise.tick(2)
    dy_move.forward()
    for step in range(1, seq_size):
        swap_arrival(step).wait_recv()
    for step in range(place.pairs):
        dy_move.across_arrived(step)
    padded = length - r.pad[0]

    @pl.loop(0, blocks)
    def _(block):
        here = pl.ds(pl.multiple_of(block * TILE, TILE), TILE)
        place_in = lax.broadcasted_iota(jnp.int32, (TILE, wide), 0) + block * TILE
        d_heads = jnp.where(place_in < padded, nt(r.dy[here, :], r.w_proj[...]), 0.0)
        for head in range(heads_n):
            at_more = pl.ds((heads_n + head) * LANES, LANES)
            r.vg[here, at_more] = head_part(d_heads, head * HEAD_DIM).astype(BF)

    second = heads_n * LANES
    head_refs = (
        r.qk.at[:, pl.ds(0, second)],
        r.qk.at[:, pl.ds(second, second)],
        r.vg.at[:, pl.ds(0, second)],
        r.vg.at[:, pl.ds(second, second)],
        r.kt,
        r.vt,
        r.s,
        r.p,
        r.ht,
        r.dqt,
        r.dk,
        r.dv,
    )

    def attend_all(head):
        for block in range(blocks):
            attend_head(head, block, head_refs)

    attend_all(0)
    rise.tick(3)
    attend_all(1)
    rise.tick(4)
    own["fall"].wait()
    fall.tick(1)
    attend_all(2)
    rise.tick(5)
    attend_all(3)
    fall.tick(2)

    r.sums[...] = jnp.zeros(r.sums.shape, F32)

    @pl.loop(0, blocks)
    def _(block):
        here = pl.ds(pl.multiple_of(block * TILE, TILE), TILE)
        place_in = lax.broadcasted_iota(jnp.int32, (TILE, wide), 0) + block * TILE
        r.attn[here, :] = jnp.where(place_in < padded, r.ht[:, here].T, 0.0).astype(BF)
        d_query = r.dqt[:, here].T * HEAD_DIM**-0.5
        cosine, sine = r.cos[here, :], -r.sin[here, :]
        lane = lanes_like((TILE, LANES))
        parts = []
        for head in range(heads_n):
            parts.append(spin(head_part(d_query, head * HEAD_DIM), cosine, sine))
            parts.append(spin(r.dk[head, here, :], cosine, sine))
            parts.append(r.dv[head, here, :])
        for index in range(len(parts) // 2):
            tile = jnp.where(lane < HEAD_DIM, parts[2 * index], pltpu.roll(parts[2 * index + 1], HEAD_DIM, 1))
            at = slice(index * LANES, (index + 1) * LANES)
            tile = tile.astype(BF)
            r.d_mixed[here, at] = tile
            r.sums[6:7, at] += jnp.sum(tile.astype(F32), axis=0, keepdims=True)
        r.sums[4:5, :] += jnp.sum(r.dy[here, :].astype(F32), axis=0, keepdims=True)

    big = 512

    def weight_grad(out, left, right):
        @pl.loop(0, left.shape[1] // big)
        def _(index):
            at = pl.ds(pl.multiple_of(index * big, big), big)
            out[at, :] = tn(left[:, at], right[...]).astype(BF)

    weight_grad(r.g_mix, r.normed1, r.d_mixed)
    r.g_proj[...] = tn(r.attn[...], r.dy[...]).astype(BF)

    def swap_back(step):
        peer = place.seq_peer(step)
        return send(
            columns_at(r.g_proj, peer, wide),
            rows_at(r.g_proj_cols, place.seq, wide),
            r.m_swap2,
            step,
            {"seq": peer},
        )

    def swap_back_arrival(step):
        source = place.seq_peer(-step)
        return send(
            columns_at(r.g_proj, source, wide),
            rows_at(r.g_proj_cols, source, wide),
            r.m_swap2,
            step,
            {"seq": place.seq_peer(step)},
        )

    for step in range(1, seq_size):
        swap_back(step).start()
    rows_at(r.g_proj_cols, place.seq, wide)[...] = columns_at(r.g_proj, place.seq, wide)[...]
    r_mix = RingReduce(place, Flat(r.g_mix, LANES), r.c_mix, r.m_rmix)
    r_proj = RingReduce(place, Flat(r.g_proj_cols, LANES), r.c_proj, r.m_rproj)
    r_rise = RingReduce(place, Flat(r.g_rise, LANES), r.c_rise, r.m_rrise)
    r_fall = RingReduce(place, Flat(r.g_fall, units), r.c_fall, r.m_rfall)
    fall.tick(3)
    r_mix.tick(1)

    def upward(first, last):
        @pl.loop(first, last)
        def _(block):
            here = pl.ds(pl.multiple_of(block * TILE, TILE), TILE)
            up = nn(r.normed2[here, :], r.w_rise[...]) + r.rows[6:7, :]
            share = 0.5 + 0.5 * lax.erf(up * 0.5**0.5)
            r.qk[here, :] = (up * share).astype(BF)
            bell = jnp.exp(-0.5 * up * up) * (2 * np.pi) ** -0.5
            r.vg[here, :] = (share + up * bell).astype(BF)

    upward(0, blocks // 2)
    fall.tick(4)
    for step in range(1, seq_size):
        swap_back_arrival(step).wait_recv()
    r_proj.tick(1)
    upward(blocks // 2, blocks)
    fall.tick(5)
    r_mix.tick(2)
    r_proj.tick(2)

    @pl.loop(0, blocks)
    def _(block):
        here = pl.ds(pl.multiple_of(block * TILE, TILE), TILE)
        d_up = (r.vg[here, :].astype(F32) * nt(r.dy[here, :], r.w_fall[...])).astype(BF)
        r.vg[here, :] = d_up
        r.sums[5:6, :] += jnp.sum(d_up.astype(F32), axis=0, keepdims=True)

    weight_grad(r.g_fall, r.qk, r.dy)
    r_mix.tick(3)
    r_proj.tick(3)
    r_fall.tick(1)
    weight_grad(r.g_rise, r.normed2, r.vg)

    out = SeqReduce(place, Flat(r.out_part, tok), r.out_cross, r.out_came, r.m_out)
    back = SeqReduce(place, Flat(r.back_part, tok), r.back_cross, r.back_came, r.m_back)

    @pl.loop(0, blocks)
    def _(block):
        here = pl.ds(pl.multiple_of(block * TILE, TILE), TILE)
        part = nn(r.attn[here, :], r.w_proj[...]) + nn(r.qk[here, :], r.w_fall[...])
        r.out_part[here, :] = part.astype(BF)

    out.begin()
    r_mix.tick(4)
    r_proj.tick(4)
    r_fall.tick(2)

    @pl.loop(0, blocks)
    def _(block):
        here = pl.ds(pl.multiple_of(block * TILE, TILE), TILE)
        d_one = nt(r.d_mixed[here, :], r.w_mix[...])
        d_two = nt(r.vg[here, :], r.w_rise[...])
        r.back_part[here, :] = (r.rows[0:1, :] * d_one + r.rows[2:3, :] * d_two).astype(BF)
        n = unit_rows(here)
        r.sums[0:1, :] += jnp.sum(d_one * n, axis=0, keepdims=True)
        r.sums[1:2, :] += jnp.sum(d_one, axis=0, keepdims=True)
        r.sums[2:3, :] += jnp.sum(d_two * n, axis=0, keepdims=True)
        r.sums[3:4, :] += jnp.sum(d_two, axis=0, keepdims=True)

    out.middle()
    back.begin()
    for index in range(dp_size):
        at = slice(index * LANES, (index + 1) * LANES)
        r.vec_part[index, 0:6, :] = r.sums[0:6, at]
        for row in range(mixed_wide // LANES):
            r.vec_part[index, 6 + row : 7 + row, :] = r.sums[6:7, row * LANES : (row + 1) * LANES]
    vec_back = DpSpread(place, lambda peer: r.vec_part.at[peer], r.vec_came, r.m_vec2)
    vec_back.begin()
    r.vec_came[place.dp] = r.vec_part[place.dp]
    r_mix.tick(5)
    r_proj.tick(5)
    r_fall.tick(3)
    r_rise.tick(1)

    f_mix = SeqGather(place, Flat(r.mix_fin, mixed_wide, True), r.m_fmix)
    f_proj = SeqGather(place, Flat(r.proj_fin, wide, True), r.m_fproj)
    f_fall = SeqGather(place, Flat(r.fall_fin, units), r.m_ffall)
    f_rise = SeqGather(place, r.rise_stage, r.m_frise)
    f_vec = SeqGather(place, r.vec_fin, r.m_fvec)
    columns_at(r.mix_fin, place.seq, mixed_wide)[...] = rows_at(r.g_mix, place.dp, LANES)[...]
    columns_at(r.proj_fin, place.seq, wide)[...] = rows_at(r.g_proj_cols, place.dp, LANES)[...]
    back.middle()
    f_mix.begin()
    f_proj.begin()
    vec_back.finish()
    r.vec_fin[place.seq] = jnp.sum(r.vec_came[...], axis=0)
    f_vec.begin()
    r_fall.tick(4)
    r_rise.tick(2)
    mine = pl.ds(pl.multiple_of(place.seq * tok, tok), tok)
    r.block_out[...] = (out.total() + r.x[mine, :].astype(F32) + (r.rows[4:5, :] + r.rows[5:6, :])).astype(BF)
    r_fall.tick(5)
    rows_at(r.fall_fin, place.seq, units)[...] = rows_at(r.g_fall, place.dp, units)[...]
    f_fall.begin()
    r_rise.tick(3)
    f_mix.forward()
    f_proj.forward()
    f_vec.forward()
    scaled = back.total()
    n = unit_rows(mine)
    rstd = r.stat[mine, HEAD_DIM : HEAD_DIM + 1]
    back_mean = jnp.sum(scaled, axis=-1, keepdims=True) * (1.0 / D)
    back_n = jnp.sum(scaled * n, axis=-1, keepdims=True) * (1.0 / D)
    r.input_grad[...] = (r.dy[mine, :].astype(F32) + rstd * (scaled - back_mean - n * back_n)).astype(BF)
    r_rise.tick(4)
    f_fall.forward()
    f_vec.finish()
    norm = r.vec_fin[0, 0:4, :]
    for index in range(1, seq_size):
        norm = norm + r.vec_fin[index, 0:4, :]
    r.norm_out[...] = norm
    r.col_out[...] = r.vec_fin[0, 4:5, :]
    for index in range(seq_size):
        r.b_rise_out[index : index + 1, :] = r.vec_fin[index, 5:6, :]
    source = r.vec_fin[place.dp // each]
    pick = place.dp % each
    part = source[6:9, :]
    for index in range(1, each):
        part = jnp.where(pick == index, source[6 + 3 * index : 9 + 3 * index, :], part)
    r.b_mix_out[...] = part
    r_rise.tick(5)
    r.rise_stage[place.seq] = rows_at(r.g_rise, place.dp, LANES)[...]
    f_rise.begin()
    f_rise.forward()
    f_mix.finish()
    f_proj.finish()
    f_fall.finish()
    f_rise.finish()
    for index in range(dp_size):
        for group in range(seq_size):
            start = (index * seq_size + group) * units
            r.rise_fin[:, start : start + units] = r.rise_stage[group, :, index * units : (index + 1) * units]
    for move in (mix, proj, rise, fall, r_mix, r_proj, r_rise, r_fall, out, back):
        move.finish()
    for move in (x_move, hot_move, dy_move):
        move.sent()
    for step in range(1, seq_size):
        swap(step).wait_send()
        swap_back(step).wait_send()


def resident_call(seq_size, dp_size, *args):
    x, _, _, _, _, w_fall, vec, _, _, _, _ = args
    tok = x.shape[0]
    length = tok * seq_size
    half, pairs = dp_size // 2, seq_size // 2
    wide = HEADS // seq_size * HEAD_DIM
    units_all = dp_size * LANES
    heads_n = wide // HEAD_DIM

    def half_vmem(*shape):
        return pltpu.VMEM(shape, BF)

    def full_vmem(*shape):
        return pltpu.VMEM(shape, F32)

    def ring(columns):
        return half_vmem(2, half, LANES, columns)

    any_spec = pl.BlockSpec(memory_space=pl.ANY)
    vmem = pl.BlockSpec(memory_space=pltpu.VMEM)
    smem = pl.BlockSpec(memory_space=pltpu.SMEM)
    scratch = [
        half_vmem(length, D),
        half_vmem(length, D),
        half_vmem(length, LANES),
        half_vmem(D, 3 * wide),
        half_vmem(D, wide),
        half_vmem(wide, D),
        half_vmem(D, units_all),
        half_vmem(units_all, D),
        full_vmem(dp_size, 16, LANES),
        full_vmem(8, D),
        half_vmem(length, D),
        half_vmem(length, D),
        full_vmem(length, LANES),
        half_vmem(length, units_all),
        half_vmem(length, units_all),
        half_vmem(wide, length),
        half_vmem(wide, length),
        full_vmem(length // TILE, TILE, TILE),
        full_vmem(length // TILE, TILE, TILE),
        full_vmem(wide, length),
        full_vmem(wide, length),
        full_vmem(heads_n, length, LANES),
        full_vmem(heads_n, length, LANES),
        half_vmem(length, wide),
        half_vmem(length, 3 * wide),
        half_vmem(length, D),
        half_vmem(length, D),
        half_vmem(D, 3 * wide),
        half_vmem(wide, D),
        half_vmem(D, wide),
        half_vmem(D, units_all),
        half_vmem(units_all, D),
        ring(3 * wide),
        ring(wide),
        ring(units_all),
        ring(D),
        half_vmem(pairs, tok, D),
        half_vmem(pairs, tok, D),
        half_vmem(pairs, tok, D),
        half_vmem(pairs, tok, D),
        half_vmem(seq_size, LANES, units_all),
        full_vmem(8, D),
        full_vmem(dp_size, 16, LANES),
        full_vmem(dp_size, 16, LANES),
        full_vmem(seq_size, 16, LANES),
    ]
    counts = [2 * pairs] * 3 + [dp_size] + [2 * half] * 4 + [seq_size]
    scratch += [sems_of(count) for count in counts]
    scratch += [pltpu.SemaphoreType.DMA((dp_size + 6,))]
    counts = [seq_size] + [2 * half] * 4 + [2 * pairs] * 2 + [dp_size] + [2 * pairs] * 5
    scratch += [sems_of(count) for count in counts]
    return pl.pallas_call(
        functools.partial(resident_kernel, seq_size, dp_size),
        out_shape=(
            jax.ShapeDtypeStruct((tok, D), BF),
            jax.ShapeDtypeStruct((tok, D), BF),
            jax.ShapeDtypeStruct((LANES, 3 * D), BF),
            jax.ShapeDtypeStruct((LANES, D), BF),
            jax.ShapeDtypeStruct((LANES, FF), BF),
            jax.ShapeDtypeStruct((seq_size * LANES, D), BF),
            jax.ShapeDtypeStruct((4, LANES), F32),
            jax.ShapeDtypeStruct((1, LANES), F32),
            jax.ShapeDtypeStruct((3, LANES), F32),
            jax.ShapeDtypeStruct((seq_size, LANES), F32),
        ),
        in_specs=[any_spec] * 6 + [vmem, any_spec, smem, vmem, vmem],
        out_specs=[vmem] * 10,
        scratch_shapes=scratch,
        compiler_params=pltpu.CompilerParams(
            collective_id=2, has_side_effects=True, vmem_limit_bytes=RESIDENT_VMEM
        ),
    )(*args)


RESIDENT_VMEM = 63 * 2**20


def resident_tables(length):
    cosine, sine = angle_tables(length)
    half = ROT // 2
    cos_table = np.ones((length, LANES), np.float32)
    sin_table = np.zeros((length, LANES), np.float32)
    cos_table[:, :half] = cosine
    cos_table[:, half:ROT] = cosine
    sin_table[:, :half] = -sine
    sin_table[:, half:ROT] = sine
    return jnp.asarray(cos_table), jnp.asarray(sin_table)


def resident_shards(
    tokens,
    cotangent,
    norm1_gain,
    norm1_bias,
    norm2_gain,
    norm2_bias,
    qkv_weight,
    qkv_bias,
    out_weight,
    out_bias,
    up_weight,
    up_bias,
    down_weight,
    down_bias,
    segment_ids,
    pad_length,
):
    seq_size, dp_size = lax.axis_size("seq"), lax.axis_size("dp")
    tok = tokens.shape[1]
    vectors = (norm1_gain, norm1_bias, norm2_gain, norm2_bias, out_bias, down_bias, qkv_bias, up_bias)
    vec = jnp.zeros((16, LANES), F32)
    start = 0
    for piece in vectors:
        rows = piece.shape[0] // LANES
        vec = vec + jnp.pad(piece.astype(F32).reshape(rows, LANES), ((start, 16 - start - rows), (0, 0)))
        start += rows
    lane = jnp.arange(LANES, dtype=jnp.int32)
    hot = (segment_ids[0][:, None] == (lane - HEAD_DIM)[None, :]).astype(BF)
    cosine, sine = resident_tables(tok * seq_size)
    block_out, input_grad, g_mix, g_proj, g_rise, g_fall, norm, col, b_mix, b_rise = resident_call(
        seq_size,
        dp_size,
        tokens[0],
        cotangent[0],
        qkv_weight,
        out_weight,
        up_weight,
        down_weight,
        vec,
        hot,
        pad_length,
        cosine,
        sine,
    )
    return (
        block_out[None],
        input_grad[None],
        norm[0],
        norm[1],
        norm[2],
        norm[3],
        g_mix.astype(F32),
        b_mix.reshape(-1),
        g_proj.astype(F32),
        col[0],
        g_rise.astype(F32),
        b_rise.reshape(-1),
        g_fall.astype(F32),
        col[0],
    )


def streamed_shards(
    tokens,
    cotangent,
    norm1_gain,
    norm1_bias,
    norm2_gain,
    norm2_bias,
    qkv_weight,
    qkv_bias,
    out_weight,
    out_bias,
    up_weight,
    up_bias,
    down_weight,
    down_bias,
    segment_ids,
    pad_length,
):
    seq_size, dp_size = lax.axis_size("seq"), lax.axis_size("dp")
    seq = lax.axis_index("seq")
    dp = lax.axis_index("dp")
    tok = tokens.shape[1]
    length = tok * seq_size
    heads_n = HEADS // seq_size
    rows = D // dp_size
    wide = heads_n * HEAD_DIM
    units = FF // dp_size // seq_size

    mix = qkv_weight.reshape(rows, seq_size, heads_n, 3, HEAD_DIM)
    mix = lax.dynamic_index_in_dim(mix, seq, 1, keepdims=False)
    mix = mix.transpose(0, 2, 1, 3).reshape(rows, 3 * wide)
    proj = lax.dynamic_slice_in_dim(out_weight, seq * wide, wide, 1)
    rise = up_weight.reshape(rows, dp_size, seq_size, units)
    rise = lax.dynamic_index_in_dim(rise, seq, 2, keepdims=False).reshape(rows, dp_size * units)
    fall = lax.dynamic_slice_in_dim(down_weight, seq * units, units, 0)
    vec = jnp.concatenate(
        [norm1_gain, norm1_bias, norm2_gain, norm2_bias, out_bias, down_bias, qkv_bias, up_bias]
    )
    vec_len = vec.shape[0]
    vec = jnp.pad(vec, (0, 2048 - vec_len)).reshape(16, 128)
    seg = jnp.broadcast_to(segment_ids, (8, tok))
    x_all, dy_all, w_mix, _, w_rise, w_fall, vec_all, seg_all, w_proj = gather_all(
        seq_size, dp_size, tokens[0], cotangent[0], mix, proj, rise, fall, vec, seg
    )
    x = x_all.reshape(length, D).astype(F32)
    dy = dy_all.reshape(length, D)
    w_mix = w_mix.reshape(D, 3 * wide)
    w_rise = w_rise.reshape(D, dp_size * units)
    w_fall = w_fall.reshape(dp_size * units, D)
    w_proj = w_proj.reshape(seq_size, wide, wide).transpose(1, 0, 2).reshape(wide, D)
    segments = seg_all[:, 0, :].reshape(length)
    vec_all = vec_all.reshape(dp_size, 2048)[:, :vec_len].astype(F32)
    g1, s1, g2, s2, b_proj, b_fall = (
        vec_all[:, i * rows : (i + 1) * rows].reshape(D) for i in range(6)
    )
    b_mix = vec_all[:, 6 * rows : 9 * rows].reshape(seq_size, heads_n, 3, HEAD_DIM)
    b_mix = lax.dynamic_index_in_dim(b_mix, seq, 0, keepdims=False)
    b_mix = b_mix.transpose(1, 0, 2).reshape(3 * wide)
    b_rise = vec_all[:, 9 * rows :].reshape(dp_size, seq_size, units)
    b_rise = lax.dynamic_index_in_dim(b_rise, seq, 1, keepdims=False).reshape(dp_size * units)

    center = x - jnp.mean(x, axis=-1, keepdims=True)
    rstd = lax.rsqrt(jnp.mean(center * center, axis=-1, keepdims=True) + EPS)
    n = center * rstd
    normed1 = (n * g1 + s1).astype(BF)
    normed2 = (n * g2 + s2).astype(BF)
    valid = (jnp.arange(length, dtype=jnp.int32) < length - pad_length[0]).astype(F32)[:, None]
    cosine, sine = (jnp.asarray(t) for t in angle_tables(length))

    mixed = dot(normed1, w_mix) + b_mix
    mixed = mixed.reshape(length, 3, heads_n, HEAD_DIM).transpose(1, 2, 0, 3)
    queries = turn(mixed[0], cosine, sine, 1.0).astype(BF)
    keys = turn(mixed[1], cosine, sine, 1.0).astype(BF)
    values = mixed[2].astype(BF)
    d_heads = (dot_nt(dy, w_proj) * valid).astype(BF)
    d_heads = d_heads.reshape(length, heads_n, HEAD_DIM).transpose(1, 0, 2)
    heads, d_q, d_k, d_v = attention(queries, keys, values, d_heads, segments)
    attn_rows = (heads.transpose(1, 0, 2).reshape(length, wide).astype(F32) * valid).astype(BF)
    d_mixed = jnp.stack(
        [
            turn(d_q.astype(F32), cosine, sine, -1.0).astype(BF),
            turn(d_k.astype(F32), cosine, sine, -1.0).astype(BF),
            d_v,
        ]
    )
    d_mixed = d_mixed.transpose(2, 0, 1, 3).reshape(length, 3 * wide)

    upward = dot(normed2, w_rise) + b_rise
    active = jax.nn.gelu(upward, approximate=False).astype(BF)
    slope = 0.5 * (1 + lax.erf(upward * (0.5**0.5))) + upward * jnp.exp(
        -0.5 * upward * upward
    ) * ((2 * np.pi) ** -0.5)
    d_up = (slope * dot_nt(dy, w_fall)).astype(BF)
    out_part = (dot(attn_rows, w_proj) + dot(active, w_fall)).astype(BF)
    d_n1 = dot_nt(d_mixed, w_mix)
    d_n2 = dot_nt(d_up, w_rise)
    back_part = (g1 * d_n1 + g2 * d_n2).astype(BF)

    g_mix = dot_t(normed1, d_mixed).astype(BF).reshape(dp_size, rows, 3 * wide)
    g_proj = dot_t(attn_rows, dy).astype(BF).reshape(dp_size // seq_size, rows, seq_size, wide)
    g_proj = g_proj.transpose(2, 0, 1, 3)
    g_rise = dot_t(normed2, d_up).astype(BF).reshape(dp_size, rows, dp_size * units)
    g_fall = dot_t(active, dy).astype(BF).reshape(dp_size, units, D)
    dyf = dy.astype(F32)
    vec_part = jnp.concatenate(
        [
            t.reshape(dp_size, -1)
            for t in (
                jnp.sum(d_n1 * n, axis=0),
                jnp.sum(d_n1, axis=0),
                jnp.sum(d_n2 * n, axis=0),
                jnp.sum(d_n2, axis=0),
                jnp.sum(dyf, axis=0),
                jnp.sum(d_up.astype(F32), axis=0),
            )
        ]
        + [jnp.broadcast_to(jnp.sum(d_mixed.astype(F32), axis=0)[None], (dp_size, 3 * wide))],
        axis=1,
    )
    part_len = vec_part.shape[1]
    vec_part = jnp.pad(vec_part, ((0, 0), (0, 2048 - part_len))).reshape(dp_size, 16, 128)
    out_sum, back_sum, f_mix, f_proj, f_rise, f_fall, f_vec = reduce_all(
        seq_size,
        dp_size,
        out_part.reshape(seq_size, tok, D),
        back_part.reshape(seq_size, tok, D),
        g_mix,
        g_proj,
        g_rise,
        g_fall,
        vec_part,
    )
    own_x = tokens[0].astype(F32)
    block_output = (own_x + out_sum + b_proj + b_fall).astype(BF)
    own_center = own_x - jnp.mean(own_x, axis=-1, keepdims=True)
    own_rstd = lax.rsqrt(jnp.mean(own_center * own_center, axis=-1, keepdims=True) + EPS)
    own_n = own_center * own_rstd
    back = own_rstd * (
        back_sum
        - jnp.mean(back_sum, axis=-1, keepdims=True)
        - own_n * jnp.mean(back_sum * own_n, axis=-1, keepdims=True)
    )
    input_grad = (cotangent[0].astype(F32) + back).astype(BF)
    f_mix = f_mix.reshape(seq_size, rows, 3, heads_n, HEAD_DIM)
    f_mix = f_mix.transpose(1, 0, 3, 2, 4).reshape(rows, 3 * D).astype(F32)
    f_proj = f_proj.transpose(1, 0, 2).reshape(rows, D).astype(F32)
    f_rise = f_rise.reshape(seq_size, rows, dp_size, units)
    f_rise = f_rise.transpose(1, 2, 0, 3).reshape(rows, FF).astype(F32)
    f_fall = f_fall.reshape(seq_size * units, D).astype(F32)
    f_vec = f_vec.reshape(seq_size, 2048)[:, :part_len]
    norm_sums = jnp.sum(f_vec[:, : 4 * rows], axis=0)
    column = f_vec[0, 4 * rows : 5 * rows]
    f_b_rise = f_vec[:, 5 * rows : 5 * rows + units].reshape(seq_size * units)
    f_b_mix = f_vec[:, 5 * rows + units :].reshape(seq_size, 3, heads_n, HEAD_DIM)
    f_b_mix = f_b_mix.transpose(0, 2, 1, 3).reshape(dp_size, 3 * rows)
    f_b_mix = lax.dynamic_index_in_dim(f_b_mix, dp, 0, keepdims=False)
    return (
        block_output[None],
        input_grad[None],
        norm_sums[:rows],
        norm_sums[rows : 2 * rows],
        norm_sums[2 * rows : 3 * rows],
        norm_sums[3 * rows :],
        f_mix,
        f_b_mix,
        f_proj,
        column,
        f_rise,
        f_b_rise,
        f_fall,
        column,
    )


def shards(*args):
    seq_size, dp_size = lax.axis_size("seq"), lax.axis_size("dp")
    if resident_fits(seq_size, dp_size, args[0].shape[1]):
        return resident_shards(*args)
    return streamed_shards(*args)


def solution(mesh):
    rows = P("dp", "seq", None)
    weight = P("dp", None)
    vector = P("dp")
    return jax.shard_map(
        shards,
        mesh=mesh,
        in_specs=(rows, rows)
        + (vector,) * 4
        + (weight, vector) * 4
        + (P("dp", "seq"), vector),
        out_specs=(rows, rows) + (vector,) * 4 + (weight, vector) * 4,
        check_vma=False,
    )
```

```python
import functools

import jax
import jax.numpy as jnp
import numpy as np
from jax import lax
from jax.experimental import pallas as pl
from jax.experimental.pallas import tpu as pltpu
from jax.sharding import PartitionSpec as P

D = 1024
HEADS = 16
HEAD_DIM = 64
ROT = 16
FF = 4096
EPS = 1e-05
BASE = 10000.0
NEG = -1e30
MESH = pl.DeviceIdType.MESH
BF = jnp.bfloat16
F32 = jnp.float32


def ring_pos(dev, size):
    return (dev // 2) * (1 - dev % 2) + (size - 1 - dev // 2) * (dev % 2)


def ring_dev(pos, size):
    high = pos // (size // 2)
    return (1 - high) * 2 * pos + high * (2 * (size - 1 - pos) + 1)


class Place:
    def __init__(self, seq_size, dp_size):
        self.seq_size, self.dp_size = seq_size, dp_size
        self.seq = lax.axis_index("seq")
        self.dp = lax.axis_index("dp")
        self.pos = ring_pos(self.dp, dp_size)
        self.half = dp_size // 2
        self.pairs = seq_size // 2
        self.core = self.seq % 2
        self.pair = self.seq // 2
        self.sibling = self.pair * 2 + 1 - self.core

    def ring(self, offset):
        return ring_dev((self.pos + offset + self.dp_size) % self.dp_size, self.dp_size)

    def dp_peer(self, step):
        return (self.dp + step + self.dp_size) % self.dp_size

    def pair_peer(self, step):
        return ((self.pair + step + self.pairs) % self.pairs) * 2 + self.core

    def across_source(self, step):
        return ((self.pair - step + self.pairs) % self.pairs) * 2 + 1 - self.core

    def seq_peer(self, step):
        return (self.seq + step + self.seq_size) % self.seq_size

    def greet_near(self):
        barrier = pltpu.get_barrier_semaphore()
        for step in (1, -1):
            pl.semaphore_signal(barrier, inc=1, device_id={"dp": self.ring(step)}, device_id_type=MESH)
        for step in range(1, self.seq_size):
            pl.semaphore_signal(
                barrier, inc=1, device_id={"seq": self.seq_peer(step)}, device_id_type=MESH
            )
        pl.semaphore_wait(barrier, 2 + self.seq_size - 1)

    def greet(self):
        barrier = pltpu.get_barrier_semaphore()
        for step in range(1, self.dp_size):
            pl.semaphore_signal(
                barrier, inc=1, device_id={"dp": self.dp_peer(step)}, device_id_type=MESH
            )
        for step in range(1, self.seq_size):
            pl.semaphore_signal(
                barrier, inc=1, device_id={"seq": self.seq_peer(step)}, device_id_type=MESH
            )
        pl.semaphore_wait(barrier, self.dp_size - 1 + self.seq_size - 1)


def send(src, dst, sems, index, target):
    return pltpu.make_async_remote_copy(
        src_ref=src,
        dst_ref=dst,
        send_sem=sems.at[0, index],
        recv_sem=sems.at[1, index],
        device_id=target,
        device_id_type=MESH,
    )


def halves(ref):
    rows = ref.shape[0]
    columns = ref.shape[1]
    if rows % 32 == 0:
        return ref.at[pl.ds(0, rows // 2)], ref.at[pl.ds(rows // 2, rows // 2)]
    return ref.at[:, pl.ds(0, columns // 2)], ref.at[:, pl.ds(columns // 2, columns // 2)]


class RingGather:
    def __init__(self, place, full, sems):
        self.place, self.full, self.sems = place, full, sems

    def piece(self, offset, step, way):
        block = self.full.at[self.place.ring(offset)]
        return block if step < self.place.half else halves(block)[way]

    def copies(self, step):
        place = self.place
        right = self.piece(-(step - 1), step, 0)
        left = self.piece(step - 1, step, 1)
        index = 2 * (step - 1)
        return (
            send(right, right, self.sems, index, {"dp": place.ring(1)}),
            send(left, left, self.sems, index + 1, {"dp": place.ring(-1)}),
        )

    def arrivals(self, step):
        right = self.piece(-step, step, 0)
        left = self.piece(step, step, 1)
        index = 2 * (step - 1)
        return (
            send(right, right, self.sems, index, {"dp": self.place.ring(1)}),
            send(left, left, self.sems, index + 1, {"dp": self.place.ring(-1)}),
        )

    def tick(self, step):
        if step > 1:
            for copy in self.arrivals(step - 1):
                copy.wait_recv()
        if step <= self.place.half:
            for copy in self.copies(step):
                copy.start()

    def finish(self):
        for step in range(1, self.place.half + 1):
            for copy in self.copies(step):
                copy.wait_send()


class RingReduce:
    def __init__(self, place, parts, arrived, sems):
        self.place, self.parts, self.arrived, self.sems = place, parts, arrived, sems

    def piece(self, ref, step, way):
        return ref if step > 1 else halves(ref)[way]

    def copies(self, step):
        place = self.place
        away = place.half - step + 1
        index = 2 * (step - 1)
        out = []
        for way, (offset, target) in enumerate(((away, 1), (-away, -1))):
            src = self.piece(self.parts.at[place.ring(offset)], step, way)
            dst = self.piece(self.arrived.at[way, step - 1], step, way)
            out.append(send(src, dst, self.sems, index + way, {"dp": place.ring(target)}))
        return out

    def tick(self, step):
        place = self.place
        if step > 1:
            for way, copy in enumerate(self.copies(step - 1)):
                copy.wait_recv()
                away = (place.half - step + 1) * (1 - 2 * way)
                held = self.piece(self.parts.at[place.ring(away)], step - 1, way)
                came = self.piece(self.arrived.at[way, step - 2], step - 1, way)
                held[...] = (held[...].astype(F32) + came[...].astype(F32)).astype(held.dtype)
        if step <= place.half:
            for copy in self.copies(step):
                copy.start()

    def finish(self):
        for step in range(1, self.place.half + 1):
            for copy in self.copies(step):
                copy.wait_send()

    def own(self):
        return self.parts.at[self.place.dp]


class SeqGather:
    def __init__(self, place, full, sems, own=None):
        self.place, self.full, self.sems = place, full, sems
        self.own = full.at[place.seq] if own is None else own

    def direct(self, step):
        place = self.place
        target = {"seq": place.pair_peer(step)}
        return send(self.own, self.full.at[place.seq], self.sems, step, target)

    def arrival(self, step):
        place = self.place
        target = {"seq": place.pair_peer(step)}
        return send(self.own, self.full.at[place.pair_peer(-step)], self.sems, step, target)

    def across(self, step):
        place = self.place
        block = self.full.at[place.pair_peer(-step)]
        src = self.own if step == 0 else block
        return send(src, block, self.sems, place.pairs + step, {"seq": place.sibling})

    def across_arrival(self, step):
        place = self.place
        block = self.full.at[place.across_source(step)]
        return send(self.own, block, self.sems, place.pairs + step, {"seq": place.sibling})

    def begin(self):
        for step in range(1, self.place.pairs):
            self.direct(step).start()
        self.across(0).start()

    def forward(self):
        for step in range(1, self.place.pairs):
            self.arrival(step).wait_recv()
            self.across(step).start()

    def across_arrived(self, step):
        self.across_arrival(step).wait_recv()

    def sent(self):
        for step in range(1, self.place.pairs):
            self.direct(step).wait_send()
        for step in range(self.place.pairs):
            self.across(step).wait_send()

    def finish(self):
        for step in range(self.place.pairs):
            self.across_arrived(step)
        self.sent()


class SeqReduce:
    def __init__(self, place, parts, crossed, arrived, sems):
        self.place, self.parts, self.crossed, self.arrived = place, parts, crossed, arrived
        self.sems = sems

    def over(self, step):
        place = self.place
        index = (place.pair + step) % place.pairs
        src = self.parts.at[index * 2 + 1 - place.core]
        return send(src, self.crossed.at[index], self.sems, step, {"seq": place.sibling})

    def direct(self, step):
        place = self.place
        return send(
            self.parts.at[place.pair_peer(step)],
            self.arrived.at[step],
            self.sems,
            place.pairs + step,
            {"seq": place.pair_peer(step)},
        )

    def over_start(self, step):
        self.over(step).start()

    def over_add(self, step):
        place = self.place
        index = (place.pair + step) % place.pairs
        self.over(step).wait_recv()
        held = self.parts.at[index * 2 + place.core]
        held[...] = (held[...].astype(F32) + self.crossed[index].astype(F32)).astype(held.dtype)
        if step > 0:
            self.direct(step).start()

    def begin(self):
        for step in range(self.place.pairs):
            self.over_start(step)

    def middle(self):
        for step in range(self.place.pairs):
            self.over_add(step)

    def total(self):
        place = self.place
        total = self.parts.at[place.seq][...].astype(F32)
        for step in range(1, place.pairs):
            self.direct(step).wait_recv()
            total = total + self.arrived[step].astype(F32)
        return total

    def finish(self):
        for step in range(self.place.pairs):
            self.over(step).wait_send()
        for step in range(1, self.place.pairs):
            self.direct(step).wait_send()


class DpSpread:
    def __init__(self, place, src_of, full, sems):
        self.place, self.src_of, self.full, self.sems = place, src_of, full, sems

    def copy(self, step):
        place = self.place
        peer = place.dp_peer(step)
        return send(self.src_of(peer), self.full.at[place.dp], self.sems, step, {"dp": peer})

    def arrival(self, step):
        place = self.place
        source = place.dp_peer(-step)
        return send(
            self.src_of(source), self.full.at[source], self.sems, step, {"dp": place.dp_peer(step)}
        )

    def begin(self):
        for step in range(1, self.place.dp_size):
            self.copy(step).start()

    def finish(self):
        for step in range(1, self.place.dp_size):
            self.arrival(step).wait_recv()
        for step in range(1, self.place.dp_size):
            self.copy(step).wait_send()


def sems_of(count):
    return pltpu.SemaphoreType.DMA((2, count))


def gather_kernel(seq_size, dp_size, *refs):
    (x_ref, dy_ref, mix_ref, proj_ref, rise_ref, fall_ref, vec_ref, seg_ref) = refs[:8]
    (x_all, dy_all, mix_all, proj_cols, rise_all, fall_all, vec_all, seg_all, proj_all) = refs[8:17]
    (x_sems, dy_sems, mix_sems, proj_sems, rise_sems, fall_sems, vec_sems, seg_sems, swap_sems, own_sems) = refs[17:]
    place = Place(seq_size, dp_size)
    own = [
        pltpu.make_async_copy(src, dst, own_sems.at[i])
        for i, (src, dst) in enumerate(
            (
                (x_ref, x_all.at[place.seq]),
                (dy_ref, dy_all.at[place.seq]),
                (mix_ref, mix_all.at[place.dp]),
                (proj_ref, proj_cols.at[place.dp]),
                (rise_ref, rise_all.at[place.dp]),
                (fall_ref, fall_all.at[place.dp]),
                (vec_ref, vec_all.at[place.dp]),
                (seg_ref, seg_all.at[place.seq]),
            )
        )
    ]
    for copy in own:
        copy.start()
    place.greet()
    for copy in own:
        copy.wait()
    x_move = SeqGather(place, x_all, x_sems)
    dy_move = SeqGather(place, dy_all, dy_sems)
    seg_move = SeqGather(place, seg_all, seg_sems)
    vec_move = DpSpread(place, lambda peer: vec_ref, vec_all, vec_sems)
    mix_move = RingGather(place, mix_all, mix_sems)
    proj_move = RingGather(place, proj_cols, proj_sems)
    rise_move = RingGather(place, rise_all, rise_sems)
    fall_move = RingGather(place, fall_all, fall_sems)
    x_move.begin()
    seg_move.begin()
    vec_move.begin()
    half = place.half
    for step in range(1, half + 1):
        mix_move.tick(step)
        proj_move.tick(step)
    x_move.forward()
    seg_move.forward()
    dy_move.begin()
    mix_move.tick(half + 1)
    proj_move.tick(half + 1)
    rise_move.tick(1)
    fall_move.tick(1)
    rows = proj_cols.shape[0] * proj_cols.shape[1] // seq_size
    each = rows // proj_cols.shape[1]
    swaps = []
    for step in range(1, seq_size):
        peer = place.seq_peer(step)
        swaps.append(
            send(
                proj_cols.at[pl.ds(peer * each, each)],
                proj_all.at[place.seq],
                swap_sems,
                step,
                {"seq": peer},
            )
        )
    for copy in swaps:
        copy.start()
    mine = pltpu.make_async_copy(
        proj_cols.at[pl.ds(place.seq * each, each)], proj_all.at[place.seq], own_sems.at[0]
    )
    mine.start()
    for step in range(2, half + 2):
        rise_move.tick(step)
        fall_move.tick(step)
        if step == 3:
            dy_move.forward()
    mine.wait()
    for step in range(1, seq_size):
        source = place.seq_peer(-step)
        send(
            proj_cols.at[pl.ds(source * each, each)],
            proj_all.at[source],
            swap_sems,
            step,
            {"seq": place.seq_peer(step)},
        ).wait_recv()
    for copy in swaps:
        copy.wait_send()
    for move in (x_move, dy_move, seg_move, vec_move, mix_move, proj_move, rise_move, fall_move):
        move.finish()


def gather_all(seq_size, dp_size, x, dy, mix, proj, rise, fall, vec, seg):
    half = dp_size // 2
    pairs = seq_size // 2

    def lead(count, like):
        return jax.ShapeDtypeStruct((count,) + like.shape, like.dtype)

    each = dp_size // seq_size
    any_spec = pl.BlockSpec(memory_space=pl.ANY)
    return pl.pallas_call(
        functools.partial(gather_kernel, seq_size, dp_size),
        out_shape=(
            lead(seq_size, x),
            lead(seq_size, dy),
            lead(dp_size, mix),
            lead(dp_size, proj),
            lead(dp_size, rise),
            lead(dp_size, fall),
            lead(dp_size, vec),
            lead(seq_size, seg),
            jax.ShapeDtypeStruct((seq_size, each) + proj.shape, proj.dtype),
        ),
        in_specs=[any_spec] * 8,
        out_specs=[any_spec] * 9,
        scratch_shapes=[
            sems_of(2 * pairs),
            sems_of(2 * pairs),
            sems_of(2 * half),
            sems_of(2 * half),
            sems_of(2 * half),
            sems_of(2 * half),
            sems_of(dp_size),
            sems_of(2 * pairs),
            sems_of(seq_size),
            pltpu.SemaphoreType.DMA((8,)),
        ],
        compiler_params=pltpu.CompilerParams(collective_id=0, has_side_effects=True),
    )(x, dy, mix, proj, rise, fall, vec, seg)


def reduce_kernel(seq_size, dp_size, *refs):
    (out_ref, back_ref, mix_ref, proj_ref, rise_ref, fall_ref, vec_ref), refs = refs[:7], refs[7:]
    (out_sum, back_sum, mix_fin, proj_fin, rise_fin, fall_fin, vec_fin), refs = refs[:7], refs[7:]
    (
        out_cross,
        out_came,
        back_cross,
        back_came,
        proj_full,
        mix_came,
        proj_came,
        rise_came,
        fall_came,
        vec_came,
        out_sems,
        back_sems,
        swap_sems,
        mix_sems,
        proj_sems,
        rise_sems,
        fall_sems,
        vec_sems,
        mix_fs,
        proj_fs,
        rise_fs,
        fall_fs,
        vec_fs,
    ) = refs
    place = Place(seq_size, dp_size)
    each = dp_size // seq_size
    half = place.half
    place.greet()

    def mine(index):
        return proj_full.at[pl.ds(index * each, each)]

    def swap(step):
        peer = place.seq_peer(step)
        return send(proj_ref.at[peer], mine(place.seq), swap_sems, step, {"seq": peer})

    def swap_arrival(step):
        source = place.seq_peer(-step)
        target = {"seq": place.seq_peer(step)}
        return send(proj_ref.at[source], mine(source), swap_sems, step, target)

    for step in range(1, seq_size):
        swap(step).start()
    mine(place.seq)[...] = proj_ref[place.seq]
    mix = RingReduce(place, mix_ref, mix_came, mix_sems)
    proj = RingReduce(place, proj_full, proj_came, proj_sems)
    rise = RingReduce(place, rise_ref, rise_came, rise_sems)
    fall = RingReduce(place, fall_ref, fall_came, fall_sems)
    out = SeqReduce(place, out_ref, out_cross, out_came, out_sems)
    back = SeqReduce(place, back_ref, back_cross, back_came, back_sems)
    vec = DpSpread(place, lambda peer: vec_ref.at[peer], vec_came, vec_sems)
    mix.tick(1)
    rise.tick(1)
    out.begin()
    back.begin()
    vec.begin()
    for step in range(1, seq_size):
        swap_arrival(step).wait_recv()
    proj.tick(1)
    fall.tick(1)
    out.middle()
    back.middle()
    for step in range(2, half + 2):
        for move in (mix, rise, proj, fall):
            move.tick(step)
    finals = []
    for move, fin, fin_sems in (
        (mix, mix_fin, mix_fs),
        (rise, rise_fin, rise_fs),
        (proj, proj_fin, proj_fs),
        (fall, fall_fin, fall_fs),
    ):
        fin[place.seq] = move.parts[place.dp]
        gather = SeqGather(place, fin, fin_sems)
        gather.begin()
        finals.append(gather)
    vec_came[place.dp] = vec_ref[place.dp]
    vec.finish()
    vec_fin[place.seq] = jnp.sum(vec_came[...], axis=0)
    gather = SeqGather(place, vec_fin, vec_fs)
    gather.begin()
    finals.append(gather)
    out_sum[...] = out.total()
    back_sum[...] = back.total()
    for gather in finals:
        gather.forward()
    for gather in finals:
        gather.finish()
    for step in range(1, seq_size):
        swap(step).wait_send()
    for move in (mix, rise, proj, fall, out, back):
        move.finish()


def reduce_all(seq_size, dp_size, out, back, mix, proj, rise, fall, vec):
    half = dp_size // 2
    pairs = seq_size // 2
    each = dp_size // seq_size

    def fin(like):
        return jax.ShapeDtypeStruct((seq_size,) + like.shape[1:], like.dtype)

    def came(like):
        return pltpu.VMEM((2, half) + like.shape[1:], like.dtype)

    proj_blocks = jax.ShapeDtypeStruct((dp_size,) + proj.shape[2:], proj.dtype)
    vmem = pl.BlockSpec(memory_space=pltpu.VMEM)
    return pl.pallas_call(
        functools.partial(reduce_kernel, seq_size, dp_size),
        out_shape=(
            jax.ShapeDtypeStruct(out.shape[1:], F32),
            jax.ShapeDtypeStruct(back.shape[1:], F32),
            fin(mix),
            fin(proj_blocks),
            fin(rise),
            fin(fall),
            fin(vec),
        ),
        in_specs=[vmem] * 7,
        out_specs=[vmem] * 7,
        scratch_shapes=[
            pltpu.VMEM((pairs,) + out.shape[1:], BF),
            pltpu.VMEM((pairs,) + out.shape[1:], BF),
            pltpu.VMEM((pairs,) + back.shape[1:], BF),
            pltpu.VMEM((pairs,) + back.shape[1:], BF),
            pltpu.VMEM(proj_blocks.shape, BF),
            came(mix),
            came(proj_blocks),
            came(rise),
            came(fall),
            pltpu.VMEM(vec.shape, F32),
            sems_of(2 * pairs),
            sems_of(2 * pairs),
            sems_of(seq_size),
            sems_of(2 * half),
            sems_of(2 * half),
            sems_of(2 * half),
            sems_of(2 * half),
            sems_of(dp_size),
            sems_of(2 * pairs),
            sems_of(2 * pairs),
            sems_of(2 * pairs),
            sems_of(2 * pairs),
            sems_of(2 * pairs),
        ],
        compiler_params=pltpu.CompilerParams(
            collective_id=1, has_side_effects=True, vmem_limit_bytes=56 * 2**20
        ),
    )(out, back, mix, proj, rise, fall, vec)


def angle_tables(length):
    frequency = BASE ** (-np.arange(0, ROT, 2).astype(np.float32) / np.float32(ROT))
    angles = np.arange(length, dtype=np.float32)[:, None] * frequency.astype(np.float32)[None, :]
    return np.cos(angles).astype(np.float32), np.sin(angles).astype(np.float32)


def turn(piece, cosine, sine, sign):
    half = ROT // 2
    low, high = piece[..., :half], piece[..., half:ROT]
    return jnp.concatenate(
        [low * cosine - sign * high * sine, high * cosine + sign * low * sine, piece[..., ROT:]],
        axis=-1,
    )


TILE = 256

def mm(a, b, dims):
    return lax.dot_general(a, b, ((dims[0], dims[1]), ((), ())), preferred_element_type=F32)

def nn(a, b):
    return mm(a, b, ((1,), (0,)))

def nt(a, b):
    return mm(a, b, ((1,), (1,)))

def tn(a, b):
    return mm(a, b, ((0,), (0,)))

def fold(count, body, init):
    if isinstance(count, int):
        for index in range(count):
            init = body(index, init)
        return init
    return lax.fori_loop(0, count, body, init)

def rows_of(index):
    start = index * TILE
    return pl.ds(start if isinstance(start, int) else pl.multiple_of(start, TILE), TILE)

def attend_block(head, block, refs):
    q_ref, k_ref, v_ref, g_ref, kt_ref, vt_ref, s_ref, p_ref, ht_ref, dqt_ref, dk_ref, dv_ref = refs
    here = rows_of(block)
    span = block + 1
    dims = pl.ds(pl.multiple_of(head * HEAD_DIM, HEAD_DIM), HEAD_DIM)
    query = q_ref[head, here, :]
    grad = g_ref[head, here, :]

    def score(index, top):
        tile = nt(k_ref[head, rows_of(index), :], query)
        if isinstance(index, int) and isinstance(block, int) and index < block:
            keep = tile
        else:
            key = lax.broadcasted_iota(jnp.int32, (TILE, TILE), 0) + (index - block) * TILE
            place = lax.broadcasted_iota(jnp.int32, (TILE, TILE), 1)
            keep = jnp.where(key <= place, tile, NEG)
        s_ref[index] = keep
        return jnp.maximum(top, jnp.max(keep, axis=0, keepdims=True))

    top = fold(span, score, jnp.full((1, TILE), 2 * NEG, F32))

    def raise_(index, total):
        raised = jnp.exp(s_ref[index] - top)
        s_ref[index] = raised
        return total + jnp.sum(raised, axis=0, keepdims=True)

    total = fold(span, raise_, jnp.zeros((1, TILE), F32))
    share = 1.0 / total

    def weigh(index, carried):
        heads, delta = carried
        weights = s_ref[index] * share
        s_ref[index] = weights
        weights_b = weights.astype(BF)
        d_weights = nt(v_ref[head, rows_of(index), :], grad)
        p_ref[index] = d_weights
        dv_ref[head, rows_of(index), :] += nn(weights_b, grad)
        heads = heads + nn(vt_ref[dims, rows_of(index)], weights_b)
        return heads, delta + jnp.sum(weights * d_weights, axis=0, keepdims=True)

    heads, delta = fold(
        span, weigh, (jnp.zeros((HEAD_DIM, TILE), F32), jnp.zeros((1, TILE), F32))
    )
    ht_ref[dims, here] = heads

    def back(index, d_query):
        d_scores = (s_ref[index] * (p_ref[index] - delta)).astype(BF)
        dk_ref[head, rows_of(index), :] += nn(d_scores, query)
        return d_query + nn(kt_ref[dims, rows_of(index)], d_scores)

    dqt_ref[dims, here] = fold(span, back, jnp.zeros((HEAD_DIM, TILE), F32))

def attend(heads_n, length, refs):
    dk_ref, dv_ref = refs[-2:]
    dk_ref[...] = jnp.zeros(dk_ref.shape, F32)
    dv_ref[...] = jnp.zeros(dv_ref.shape, F32)
    blocks = length // TILE

    @pl.loop(0, heads_n)
    def _(head):
        if blocks <= 4:
            for block in range(blocks):
                attend_block(head, block, refs)
        else:
            @pl.loop(0, blocks)
            def _(block):
                attend_block(head, block, refs)

def attend_kernel(H, L, q, k, v, g, kt, vt, ht, dqt, dk, dv, s_ref, p_ref):
    attend(H, L, (q, k, v, g, kt, vt, s_ref, p_ref, ht, dqt, dk, dv))

def attention_call(q, k, v, g, kt, vt):
    H, L, _ = q.shape
    vm = pl.BlockSpec(memory_space=pltpu.VMEM)
    nb = L // TILE
    return pl.pallas_call(functools.partial(attend_kernel, H, L),
        out_shape=(jax.ShapeDtypeStruct((H*64, L), F32), jax.ShapeDtypeStruct((H*64, L), F32), jax.ShapeDtypeStruct((H, L, 128), F32), jax.ShapeDtypeStruct((H, L, 128), F32)),
        in_specs=[vm]*6, out_specs=[vm]*4,
        scratch_shapes=[pltpu.VMEM((nb, TILE, TILE), F32), pltpu.VMEM((nb, TILE, TILE), F32)],
        compiler_params=pltpu.CompilerParams(vmem_limit_bytes=56 * 2**20))(q, k, v, g, kt, vt)

def prep(queries, keys, values, d_heads, segments):
    seg = segments[:, None] == jnp.arange(64)[None, :]
    e = jnp.broadcast_to(seg.astype(BF)[None], queries.shape)
    f = jnp.broadcast_to(jnp.where(seg, 0.0, NEG).astype(BF)[None], queries.shape)
    lane = jnp.arange(64)
    f = jnp.where(lane < 4, f, 0).astype(BF)
    qa = jnp.concatenate([(queries.astype(F32) * 0.125).astype(BF), e], -1)
    ka = jnp.concatenate([keys, f], -1)
    z = jnp.zeros_like(values)
    va = jnp.concatenate([values, z], -1)
    ga = jnp.concatenate([d_heads, z], -1)
    kt = keys.transpose(0, 2, 1).reshape(-1, keys.shape[1])
    vt = values.transpose(0, 2, 1).reshape(-1, keys.shape[1])
    return qa, ka, va, ga, kt, vt

def attention(queries, keys, values, d_heads, segments):
    H, L, _ = queries.shape
    ht, dqt, dk, dv = attention_call(*prep(queries, keys, values, d_heads, segments))

    def back(t):
        return t.reshape(H, 64, L).transpose(0, 2, 1)

    return back(ht).astype(BF), (back(dqt) * 0.125).astype(BF), dk[..., :64].astype(BF), dv[..., :64].astype(BF)


def dot(a, b):
    return jnp.dot(a, b, preferred_element_type=F32)


def dot_t(a, b):
    return lax.dot_general(a, b, (((0,), (0,)), ((), ())), preferred_element_type=F32)


def dot_nt(a, b):
    return lax.dot_general(a, b, (((1,), (1,)), ((), ())), preferred_element_type=F32)


ORDER = (
    "own",
    "xgo",
    "gpr1",
    "gvc1",
    "gmb1",
    "gra1",
    "gpr2",
    "dygo",
    "gvc2",
    "grb1",
    "gmb2",
    "gpr3",
    "gvc3",
    "gra2",
    "xfwd",
    "grb2",
    "hots",
    "gpr4",
    "gvc4",
    "gmb3",
    "gra3",
    "gpr5",
    "swgo",
    "gvc5",
    "vrows",
    "grb3",
    "ln3",
    "ln0",
    "dyfwd",
    "ln2",
    "gmb4",
    "ln1",
    "dyall",
    "gma1",
    "gra4",
    "gfa1",
    "swin",
    "dh",
    "gmb5",
    "grb4",
    "gma2",
    "gra5",
    "gfb1",
    "grb5",
    "up0",
    "gma3",
    "gfa2",
    "up2",
    "up3",
    "gfb2",
    "up1",
    "gma4",
    "gf1",
    "gfa3",
    "gf0",
    "rfb1",
    "gfb3",
    "gma5",
    "qkv1",
    "rfa1",
    "qkv0",
    "rfb2",
    "at30",
    "at32",
    "gfa4",
    "at33",
    "gfb4",
    "rfa2",
    "at20",
    "at22",
    "rfb3",
    "gfa5",
    "at23",
    "gfb5",
    "dn1",
    "dn0",
    "rfa3",
    "gr0",
    "rfb4",
    "gr1",
    "at00",
    "rrb1",
    "at02",
    "rfa4",
    "at03",
    "rra1",
    "at10",
    "rfb5",
    "sfb",
    "at12",
    "rrb2",
    "at13",
    "rfa5",
    "sfa",
    "post0",
    "rra2",
    "post1",
    "wfb",
    "gp",
    "sbgo",
    "rrb3",
    "op1",
    "wfa",
    "gm0",
    "rra3",
    "om1",
    "op0",
    "rrb4",
    "bk0",
    "sbin",
    "om0",
    "rpr1",
    "rra4",
    "bk1",
    "rpr2",
    "rrb5",
    "srb",
    "vp",
    "rvc1",
    "gm1",
    "bm1",
    "bm0",
    "rma1",
    "rmb1",
    "rra5",
    "rpr3",
    "rvc2",
    "rma2",
    "rmb2",
    "bo",
    "rpr4",
    "wrb",
    "rvc3",
    "sra",
    "rma3",
    "rmb3",
    "rpr5",
    "spr",
    "rvc4",
    "rma4",
    "rmb4",
    "rvc5",
    "sv",
    "ig",
    "rma5",
    "sma",
    "wra",
    "rmb5",
    "smb",
    "wpr",
    "wv",
    "vo",
    "wma",
    "wmb",
)
LANES = 128
HALF = LANES // 2
VEC_ROWS = 32


def resident_fits(seq_size, dp_size, tok):
    return (
        D // dp_size == LANES
        and FF // dp_size // seq_size == LANES
        and HEADS // seq_size == 4
        and tok * seq_size <= 1024
        and tok % TILE == 0
    )


def rows_at(ref, index, count):
    return ref.at[pl.ds(pl.multiple_of(index * count, count), count)]


def columns_at(ref, index, count):
    return ref.at[:, pl.ds(pl.multiple_of(index * count, count), count)]


class Flat:
    def __init__(self, ref, count, stride=None, start=0):
        self.ref, self.count, self.start = ref, count, start
        self.stride = count if stride is None else stride

    @property
    def at(self):
        return self

    def __getitem__(self, index):
        first = pl.multiple_of(index * self.stride + self.start, self.count)
        return self.ref.at[pl.ds(first, self.count)]


class Stack:
    def __init__(self, ref, start, count):
        self.ref, self.start, self.count = ref, start, count

    @property
    def at(self):
        return self

    def __getitem__(self, index):
        return self.ref.at[index, pl.ds(self.start, self.count)]


def two(ref, make):
    return [make(Flat(ref, HALF, LANES, start), index) for index, start in enumerate((0, HALF))]


def lanes_like(shape):
    return lax.broadcasted_iota(jnp.int32, shape, len(shape) - 1)


def head_part(values, start):
    tile = values[:, start // LANES * LANES : start // LANES * LANES + LANES]
    return tile if start % LANES == 0 else pltpu.roll(tile, HEAD_DIM, 1)


def spin(tile, cosine, sine):
    lane = lanes_like(tile.shape)
    partner = jnp.where(lane < ROT // 2, pltpu.roll(tile, LANES - ROT // 2, 1), pltpu.roll(tile, ROT // 2, 1))
    return tile * cosine + partner * sine


def attend_head(head, block, refs):
    q_ref, k_ref, v_ref, g_ref, kt_ref, vt_ref, s_ref, p_ref, ht_ref, dqt_ref, dk_ref, dv_ref = refs
    here = pl.ds(block * TILE, TILE)
    wide = pl.ds(head * LANES, LANES)
    dims = pl.ds(head * HEAD_DIM, HEAD_DIM)
    query = q_ref[here, wide]
    grad = g_ref[here, wide]
    span = block + 1
    top = jnp.full((1, TILE), 2 * NEG, F32)
    for index in range(span):
        tile = nt(k_ref[pl.ds(index * TILE, TILE), wide], query)
        if index == block:
            key = lax.broadcasted_iota(jnp.int32, (TILE, TILE), 0)
            place = lax.broadcasted_iota(jnp.int32, (TILE, TILE), 1)
            tile = jnp.where(key <= place, tile, NEG)
        s_ref[index] = tile
        top = jnp.maximum(top, jnp.max(tile, axis=0, keepdims=True))
    total = jnp.zeros((1, TILE), F32)
    for index in range(span):
        raised = jnp.exp(s_ref[index] - top)
        s_ref[index] = raised
        total = total + jnp.sum(raised, axis=0, keepdims=True)
    share = 1.0 / total
    delta = jnp.zeros((1, TILE), F32)
    heads = jnp.zeros((HEAD_DIM, TILE), F32)
    for index in range(span):
        there = pl.ds(index * TILE, TILE)
        weights = s_ref[index] * share
        s_ref[index] = weights
        weights_b = weights.astype(BF)
        d_weights = nt(v_ref[there, wide], grad)
        p_ref[index] = d_weights
        d_value = nn(weights_b, grad)
        dv_ref[head, there, :] = d_value if index == block else dv_ref[head, there, :] + d_value
        heads = heads + nn(vt_ref[dims, there], weights_b)
        delta = delta + jnp.sum(weights * d_weights, axis=0, keepdims=True)
    ht_ref[dims, here] = heads
    d_query = jnp.zeros((HEAD_DIM, TILE), F32)
    for index in range(span):
        there = pl.ds(index * TILE, TILE)
        d_scores = (s_ref[index] * (p_ref[index] - delta)).astype(BF)
        d_key = nn(d_scores, query)
        dk_ref[head, there, :] = d_key if index == block else dk_ref[head, there, :] + d_key
        d_query = d_query + nn(kt_ref[dims, there], d_scores)
    dqt_ref[dims, here] = d_query


RESIDENT_NAMES = (
    "x_own",
    "dy_own",
    "w_mix_own",
    "w_proj_own",
    "w_rise_own",
    "w_fall_own",
    "vec_own",
    "seg_own",
    "pad",
    "cos",
    "sin",
    "block_out",
    "input_grad",
    "mix_fin",
    "proj_fin",
    "rise_fin",
    "fall_fin",
    "vec_out",
    "x",
    "dy",
    "hot",
    "w_mix",
    "w_proj_cols",
    "w_proj",
    "w_rise",
    "w_fall",
    "vec_all",
    "rows",
    "normed1",
    "normed2",
    "stat",
    "qk",
    "vg",
    "kt",
    "vt",
    "s",
    "p",
    "ht",
    "dqt",
    "dk",
    "dv",
    "attn",
    "d_mixed",
    "out_part",
    "back_part",
    "active",
    "d_up",
    "g_mix",
    "g_proj",
    "g_proj_cols",
    "g_rise",
    "g_fall",
    "c_mix",
    "c_proj",
    "c_rise",
    "c_fall",
    "out_cross",
    "out_came",
    "back_cross",
    "back_came",
    "sums",
    "vec_part",
    "vec_came",
    "vec_fin",
    "m_x",
    "m_dy",
    "m_hot",
    "m_vec",
    "m_mix",
    "m_proj",
    "m_rise",
    "m_fall",
    "m_swap",
    "m_own",
    "m_swap2",
    "m_rmix",
    "m_rproj",
    "m_rrise",
    "m_rfall",
    "m_out",
    "m_back",
    "m_vec2",
    "m_fmix",
    "m_fproj",
    "m_frise",
    "m_ffall",
    "m_fvec",
    "m_fin",
)


class Names:
    def __init__(self, refs):
        for name, ref in zip(RESIDENT_NAMES, refs, strict=True):
            setattr(self, name, ref)


def resident_kernel(seq_size, dp_size, *refs):
    r = Names(refs)
    place = Place(seq_size, dp_size)
    half = place.half
    tok = r.x_own.shape[0]
    length = r.x.shape[0]
    wide = r.w_proj.shape[0]
    mixed_wide = 3 * wide
    units = LANES
    each = dp_size // seq_size
    heads_n = wide // HEAD_DIM
    blocks = length // TILE

    own = {}

    def bring(name, src, dst):
        copy = pltpu.make_async_copy(src, dst, r.m_own.at[len(own)])
        copy.start()
        own[name] = copy

    bring("mix", columns_at(r.w_mix_own, place.seq, mixed_wide), rows_at(r.w_mix, place.dp, LANES))
    bring("proj", columns_at(r.w_proj_own, place.seq, wide), rows_at(r.w_proj_cols, place.dp, LANES))
    bring("x", r.x_own, rows_at(r.x, place.seq, tok))
    bring("dy", r.dy_own, rows_at(r.dy, place.seq, tok))
    for index in range(dp_size):
        bring(
            ("rise", index),
            columns_at(r.w_rise_own, index * seq_size + place.seq, units),
            rows_at(r.w_rise, place.dp, LANES).at[:, pl.ds(index * units, units)],
        )
    bring("fall", rows_at(r.w_fall_own, place.seq, units), rows_at(r.w_fall, place.dp, units))
    r.vec_all[place.dp] = r.vec_own[...]
    kind = lax.broadcasted_iota(jnp.int32, (LANES, tok), 0) - HEAD_DIM
    hot_own = jnp.where(r.seg_own[...] == kind, 1.0, 0.0)
    rows_at(r.hot, place.seq, tok)[...] = hot_own.T.astype(BF)

    gathers = {"pr": RingGather(place, Flat(r.w_proj_cols, LANES), r.m_proj), "vc": RingGather(place, r.vec_all, r.m_vec)}
    for name, ref, sems in (("m", r.w_mix, r.m_mix), ("r", r.w_rise, r.m_rise), ("f", r.w_fall, r.m_fall)):
        gathers[name + "a"], gathers[name + "b"] = two(
            ref, lambda part, index: RingGather(place, part, sems.at[index])
        )
    reduces = {
        "pr": RingReduce(place, Flat(r.g_proj_cols, LANES), r.c_proj, r.m_rproj),
        "vc": RingReduce(place, r.vec_part, r.vec_came, r.m_vec2),
    }
    for name, ref, came, sems in (
        ("m", r.g_mix, r.c_mix, r.m_rmix),
        ("r", r.g_rise, r.c_rise, r.m_rrise),
        ("f", r.g_fall, r.c_fall, r.m_rfall),
    ):
        reduces[name + "a"], reduces[name + "b"] = two(
            ref, lambda part, index: RingReduce(place, part, came.at[index], sems.at[index])
        )

    def gather(*ticks):
        for tick in ticks:
            gathers[tick[:2]].tick(int(tick[2]))

    def reduce(*ticks):
        for tick in ticks:
            reduces[tick[:2]].tick(int(tick[2]))

    x_move = SeqGather(place, Flat(r.x, tok), r.m_x)
    dy_move = SeqGather(place, Flat(r.dy, tok), r.m_dy)
    hot_move = SeqGather(place, Flat(r.hot, tok), r.m_hot)
    out = SeqReduce(place, Flat(r.out_part, tok), r.out_cross, r.out_came, r.m_out)
    back = SeqReduce(place, Flat(r.back_part, tok), r.back_cross, r.back_came, r.m_back)

    def final(out_ref, sems, own_part):
        return SeqGather(place, out_ref, sems, own_part)

    finals = {"pr": final(r.proj_fin, r.m_fproj, rows_at(r.g_proj_cols, place.dp, LANES))}
    for name, out_ref, sems, ref in (
        ("m", r.mix_fin, r.m_fmix, r.g_mix),
        ("r", r.rise_fin, r.m_frise, r.g_rise),
        ("f", r.fall_fin, r.m_ffall, r.g_fall),
    ):
        for index, side in enumerate("ab"):
            start = index * HALF
            own_part = Flat(ref, HALF, LANES, start)[place.dp]
            finals[name + side] = final(Stack(out_ref, start, HALF), sems.at[index], own_part)
    f_vec = final(r.vec_fin, r.m_fvec, None)
    leaving = []

    def leave(src, dst):
        copy = pltpu.make_async_copy(src, dst, r.m_fin.at[len(leaving)])
        copy.start()
        leaving.append(copy)

    pieces = {}

    def piece(name, *given):
        def note(run):
            pieces[name] = functools.partial(run, *given)
            return run

        return note

    def tile_rows(block):
        return pl.ds(pl.multiple_of(block * TILE, TILE), TILE)

    def gather(stream, step):
        gathers[stream].tick(step)

    def reduce(stream, step):
        reduces[stream].tick(step)

    for stream in gathers:
        for step in range(1, half + 2):
            piece(f"g{stream}{step}", stream, step)(gather)
            piece(f"r{stream}{step}", stream, step)(reduce)

    @piece("own")
    def _():
        for copy in own.values():
            copy.wait()

    @piece("xgo")
    def _():
        x_move.begin()
        hot_move.begin()

    piece("dygo")(dy_move.begin)

    @piece("xfwd")
    def _():
        x_move.forward()
        hot_move.forward()

    piece("dyfwd")(dy_move.forward)

    @piece("hots")
    def _():
        for step in range(place.pairs):
            hot_move.across_arrived(step)

    @piece("dyall")
    def _():
        for step in range(place.pairs):
            dy_move.across_arrived(step)

    @piece("vrows")
    def _():
        for index in range(dp_size):
            at = slice(index * LANES, (index + 1) * LANES)
            for row in range(6):
                r.rows[row : row + 1, at] = r.vec_all[index, row : row + 1, :]
            r.rows[6:7, at] = r.vec_all[index, pl.ds(9 + place.seq, 1), :]
        for index in range(each):
            for row in range(3):
                start = (index * 3 + row) * LANES
                r.rows[7:8, start : start + LANES] = r.vec_all[place.seq * each + index, 6 + row : 7 + row, :]

    chunk = 64

    def normalize(block):
        @pl.loop(0, tok // chunk)
        def _(step):
            here = pl.ds(pl.multiple_of(block * tok + step * chunk, chunk), chunk)
            values = r.x[here, :].astype(F32)
            mean = jnp.sum(values, axis=-1, keepdims=True) * (1.0 / D)
            center = values - mean
            rstd = lax.rsqrt(jnp.sum(center * center, axis=-1, keepdims=True) * (1.0 / D) + EPS)
            n = center * rstd
            r.normed1[here, :] = (n * r.rows[0:1, :] + r.rows[1:2, :]).astype(BF)
            r.normed2[here, :] = (n * r.rows[2:3, :] + r.rows[3:4, :]).astype(BF)
            lane = lanes_like((chunk, LANES))
            r.stat[here, :] = jnp.where(lane < HEAD_DIM, mean, rstd)

    def unit_rows(here):
        stat = r.stat[here, :]
        return (r.x[here, :].astype(F32) - stat[:, 0:1]) * stat[:, HEAD_DIM : HEAD_DIM + 1]

    @piece("ln0")
    def _():
        normalize(place.seq)

    @piece("ln1")
    def _():
        x_move.across_arrived(0)
        normalize(place.sibling)

    @piece("ln2")
    def _():
        normalize(place.pair_peer(1))

    @piece("ln3")
    def _():
        x_move.across_arrived(1)
        normalize(place.across_source(1))

    def swap(step):
        peer = place.seq_peer(step)
        src, dst = rows_at(r.w_proj_cols, peer, wide), columns_at(r.w_proj, place.seq, wide)
        return send(src, dst, r.m_swap, step, {"seq": peer})

    def swap_arrival(step):
        source = place.seq_peer(-step)
        src, dst = rows_at(r.w_proj_cols, source, wide), columns_at(r.w_proj, source, wide)
        return send(src, dst, r.m_swap, step, {"seq": place.seq_peer(step)})

    @piece("swgo")
    def _():
        for step in range(1, seq_size):
            swap(step).start()
        columns_at(r.w_proj, place.seq, wide)[...] = rows_at(r.w_proj_cols, place.seq, wide)[...]

    @piece("swin")
    def _():
        for step in range(1, seq_size):
            swap_arrival(step).wait_recv()

    def mix_columns(first, last):
        @pl.loop(first, last)
        def _(block):
            here = tile_rows(block)
            mixed = nn(r.normed1[here, :], r.w_mix[...]) + r.rows[7:8, 0:mixed_wide]
            cosine, sine = r.cos[here, :], r.sin[here, :]
            lane = lanes_like((TILE, LANES))
            hot = r.hot[here, :].astype(F32)
            cold = jnp.where((lane >= HEAD_DIM) & (lane < HEAD_DIM + 4), (1.0 - hot) * NEG, 0.0)
            for head in range(heads_n):
                start = head * 3 * HEAD_DIM
                query = spin(head_part(mixed, start), cosine, sine) * HEAD_DIM**-0.5
                key = spin(head_part(mixed, start + HEAD_DIM), cosine, sine)
                value = head_part(mixed, start + 2 * HEAD_DIM)
                at = pl.ds(head * LANES, LANES)
                at_more = pl.ds((heads_n + head) * LANES, LANES)
                dims = pl.ds(head * HEAD_DIM, HEAD_DIM)
                r.qk[here, at] = jnp.where(lane < HEAD_DIM, query, hot).astype(BF)
                r.qk[here, at_more] = jnp.where(lane < HEAD_DIM, key, cold).astype(BF)
                r.vg[here, at] = jnp.where(lane < HEAD_DIM, value, 0.0).astype(BF)
                r.kt[dims, here] = key.T[:HEAD_DIM, :].astype(BF)
                r.vt[dims, here] = value.T[:HEAD_DIM, :].astype(BF)

    middle = blocks // 2
    piece("qkv0", 0, middle)(mix_columns)
    piece("qkv1", middle, blocks)(mix_columns)
    padded = length - r.pad[0]

    @piece("dh")
    def _():
        @pl.loop(0, blocks)
        def _(block):
            here = tile_rows(block)
            place_in = lax.broadcasted_iota(jnp.int32, (TILE, wide), 0) + block * TILE
            d_heads = jnp.where(place_in < padded, nt(r.dy[here, :], r.w_proj[...]), 0.0)
            for head in range(heads_n):
                at_more = pl.ds((heads_n + head) * LANES, LANES)
                r.vg[here, at_more] = head_part(d_heads, head * HEAD_DIM).astype(BF)

    second = heads_n * LANES
    head_refs = (
        r.qk.at[:, pl.ds(0, second)],
        r.qk.at[:, pl.ds(second, second)],
        r.vg.at[:, pl.ds(0, second)],
        r.vg.at[:, pl.ds(second, second)],
        r.kt,
        r.vt,
        r.s,
        r.p,
        r.ht,
        r.dqt,
        r.dk,
        r.dv,
    )

    def attend_blocks(head, first, last):
        for block in range(first, last):
            if block == 0:
                attend_head(head, block, head_refs)
            elif block == 1:
                attend_head(head, block, head_refs)
            elif block == 2:
                attend_head(head, block, head_refs)
            else:
                attend_head(head, block, head_refs)

    for head in range(heads_n):
        piece(f"at{head}0", head, 0, middle)(attend_blocks)
        for block in range(middle, blocks):
            piece(f"at{head}{block}", head, block, block + 1)(attend_blocks)

    def heads_back(first, last):
        @pl.loop(first, last)
        def _(block):
            here = tile_rows(block)
            place_in = lax.broadcasted_iota(jnp.int32, (TILE, wide), 0) + block * TILE
            r.attn[here, :] = jnp.where(place_in < padded, r.ht[:, here].T, 0.0).astype(BF)
            d_query = r.dqt[:, here].T * HEAD_DIM**-0.5
            cosine, sine = r.cos[here, :], -r.sin[here, :]
            lane = lanes_like((TILE, LANES))
            parts = []
            for head in range(heads_n):
                parts.append(spin(head_part(d_query, head * HEAD_DIM), cosine, sine))
                parts.append(spin(r.dk[head, here, :], cosine, sine))
                parts.append(r.dv[head, here, :])
            for index in range(len(parts) // 2):
                tile = jnp.where(lane < HEAD_DIM, parts[2 * index], pltpu.roll(parts[2 * index + 1], HEAD_DIM, 1))
                at = slice(index * LANES, (index + 1) * LANES)
                tile = tile.astype(BF)
                r.d_mixed[here, at] = tile
                r.sums[6:7, at] += jnp.sum(tile.astype(F32), axis=0, keepdims=True)

    piece("post0", 0, middle)(heads_back)
    piece("post1", middle, blocks)(heads_back)
    big = 512

    def weight_grad(out_ref, left, right, index):
        at = pl.ds(index * big, big)
        out_ref[at, :] = tn(left[:, at], right[...]).astype(BF)

    for index in range(D // big):
        piece(f"gm{index}", r.g_mix, r.normed1, r.d_mixed, index)(weight_grad)
        piece(f"gr{index}", r.g_rise, r.normed2, r.d_up, index)(weight_grad)
        piece(f"gf{index}", r.g_fall, r.active, r.dy, index)(weight_grad)

    @piece("gp")
    def _():
        r.g_proj[...] = tn(r.attn[...], r.dy[...]).astype(BF)

    def swap_back(step):
        peer = place.seq_peer(step)
        src, dst = columns_at(r.g_proj, peer, wide), rows_at(r.g_proj_cols, place.seq, wide)
        return send(src, dst, r.m_swap2, step, {"seq": peer})

    def swap_back_arrival(step):
        source = place.seq_peer(-step)
        src, dst = columns_at(r.g_proj, source, wide), rows_at(r.g_proj_cols, source, wide)
        return send(src, dst, r.m_swap2, step, {"seq": place.seq_peer(step)})

    @piece("sbgo")
    def _():
        for step in range(1, seq_size):
            swap_back(step).start()
        rows_at(r.g_proj_cols, place.seq, wide)[...] = columns_at(r.g_proj, place.seq, wide)[...]

    @piece("sbin")
    def _():
        for step in range(1, seq_size):
            swap_back_arrival(step).wait_recv()

    def upward(block):
        here = tile_rows(block)
        up = nn(r.normed2[here, :], r.w_rise[...]) + r.rows[6:7, :]
        share = 0.5 + 0.5 * lax.erf(up * 0.5**0.5)
        r.active[here, :] = (up * share).astype(BF)
        bell = jnp.exp(-0.5 * up * up) * (2 * np.pi) ** -0.5
        r.d_up[here, :] = (share + up * bell).astype(BF)

    def downward(first, last):
        @pl.loop(first, last)
        def _(block):
            here = tile_rows(block)
            d_up = (r.d_up[here, :].astype(F32) * nt(r.dy[here, :], r.w_fall[...])).astype(BF)
            r.d_up[here, :] = d_up
            r.sums[5:6, :] += jnp.sum(d_up.astype(F32), axis=0, keepdims=True)

    for block in range(blocks):
        piece(f"up{block}", block)(upward)
    piece("dn0", 0, middle)(downward)
    piece("dn1", middle, blocks)(downward)

    def out_rows(step):
        first = ((place.pair + step) % place.pairs) * (2 * tok // TILE)
        @pl.loop(0, 2 * tok // TILE)
        def _(block):
            here = tile_rows(first + block)
            part = nn(r.attn[here, :], r.w_proj[...]) + nn(r.active[here, :], r.w_fall[...])
            r.out_part[here, :] = part.astype(BF)

        out.over_start(step)

    def back_rows(step):
        first = ((place.pair + step) % place.pairs) * (2 * tok // TILE)
        @pl.loop(0, 2 * tok // TILE)
        def _(block):
            here = tile_rows(first + block)
            d_one = nt(r.d_mixed[here, :], r.w_mix[...])
            d_two = nt(r.d_up[here, :], r.w_rise[...])
            r.back_part[here, :] = (r.rows[0:1, :] * d_one + r.rows[2:3, :] * d_two).astype(BF)
            n = unit_rows(here)
            r.sums[0:1, :] += jnp.sum(d_one * n, axis=0, keepdims=True)
            r.sums[1:2, :] += jnp.sum(d_one, axis=0, keepdims=True)
            r.sums[2:3, :] += jnp.sum(d_two * n, axis=0, keepdims=True)
            r.sums[3:4, :] += jnp.sum(d_two, axis=0, keepdims=True)
            r.sums[4:5, :] += jnp.sum(r.dy[here, :].astype(F32), axis=0, keepdims=True)

        back.over_start(step)

    for step in range(2):
        piece(f"op{step}", step)(out_rows)
        piece(f"bk{step}", step)(back_rows)
        piece(f"om{step}", step)(out.over_add)
        piece(f"bm{step}", step)(back.over_add)

    @piece("vp")
    def _():
        for index in range(dp_size):
            at = slice(index * LANES, (index + 1) * LANES)
            r.vec_part[index, 0:6, :] = r.sums[0:6, at]
            for row in range(mixed_wide // LANES):
                r.vec_part[index, 6 + row : 7 + row, :] = r.sums[6:7, row * LANES : (row + 1) * LANES]

    def settle(name):
        move = finals[name]
        move.begin()
        leave(move.own, move.full.at[place.seq])

    for name in finals:
        piece(f"s{name}", name)(settle)
        piece(f"w{name}")(finals[name].forward)

    mine = pl.ds(pl.multiple_of(place.seq * tok, tok), tok)

    @piece("bo")
    def _():
        total = out.total()
        block_out = total + r.x[mine, :].astype(F32) + (r.rows[4:5, :] + r.rows[5:6, :])
        r.out_cross[0] = block_out.astype(BF)
        leave(r.out_cross.at[0], r.block_out)

    @piece("ig")
    def _():
        scaled = back.total()
        n = unit_rows(mine)
        rstd = r.stat[mine, HEAD_DIM : HEAD_DIM + 1]
        back_mean = jnp.sum(scaled, axis=-1, keepdims=True) * (1.0 / D)
        back_n = jnp.sum(scaled * n, axis=-1, keepdims=True) * (1.0 / D)
        input_grad = r.dy[mine, :].astype(F32) + rstd * (scaled - back_mean - n * back_n)
        r.back_cross[0] = input_grad.astype(BF)
        leave(r.back_cross.at[0], r.input_grad)

    @piece("sv")
    def _():
        r.vec_fin[place.seq] = r.vec_part[place.dp]
        f_vec.begin()

    piece("wv")(f_vec.forward)

    @piece("vo")
    def _():
        f_vec.finish()
        norm = r.vec_fin[0, 0:4, :]
        for index in range(1, seq_size):
            norm = norm + r.vec_fin[index, 0:4, :]
        r.vec_out[0:4, :] = norm
        r.vec_out[4:5, :] = r.vec_fin[0, 4:5, :]
        source = r.vec_fin[place.dp // each]
        pick = place.dp % each
        part = source[6:9, :]
        for index in range(1, each):
            part = jnp.where(pick == index, source[6 + 3 * index : 9 + 3 * index, :], part)
        r.vec_out[5:8, :] = part
        for index in range(seq_size):
            r.vec_out[8 + index : 9 + index, :] = r.vec_fin[index, 5:6, :]

    place.greet_near()
    r.sums[...] = jnp.zeros(r.sums.shape, F32)
    r.vec_part[...] = jnp.zeros(r.vec_part.shape, F32)
    assert sorted(ORDER) == sorted(pieces)
    for name in ORDER:
        pieces[name]()
    for move in finals.values():
        move.finish()
    for copy in leaving:
        copy.wait()
    for move in (*gathers.values(), *reduces.values(), out, back):
        move.finish()
    for move in (x_move, hot_move, dy_move):
        move.sent()
    for step in range(1, seq_size):
        swap(step).wait_send()
        swap_back(step).wait_send()


def resident_call(seq_size, dp_size, *args):
    x, _, _, _, _, w_fall, vec, _, _, _, _ = args
    tok = x.shape[0]
    length = tok * seq_size
    half, pairs = dp_size // 2, seq_size // 2
    wide = HEADS // seq_size * HEAD_DIM
    units_all = dp_size * LANES
    heads_n = wide // HEAD_DIM

    def half_vmem(*shape):
        return pltpu.VMEM(shape, BF)

    def full_vmem(*shape):
        return pltpu.VMEM(shape, F32)

    def ring(columns):
        return half_vmem(2, 2, half, HALF, columns)

    def pair_of_sems(count):
        return pltpu.SemaphoreType.DMA((2, 2, count))

    any_spec = pl.BlockSpec(memory_space=pl.ANY)
    vmem = pl.BlockSpec(memory_space=pltpu.VMEM)
    smem = pl.BlockSpec(memory_space=pltpu.SMEM)
    scratch = [
        half_vmem(length, D),
        half_vmem(length, D),
        half_vmem(length, LANES),
        half_vmem(D, 3 * wide),
        half_vmem(D, wide),
        half_vmem(wide, D),
        half_vmem(D, units_all),
        half_vmem(units_all, D),
        full_vmem(dp_size, VEC_ROWS, LANES),
        full_vmem(8, D),
        half_vmem(length, D),
        half_vmem(length, D),
        full_vmem(length, LANES),
        half_vmem(length, units_all),
        half_vmem(length, units_all),
        half_vmem(wide, length),
        half_vmem(wide, length),
        full_vmem(length // TILE, TILE, TILE),
        full_vmem(length // TILE, TILE, TILE),
        full_vmem(wide, length),
        full_vmem(wide, length),
        full_vmem(heads_n, length, LANES),
        full_vmem(heads_n, length, LANES),
        half_vmem(length, wide),
        half_vmem(length, 3 * wide),
        half_vmem(length, D),
        half_vmem(length, D),
        half_vmem(length, units_all),
        half_vmem(length, units_all),
        half_vmem(D, 3 * wide),
        half_vmem(wide, D),
        half_vmem(D, wide),
        half_vmem(D, units_all),
        half_vmem(units_all, D),
        ring(3 * wide),
        half_vmem(2, half, LANES, wide),
        ring(units_all),
        ring(D),
        half_vmem(pairs, tok, D),
        half_vmem(pairs, tok, D),
        half_vmem(pairs, tok, D),
        half_vmem(pairs, tok, D),
        full_vmem(8, D),
        full_vmem(dp_size, VEC_ROWS, LANES),
        full_vmem(2, half, VEC_ROWS, LANES),
        full_vmem(seq_size, VEC_ROWS, LANES),
    ]
    scratch += [sems_of(2 * pairs)] * 3 + [sems_of(2 * half)]
    scratch += [pair_of_sems(2 * half), sems_of(2 * half), pair_of_sems(2 * half), pair_of_sems(2 * half)]
    scratch += [sems_of(seq_size), pltpu.SemaphoreType.DMA((dp_size + 6,)), sems_of(seq_size)]
    scratch += [pair_of_sems(2 * half), sems_of(2 * half), pair_of_sems(2 * half), pair_of_sems(2 * half)]
    scratch += [sems_of(2 * pairs)] * 2 + [sems_of(2 * half)]
    scratch += [pair_of_sems(2 * pairs), sems_of(2 * pairs), pair_of_sems(2 * pairs), pair_of_sems(2 * pairs)]
    scratch += [sems_of(2 * pairs)]
    scratch += [pltpu.SemaphoreType.DMA((12,))]
    return pl.pallas_call(
        functools.partial(resident_kernel, seq_size, dp_size),
        out_shape=(
            jax.ShapeDtypeStruct((tok, D), BF),
            jax.ShapeDtypeStruct((tok, D), BF),
            jax.ShapeDtypeStruct((seq_size, LANES, 3 * wide), BF),
            jax.ShapeDtypeStruct((seq_size, LANES, wide), BF),
            jax.ShapeDtypeStruct((seq_size, LANES, units_all), BF),
            jax.ShapeDtypeStruct((seq_size, LANES, D), BF),
            jax.ShapeDtypeStruct((16, LANES), F32),
        ),
        in_specs=[any_spec] * 6 + [vmem, vmem, smem, vmem, vmem],
        out_specs=[any_spec] * 6 + [vmem],
        scratch_shapes=scratch,
        compiler_params=pltpu.CompilerParams(
            collective_id=2, has_side_effects=True, vmem_limit_bytes=RESIDENT_VMEM
        ),
    )(*args)


RESIDENT_VMEM = 63 * 2**20


def finish_kernel(seq_size, dp_size, refs):
    (block, grad, mix, proj, rise, fall, vec), outs = refs[:7], refs[7:]
    (block_out, grad_out, mix_out, proj_out, rise_out, fall_out), vec_outs = outs[:6], outs[6:]
    block_out[...] = block[...]
    grad_out[...] = grad[...]
    fall_out[...] = fall[...].astype(F32)
    for group in range(seq_size):
        for ref, out in ((mix, mix_out), (proj, proj_out)):
            columns = ref.shape[2]
            out[:, group * columns : (group + 1) * columns] = ref[group].astype(F32)
        for index in range(dp_size):
            start = (index * seq_size + group) * LANES
            part = rise[group, :, index * LANES : (index + 1) * LANES]
            rise_out[:, start : start + LANES] = part.astype(F32)

    @pl.when(pl.program_id(0) == 0)
    def _():
        row = 0
        for out in vec_outs:
            for start in range(0, out.shape[0], LANES):
                out[start : start + LANES] = vec[row]
                row += 1


def finish_call(seq_size, dp_size, block, grad, mix, proj, rise, fall, vec):
    steps = 4
    tok = block.shape[0]
    few = LANES // steps
    fall = fall.reshape(seq_size * LANES, D)

    def rows_spec(array):
        return pl.BlockSpec((array.shape[0] // steps, array.shape[1]), lambda i: (i, 0))

    def group_spec(array):
        return pl.BlockSpec((seq_size, few, array.shape[2]), lambda i: (0, i, 0))

    def vec_spec(size):
        return pl.BlockSpec((size,), lambda i: (0,))

    vec_sizes = (LANES,) * 5 + (3 * LANES, seq_size * LANES)
    return pl.pallas_call(
        lambda *refs: finish_kernel(seq_size, dp_size, refs),
        grid=(steps,),
        out_shape=(
            jax.ShapeDtypeStruct((tok, D), BF),
            jax.ShapeDtypeStruct((tok, D), BF),
            jax.ShapeDtypeStruct((LANES, 3 * D), F32),
            jax.ShapeDtypeStruct((LANES, D), F32),
            jax.ShapeDtypeStruct((LANES, FF), F32),
            jax.ShapeDtypeStruct((seq_size * LANES, D), F32),
        )
        + tuple(jax.ShapeDtypeStruct((size,), F32) for size in vec_sizes),
        in_specs=[rows_spec(block), rows_spec(grad), group_spec(mix), group_spec(proj), group_spec(rise)]
        + [rows_spec(fall), pl.BlockSpec((16, LANES), lambda i: (0, 0))],
        out_specs=[
            pl.BlockSpec((tok // steps, D), lambda i: (i, 0)),
            pl.BlockSpec((tok // steps, D), lambda i: (i, 0)),
            pl.BlockSpec((few, 3 * D), lambda i: (i, 0)),
            pl.BlockSpec((few, D), lambda i: (i, 0)),
            pl.BlockSpec((few, FF), lambda i: (i, 0)),
            pl.BlockSpec((seq_size * few, D), lambda i: (i, 0)),
        ]
        + [vec_spec(size) for size in vec_sizes],
    )(block, grad, mix, proj, rise, fall, vec)


def resident_tables(length):
    cosine, sine = angle_tables(length)
    half = ROT // 2
    cos_table = np.ones((length, LANES), np.float32)
    sin_table = np.zeros((length, LANES), np.float32)
    cos_table[:, :half] = cosine
    cos_table[:, half:ROT] = cosine
    sin_table[:, :half] = -sine
    sin_table[:, half:ROT] = sine
    return jnp.asarray(cos_table), jnp.asarray(sin_table)


def resident_shards(
    tokens,
    cotangent,
    norm1_gain,
    norm1_bias,
    norm2_gain,
    norm2_bias,
    qkv_weight,
    qkv_bias,
    out_weight,
    out_bias,
    up_weight,
    up_bias,
    down_weight,
    down_bias,
    segment_ids,
    pad_length,
):
    seq_size, dp_size = lax.axis_size("seq"), lax.axis_size("dp")
    tok = tokens.shape[1]
    vectors = (norm1_gain, norm1_bias, norm2_gain, norm2_bias, out_bias, down_bias, qkv_bias, up_bias)
    vec = jnp.zeros((VEC_ROWS, LANES), F32)
    start = 0
    for piece in vectors:
        rows = piece.shape[0] // LANES
        vec = vec + jnp.pad(piece.astype(F32).reshape(rows, LANES), ((start, VEC_ROWS - start - rows), (0, 0)))
        start += rows
    cosine, sine = resident_tables(tok * seq_size)
    parts = resident_call(
        seq_size,
        dp_size,
        tokens[0],
        cotangent[0],
        qkv_weight,
        out_weight,
        up_weight,
        down_weight,
        vec,
        segment_ids,
        pad_length,
        cosine,
        sine,
    )
    done = finish_call(seq_size, dp_size, *parts)
    block_out, input_grad, g_mix, g_proj, g_rise, g_fall = done[:6]
    norm1_g, norm1_b, norm2_g, norm2_b, column, b_mix, b_rise = done[6:]
    return (
        block_out[None],
        input_grad[None],
        norm1_g,
        norm1_b,
        norm2_g,
        norm2_b,
        g_mix,
        b_mix,
        g_proj,
        column,
        g_rise,
        b_rise,
        g_fall,
        column,
    )


def streamed_shards(
    tokens,
    cotangent,
    norm1_gain,
    norm1_bias,
    norm2_gain,
    norm2_bias,
    qkv_weight,
    qkv_bias,
    out_weight,
    out_bias,
    up_weight,
    up_bias,
    down_weight,
    down_bias,
    segment_ids,
    pad_length,
):
    seq_size, dp_size = lax.axis_size("seq"), lax.axis_size("dp")
    seq = lax.axis_index("seq")
    dp = lax.axis_index("dp")
    tok = tokens.shape[1]
    length = tok * seq_size
    heads_n = HEADS // seq_size
    rows = D // dp_size
    wide = heads_n * HEAD_DIM
    units = FF // dp_size // seq_size

    mix = qkv_weight.reshape(rows, seq_size, heads_n, 3, HEAD_DIM)
    mix = lax.dynamic_index_in_dim(mix, seq, 1, keepdims=False)
    mix = mix.transpose(0, 2, 1, 3).reshape(rows, 3 * wide)
    proj = lax.dynamic_slice_in_dim(out_weight, seq * wide, wide, 1)
    rise = up_weight.reshape(rows, dp_size, seq_size, units)
    rise = lax.dynamic_index_in_dim(rise, seq, 2, keepdims=False).reshape(rows, dp_size * units)
    fall = lax.dynamic_slice_in_dim(down_weight, seq * units, units, 0)
    vec = jnp.concatenate(
        [norm1_gain, norm1_bias, norm2_gain, norm2_bias, out_bias, down_bias, qkv_bias, up_bias]
    )
    vec_len = vec.shape[0]
    vec = jnp.pad(vec, (0, 2048 - vec_len)).reshape(16, 128)
    seg = jnp.broadcast_to(segment_ids, (8, tok))
    x_all, dy_all, w_mix, _, w_rise, w_fall, vec_all, seg_all, w_proj = gather_all(
        seq_size, dp_size, tokens[0], cotangent[0], mix, proj, rise, fall, vec, seg
    )
    x = x_all.reshape(length, D).astype(F32)
    dy = dy_all.reshape(length, D)
    w_mix = w_mix.reshape(D, 3 * wide)
    w_rise = w_rise.reshape(D, dp_size * units)
    w_fall = w_fall.reshape(dp_size * units, D)
    w_proj = w_proj.reshape(seq_size, wide, wide).transpose(1, 0, 2).reshape(wide, D)
    segments = seg_all[:, 0, :].reshape(length)
    vec_all = vec_all.reshape(dp_size, 2048)[:, :vec_len].astype(F32)
    g1, s1, g2, s2, b_proj, b_fall = (
        vec_all[:, i * rows : (i + 1) * rows].reshape(D) for i in range(6)
    )
    b_mix = vec_all[:, 6 * rows : 9 * rows].reshape(seq_size, heads_n, 3, HEAD_DIM)
    b_mix = lax.dynamic_index_in_dim(b_mix, seq, 0, keepdims=False)
    b_mix = b_mix.transpose(1, 0, 2).reshape(3 * wide)
    b_rise = vec_all[:, 9 * rows :].reshape(dp_size, seq_size, units)
    b_rise = lax.dynamic_index_in_dim(b_rise, seq, 1, keepdims=False).reshape(dp_size * units)

    center = x - jnp.mean(x, axis=-1, keepdims=True)
    rstd = lax.rsqrt(jnp.mean(center * center, axis=-1, keepdims=True) + EPS)
    n = center * rstd
    normed1 = (n * g1 + s1).astype(BF)
    normed2 = (n * g2 + s2).astype(BF)
    valid = (jnp.arange(length, dtype=jnp.int32) < length - pad_length[0]).astype(F32)[:, None]
    cosine, sine = (jnp.asarray(t) for t in angle_tables(length))

    mixed = dot(normed1, w_mix) + b_mix
    mixed = mixed.reshape(length, 3, heads_n, HEAD_DIM).transpose(1, 2, 0, 3)
    queries = turn(mixed[0], cosine, sine, 1.0).astype(BF)
    keys = turn(mixed[1], cosine, sine, 1.0).astype(BF)
    values = mixed[2].astype(BF)
    d_heads = (dot_nt(dy, w_proj) * valid).astype(BF)
    d_heads = d_heads.reshape(length, heads_n, HEAD_DIM).transpose(1, 0, 2)
    heads, d_q, d_k, d_v = attention(queries, keys, values, d_heads, segments)
    attn_rows = (heads.transpose(1, 0, 2).reshape(length, wide).astype(F32) * valid).astype(BF)
    d_mixed = jnp.stack(
        [
            turn(d_q.astype(F32), cosine, sine, -1.0).astype(BF),
            turn(d_k.astype(F32), cosine, sine, -1.0).astype(BF),
            d_v,
        ]
    )
    d_mixed = d_mixed.transpose(2, 0, 1, 3).reshape(length, 3 * wide)

    upward = dot(normed2, w_rise) + b_rise
    active = jax.nn.gelu(upward, approximate=False).astype(BF)
    slope = 0.5 * (1 + lax.erf(upward * (0.5**0.5))) + upward * jnp.exp(
        -0.5 * upward * upward
    ) * ((2 * np.pi) ** -0.5)
    d_up = (slope * dot_nt(dy, w_fall)).astype(BF)
    out_part = (dot(attn_rows, w_proj) + dot(active, w_fall)).astype(BF)
    d_n1 = dot_nt(d_mixed, w_mix)
    d_n2 = dot_nt(d_up, w_rise)
    back_part = (g1 * d_n1 + g2 * d_n2).astype(BF)

    g_mix = dot_t(normed1, d_mixed).astype(BF).reshape(dp_size, rows, 3 * wide)
    g_proj = dot_t(attn_rows, dy).astype(BF).reshape(dp_size // seq_size, rows, seq_size, wide)
    g_proj = g_proj.transpose(2, 0, 1, 3)
    g_rise = dot_t(normed2, d_up).astype(BF).reshape(dp_size, rows, dp_size * units)
    g_fall = dot_t(active, dy).astype(BF).reshape(dp_size, units, D)
    dyf = dy.astype(F32)
    vec_part = jnp.concatenate(
        [
            t.reshape(dp_size, -1)
            for t in (
                jnp.sum(d_n1 * n, axis=0),
                jnp.sum(d_n1, axis=0),
                jnp.sum(d_n2 * n, axis=0),
                jnp.sum(d_n2, axis=0),
                jnp.sum(dyf, axis=0),
                jnp.sum(d_up.astype(F32), axis=0),
            )
        ]
        + [jnp.broadcast_to(jnp.sum(d_mixed.astype(F32), axis=0)[None], (dp_size, 3 * wide))],
        axis=1,
    )
    part_len = vec_part.shape[1]
    vec_part = jnp.pad(vec_part, ((0, 0), (0, 2048 - part_len))).reshape(dp_size, 16, 128)
    out_sum, back_sum, f_mix, f_proj, f_rise, f_fall, f_vec = reduce_all(
        seq_size,
        dp_size,
        out_part.reshape(seq_size, tok, D),
        back_part.reshape(seq_size, tok, D),
        g_mix,
        g_proj,
        g_rise,
        g_fall,
        vec_part,
    )
    own_x = tokens[0].astype(F32)
    block_output = (own_x + out_sum + b_proj + b_fall).astype(BF)
    own_center = own_x - jnp.mean(own_x, axis=-1, keepdims=True)
    own_rstd = lax.rsqrt(jnp.mean(own_center * own_center, axis=-1, keepdims=True) + EPS)
    own_n = own_center * own_rstd
    back = own_rstd * (
        back_sum
        - jnp.mean(back_sum, axis=-1, keepdims=True)
        - own_n * jnp.mean(back_sum * own_n, axis=-1, keepdims=True)
    )
    input_grad = (cotangent[0].astype(F32) + back).astype(BF)
    f_mix = f_mix.reshape(seq_size, rows, 3, heads_n, HEAD_DIM)
    f_mix = f_mix.transpose(1, 0, 3, 2, 4).reshape(rows, 3 * D).astype(F32)
    f_proj = f_proj.transpose(1, 0, 2).reshape(rows, D).astype(F32)
    f_rise = f_rise.reshape(seq_size, rows, dp_size, units)
    f_rise = f_rise.transpose(1, 2, 0, 3).reshape(rows, FF).astype(F32)
    f_fall = f_fall.reshape(seq_size * units, D).astype(F32)
    f_vec = f_vec.reshape(seq_size, 2048)[:, :part_len]
    norm_sums = jnp.sum(f_vec[:, : 4 * rows], axis=0)
    column = f_vec[0, 4 * rows : 5 * rows]
    f_b_rise = f_vec[:, 5 * rows : 5 * rows + units].reshape(seq_size * units)
    f_b_mix = f_vec[:, 5 * rows + units :].reshape(seq_size, 3, heads_n, HEAD_DIM)
    f_b_mix = f_b_mix.transpose(0, 2, 1, 3).reshape(dp_size, 3 * rows)
    f_b_mix = lax.dynamic_index_in_dim(f_b_mix, dp, 0, keepdims=False)
    return (
        block_output[None],
        input_grad[None],
        norm_sums[:rows],
        norm_sums[rows : 2 * rows],
        norm_sums[2 * rows : 3 * rows],
        norm_sums[3 * rows :],
        f_mix,
        f_b_mix,
        f_proj,
        column,
        f_rise,
        f_b_rise,
        f_fall,
        column,
    )


def shards(*args):
    seq_size, dp_size = lax.axis_size("seq"), lax.axis_size("dp")
    if resident_fits(seq_size, dp_size, args[0].shape[1]):
        return resident_shards(*args)
    return streamed_shards(*args)


def solution(mesh):
    rows = P("dp", "seq", None)
    weight = P("dp", None)
    vector = P("dp")
    return jax.shard_map(
        shards,
        mesh=mesh,
        in_specs=(rows, rows)
        + (vector,) * 4
        + (weight, vector) * 4
        + (P("dp", "seq"), vector),
        out_specs=(rows, rows) + (vector,) * 4 + (weight, vector) * 4,
        check_vma=False,
    )
```

```python
import functools
import typing

import jax
import jax.numpy as jnp
import numpy as np
from jax import lax
from jax.experimental import pallas as pl
from jax.experimental.pallas import tpu as pltpu
from jax.sharding import PartitionSpec as P

D = 1024
HEADS = 16
HEAD_DIM = 64
ROT = 16
FF = 4096
EPS = 1e-05
BASE = 10000.0
NEG = -1e30
MESH = pl.DeviceIdType.MESH
BF = jnp.bfloat16
F32 = jnp.float32


def ring_pos(dev, size):
    return (dev // 2) * (1 - dev % 2) + (size - 1 - dev // 2) * (dev % 2)


def ring_dev(pos, size):
    high = pos // (size // 2)
    return (1 - high) * 2 * pos + high * (2 * (size - 1 - pos) + 1)


class Place:
    def __init__(self, seq_size, dp_size):
        self.seq_size, self.dp_size = seq_size, dp_size
        self.seq = lax.axis_index("seq")
        self.dp = lax.axis_index("dp")
        self.pos = ring_pos(self.dp, dp_size)
        self.half = dp_size // 2
        self.pairs = seq_size // 2
        self.core = self.seq % 2
        self.pair = self.seq // 2
        self.sibling = self.pair * 2 + 1 - self.core

    def ring(self, offset):
        return ring_dev((self.pos + offset + self.dp_size) % self.dp_size, self.dp_size)

    def dp_peer(self, step):
        return (self.dp + step + self.dp_size) % self.dp_size

    def pair_peer(self, step):
        return ((self.pair + step + self.pairs) % self.pairs) * 2 + self.core

    def across_source(self, step):
        return ((self.pair - step + self.pairs) % self.pairs) * 2 + 1 - self.core

    def seq_peer(self, step):
        return (self.seq + step + self.seq_size) % self.seq_size

    def greet_near(self):
        barrier = pltpu.get_barrier_semaphore()
        for step in (1, -1):
            pl.semaphore_signal(barrier, inc=1, device_id={"dp": self.ring(step)}, device_id_type=MESH)
        for step in range(1, self.seq_size):
            pl.semaphore_signal(
                barrier, inc=1, device_id={"seq": self.seq_peer(step)}, device_id_type=MESH
            )

    def met_near(self):
        pl.semaphore_wait(pltpu.get_barrier_semaphore(), 2 + self.seq_size - 1)

    def greet(self):
        barrier = pltpu.get_barrier_semaphore()
        for step in range(1, self.dp_size):
            pl.semaphore_signal(
                barrier, inc=1, device_id={"dp": self.dp_peer(step)}, device_id_type=MESH
            )
        for step in range(1, self.seq_size):
            pl.semaphore_signal(
                barrier, inc=1, device_id={"seq": self.seq_peer(step)}, device_id_type=MESH
            )
        pl.semaphore_wait(barrier, self.dp_size - 1 + self.seq_size - 1)


def send(src, dst, sems, index, target):
    return pltpu.make_async_remote_copy(
        src_ref=src,
        dst_ref=dst,
        send_sem=sems.at[0, index],
        recv_sem=sems.at[1, index],
        device_id=target,
        device_id_type=MESH,
    )


def halves(ref):
    rows = ref.shape[0]
    columns = ref.shape[1]
    if rows % (32 if ref.dtype == BF else 16) == 0:
        return ref.at[pl.ds(0, rows // 2)], ref.at[pl.ds(rows // 2, rows // 2)]
    return ref.at[:, pl.ds(0, columns // 2)], ref.at[:, pl.ds(columns // 2, columns // 2)]


class RingGather:
    def __init__(self, place, full, sems):
        self.place, self.full, self.sems = place, full, sems

    def piece(self, offset, step, way):
        block = self.full.at[self.place.ring(offset)]
        return block if step < self.place.half else halves(block)[way]

    def copies(self, step):
        place = self.place
        right = self.piece(-(step - 1), step, 0)
        left = self.piece(step - 1, step, 1)
        index = 2 * (step - 1)
        return (
            send(right, right, self.sems, index, {"dp": place.ring(1)}),
            send(left, left, self.sems, index + 1, {"dp": place.ring(-1)}),
        )

    def arrivals(self, step):
        right = self.piece(-step, step, 0)
        left = self.piece(step, step, 1)
        index = 2 * (step - 1)
        return (
            send(right, right, self.sems, index, {"dp": self.place.ring(1)}),
            send(left, left, self.sems, index + 1, {"dp": self.place.ring(-1)}),
        )

    def tick(self, step):
        if step > 1:
            for copy in self.arrivals(step - 1):
                copy.wait_recv()
        if step <= self.place.half:
            for copy in self.copies(step):
                copy.start()

    def finish(self):
        for step in range(1, self.place.half + 1):
            for copy in self.copies(step):
                copy.wait_send()


class RingReduce:
    def __init__(self, place, parts, arrived, sems):
        self.place, self.parts, self.arrived, self.sems = place, parts, arrived, sems

    def piece(self, ref, step, way):
        return ref if step > 1 else halves(ref)[way]

    def copies(self, step):
        place = self.place
        away = place.half - step + 1
        index = 2 * (step - 1)
        out = []
        for way, (offset, target) in enumerate(((away, 1), (-away, -1))):
            src = self.piece(self.parts.at[place.ring(offset)], step, way)
            dst = self.piece(self.arrived.at[way, step - 1], step, way)
            out.append(send(src, dst, self.sems, index + way, {"dp": place.ring(target)}))
        return out

    def tick(self, step):
        place = self.place
        if step > 1:
            for way, copy in enumerate(self.copies(step - 1)):
                copy.wait_recv()
                away = (place.half - step + 1) * (1 - 2 * way)
                held = self.piece(self.parts.at[place.ring(away)], step - 1, way)
                came = self.piece(self.arrived.at[way, step - 2], step - 1, way)
                held[...] = (held[...].astype(F32) + came[...].astype(F32)).astype(held.dtype)
        if step <= place.half:
            for copy in self.copies(step):
                copy.start()

    def finish(self):
        for step in range(1, self.place.half + 1):
            for copy in self.copies(step):
                copy.wait_send()

    def own(self):
        return self.parts.at[self.place.dp]


class SeqGather:
    def __init__(self, place, full, sems, own=None):
        self.place, self.full, self.sems = place, full, sems
        self.own = full.at[place.seq] if own is None else own

    def direct(self, step):
        place = self.place
        target = {"seq": place.pair_peer(step)}
        return send(self.own, self.full.at[place.seq], self.sems, step, target)

    def arrival(self, step):
        place = self.place
        target = {"seq": place.pair_peer(step)}
        return send(self.own, self.full.at[place.pair_peer(-step)], self.sems, step, target)

    def across(self, step):
        place = self.place
        block = self.full.at[place.pair_peer(-step)]
        src = self.own if step == 0 else block
        return send(src, block, self.sems, place.pairs + step, {"seq": place.sibling})

    def across_arrival(self, step):
        place = self.place
        block = self.full.at[place.across_source(step)]
        return send(self.own, block, self.sems, place.pairs + step, {"seq": place.sibling})

    def begin(self):
        for step in range(1, self.place.pairs):
            self.direct(step).start()
        self.across(0).start()

    def forward(self):
        for step in range(1, self.place.pairs):
            self.arrival(step).wait_recv()
            self.across(step).start()

    def across_arrived(self, step):
        self.across_arrival(step).wait_recv()

    def sent(self):
        for step in range(1, self.place.pairs):
            self.direct(step).wait_send()
        for step in range(self.place.pairs):
            self.across(step).wait_send()

    def finish(self):
        for step in range(self.place.pairs):
            self.across_arrived(step)
        self.sent()


class SeqReduce:
    def __init__(self, place, parts, crossed, arrived, sems):
        self.place, self.parts, self.crossed, self.arrived = place, parts, crossed, arrived
        self.sems = sems

    def over(self, step):
        place = self.place
        index = (place.pair + step) % place.pairs
        src = self.parts.at[index * 2 + 1 - place.core]
        return send(src, self.crossed.at[index], self.sems, step, {"seq": place.sibling})

    def direct(self, step):
        place = self.place
        return send(
            self.parts.at[place.pair_peer(step)],
            self.arrived.at[step],
            self.sems,
            place.pairs + step,
            {"seq": place.pair_peer(step)},
        )

    def over_start(self, step):
        self.over(step).start()

    def over_add(self, step):
        place = self.place
        index = (place.pair + step) % place.pairs
        self.over(step).wait_recv()
        held = self.parts.at[index * 2 + place.core]
        held[...] = (held[...].astype(F32) + self.crossed[index].astype(F32)).astype(held.dtype)
        if step > 0:
            self.direct(step).start()

    def begin(self):
        for step in range(self.place.pairs):
            self.over_start(step)

    def middle(self):
        for step in range(self.place.pairs):
            self.over_add(step)

    def total(self):
        place = self.place
        total = self.parts.at[place.seq][...].astype(F32)
        for step in range(1, place.pairs):
            self.direct(step).wait_recv()
            total = total + self.arrived[step].astype(F32)
        return total

    def finish(self):
        for step in range(self.place.pairs):
            self.over(step).wait_send()
        for step in range(1, self.place.pairs):
            self.direct(step).wait_send()


class DpSpread:
    def __init__(self, place, src_of, full, sems):
        self.place, self.src_of, self.full, self.sems = place, src_of, full, sems

    def copy(self, step):
        place = self.place
        peer = place.dp_peer(step)
        return send(self.src_of(peer), self.full.at[place.dp], self.sems, step, {"dp": peer})

    def arrival(self, step):
        place = self.place
        source = place.dp_peer(-step)
        return send(
            self.src_of(source), self.full.at[source], self.sems, step, {"dp": place.dp_peer(step)}
        )

    def begin(self):
        for step in range(1, self.place.dp_size):
            self.copy(step).start()

    def finish(self):
        for step in range(1, self.place.dp_size):
            self.arrival(step).wait_recv()
        for step in range(1, self.place.dp_size):
            self.copy(step).wait_send()


def sems_of(count):
    return pltpu.SemaphoreType.DMA((2, count))


def gather_kernel(seq_size, dp_size, *refs):
    (x_ref, dy_ref, mix_ref, proj_ref, rise_ref, fall_ref, vec_ref, seg_ref) = refs[:8]
    (x_all, dy_all, mix_all, proj_cols, rise_all, fall_all, vec_all, seg_all, proj_all) = refs[8:17]
    (x_sems, dy_sems, mix_sems, proj_sems, rise_sems, fall_sems, vec_sems, seg_sems, swap_sems, own_sems) = refs[17:]
    place = Place(seq_size, dp_size)
    own = [
        pltpu.make_async_copy(src, dst, own_sems.at[i])
        for i, (src, dst) in enumerate(
            (
                (x_ref, x_all.at[place.seq]),
                (dy_ref, dy_all.at[place.seq]),
                (mix_ref, mix_all.at[place.dp]),
                (proj_ref, proj_cols.at[place.dp]),
                (rise_ref, rise_all.at[place.dp]),
                (fall_ref, fall_all.at[place.dp]),
                (vec_ref, vec_all.at[place.dp]),
                (seg_ref, seg_all.at[place.seq]),
            )
        )
    ]
    for copy in own:
        copy.start()
    place.greet()
    for copy in own:
        copy.wait()
    x_move = SeqGather(place, x_all, x_sems)
    dy_move = SeqGather(place, dy_all, dy_sems)
    seg_move = SeqGather(place, seg_all, seg_sems)
    vec_move = DpSpread(place, lambda peer: vec_ref, vec_all, vec_sems)
    mix_move = RingGather(place, mix_all, mix_sems)
    proj_move = RingGather(place, proj_cols, proj_sems)
    rise_move = RingGather(place, rise_all, rise_sems)
    fall_move = RingGather(place, fall_all, fall_sems)
    x_move.begin()
    seg_move.begin()
    vec_move.begin()
    half = place.half
    for step in range(1, half + 1):
        mix_move.tick(step)
        proj_move.tick(step)
    x_move.forward()
    seg_move.forward()
    dy_move.begin()
    mix_move.tick(half + 1)
    proj_move.tick(half + 1)
    rise_move.tick(1)
    fall_move.tick(1)
    rows = proj_cols.shape[0] * proj_cols.shape[1] // seq_size
    each = rows // proj_cols.shape[1]
    swaps = []
    for step in range(1, seq_size):
        peer = place.seq_peer(step)
        swaps.append(
            send(
                proj_cols.at[pl.ds(peer * each, each)],
                proj_all.at[place.seq],
                swap_sems,
                step,
                {"seq": peer},
            )
        )
    for copy in swaps:
        copy.start()
    mine = pltpu.make_async_copy(
        proj_cols.at[pl.ds(place.seq * each, each)], proj_all.at[place.seq], own_sems.at[0]
    )
    mine.start()
    for step in range(2, half + 2):
        rise_move.tick(step)
        fall_move.tick(step)
        if step == 3:
            dy_move.forward()
    mine.wait()
    for step in range(1, seq_size):
        source = place.seq_peer(-step)
        send(
            proj_cols.at[pl.ds(source * each, each)],
            proj_all.at[source],
            swap_sems,
            step,
            {"seq": place.seq_peer(step)},
        ).wait_recv()
    for copy in swaps:
        copy.wait_send()
    for move in (x_move, dy_move, seg_move, vec_move, mix_move, proj_move, rise_move, fall_move):
        move.finish()


def gather_all(seq_size, dp_size, x, dy, mix, proj, rise, fall, vec, seg):
    half = dp_size // 2
    pairs = seq_size // 2

    def lead(count, like):
        return jax.ShapeDtypeStruct((count,) + like.shape, like.dtype)

    each = dp_size // seq_size
    any_spec = pl.BlockSpec(memory_space=pl.ANY)
    return pl.pallas_call(
        functools.partial(gather_kernel, seq_size, dp_size),
        out_shape=(
            lead(seq_size, x),
            lead(seq_size, dy),
            lead(dp_size, mix),
            lead(dp_size, proj),
            lead(dp_size, rise),
            lead(dp_size, fall),
            lead(dp_size, vec),
            lead(seq_size, seg),
            jax.ShapeDtypeStruct((seq_size, each) + proj.shape, proj.dtype),
        ),
        in_specs=[any_spec] * 8,
        out_specs=[any_spec] * 9,
        scratch_shapes=[
            sems_of(2 * pairs),
            sems_of(2 * pairs),
            sems_of(2 * half),
            sems_of(2 * half),
            sems_of(2 * half),
            sems_of(2 * half),
            sems_of(dp_size),
            sems_of(2 * pairs),
            sems_of(seq_size),
            pltpu.SemaphoreType.DMA((8,)),
        ],
        compiler_params=pltpu.CompilerParams(collective_id=0, has_side_effects=True),
    )(x, dy, mix, proj, rise, fall, vec, seg)


def reduce_kernel(seq_size, dp_size, *refs):
    (out_ref, back_ref, mix_ref, proj_ref, rise_ref, fall_ref, vec_ref), refs = refs[:7], refs[7:]
    (out_sum, back_sum, mix_fin, proj_fin, rise_fin, fall_fin, vec_fin), refs = refs[:7], refs[7:]
    (
        out_cross,
        out_came,
        back_cross,
        back_came,
        proj_full,
        mix_came,
        proj_came,
        rise_came,
        fall_came,
        vec_came,
        out_sems,
        back_sems,
        swap_sems,
        mix_sems,
        proj_sems,
        rise_sems,
        fall_sems,
        vec_sems,
        mix_fs,
        proj_fs,
        rise_fs,
        fall_fs,
        vec_fs,
    ) = refs
    place = Place(seq_size, dp_size)
    each = dp_size // seq_size
    half = place.half
    place.greet()

    def mine(index):
        return proj_full.at[pl.ds(index * each, each)]

    def swap(step):
        peer = place.seq_peer(step)
        return send(proj_ref.at[peer], mine(place.seq), swap_sems, step, {"seq": peer})

    def swap_arrival(step):
        source = place.seq_peer(-step)
        target = {"seq": place.seq_peer(step)}
        return send(proj_ref.at[source], mine(source), swap_sems, step, target)

    for step in range(1, seq_size):
        swap(step).start()
    mine(place.seq)[...] = proj_ref[place.seq]
    mix = RingReduce(place, mix_ref, mix_came, mix_sems)
    proj = RingReduce(place, proj_full, proj_came, proj_sems)
    rise = RingReduce(place, rise_ref, rise_came, rise_sems)
    fall = RingReduce(place, fall_ref, fall_came, fall_sems)
    out = SeqReduce(place, out_ref, out_cross, out_came, out_sems)
    back = SeqReduce(place, back_ref, back_cross, back_came, back_sems)
    vec = DpSpread(place, lambda peer: vec_ref.at[peer], vec_came, vec_sems)
    mix.tick(1)
    rise.tick(1)
    out.begin()
    back.begin()
    vec.begin()
    for step in range(1, seq_size):
        swap_arrival(step).wait_recv()
    proj.tick(1)
    fall.tick(1)
    out.middle()
    back.middle()
    for step in range(2, half + 2):
        for move in (mix, rise, proj, fall):
            move.tick(step)
    finals = []
    for move, fin, fin_sems in (
        (mix, mix_fin, mix_fs),
        (rise, rise_fin, rise_fs),
        (proj, proj_fin, proj_fs),
        (fall, fall_fin, fall_fs),
    ):
        fin[place.seq] = move.parts[place.dp]
        gather = SeqGather(place, fin, fin_sems)
        gather.begin()
        finals.append(gather)
    vec_came[place.dp] = vec_ref[place.dp]
    vec.finish()
    vec_fin[place.seq] = jnp.sum(vec_came[...], axis=0)
    gather = SeqGather(place, vec_fin, vec_fs)
    gather.begin()
    finals.append(gather)
    out_sum[...] = out.total()
    back_sum[...] = back.total()
    for gather in finals:
        gather.forward()
    for gather in finals:
        gather.finish()
    for step in range(1, seq_size):
        swap(step).wait_send()
    for move in (mix, rise, proj, fall, out, back):
        move.finish()


def reduce_all(seq_size, dp_size, out, back, mix, proj, rise, fall, vec):
    half = dp_size // 2
    pairs = seq_size // 2
    each = dp_size // seq_size

    def fin(like):
        return jax.ShapeDtypeStruct((seq_size,) + like.shape[1:], like.dtype)

    def came(like):
        return pltpu.VMEM((2, half) + like.shape[1:], like.dtype)

    proj_blocks = jax.ShapeDtypeStruct((dp_size,) + proj.shape[2:], proj.dtype)
    vmem = pl.BlockSpec(memory_space=pltpu.VMEM)
    return pl.pallas_call(
        functools.partial(reduce_kernel, seq_size, dp_size),
        out_shape=(
            jax.ShapeDtypeStruct(out.shape[1:], F32),
            jax.ShapeDtypeStruct(back.shape[1:], F32),
            fin(mix),
            fin(proj_blocks),
            fin(rise),
            fin(fall),
            fin(vec),
        ),
        in_specs=[vmem] * 7,
        out_specs=[vmem] * 7,
        scratch_shapes=[
            pltpu.VMEM((pairs,) + out.shape[1:], BF),
            pltpu.VMEM((pairs,) + out.shape[1:], BF),
            pltpu.VMEM((pairs,) + back.shape[1:], BF),
            pltpu.VMEM((pairs,) + back.shape[1:], BF),
            pltpu.VMEM(proj_blocks.shape, BF),
            came(mix),
            came(proj_blocks),
            came(rise),
            came(fall),
            pltpu.VMEM(vec.shape, F32),
            sems_of(2 * pairs),
            sems_of(2 * pairs),
            sems_of(seq_size),
            sems_of(2 * half),
            sems_of(2 * half),
            sems_of(2 * half),
            sems_of(2 * half),
            sems_of(dp_size),
            sems_of(2 * pairs),
            sems_of(2 * pairs),
            sems_of(2 * pairs),
            sems_of(2 * pairs),
            sems_of(2 * pairs),
        ],
        compiler_params=pltpu.CompilerParams(
            collective_id=1, has_side_effects=True, vmem_limit_bytes=56 * 2**20
        ),
    )(out, back, mix, proj, rise, fall, vec)


def angle_tables(length):
    frequency = BASE ** (-np.arange(0, ROT, 2).astype(np.float32) / np.float32(ROT))
    angles = np.arange(length, dtype=np.float32)[:, None] * frequency.astype(np.float32)[None, :]
    return np.cos(angles).astype(np.float32), np.sin(angles).astype(np.float32)


def turn(piece, cosine, sine, sign):
    half = ROT // 2
    low, high = piece[..., :half], piece[..., half:ROT]
    return jnp.concatenate(
        [low * cosine - sign * high * sine, high * cosine + sign * low * sine, piece[..., ROT:]],
        axis=-1,
    )


TILE = 256

def mm(a, b, dims):
    return lax.dot_general(a, b, ((dims[0], dims[1]), ((), ())), preferred_element_type=F32)

def nn(a, b):
    return mm(a, b, ((1,), (0,)))

def nt(a, b):
    return mm(a, b, ((1,), (1,)))

def tn(a, b):
    return mm(a, b, ((0,), (0,)))

def fold(count, body, init):
    if isinstance(count, int):
        for index in range(count):
            init = body(index, init)
        return init
    return lax.fori_loop(0, count, body, init)

def rows_of(index):
    start = index * TILE
    return pl.ds(start if isinstance(start, int) else pl.multiple_of(start, TILE), TILE)

def attend_block(head, block, refs):
    q_ref, k_ref, v_ref, g_ref, kt_ref, vt_ref, s_ref, p_ref, ht_ref, dqt_ref, dk_ref, dv_ref = refs
    here = rows_of(block)
    span = block + 1
    dims = pl.ds(pl.multiple_of(head * HEAD_DIM, HEAD_DIM), HEAD_DIM)
    query = q_ref[head, here, :]
    grad = g_ref[head, here, :]

    def score(index, top):
        tile = nt(k_ref[head, rows_of(index), :], query)
        if isinstance(index, int) and isinstance(block, int) and index < block:
            keep = tile
        else:
            key = lax.broadcasted_iota(jnp.int32, (TILE, TILE), 0) + (index - block) * TILE
            place = lax.broadcasted_iota(jnp.int32, (TILE, TILE), 1)
            keep = jnp.where(key <= place, tile, NEG)
        s_ref[index] = keep
        return jnp.maximum(top, jnp.max(keep, axis=0, keepdims=True))

    top = fold(span, score, jnp.full((1, TILE), 2 * NEG, F32))

    def raise_(index, total):
        raised = jnp.exp(s_ref[index] - top)
        s_ref[index] = raised
        return total + jnp.sum(raised, axis=0, keepdims=True)

    total = fold(span, raise_, jnp.zeros((1, TILE), F32))
    share = 1.0 / total

    def weigh(index, carried):
        heads, delta = carried
        weights = s_ref[index] * share
        s_ref[index] = weights
        weights_b = weights.astype(BF)
        d_weights = nt(v_ref[head, rows_of(index), :], grad)
        p_ref[index] = d_weights
        dv_ref[head, rows_of(index), :] += nn(weights_b, grad)
        heads = heads + nn(vt_ref[dims, rows_of(index)], weights_b)
        return heads, delta + jnp.sum(weights * d_weights, axis=0, keepdims=True)

    heads, delta = fold(
        span, weigh, (jnp.zeros((HEAD_DIM, TILE), F32), jnp.zeros((1, TILE), F32))
    )
    ht_ref[dims, here] = heads

    def back(index, d_query):
        d_scores = (s_ref[index] * (p_ref[index] - delta)).astype(BF)
        dk_ref[head, rows_of(index), :] += nn(d_scores, query)
        return d_query + nn(kt_ref[dims, rows_of(index)], d_scores)

    dqt_ref[dims, here] = fold(span, back, jnp.zeros((HEAD_DIM, TILE), F32))

def attend(heads_n, length, refs):
    dk_ref, dv_ref = refs[-2:]
    dk_ref[...] = jnp.zeros(dk_ref.shape, F32)
    dv_ref[...] = jnp.zeros(dv_ref.shape, F32)
    blocks = length // TILE

    @pl.loop(0, heads_n)
    def _(head):
        if blocks <= 4:
            for block in range(blocks):
                attend_block(head, block, refs)
        else:
            @pl.loop(0, blocks)
            def _(block):
                attend_block(head, block, refs)

def attend_kernel(H, L, q, k, v, g, kt, vt, ht, dqt, dk, dv, s_ref, p_ref):
    attend(H, L, (q, k, v, g, kt, vt, s_ref, p_ref, ht, dqt, dk, dv))

def attention_call(q, k, v, g, kt, vt):
    H, L, _ = q.shape
    vm = pl.BlockSpec(memory_space=pltpu.VMEM)
    nb = L // TILE
    return pl.pallas_call(functools.partial(attend_kernel, H, L),
        out_shape=(jax.ShapeDtypeStruct((H*64, L), F32), jax.ShapeDtypeStruct((H*64, L), F32), jax.ShapeDtypeStruct((H, L, 128), F32), jax.ShapeDtypeStruct((H, L, 128), F32)),
        in_specs=[vm]*6, out_specs=[vm]*4,
        scratch_shapes=[pltpu.VMEM((nb, TILE, TILE), F32), pltpu.VMEM((nb, TILE, TILE), F32)],
        compiler_params=pltpu.CompilerParams(vmem_limit_bytes=56 * 2**20))(q, k, v, g, kt, vt)

def prep(queries, keys, values, d_heads, segments):
    seg = segments[:, None] == jnp.arange(64)[None, :]
    e = jnp.broadcast_to(seg.astype(BF)[None], queries.shape)
    f = jnp.broadcast_to(jnp.where(seg, 0.0, NEG).astype(BF)[None], queries.shape)
    lane = jnp.arange(64)
    f = jnp.where(lane < 4, f, 0).astype(BF)
    qa = jnp.concatenate([(queries.astype(F32) * 0.125).astype(BF), e], -1)
    ka = jnp.concatenate([keys, f], -1)
    z = jnp.zeros_like(values)
    va = jnp.concatenate([values, z], -1)
    ga = jnp.concatenate([d_heads, z], -1)
    kt = keys.transpose(0, 2, 1).reshape(-1, keys.shape[1])
    vt = values.transpose(0, 2, 1).reshape(-1, keys.shape[1])
    return qa, ka, va, ga, kt, vt

def attention(queries, keys, values, d_heads, segments):
    H, L, _ = queries.shape
    ht, dqt, dk, dv = attention_call(*prep(queries, keys, values, d_heads, segments))

    def back(t):
        return t.reshape(H, 64, L).transpose(0, 2, 1)

    return back(ht).astype(BF), (back(dqt) * 0.125).astype(BF), dk[..., :64].astype(BF), dv[..., :64].astype(BF)


def dot(a, b):
    return jnp.dot(a, b, preferred_element_type=F32)


def dot_t(a, b):
    return lax.dot_general(a, b, (((0,), (0,)), ((), ())), preferred_element_type=F32)


def dot_nt(a, b):
    return lax.dot_general(a, b, (((1,), (1,)), ((), ())), preferred_element_type=F32)


(
    OWN, XGO, DYGO, XFWD, DYFWD, HOTS, DYALL, VROWS, LN0, LN1, LN2, LN3, SWGO, SWIN, QKV0, QKV1,
    DH, GVC1, GVC2, GVC3, GVC4, GVC5, GMA1, GMA2, GMA3, GMA4, GMA5, GMB1, GMB2, GMB3, GMB4,
    GMB5, GPR1, GPR2, GPR3, GPR4, GPR5, GRA1, GRA2, GRA3, GRA4, GRA5, GRB1, GRB2, GRB3, GRB4,
    GRB5, GFA1, GFA2, GFA3, GFA4, GFA5, GFB1, GFB2, GFB3, GFB4, GFB5, RVC1, RVC2, RVC3, RVC4,
    RVC5, RMA1, RMA2, RMA3, RMA4, RMA5, RMB1, RMB2, RMB3, RMB4, RMB5, RPR1, RPR2, RPR3, RPR4,
    RPR5, RRA1, RRA2, RRA3, RRA4, RRA5, RRB1, RRB2, RRB3, RRB4, RRB5, RFA1, RFA2, RFA3, RFA4,
    RFA5, RFB1, RFB2, RFB3, RFB4, RFB5, AT00, AT02, AT03, AT10, AT12, AT13, AT20, AT22, AT23,
    AT30, AT32, AT33, POST0, POST1, GM0, GM1, GR0, GR1, GF0, GF1, GP, SBGO, SBIN, UP0, UP1, UP2,
    UP3, DN0, DN1, OP0, OP1, BK0, BK1, OM0, OM1, BM0, BM1, VP, BO, IG, SV, WV, VO, SMA, SMB,
    SPR, SRA, SRB, SFA, SFB, WMA, WMB, WPR, WRA, WRB, WFA, WFB,
) = range(154)

ORDER = (
    OWN, XGO, GVC1, GRB1, GRA1, GMA1, DYGO, GVC2, GPR1, GMB1, GRB2, GRA2, GVC3, GMA2, XFWD,
    GPR2, HOTS, GMB2, GRB3, GVC4, GRA3, GMA3, DYFWD, GPR3, DYALL, GMB3, GVC5, VROWS, LN0, GRB4,
    LN2, LN1, GRA4, LN3, GFB1, GMA4, GPR4, GFA1, GRB5, GMB4, GRA5, UP2, UP3, GMA5, GFB2, UP1,
    GPR5, SWGO, UP0, GMB5, GFA2, GF1, GF0, RFB1, RFA1, GFB3, QKV0, GFA3, QKV1, SWIN, RFB2, DH,
    RFA2, AT20, AT10, GFB4, AT00, GFA4, AT02, AT03, RFB3, AT30, AT12, RFA3, AT32, GFB5, AT33,
    GFA5, DN1, RFB4, DN0, GR1, RFA4, GR0, RRA1, RRB1, AT13, RFB5, SFB, AT22, AT23, RFA5, SFA,
    RRA2, POST1, RRB2, POST0, WFB, GP, SBGO, OP1, WFA, RRA3, GM0, OM1, GM1, RMA1, RRB3, RMB1,
    OP0, RRA4, BK1, SBIN, OM0, RPR1, RMA2, BK0, BM1, RRB4, RMB2, VP, RRA5, RVC1, BM0, RPR2,
    RMA3, SRA, BO, RRB5, SRB, RVC2, RMB3, RPR3, RMA4, RVC3, RMB4, RPR4, IG, RMA5, SMA, RVC4,
    WRA, RMB5, SMB, WRB, RVC5, SV, RPR5, SPR, WMA, WMB, WV, VO, WPR,
)
LANES = 128
HALF = LANES // 2
VEC_ROWS = 16


def resident_fits(seq_size, dp_size, tok):
    return (
        D // dp_size == LANES
        and FF // dp_size // seq_size == LANES
        and HEADS // seq_size == 4
        and tok * seq_size <= 1024
        and tok % TILE == 0
    )


def rows_at(ref, index, count):
    return ref.at[pl.ds(pl.multiple_of(index * count, count), count)]


def columns_at(ref, index, count):
    return ref.at[:, pl.ds(pl.multiple_of(index * count, count), count)]


class Flat:
    def __init__(self, ref, count, stride=None, start=0):
        self.ref, self.count, self.start = ref, count, start
        self.stride = count if stride is None else stride

    @property
    def at(self):
        return self

    def __getitem__(self, index):
        first = pl.multiple_of(index * self.stride + self.start, self.count)
        return self.ref.at[pl.ds(first, self.count)]


class Stack:
    def __init__(self, ref, start, count):
        self.ref, self.start, self.count = ref, start, count

    @property
    def at(self):
        return self

    def __getitem__(self, index):
        return self.ref.at[index, pl.ds(self.start, self.count)]


def lanes_like(shape):
    return lax.broadcasted_iota(jnp.int32, shape, len(shape) - 1)


def head_part(values, start):
    tile = values[:, start // LANES * LANES : start // LANES * LANES + LANES]
    return tile if start % LANES == 0 else pltpu.roll(tile, HEAD_DIM, 1)


def spin(tile, cosine, sine):
    lane = lanes_like(tile.shape)
    partner = jnp.where(lane < ROT // 2, pltpu.roll(tile, LANES - ROT // 2, 1), pltpu.roll(tile, ROT // 2, 1))
    return tile * cosine + partner * sine


def attend_head(head, block, refs):
    q_ref, k_ref, v_ref, g_ref, kt_ref, vt_ref, s_ref, p_ref, ht_ref, dqt_ref, dk_ref, dv_ref = refs
    here = pl.ds(block * TILE, TILE)
    wide = pl.ds(head * LANES, LANES)
    dims = pl.ds(head * HEAD_DIM, HEAD_DIM)
    query = q_ref[here, wide]
    grad = g_ref[here, wide]
    span = block + 1
    top = jnp.full((1, TILE), 2 * NEG, F32)
    for index in range(span):
        tile = nt(k_ref[pl.ds(index * TILE, TILE), wide], query)
        if index == block:
            key = lax.broadcasted_iota(jnp.int32, (TILE, TILE), 0)
            place = lax.broadcasted_iota(jnp.int32, (TILE, TILE), 1)
            tile = jnp.where(key <= place, tile, NEG)
        s_ref[index] = tile
        top = jnp.maximum(top, jnp.max(tile, axis=0, keepdims=True))
    total = jnp.zeros((1, TILE), F32)
    for index in range(span):
        raised = jnp.exp(s_ref[index] - top)
        s_ref[index] = raised
        total = total + jnp.sum(raised, axis=0, keepdims=True)
    share = 1.0 / total
    delta = jnp.zeros((1, TILE), F32)
    heads = jnp.zeros((HEAD_DIM, TILE), F32)
    for index in range(span):
        there = pl.ds(index * TILE, TILE)
        weights = s_ref[index] * share
        s_ref[index] = weights
        weights_b = weights.astype(BF)
        d_weights = nt(v_ref[there, wide], grad)
        p_ref[index] = d_weights
        d_value = nn(weights_b, grad)
        dv_ref[head, there, :] = d_value if index == block else dv_ref[head, there, :] + d_value
        heads = heads + nn(vt_ref[dims, there], weights_b)
        delta = delta + jnp.sum(weights * d_weights, axis=0, keepdims=True)
    ht_ref[dims, here] = heads
    d_query = jnp.zeros((HEAD_DIM, TILE), F32)
    for index in range(span):
        there = pl.ds(index * TILE, TILE)
        d_scores = (s_ref[index] * (p_ref[index] - delta)).astype(BF)
        d_key = nn(d_scores, query)
        dk_ref[head, there, :] = d_key if index == block else dk_ref[head, there, :] + d_key
        d_query = d_query + nn(kt_ref[dims, there], d_scores)
    dqt_ref[dims, here] = d_query


class Refs(typing.NamedTuple):
    x_own: typing.Any
    dy_own: typing.Any
    w_mix_own: typing.Any
    w_proj_own: typing.Any
    w_rise_own: typing.Any
    w_fall_own: typing.Any
    gain1_own: typing.Any
    shift1_own: typing.Any
    gain2_own: typing.Any
    shift2_own: typing.Any
    b_proj_own: typing.Any
    b_fall_own: typing.Any
    b_mix_own: typing.Any
    b_rise_own: typing.Any
    seg_own: typing.Any
    pad_own: typing.Any
    cos_own: typing.Any
    sin_own: typing.Any
    block_out: typing.Any
    input_grad: typing.Any
    mix_fin: typing.Any
    proj_fin: typing.Any
    rise_fin: typing.Any
    fall_fin: typing.Any
    vec_result: typing.Any
    pad: typing.Any
    cos: typing.Any
    sin: typing.Any
    x: typing.Any
    dy: typing.Any
    hot: typing.Any
    segs: typing.Any
    w_mix: typing.Any
    w_proj_cols: typing.Any
    w_proj: typing.Any
    w_rise: typing.Any
    w_fall: typing.Any
    vec_all: typing.Any
    rows: typing.Any
    normed1: typing.Any
    normed2: typing.Any
    stat: typing.Any
    qk: typing.Any
    vg: typing.Any
    kt: typing.Any
    vt: typing.Any
    s: typing.Any
    p: typing.Any
    ht: typing.Any
    dqt: typing.Any
    dk: typing.Any
    dv: typing.Any
    attn: typing.Any
    d_mixed: typing.Any
    out_part: typing.Any
    back_part: typing.Any
    active: typing.Any
    d_up: typing.Any
    g_mix: typing.Any
    g_proj: typing.Any
    g_proj_cols: typing.Any
    g_rise: typing.Any
    g_fall: typing.Any
    c_mix: typing.Any
    c_proj: typing.Any
    c_rise: typing.Any
    c_fall: typing.Any
    out_cross: typing.Any
    out_came: typing.Any
    back_cross: typing.Any
    back_came: typing.Any
    sums: typing.Any
    vec_part: typing.Any
    vec_came: typing.Any
    vec_fin: typing.Any
    vec_out: typing.Any
    m_x: typing.Any
    m_dy: typing.Any
    m_hot: typing.Any
    m_vec: typing.Any
    m_mix: typing.Any
    m_proj: typing.Any
    m_rise: typing.Any
    m_fall: typing.Any
    m_swap: typing.Any
    m_own: typing.Any
    m_swap2: typing.Any
    m_rmix: typing.Any
    m_rproj: typing.Any
    m_rrise: typing.Any
    m_rfall: typing.Any
    m_out: typing.Any
    m_back: typing.Any
    m_vec2: typing.Any
    m_fmix: typing.Any
    m_fproj: typing.Any
    m_frise: typing.Any
    m_ffall: typing.Any
    m_fvec: typing.Any
    m_fin: typing.Any


def resident_kernel(seq_size, dp_size, *refs):
    r = Refs(*refs)
    place = Place(seq_size, dp_size)
    half = place.half
    tok = r.x_own.shape[0]
    length = r.x.shape[0]
    wide = r.w_proj.shape[0]
    mixed_wide = 3 * wide
    units = LANES
    each = dp_size // seq_size
    heads_n = wide // HEAD_DIM
    blocks = length // TILE

    place.greet_near()
    own = []

    def bring(src, dst):
        copy = pltpu.make_async_copy(src, dst, r.m_own.at[len(own)])
        copy.start()
        own.append(copy)

    bring(columns_at(r.w_mix_own, place.seq, mixed_wide), rows_at(r.w_mix, place.dp, LANES))
    bring(columns_at(r.w_proj_own, place.seq, wide), rows_at(r.w_proj_cols, place.dp, LANES))
    bring(r.x_own, rows_at(r.x, place.seq, tok))
    bring(r.dy_own, rows_at(r.dy, place.seq, tok))
    for index in range(dp_size):
        bring(
            columns_at(r.w_rise_own, index * seq_size + place.seq, units),
            rows_at(r.w_rise, place.dp, LANES).at[:, pl.ds(index * units, units)],
        )
    bring(rows_at(r.w_fall_own, place.seq, units), rows_at(r.w_fall, place.dp, units))
    bring(r.pad_own, r.pad)
    bring(r.cos_own, r.cos)
    bring(r.sin_own, r.sin)
    row = 0
    vectors = (r.gain1_own, r.shift1_own, r.gain2_own, r.shift2_own, r.b_proj_own, r.b_fall_own, r.b_mix_own, r.b_rise_own)
    for vector in vectors:
        count = vector.shape[0]
        r.vec_all[place.dp, row : row + count, :] = vector[...].astype(F32)
        row += count
    r.vec_all[place.dp, row:, :] = jnp.zeros((VEC_ROWS - row, LANES), F32)
    rows_at(r.segs, place.seq, 8)[...] = jnp.broadcast_to(r.seg_own[...], (8, tok)).astype(F32)

    def pair_of(ref, make):
        return [make(Flat(ref, HALF, LANES, start), index) for index, start in enumerate((0, HALF))]

    def gather_pair(ref, sems):
        return pair_of(ref, lambda part, index: RingGather(place, part, sems.at[index]))

    def reduce_pair(ref, came, sems):
        return pair_of(ref, lambda part, index: RingReduce(place, part, came.at[index], sems.at[index]))

    def final_pair(out_ref, sems, ref):
        return pair_of(
            ref,
            lambda part, index: SeqGather(
                place, Stack(out_ref, index * HALF, HALF), sems.at[index], part[place.dp]
            ),
        )

    gathers = [
        RingGather(place, r.vec_all, r.m_vec),
        *gather_pair(r.w_mix, r.m_mix),
        RingGather(place, Flat(r.w_proj_cols, LANES), r.m_proj),
        *gather_pair(r.w_rise, r.m_rise),
        *gather_pair(r.w_fall, r.m_fall),
    ]
    reduces = [
        RingReduce(place, r.vec_part, r.vec_came, r.m_vec2),
        *reduce_pair(r.g_mix, r.c_mix, r.m_rmix),
        RingReduce(place, Flat(r.g_proj_cols, LANES), r.c_proj, r.m_rproj),
        *reduce_pair(r.g_rise, r.c_rise, r.m_rrise),
        *reduce_pair(r.g_fall, r.c_fall, r.m_rfall),
    ]
    finals = [
        *final_pair(r.mix_fin, r.m_fmix, r.g_mix),
        SeqGather(place, r.proj_fin, r.m_fproj, rows_at(r.g_proj_cols, place.dp, LANES)),
        *final_pair(r.rise_fin, r.m_frise, r.g_rise),
        *final_pair(r.fall_fin, r.m_ffall, r.g_fall),
    ]
    f_vec = SeqGather(place, r.vec_fin, r.m_fvec)

    x_move = SeqGather(place, Flat(r.x, tok), r.m_x)
    dy_move = SeqGather(place, Flat(r.dy, tok), r.m_dy)
    seg_move = SeqGather(place, Flat(r.segs, 8), r.m_hot)
    out = SeqReduce(place, Flat(r.out_part, tok), r.out_cross, r.out_came, r.m_out)
    back = SeqReduce(place, Flat(r.back_part, tok), r.back_cross, r.back_came, r.m_back)

    leaving = []

    def leave(src, dst):
        copy = pltpu.make_async_copy(src, dst, r.m_fin.at[len(leaving)])
        copy.start()
        leaving.append(copy)

    pieces = {}

    def piece(name, *given):
        def note(run):
            pieces[name] = functools.partial(run, *given)
            return run

        return note

    def tile_rows(block):
        return pl.ds(pl.multiple_of(block * TILE, TILE), TILE)

    def gather(stream, step):
        gathers[stream].tick(step)

    def reduce(stream, step):
        reduces[stream].tick(step)

    for stream in range(len(gathers)):
        for step in range(1, half + 2):
            tick = stream * (half + 1) + step - 1
            piece(GVC1 + tick, stream, step)(gather)
            piece(RVC1 + tick, stream, step)(reduce)

    @piece(OWN)
    def _():
        for copy in own:
            copy.wait()

    @piece(XGO)
    def _():
        x_move.begin()
        seg_move.begin()

    piece(DYGO)(dy_move.begin)

    @piece(XFWD)
    def _():
        x_move.forward()
        seg_move.forward()

    piece(DYFWD)(dy_move.forward)

    @piece(HOTS)
    def _():
        for step in range(place.pairs):
            seg_move.across_arrived(step)
        kind = lax.broadcasted_iota(jnp.int32, (LANES, tok), 0) - HEAD_DIM
        for index in range(seq_size):
            segment = r.segs[index * 8 : index * 8 + 1, :].astype(jnp.int32)
            r.hot[index * tok : (index + 1) * tok, :] = jnp.where(segment == kind, 1.0, 0.0).T.astype(BF)

    @piece(DYALL)
    def _():
        for step in range(place.pairs):
            dy_move.across_arrived(step)

    @piece(VROWS)
    def _():
        for index in range(dp_size):
            at = slice(index * LANES, (index + 1) * LANES)
            for row in range(6):
                r.rows[row : row + 1, at] = r.vec_all[index, row : row + 1, :]
            r.rows[6:7, at] = r.vec_all[index, pl.ds(9 + place.seq, 1), :]
        for index in range(each):
            for row in range(3):
                start = (index * 3 + row) * LANES
                r.rows[7:8, start : start + LANES] = r.vec_all[place.seq * each + index, 6 + row : 7 + row, :]

    chunk = 64

    def normalize(block):
        @pl.loop(0, tok // chunk)
        def _(step):
            here = pl.ds(pl.multiple_of(block * tok + step * chunk, chunk), chunk)
            values = r.x[here, :].astype(F32)
            mean = jnp.sum(values, axis=-1, keepdims=True) * (1.0 / D)
            center = values - mean
            rstd = lax.rsqrt(jnp.sum(center * center, axis=-1, keepdims=True) * (1.0 / D) + EPS)
            n = center * rstd
            r.normed1[here, :] = (n * r.rows[0:1, :] + r.rows[1:2, :]).astype(BF)
            r.normed2[here, :] = (n * r.rows[2:3, :] + r.rows[3:4, :]).astype(BF)
            lane = lanes_like((chunk, LANES))
            r.stat[here, :] = jnp.where(lane < HEAD_DIM, mean, rstd)

    def unit_rows(here):
        stat = r.stat[here, :]
        return (r.x[here, :].astype(F32) - stat[:, 0:1]) * stat[:, HEAD_DIM : HEAD_DIM + 1]

    @piece(LN0)
    def _():
        normalize(place.seq)

    @piece(LN1)
    def _():
        x_move.across_arrived(0)
        normalize(place.sibling)

    @piece(LN2)
    def _():
        normalize(place.pair_peer(1))

    @piece(LN3)
    def _():
        x_move.across_arrived(1)
        normalize(place.across_source(1))

    def swap(step):
        peer = place.seq_peer(step)
        src, dst = rows_at(r.w_proj_cols, peer, wide), columns_at(r.w_proj, place.seq, wide)
        return send(src, dst, r.m_swap, step, {"seq": peer})

    def swap_arrival(step):
        source = place.seq_peer(-step)
        src, dst = rows_at(r.w_proj_cols, source, wide), columns_at(r.w_proj, source, wide)
        return send(src, dst, r.m_swap, step, {"seq": place.seq_peer(step)})

    @piece(SWGO)
    def _():
        for step in range(1, seq_size):
            swap(step).start()
        columns_at(r.w_proj, place.seq, wide)[...] = rows_at(r.w_proj_cols, place.seq, wide)[...]

    @piece(SWIN)
    def _():
        for step in range(1, seq_size):
            swap_arrival(step).wait_recv()

    def mix_columns(first, last):
        @pl.loop(first, last)
        def _(block):
            here = tile_rows(block)
            mixed = nn(r.normed1[here, :], r.w_mix[...]) + r.rows[7:8, 0:mixed_wide]
            cosine, sine = r.cos[here, :], r.sin[here, :]
            lane = lanes_like((TILE, LANES))
            hot = r.hot[here, :].astype(F32)
            cold = jnp.where((lane >= HEAD_DIM) & (lane < HEAD_DIM + 4), (1.0 - hot) * NEG, 0.0)
            for head in range(heads_n):
                start = head * 3 * HEAD_DIM
                query = spin(head_part(mixed, start), cosine, sine) * HEAD_DIM**-0.5
                key = spin(head_part(mixed, start + HEAD_DIM), cosine, sine)
                value = head_part(mixed, start + 2 * HEAD_DIM)
                at = pl.ds(head * LANES, LANES)
                at_more = pl.ds((heads_n + head) * LANES, LANES)
                dims = pl.ds(head * HEAD_DIM, HEAD_DIM)
                r.qk[here, at] = jnp.where(lane < HEAD_DIM, query, hot).astype(BF)
                r.qk[here, at_more] = jnp.where(lane < HEAD_DIM, key, cold).astype(BF)
                r.vg[here, at] = jnp.where(lane < HEAD_DIM, value, 0.0).astype(BF)
                r.kt[dims, here] = key.T[:HEAD_DIM, :].astype(BF)
                r.vt[dims, here] = value.T[:HEAD_DIM, :].astype(BF)

    middle = blocks // 2
    piece(QKV0, 0, middle)(mix_columns)
    piece(QKV1, middle, blocks)(mix_columns)
    @piece(DH)
    def _():
        @pl.loop(0, blocks)
        def _(block):
            here = tile_rows(block)
            place_in = lax.broadcasted_iota(jnp.int32, (TILE, wide), 0) + block * TILE
            d_heads = jnp.where(place_in < length - r.pad[0], nt(r.dy[here, :], r.w_proj[...]), 0.0)
            for head in range(heads_n):
                at_more = pl.ds((heads_n + head) * LANES, LANES)
                r.vg[here, at_more] = head_part(d_heads, head * HEAD_DIM).astype(BF)

    second = heads_n * LANES
    head_refs = (
        r.qk.at[:, pl.ds(0, second)],
        r.qk.at[:, pl.ds(second, second)],
        r.vg.at[:, pl.ds(0, second)],
        r.vg.at[:, pl.ds(second, second)],
        r.kt,
        r.vt,
        r.s,
        r.p,
        r.ht,
        r.dqt,
        r.dk,
        r.dv,
    )

    def attend_blocks(head, first, last):
        for block in range(first, last):
            if block == 0:
                attend_head(head, block, head_refs)
            elif block == 1:
                attend_head(head, block, head_refs)
            elif block == 2:
                attend_head(head, block, head_refs)
            else:
                attend_head(head, block, head_refs)

    for head in range(heads_n):
        first = AT00 + head * (middle + 1)
        piece(first, head, 0, middle)(attend_blocks)
        for block in range(middle, blocks):
            piece(first + block - middle + 1, head, block, block + 1)(attend_blocks)

    def heads_back(first, last):
        @pl.loop(first, last)
        def _(block):
            here = tile_rows(block)
            place_in = lax.broadcasted_iota(jnp.int32, (TILE, wide), 0) + block * TILE
            r.attn[here, :] = jnp.where(place_in < length - r.pad[0], r.ht[:, here].T, 0.0).astype(BF)
            d_query = r.dqt[:, here].T * HEAD_DIM**-0.5
            cosine, sine = r.cos[here, :], -r.sin[here, :]
            lane = lanes_like((TILE, LANES))
            parts = []
            for head in range(heads_n):
                parts.append(spin(head_part(d_query, head * HEAD_DIM), cosine, sine))
                parts.append(spin(r.dk[head, here, :], cosine, sine))
                parts.append(r.dv[head, here, :])
            for index in range(len(parts) // 2):
                tile = jnp.where(lane < HEAD_DIM, parts[2 * index], pltpu.roll(parts[2 * index + 1], HEAD_DIM, 1))
                at = slice(index * LANES, (index + 1) * LANES)
                tile = tile.astype(BF)
                r.d_mixed[here, at] = tile
                r.sums[6:7, at] += jnp.sum(tile.astype(F32), axis=0, keepdims=True)

    piece(POST0, 0, middle)(heads_back)
    piece(POST1, middle, blocks)(heads_back)
    big = 512

    def weight_grad(out_ref, left, right, index):
        at = pl.ds(index * big, big)
        out_ref[at, :] = tn(left[:, at], right[...]).astype(BF)

    for index in range(D // big):
        piece(GM0 + index, r.g_mix, r.normed1, r.d_mixed, index)(weight_grad)
        piece(GR0 + index, r.g_rise, r.normed2, r.d_up, index)(weight_grad)
        piece(GF0 + index, r.g_fall, r.active, r.dy, index)(weight_grad)

    @piece(GP)
    def _():
        r.g_proj[...] = tn(r.attn[...], r.dy[...]).astype(BF)

    def swap_back(step):
        peer = place.seq_peer(step)
        src, dst = columns_at(r.g_proj, peer, wide), rows_at(r.g_proj_cols, place.seq, wide)
        return send(src, dst, r.m_swap2, step, {"seq": peer})

    def swap_back_arrival(step):
        source = place.seq_peer(-step)
        src, dst = columns_at(r.g_proj, source, wide), rows_at(r.g_proj_cols, source, wide)
        return send(src, dst, r.m_swap2, step, {"seq": place.seq_peer(step)})

    @piece(SBGO)
    def _():
        for step in range(1, seq_size):
            swap_back(step).start()
        rows_at(r.g_proj_cols, place.seq, wide)[...] = columns_at(r.g_proj, place.seq, wide)[...]

    @piece(SBIN)
    def _():
        for step in range(1, seq_size):
            swap_back_arrival(step).wait_recv()

    def upward(block):
        here = tile_rows(block)
        up = nn(r.normed2[here, :], r.w_rise[...]) + r.rows[6:7, :]
        share = 0.5 + 0.5 * lax.erf(up * 0.5**0.5)
        r.active[here, :] = (up * share).astype(BF)
        bell = jnp.exp(-0.5 * up * up) * (2 * np.pi) ** -0.5
        r.d_up[here, :] = (share + up * bell).astype(BF)

    def downward(first, last):
        @pl.loop(first, last)
        def _(block):
            here = tile_rows(block)
            d_up = (r.d_up[here, :].astype(F32) * nt(r.dy[here, :], r.w_fall[...])).astype(BF)
            r.d_up[here, :] = d_up
            r.sums[5:6, :] += jnp.sum(d_up.astype(F32), axis=0, keepdims=True)

    for block in range(blocks):
        piece(UP0 + block, block)(upward)
    piece(DN0, 0, middle)(downward)
    piece(DN1, middle, blocks)(downward)

    def out_rows(step):
        first = ((place.pair + step) % place.pairs) * (2 * tok // TILE)
        @pl.loop(0, 2 * tok // TILE)
        def _(block):
            here = tile_rows(first + block)
            part = nn(r.attn[here, :], r.w_proj[...]) + nn(r.active[here, :], r.w_fall[...])
            r.out_part[here, :] = part.astype(BF)

        out.over_start(step)

    def back_rows(step):
        first = ((place.pair + step) % place.pairs) * (2 * tok // TILE)
        @pl.loop(0, 2 * tok // TILE)
        def _(block):
            here = tile_rows(first + block)
            d_one = nt(r.d_mixed[here, :], r.w_mix[...])
            d_two = nt(r.d_up[here, :], r.w_rise[...])
            r.back_part[here, :] = (r.rows[0:1, :] * d_one + r.rows[2:3, :] * d_two).astype(BF)
            n = unit_rows(here)
            r.sums[0:1, :] += jnp.sum(d_one * n, axis=0, keepdims=True)
            r.sums[1:2, :] += jnp.sum(d_one, axis=0, keepdims=True)
            r.sums[2:3, :] += jnp.sum(d_two * n, axis=0, keepdims=True)
            r.sums[3:4, :] += jnp.sum(d_two, axis=0, keepdims=True)
            r.sums[4:5, :] += jnp.sum(r.dy[here, :].astype(F32), axis=0, keepdims=True)

        back.over_start(step)

    for step in range(2):
        piece(OP0 + step, step)(out_rows)
        piece(BK0 + step, step)(back_rows)
        piece(OM0 + step, step)(out.over_add)
        piece(BM0 + step, step)(back.over_add)

    @piece(VP)
    def _():
        for index in range(dp_size):
            at = slice(index * LANES, (index + 1) * LANES)
            r.vec_part[index, 0:6, :] = r.sums[0:6, at]
            for row in range(mixed_wide // LANES):
                r.vec_part[index, 6 + row : 7 + row, :] = r.sums[6:7, row * LANES : (row + 1) * LANES]

    def settle(move):
        move.begin()
        leave(move.own, move.full.at[place.seq])

    for index, move in enumerate(finals):
        piece(SMA + index, move)(settle)
        piece(WMA + index)(move.forward)

    mine = pl.ds(pl.multiple_of(place.seq * tok, tok), tok)

    @piece(BO)
    def _():
        total = out.total()
        block_out = total + r.x[mine, :].astype(F32) + (r.rows[4:5, :] + r.rows[5:6, :])
        r.out_cross[0] = block_out.astype(BF)
        leave(r.out_cross.at[0], r.block_out)

    @piece(IG)
    def _():
        scaled = back.total()
        n = unit_rows(mine)
        rstd = r.stat[mine, HEAD_DIM : HEAD_DIM + 1]
        back_mean = jnp.sum(scaled, axis=-1, keepdims=True) * (1.0 / D)
        back_n = jnp.sum(scaled * n, axis=-1, keepdims=True) * (1.0 / D)
        input_grad = r.dy[mine, :].astype(F32) + rstd * (scaled - back_mean - n * back_n)
        r.back_cross[0] = input_grad.astype(BF)
        leave(r.back_cross.at[0], r.input_grad)

    @piece(SV)
    def _():
        r.vec_fin[place.seq] = r.vec_part[place.dp]
        f_vec.begin()

    piece(WV)(f_vec.forward)

    @piece(VO)
    def _():
        f_vec.finish()
        norm = r.vec_fin[0, 0:4, :]
        for index in range(1, seq_size):
            norm = norm + r.vec_fin[index, 0:4, :]
        r.vec_out[0:4, :] = norm
        r.vec_out[4:5, :] = r.vec_fin[0, 4:5, :]
        source = r.vec_fin[place.dp // each]
        pick = place.dp % each
        part = source[6:9, :]
        for index in range(1, each):
            part = jnp.where(pick == index, source[6 + 3 * index : 9 + 3 * index, :], part)
        r.vec_out[5:8, :] = part
        for index in range(seq_size):
            r.vec_out[8 + index : 9 + index, :] = r.vec_fin[index, 5:6, :]
        leave(r.vec_out, r.vec_result)

    place.met_near()
    r.sums[...] = jnp.zeros(r.sums.shape, F32)
    r.vec_part[...] = jnp.zeros(r.vec_part.shape, F32)
    assert sorted(ORDER) == sorted(pieces)
    for name in ORDER:
        pieces[name]()
    for move in finals:
        move.finish()
    for copy in leaving:
        copy.wait()
    for move in (*gathers, *reduces, out, back):
        move.finish()
    for move in (x_move, seg_move, dy_move):
        move.sent()
    for step in range(1, seq_size):
        swap(step).wait_send()
        swap_back(step).wait_send()


def resident_call(seq_size, dp_size, *args):
    tok = args[0].shape[0]
    length = tok * seq_size
    half, pairs = dp_size // 2, seq_size // 2
    wide = HEADS // seq_size * HEAD_DIM
    units_all = dp_size * LANES
    heads_n = wide // HEAD_DIM

    def half_vmem(*shape):
        return pltpu.VMEM(shape, BF)

    def full_vmem(*shape):
        return pltpu.VMEM(shape, F32)

    def ring(columns):
        return half_vmem(2, 2, half, HALF, columns)

    def pair_of_sems(count):
        return pltpu.SemaphoreType.DMA((2, 2, count))

    any_spec = pl.BlockSpec(memory_space=pl.ANY)
    vmem = pl.BlockSpec(memory_space=pltpu.VMEM)
    scratch = [
        pltpu.SMEM((1,), jnp.int32),
        full_vmem(length, LANES),
        full_vmem(length, LANES),
        half_vmem(length, D),
        half_vmem(length, D),
        half_vmem(length, LANES),
        full_vmem(seq_size * 8, tok),
        half_vmem(D, 3 * wide),
        half_vmem(D, wide),
        half_vmem(wide, D),
        half_vmem(D, units_all),
        half_vmem(units_all, D),
        full_vmem(dp_size, VEC_ROWS, LANES),
        full_vmem(8, D),
        half_vmem(length, D),
        half_vmem(length, D),
        full_vmem(length, LANES),
        half_vmem(length, units_all),
        half_vmem(length, units_all),
        half_vmem(wide, length),
        half_vmem(wide, length),
        full_vmem(length // TILE, TILE, TILE),
        full_vmem(length // TILE, TILE, TILE),
        full_vmem(wide, length),
        full_vmem(wide, length),
        full_vmem(heads_n, length, LANES),
        full_vmem(heads_n, length, LANES),
        half_vmem(length, wide),
        half_vmem(length, 3 * wide),
        half_vmem(length, D),
        half_vmem(length, D),
        half_vmem(length, units_all),
        half_vmem(length, units_all),
        half_vmem(D, 3 * wide),
        half_vmem(wide, D),
        half_vmem(D, wide),
        half_vmem(D, units_all),
        half_vmem(units_all, D),
        ring(3 * wide),
        half_vmem(2, half, LANES, wide),
        ring(units_all),
        ring(D),
        half_vmem(pairs, tok, D),
        half_vmem(pairs, tok, D),
        half_vmem(pairs, tok, D),
        half_vmem(pairs, tok, D),
        full_vmem(8, D),
        full_vmem(dp_size, VEC_ROWS, LANES),
        full_vmem(2, half, VEC_ROWS, LANES),
        full_vmem(seq_size, VEC_ROWS, LANES),
        full_vmem(16, LANES),
    ]
    scratch += [sems_of(2 * pairs)] * 3 + [sems_of(2 * half)]
    scratch += [pair_of_sems(2 * half), sems_of(2 * half), pair_of_sems(2 * half), pair_of_sems(2 * half)]
    scratch += [sems_of(seq_size), pltpu.SemaphoreType.DMA((dp_size + 8,)), sems_of(seq_size)]
    scratch += [pair_of_sems(2 * half), sems_of(2 * half), pair_of_sems(2 * half), pair_of_sems(2 * half)]
    scratch += [sems_of(2 * pairs)] * 2 + [sems_of(2 * half)]
    scratch += [pair_of_sems(2 * pairs), sems_of(2 * pairs), pair_of_sems(2 * pairs), pair_of_sems(2 * pairs)]
    scratch += [sems_of(2 * pairs)]
    scratch += [pltpu.SemaphoreType.DMA((12,))]
    return pl.pallas_call(
        functools.partial(resident_kernel, seq_size, dp_size),
        out_shape=(
            jax.ShapeDtypeStruct((tok, D), BF),
            jax.ShapeDtypeStruct((tok, D), BF),
            jax.ShapeDtypeStruct((seq_size, LANES, 3 * wide), BF),
            jax.ShapeDtypeStruct((seq_size, LANES, wide), BF),
            jax.ShapeDtypeStruct((seq_size, LANES, units_all), BF),
            jax.ShapeDtypeStruct((seq_size, LANES, D), BF),
            jax.ShapeDtypeStruct((16, LANES), F32),
        ),
        in_specs=[any_spec] * 6 + [vmem] * 9 + [any_spec] * 3,
        out_specs=[any_spec] * 7,
        scratch_shapes=scratch,
        compiler_params=pltpu.CompilerParams(
            collective_id=2, has_side_effects=True, vmem_limit_bytes=RESIDENT_VMEM
        ),
    )(*args)


RESIDENT_VMEM = 63 * 2**20


def finish_kernel(seq_size, dp_size, *refs):
    (block, grad, mix, proj, rise, fall, vec), refs = refs[:7], refs[7:]
    (block_out, grad_out, mix_out, proj_out, rise_out, fall_out), refs = refs[:6], refs[6:]
    vec_outs, refs = refs[:8], refs[8:]
    (block_in, grad_in, mix_in, proj_in, rise_in, fall_in, vec_in, mix_f, proj_f, rise_f, fall_f), refs = refs[:11], refs[11:]
    vec_fs, (in_sems, out_sems) = refs[:8], refs[8:]
    parts = [(fall.at[group], fall_in.at[group]) for group in range(seq_size)]
    parts += [(rise, rise_in), (mix, mix_in), (proj, proj_in), (block, block_in), (grad, grad_in), (vec, vec_in)]
    coming = []
    for src, dst in parts:
        copy = pltpu.make_async_copy(src, dst, in_sems.at[len(coming)])
        copy.start()
        coming.append(copy)
    *fall_copies, rise_copy, mix_copy, proj_copy, block_copy, grad_copy, vec_copy = coming
    leaving = []

    def leave(src, dst):
        copy = pltpu.make_async_copy(src, dst, out_sems.at[len(leaving)])
        copy.start()
        leaving.append(copy)

    for group in range(seq_size):
        fall_copies[group].wait()
        at = pl.ds(group * LANES, LANES)
        fall_f[at, :] = fall_in[group].astype(F32)
        leave(fall_f.at[at], fall_out.at[at])
    few = 32
    rise_copy.wait()
    for start in range(0, LANES, few):
        at = pl.ds(start, few)
        for group in range(seq_size):
            for index in range(dp_size):
                column = (index * seq_size + group) * LANES
                rise_f[at, column : column + LANES] = rise_in[group, at, index * LANES : (index + 1) * LANES].astype(F32)
        leave(rise_f.at[at], rise_out.at[at])
    mix_copy.wait()
    proj_copy.wait()
    for start in range(0, LANES, 2 * few):
        at = pl.ds(start, 2 * few)
        for held, full, out in ((mix_in, mix_f, mix_out), (proj_in, proj_f, proj_out)):
            columns = held.shape[2]
            for group in range(seq_size):
                full[at, group * columns : (group + 1) * columns] = held[group, at, :].astype(F32)
            leave(full.at[at], out.at[at])
    block_copy.wait()
    leave(block_in, block_out)
    grad_copy.wait()
    leave(grad_in, grad_out)
    vec_copy.wait()
    for held, out, row in zip(vec_fs, vec_outs, (0, 1, 2, 3, 4, 4, 5, 8), strict=True):
        for start in range(0, out.shape[0], LANES):
            held[start : start + LANES] = vec_in[row + start // LANES]
        leave(held, out)
    for copy in leaving:
        copy.wait()


def finish_call(seq_size, dp_size, block, grad, mix, proj, rise, fall, vec):
    tok = block.shape[0]
    vec_sizes = (LANES,) * 6 + (3 * LANES, seq_size * LANES)
    full_sizes = ((LANES, 3 * D), (LANES, D), (LANES, FF), (seq_size * LANES, D))
    any_spec = pl.BlockSpec(memory_space=pl.ANY)
    return pl.pallas_call(
        functools.partial(finish_kernel, seq_size, dp_size),
        out_shape=(jax.ShapeDtypeStruct((tok, D), BF),) * 2
        + tuple(jax.ShapeDtypeStruct(size, F32) for size in full_sizes)
        + tuple(jax.ShapeDtypeStruct((size,), F32) for size in vec_sizes),
        in_specs=[any_spec] * 7,
        out_specs=[any_spec] * 14,
        scratch_shapes=[pltpu.VMEM(array.shape, array.dtype) for array in (block, grad, mix, proj, rise, fall, vec)]
        + [pltpu.VMEM(size, F32) for size in full_sizes]
        + [pltpu.VMEM((size,), F32) for size in vec_sizes]
        + [pltpu.SemaphoreType.DMA((seq_size + 6,)), pltpu.SemaphoreType.DMA((24,))],
        compiler_params=pltpu.CompilerParams(vmem_limit_bytes=RESIDENT_VMEM),
    )(block, grad, mix, proj, rise, fall, vec)


def resident_tables(length):
    cosine, sine = angle_tables(length)
    half = ROT // 2
    cos_table = np.ones((length, LANES), np.float32)
    sin_table = np.zeros((length, LANES), np.float32)
    cos_table[:, :half] = cosine
    cos_table[:, half:ROT] = cosine
    sin_table[:, :half] = -sine
    sin_table[:, half:ROT] = sine
    return jnp.asarray(cos_table), jnp.asarray(sin_table)


def resident_shards(
    tokens,
    cotangent,
    norm1_gain,
    norm1_bias,
    norm2_gain,
    norm2_bias,
    qkv_weight,
    qkv_bias,
    out_weight,
    out_bias,
    up_weight,
    up_bias,
    down_weight,
    down_bias,
    segment_ids,
    pad_length,
):
    seq_size, dp_size = lax.axis_size("seq"), lax.axis_size("dp")
    tok = tokens.shape[1]
    vectors = (norm1_gain, norm1_bias, norm2_gain, norm2_bias, out_bias, down_bias, qkv_bias, up_bias)
    cosine, sine = resident_tables(tok * seq_size)
    parts = resident_call(
        seq_size,
        dp_size,
        tokens[0],
        cotangent[0],
        qkv_weight,
        out_weight,
        up_weight,
        down_weight,
        *(vector.reshape(-1, LANES) for vector in vectors),
        segment_ids,
        pad_length,
        cosine,
        sine,
    )
    done = finish_call(seq_size, dp_size, *parts)
    block_out, input_grad, g_mix, g_proj, g_rise, g_fall = done[:6]
    norm1_g, norm1_b, norm2_g, norm2_b, out_b, down_b, b_mix, b_rise = done[6:]
    return (
        block_out[None],
        input_grad[None],
        norm1_g,
        norm1_b,
        norm2_g,
        norm2_b,
        g_mix,
        b_mix,
        g_proj,
        out_b,
        g_rise,
        b_rise,
        g_fall,
        down_b,
    )


def streamed_shards(
    tokens,
    cotangent,
    norm1_gain,
    norm1_bias,
    norm2_gain,
    norm2_bias,
    qkv_weight,
    qkv_bias,
    out_weight,
    out_bias,
    up_weight,
    up_bias,
    down_weight,
    down_bias,
    segment_ids,
    pad_length,
):
    seq_size, dp_size = lax.axis_size("seq"), lax.axis_size("dp")
    seq = lax.axis_index("seq")
    dp = lax.axis_index("dp")
    tok = tokens.shape[1]
    length = tok * seq_size
    heads_n = HEADS // seq_size
    rows = D // dp_size
    wide = heads_n * HEAD_DIM
    units = FF // dp_size // seq_size

    mix = qkv_weight.reshape(rows, seq_size, heads_n, 3, HEAD_DIM)
    mix = lax.dynamic_index_in_dim(mix, seq, 1, keepdims=False)
    mix = mix.transpose(0, 2, 1, 3).reshape(rows, 3 * wide)
    proj = lax.dynamic_slice_in_dim(out_weight, seq * wide, wide, 1)
    rise = up_weight.reshape(rows, dp_size, seq_size, units)
    rise = lax.dynamic_index_in_dim(rise, seq, 2, keepdims=False).reshape(rows, dp_size * units)
    fall = lax.dynamic_slice_in_dim(down_weight, seq * units, units, 0)
    vec = jnp.concatenate(
        [norm1_gain, norm1_bias, norm2_gain, norm2_bias, out_bias, down_bias, qkv_bias, up_bias]
    )
    vec_len = vec.shape[0]
    vec = jnp.pad(vec, (0, 2048 - vec_len)).reshape(16, 128)
    seg = jnp.broadcast_to(segment_ids, (8, tok))
    x_all, dy_all, w_mix, _, w_rise, w_fall, vec_all, seg_all, w_proj = gather_all(
        seq_size, dp_size, tokens[0], cotangent[0], mix, proj, rise, fall, vec, seg
    )
    x = x_all.reshape(length, D).astype(F32)
    dy = dy_all.reshape(length, D)
    w_mix = w_mix.reshape(D, 3 * wide)
    w_rise = w_rise.reshape(D, dp_size * units)
    w_fall = w_fall.reshape(dp_size * units, D)
    w_proj = w_proj.reshape(seq_size, wide, wide).transpose(1, 0, 2).reshape(wide, D)
    segments = seg_all[:, 0, :].reshape(length)
    vec_all = vec_all.reshape(dp_size, 2048)[:, :vec_len].astype(F32)
    g1, s1, g2, s2, b_proj, b_fall = (
        vec_all[:, i * rows : (i + 1) * rows].reshape(D) for i in range(6)
    )
    b_mix = vec_all[:, 6 * rows : 9 * rows].reshape(seq_size, heads_n, 3, HEAD_DIM)
    b_mix = lax.dynamic_index_in_dim(b_mix, seq, 0, keepdims=False)
    b_mix = b_mix.transpose(1, 0, 2).reshape(3 * wide)
    b_rise = vec_all[:, 9 * rows :].reshape(dp_size, seq_size, units)
    b_rise = lax.dynamic_index_in_dim(b_rise, seq, 1, keepdims=False).reshape(dp_size * units)

    center = x - jnp.mean(x, axis=-1, keepdims=True)
    rstd = lax.rsqrt(jnp.mean(center * center, axis=-1, keepdims=True) + EPS)
    n = center * rstd
    normed1 = (n * g1 + s1).astype(BF)
    normed2 = (n * g2 + s2).astype(BF)
    valid = (jnp.arange(length, dtype=jnp.int32) < length - pad_length[0]).astype(F32)[:, None]
    cosine, sine = (jnp.asarray(t) for t in angle_tables(length))

    mixed = dot(normed1, w_mix) + b_mix
    mixed = mixed.reshape(length, 3, heads_n, HEAD_DIM).transpose(1, 2, 0, 3)
    queries = turn(mixed[0], cosine, sine, 1.0).astype(BF)
    keys = turn(mixed[1], cosine, sine, 1.0).astype(BF)
    values = mixed[2].astype(BF)
    d_heads = (dot_nt(dy, w_proj) * valid).astype(BF)
    d_heads = d_heads.reshape(length, heads_n, HEAD_DIM).transpose(1, 0, 2)
    heads, d_q, d_k, d_v = attention(queries, keys, values, d_heads, segments)
    attn_rows = (heads.transpose(1, 0, 2).reshape(length, wide).astype(F32) * valid).astype(BF)
    d_mixed = jnp.stack(
        [
            turn(d_q.astype(F32), cosine, sine, -1.0).astype(BF),
            turn(d_k.astype(F32), cosine, sine, -1.0).astype(BF),
            d_v,
        ]
    )
    d_mixed = d_mixed.transpose(2, 0, 1, 3).reshape(length, 3 * wide)

    upward = dot(normed2, w_rise) + b_rise
    active = jax.nn.gelu(upward, approximate=False).astype(BF)
    slope = 0.5 * (1 + lax.erf(upward * (0.5**0.5))) + upward * jnp.exp(
        -0.5 * upward * upward
    ) * ((2 * np.pi) ** -0.5)
    d_up = (slope * dot_nt(dy, w_fall)).astype(BF)
    out_part = (dot(attn_rows, w_proj) + dot(active, w_fall)).astype(BF)
    d_n1 = dot_nt(d_mixed, w_mix)
    d_n2 = dot_nt(d_up, w_rise)
    back_part = (g1 * d_n1 + g2 * d_n2).astype(BF)

    g_mix = dot_t(normed1, d_mixed).astype(BF).reshape(dp_size, rows, 3 * wide)
    g_proj = dot_t(attn_rows, dy).astype(BF).reshape(dp_size // seq_size, rows, seq_size, wide)
    g_proj = g_proj.transpose(2, 0, 1, 3)
    g_rise = dot_t(normed2, d_up).astype(BF).reshape(dp_size, rows, dp_size * units)
    g_fall = dot_t(active, dy).astype(BF).reshape(dp_size, units, D)
    dyf = dy.astype(F32)
    vec_part = jnp.concatenate(
        [
            t.reshape(dp_size, -1)
            for t in (
                jnp.sum(d_n1 * n, axis=0),
                jnp.sum(d_n1, axis=0),
                jnp.sum(d_n2 * n, axis=0),
                jnp.sum(d_n2, axis=0),
                jnp.sum(dyf, axis=0),
                jnp.sum(d_up.astype(F32), axis=0),
            )
        ]
        + [jnp.broadcast_to(jnp.sum(d_mixed.astype(F32), axis=0)[None], (dp_size, 3 * wide))],
        axis=1,
    )
    part_len = vec_part.shape[1]
    vec_part = jnp.pad(vec_part, ((0, 0), (0, 2048 - part_len))).reshape(dp_size, 16, 128)
    out_sum, back_sum, f_mix, f_proj, f_rise, f_fall, f_vec = reduce_all(
        seq_size,
        dp_size,
        out_part.reshape(seq_size, tok, D),
        back_part.reshape(seq_size, tok, D),
        g_mix,
        g_proj,
        g_rise,
        g_fall,
        vec_part,
    )
    own_x = tokens[0].astype(F32)
    block_output = (own_x + out_sum + b_proj + b_fall).astype(BF)
    own_center = own_x - jnp.mean(own_x, axis=-1, keepdims=True)
    own_rstd = lax.rsqrt(jnp.mean(own_center * own_center, axis=-1, keepdims=True) + EPS)
    own_n = own_center * own_rstd
    back = own_rstd * (
        back_sum
        - jnp.mean(back_sum, axis=-1, keepdims=True)
        - own_n * jnp.mean(back_sum * own_n, axis=-1, keepdims=True)
    )
    input_grad = (cotangent[0].astype(F32) + back).astype(BF)
    f_mix = f_mix.reshape(seq_size, rows, 3, heads_n, HEAD_DIM)
    f_mix = f_mix.transpose(1, 0, 3, 2, 4).reshape(rows, 3 * D).astype(F32)
    f_proj = f_proj.transpose(1, 0, 2).reshape(rows, D).astype(F32)
    f_rise = f_rise.reshape(seq_size, rows, dp_size, units)
    f_rise = f_rise.transpose(1, 2, 0, 3).reshape(rows, FF).astype(F32)
    f_fall = f_fall.reshape(seq_size * units, D).astype(F32)
    f_vec = f_vec.reshape(seq_size, 2048)[:, :part_len]
    norm_sums = jnp.sum(f_vec[:, : 4 * rows], axis=0)
    column = f_vec[0, 4 * rows : 5 * rows]
    f_b_rise = f_vec[:, 5 * rows : 5 * rows + units].reshape(seq_size * units)
    f_b_mix = f_vec[:, 5 * rows + units :].reshape(seq_size, 3, heads_n, HEAD_DIM)
    f_b_mix = f_b_mix.transpose(0, 2, 1, 3).reshape(dp_size, 3 * rows)
    f_b_mix = lax.dynamic_index_in_dim(f_b_mix, dp, 0, keepdims=False)
    return (
        block_output[None],
        input_grad[None],
        norm_sums[:rows],
        norm_sums[rows : 2 * rows],
        norm_sums[2 * rows : 3 * rows],
        norm_sums[3 * rows :],
        f_mix,
        f_b_mix,
        f_proj,
        column,
        f_rise,
        f_b_rise,
        f_fall,
        column,
    )


def shards(*args):
    seq_size, dp_size = lax.axis_size("seq"), lax.axis_size("dp")
    if resident_fits(seq_size, dp_size, args[0].shape[1]):
        return resident_shards(*args)
    return streamed_shards(*args)


def solution(mesh):
    rows = P("dp", "seq", None)
    weight = P("dp", None)
    vector = P("dp")
    return jax.shard_map(
        shards,
        mesh=mesh,
        in_specs=(rows, rows)
        + (vector,) * 4
        + (weight, vector) * 4
        + (P("dp", "seq"), vector),
        out_specs=(rows, rows) + (vector,) * 4 + (weight, vector) * 4,
        check_vma=False,
    )
```

```python
import functools
import typing

import jax
import jax.numpy as jnp
import numpy as np
from jax import lax
from jax.experimental import pallas as pl
from jax.experimental.pallas import tpu as pltpu
from jax.sharding import PartitionSpec as P

D = 1024
HEADS = 16
HEAD_DIM = 64
ROT = 16
FF = 4096
EPS = 1e-05
BASE = 10000.0
NEG = -1e30
MESH = pl.DeviceIdType.MESH
BF = jnp.bfloat16
F32 = jnp.float32


def ring_pos(dev, size):
    return (dev // 2) * (1 - dev % 2) + (size - 1 - dev // 2) * (dev % 2)


def ring_dev(pos, size):
    high = pos // (size // 2)
    return (1 - high) * 2 * pos + high * (2 * (size - 1 - pos) + 1)


class Place:
    def __init__(self, seq_size, dp_size):
        self.seq_size, self.dp_size = seq_size, dp_size
        self.seq = lax.axis_index("seq")
        self.dp = lax.axis_index("dp")
        self.pos = ring_pos(self.dp, dp_size)
        self.half = dp_size // 2
        self.pairs = seq_size // 2
        self.core = self.seq % 2
        self.pair = self.seq // 2
        self.sibling = self.pair * 2 + 1 - self.core

    def ring(self, offset):
        return ring_dev((self.pos + offset + self.dp_size) % self.dp_size, self.dp_size)

    def dp_peer(self, step):
        return (self.dp + step + self.dp_size) % self.dp_size

    def pair_peer(self, step):
        return ((self.pair + step + self.pairs) % self.pairs) * 2 + self.core

    def across_source(self, step):
        return ((self.pair - step + self.pairs) % self.pairs) * 2 + 1 - self.core

    def seq_peer(self, step):
        return (self.seq + step + self.seq_size) % self.seq_size

    def greet_near(self):
        barrier = pltpu.get_barrier_semaphore()
        for step in (1, -1):
            pl.semaphore_signal(barrier, inc=1, device_id={"dp": self.ring(step)}, device_id_type=MESH)
        for step in range(1, self.seq_size):
            pl.semaphore_signal(
                barrier, inc=1, device_id={"seq": self.seq_peer(step)}, device_id_type=MESH
            )

    def met_near(self):
        pl.semaphore_wait(pltpu.get_barrier_semaphore(), 2 + self.seq_size - 1)

    def greet(self):
        barrier = pltpu.get_barrier_semaphore()
        for step in range(1, self.dp_size):
            pl.semaphore_signal(
                barrier, inc=1, device_id={"dp": self.dp_peer(step)}, device_id_type=MESH
            )
        for step in range(1, self.seq_size):
            pl.semaphore_signal(
                barrier, inc=1, device_id={"seq": self.seq_peer(step)}, device_id_type=MESH
            )
        pl.semaphore_wait(barrier, self.dp_size - 1 + self.seq_size - 1)


def send(src, dst, sems, index, target):
    return pltpu.make_async_remote_copy(
        src_ref=src,
        dst_ref=dst,
        send_sem=sems.at[0, index],
        recv_sem=sems.at[1, index],
        device_id=target,
        device_id_type=MESH,
    )


def halves(ref):
    rows = ref.shape[0]
    columns = ref.shape[1]
    if rows % (32 if ref.dtype == BF else 16) == 0:
        return ref.at[pl.ds(0, rows // 2)], ref.at[pl.ds(rows // 2, rows // 2)]
    return ref.at[:, pl.ds(0, columns // 2)], ref.at[:, pl.ds(columns // 2, columns // 2)]


class RingGather:
    def __init__(self, place, full, sems):
        self.place, self.full, self.sems = place, full, sems

    def piece(self, offset, step, way):
        block = self.full.at[self.place.ring(offset)]
        return block if step < self.place.half else halves(block)[way]

    def copies(self, step):
        place = self.place
        right = self.piece(-(step - 1), step, 0)
        left = self.piece(step - 1, step, 1)
        index = 2 * (step - 1)
        return (
            send(right, right, self.sems, index, {"dp": place.ring(1)}),
            send(left, left, self.sems, index + 1, {"dp": place.ring(-1)}),
        )

    def arrivals(self, step):
        right = self.piece(-step, step, 0)
        left = self.piece(step, step, 1)
        index = 2 * (step - 1)
        return (
            send(right, right, self.sems, index, {"dp": self.place.ring(1)}),
            send(left, left, self.sems, index + 1, {"dp": self.place.ring(-1)}),
        )

    def tick(self, step):
        if step > 1:
            for copy in self.arrivals(step - 1):
                copy.wait_recv()
        if step <= self.place.half:
            for copy in self.copies(step):
                copy.start()

    def finish(self):
        for step in range(1, self.place.half + 1):
            for copy in self.copies(step):
                copy.wait_send()


class RingReduce:
    def __init__(self, place, parts, arrived, sems):
        self.place, self.parts, self.arrived, self.sems = place, parts, arrived, sems

    def piece(self, ref, step, way):
        return ref if step > 1 else halves(ref)[way]

    def copies(self, step):
        place = self.place
        away = place.half - step + 1
        index = 2 * (step - 1)
        out = []
        for way, (offset, target) in enumerate(((away, 1), (-away, -1))):
            src = self.piece(self.parts.at[place.ring(offset)], step, way)
            dst = self.piece(self.arrived.at[way, step - 1], step, way)
            out.append(send(src, dst, self.sems, index + way, {"dp": place.ring(target)}))
        return out

    def tick(self, step):
        place = self.place
        if step > 1:
            for way, copy in enumerate(self.copies(step - 1)):
                copy.wait_recv()
                away = (place.half - step + 1) * (1 - 2 * way)
                held = self.piece(self.parts.at[place.ring(away)], step - 1, way)
                came = self.piece(self.arrived.at[way, step - 2], step - 1, way)
                held[...] = (held[...].astype(F32) + came[...].astype(F32)).astype(held.dtype)
        if step <= place.half:
            for copy in self.copies(step):
                copy.start()

    def finish(self):
        for step in range(1, self.place.half + 1):
            for copy in self.copies(step):
                copy.wait_send()

    def own(self):
        return self.parts.at[self.place.dp]


class SeqGather:
    def __init__(self, place, full, sems, own=None):
        self.place, self.full, self.sems = place, full, sems
        self.own = full.at[place.seq] if own is None else own

    def direct(self, step):
        place = self.place
        target = {"seq": place.pair_peer(step)}
        return send(self.own, self.full.at[place.seq], self.sems, step, target)

    def arrival(self, step):
        place = self.place
        target = {"seq": place.pair_peer(step)}
        return send(self.own, self.full.at[place.pair_peer(-step)], self.sems, step, target)

    def across(self, step):
        place = self.place
        block = self.full.at[place.pair_peer(-step)]
        src = self.own if step == 0 else block
        return send(src, block, self.sems, place.pairs + step, {"seq": place.sibling})

    def across_arrival(self, step):
        place = self.place
        block = self.full.at[place.across_source(step)]
        return send(self.own, block, self.sems, place.pairs + step, {"seq": place.sibling})

    def begin(self):
        for step in range(1, self.place.pairs):
            self.direct(step).start()
        self.across(0).start()

    def forward(self):
        for step in range(1, self.place.pairs):
            self.arrival(step).wait_recv()
            self.across(step).start()

    def across_arrived(self, step):
        self.across_arrival(step).wait_recv()

    def sent(self):
        for step in range(1, self.place.pairs):
            self.direct(step).wait_send()
        for step in range(self.place.pairs):
            self.across(step).wait_send()

    def finish(self):
        for step in range(self.place.pairs):
            self.across_arrived(step)
        self.sent()


class SeqReduce:
    def __init__(self, place, parts, crossed, arrived, sems):
        self.place, self.parts, self.crossed, self.arrived = place, parts, crossed, arrived
        self.sems = sems

    def over(self, step):
        place = self.place
        index = (place.pair + step) % place.pairs
        src = self.parts.at[index * 2 + 1 - place.core]
        return send(src, self.crossed.at[index], self.sems, step, {"seq": place.sibling})

    def direct(self, step):
        place = self.place
        return send(
            self.parts.at[place.pair_peer(step)],
            self.arrived.at[step],
            self.sems,
            place.pairs + step,
            {"seq": place.pair_peer(step)},
        )

    def over_start(self, step):
        self.over(step).start()

    def over_add(self, step):
        place = self.place
        index = (place.pair + step) % place.pairs
        self.over(step).wait_recv()
        held = self.parts.at[index * 2 + place.core]
        held[...] = (held[...].astype(F32) + self.crossed[index].astype(F32)).astype(held.dtype)
        if step > 0:
            self.direct(step).start()

    def begin(self):
        for step in range(self.place.pairs):
            self.over_start(step)

    def middle(self):
        for step in range(self.place.pairs):
            self.over_add(step)

    def total(self):
        place = self.place
        total = self.parts.at[place.seq][...].astype(F32)
        for step in range(1, place.pairs):
            self.direct(step).wait_recv()
            total = total + self.arrived[step].astype(F32)
        return total

    def finish(self):
        for step in range(self.place.pairs):
            self.over(step).wait_send()
        for step in range(1, self.place.pairs):
            self.direct(step).wait_send()


class DpSpread:
    def __init__(self, place, src_of, full, sems):
        self.place, self.src_of, self.full, self.sems = place, src_of, full, sems

    def copy(self, step):
        place = self.place
        peer = place.dp_peer(step)
        return send(self.src_of(peer), self.full.at[place.dp], self.sems, step, {"dp": peer})

    def arrival(self, step):
        place = self.place
        source = place.dp_peer(-step)
        return send(
            self.src_of(source), self.full.at[source], self.sems, step, {"dp": place.dp_peer(step)}
        )

    def begin(self):
        for step in range(1, self.place.dp_size):
            self.copy(step).start()

    def finish(self):
        for step in range(1, self.place.dp_size):
            self.arrival(step).wait_recv()
        for step in range(1, self.place.dp_size):
            self.copy(step).wait_send()


def sems_of(count):
    return pltpu.SemaphoreType.DMA((2, count))


def gather_kernel(seq_size, dp_size, *refs):
    (x_ref, dy_ref, mix_ref, proj_ref, rise_ref, fall_ref, vec_ref, seg_ref) = refs[:8]
    (x_all, dy_all, mix_all, proj_cols, rise_all, fall_all, vec_all, seg_all, proj_all) = refs[8:17]
    (x_sems, dy_sems, mix_sems, proj_sems, rise_sems, fall_sems, vec_sems, seg_sems, swap_sems, own_sems) = refs[17:]
    place = Place(seq_size, dp_size)
    own = [
        pltpu.make_async_copy(src, dst, own_sems.at[i])
        for i, (src, dst) in enumerate(
            (
                (x_ref, x_all.at[place.seq]),
                (dy_ref, dy_all.at[place.seq]),
                (mix_ref, mix_all.at[place.dp]),
                (proj_ref, proj_cols.at[place.dp]),
                (rise_ref, rise_all.at[place.dp]),
                (fall_ref, fall_all.at[place.dp]),
                (vec_ref, vec_all.at[place.dp]),
                (seg_ref, seg_all.at[place.seq]),
            )
        )
    ]
    for copy in own:
        copy.start()
    place.greet()
    for copy in own:
        copy.wait()
    x_move = SeqGather(place, x_all, x_sems)
    dy_move = SeqGather(place, dy_all, dy_sems)
    seg_move = SeqGather(place, seg_all, seg_sems)
    vec_move = DpSpread(place, lambda peer: vec_ref, vec_all, vec_sems)
    mix_move = RingGather(place, mix_all, mix_sems)
    proj_move = RingGather(place, proj_cols, proj_sems)
    rise_move = RingGather(place, rise_all, rise_sems)
    fall_move = RingGather(place, fall_all, fall_sems)
    x_move.begin()
    seg_move.begin()
    vec_move.begin()
    half = place.half
    for step in range(1, half + 1):
        mix_move.tick(step)
        proj_move.tick(step)
    x_move.forward()
    seg_move.forward()
    dy_move.begin()
    mix_move.tick(half + 1)
    proj_move.tick(half + 1)
    rise_move.tick(1)
    fall_move.tick(1)
    rows = proj_cols.shape[0] * proj_cols.shape[1] // seq_size
    each = rows // proj_cols.shape[1]
    swaps = []
    for step in range(1, seq_size):
        peer = place.seq_peer(step)
        swaps.append(
            send(
                proj_cols.at[pl.ds(peer * each, each)],
                proj_all.at[place.seq],
                swap_sems,
                step,
                {"seq": peer},
            )
        )
    for copy in swaps:
        copy.start()
    mine = pltpu.make_async_copy(
        proj_cols.at[pl.ds(place.seq * each, each)], proj_all.at[place.seq], own_sems.at[0]
    )
    mine.start()
    for step in range(2, half + 2):
        rise_move.tick(step)
        fall_move.tick(step)
        if step == 3:
            dy_move.forward()
    mine.wait()
    for step in range(1, seq_size):
        source = place.seq_peer(-step)
        send(
            proj_cols.at[pl.ds(source * each, each)],
            proj_all.at[source],
            swap_sems,
            step,
            {"seq": place.seq_peer(step)},
        ).wait_recv()
    for copy in swaps:
        copy.wait_send()
    for move in (x_move, dy_move, seg_move, vec_move, mix_move, proj_move, rise_move, fall_move):
        move.finish()


def gather_all(seq_size, dp_size, x, dy, mix, proj, rise, fall, vec, seg):
    half = dp_size // 2
    pairs = seq_size // 2

    def lead(count, like):
        return jax.ShapeDtypeStruct((count,) + like.shape, like.dtype)

    each = dp_size // seq_size
    any_spec = pl.BlockSpec(memory_space=pl.ANY)
    return pl.pallas_call(
        functools.partial(gather_kernel, seq_size, dp_size),
        out_shape=(
            lead(seq_size, x),
            lead(seq_size, dy),
            lead(dp_size, mix),
            lead(dp_size, proj),
            lead(dp_size, rise),
            lead(dp_size, fall),
            lead(dp_size, vec),
            lead(seq_size, seg),
            jax.ShapeDtypeStruct((seq_size, each) + proj.shape, proj.dtype),
        ),
        in_specs=[any_spec] * 8,
        out_specs=[any_spec] * 9,
        scratch_shapes=[
            sems_of(2 * pairs),
            sems_of(2 * pairs),
            sems_of(2 * half),
            sems_of(2 * half),
            sems_of(2 * half),
            sems_of(2 * half),
            sems_of(dp_size),
            sems_of(2 * pairs),
            sems_of(seq_size),
            pltpu.SemaphoreType.DMA((8,)),
        ],
        compiler_params=pltpu.CompilerParams(collective_id=0, has_side_effects=True),
    )(x, dy, mix, proj, rise, fall, vec, seg)


def reduce_kernel(seq_size, dp_size, *refs):
    (out_ref, back_ref, mix_ref, proj_ref, rise_ref, fall_ref, vec_ref), refs = refs[:7], refs[7:]
    (out_sum, back_sum, mix_fin, proj_fin, rise_fin, fall_fin, vec_fin), refs = refs[:7], refs[7:]
    (
        out_cross,
        out_came,
        back_cross,
        back_came,
        proj_full,
        mix_came,
        proj_came,
        rise_came,
        fall_came,
        vec_came,
        out_sems,
        back_sems,
        swap_sems,
        mix_sems,
        proj_sems,
        rise_sems,
        fall_sems,
        vec_sems,
        mix_fs,
        proj_fs,
        rise_fs,
        fall_fs,
        vec_fs,
    ) = refs
    place = Place(seq_size, dp_size)
    each = dp_size // seq_size
    half = place.half
    place.greet()

    def mine(index):
        return proj_full.at[pl.ds(index * each, each)]

    def swap(step):
        peer = place.seq_peer(step)
        return send(proj_ref.at[peer], mine(place.seq), swap_sems, step, {"seq": peer})

    def swap_arrival(step):
        source = place.seq_peer(-step)
        target = {"seq": place.seq_peer(step)}
        return send(proj_ref.at[source], mine(source), swap_sems, step, target)

    for step in range(1, seq_size):
        swap(step).start()
    mine(place.seq)[...] = proj_ref[place.seq]
    mix = RingReduce(place, mix_ref, mix_came, mix_sems)
    proj = RingReduce(place, proj_full, proj_came, proj_sems)
    rise = RingReduce(place, rise_ref, rise_came, rise_sems)
    fall = RingReduce(place, fall_ref, fall_came, fall_sems)
    out = SeqReduce(place, out_ref, out_cross, out_came, out_sems)
    back = SeqReduce(place, back_ref, back_cross, back_came, back_sems)
    vec = DpSpread(place, lambda peer: vec_ref.at[peer], vec_came, vec_sems)
    mix.tick(1)
    rise.tick(1)
    out.begin()
    back.begin()
    vec.begin()
    for step in range(1, seq_size):
        swap_arrival(step).wait_recv()
    proj.tick(1)
    fall.tick(1)
    out.middle()
    back.middle()
    for step in range(2, half + 2):
        for move in (mix, rise, proj, fall):
            move.tick(step)
    finals = []
    for move, fin, fin_sems in (
        (mix, mix_fin, mix_fs),
        (rise, rise_fin, rise_fs),
        (proj, proj_fin, proj_fs),
        (fall, fall_fin, fall_fs),
    ):
        fin[place.seq] = move.parts[place.dp]
        gather = SeqGather(place, fin, fin_sems)
        gather.begin()
        finals.append(gather)
    vec_came[place.dp] = vec_ref[place.dp]
    vec.finish()
    vec_fin[place.seq] = jnp.sum(vec_came[...], axis=0)
    gather = SeqGather(place, vec_fin, vec_fs)
    gather.begin()
    finals.append(gather)
    out_sum[...] = out.total()
    back_sum[...] = back.total()
    for gather in finals:
        gather.forward()
    for gather in finals:
        gather.finish()
    for step in range(1, seq_size):
        swap(step).wait_send()
    for move in (mix, rise, proj, fall, out, back):
        move.finish()


def reduce_all(seq_size, dp_size, out, back, mix, proj, rise, fall, vec):
    half = dp_size // 2
    pairs = seq_size // 2
    each = dp_size // seq_size

    def fin(like):
        return jax.ShapeDtypeStruct((seq_size,) + like.shape[1:], like.dtype)

    def came(like):
        return pltpu.VMEM((2, half) + like.shape[1:], like.dtype)

    proj_blocks = jax.ShapeDtypeStruct((dp_size,) + proj.shape[2:], proj.dtype)
    vmem = pl.BlockSpec(memory_space=pltpu.VMEM)
    return pl.pallas_call(
        functools.partial(reduce_kernel, seq_size, dp_size),
        out_shape=(
            jax.ShapeDtypeStruct(out.shape[1:], F32),
            jax.ShapeDtypeStruct(back.shape[1:], F32),
            fin(mix),
            fin(proj_blocks),
            fin(rise),
            fin(fall),
            fin(vec),
        ),
        in_specs=[vmem] * 7,
        out_specs=[vmem] * 7,
        scratch_shapes=[
            pltpu.VMEM((pairs,) + out.shape[1:], BF),
            pltpu.VMEM((pairs,) + out.shape[1:], BF),
            pltpu.VMEM((pairs,) + back.shape[1:], BF),
            pltpu.VMEM((pairs,) + back.shape[1:], BF),
            pltpu.VMEM(proj_blocks.shape, BF),
            came(mix),
            came(proj_blocks),
            came(rise),
            came(fall),
            pltpu.VMEM(vec.shape, F32),
            sems_of(2 * pairs),
            sems_of(2 * pairs),
            sems_of(seq_size),
            sems_of(2 * half),
            sems_of(2 * half),
            sems_of(2 * half),
            sems_of(2 * half),
            sems_of(dp_size),
            sems_of(2 * pairs),
            sems_of(2 * pairs),
            sems_of(2 * pairs),
            sems_of(2 * pairs),
            sems_of(2 * pairs),
        ],
        compiler_params=pltpu.CompilerParams(
            collective_id=1, has_side_effects=True, vmem_limit_bytes=56 * 2**20
        ),
    )(out, back, mix, proj, rise, fall, vec)


def angle_tables(length):
    frequency = BASE ** (-np.arange(0, ROT, 2).astype(np.float32) / np.float32(ROT))
    angles = np.arange(length, dtype=np.float32)[:, None] * frequency.astype(np.float32)[None, :]
    return np.cos(angles).astype(np.float32), np.sin(angles).astype(np.float32)


def turn(piece, cosine, sine, sign):
    half = ROT // 2
    low, high = piece[..., :half], piece[..., half:ROT]
    return jnp.concatenate(
        [low * cosine - sign * high * sine, high * cosine + sign * low * sine, piece[..., ROT:]],
        axis=-1,
    )


TILE = 256

def mm(a, b, dims):
    return lax.dot_general(a, b, ((dims[0], dims[1]), ((), ())), preferred_element_type=F32)

def nn(a, b):
    return mm(a, b, ((1,), (0,)))

def nt(a, b):
    return mm(a, b, ((1,), (1,)))

def tn(a, b):
    return mm(a, b, ((0,), (0,)))

def fold(count, body, init):
    if isinstance(count, int):
        for index in range(count):
            init = body(index, init)
        return init
    return lax.fori_loop(0, count, body, init)

def rows_of(index):
    start = index * TILE
    return pl.ds(start if isinstance(start, int) else pl.multiple_of(start, TILE), TILE)

def attend_block(head, block, refs):
    q_ref, k_ref, v_ref, g_ref, kt_ref, vt_ref, s_ref, p_ref, ht_ref, dqt_ref, dk_ref, dv_ref = refs
    here = rows_of(block)
    span = block + 1
    dims = pl.ds(pl.multiple_of(head * HEAD_DIM, HEAD_DIM), HEAD_DIM)
    query = q_ref[head, here, :]
    grad = g_ref[head, here, :]

    def score(index, top):
        tile = nt(k_ref[head, rows_of(index), :], query)
        if isinstance(index, int) and isinstance(block, int) and index < block:
            keep = tile
        else:
            key = lax.broadcasted_iota(jnp.int32, (TILE, TILE), 0) + (index - block) * TILE
            place = lax.broadcasted_iota(jnp.int32, (TILE, TILE), 1)
            keep = jnp.where(key <= place, tile, NEG)
        s_ref[index] = keep
        return jnp.maximum(top, jnp.max(keep, axis=0, keepdims=True))

    top = fold(span, score, jnp.full((1, TILE), 2 * NEG, F32))

    def raise_(index, total):
        raised = jnp.exp(s_ref[index] - top)
        s_ref[index] = raised
        return total + jnp.sum(raised, axis=0, keepdims=True)

    total = fold(span, raise_, jnp.zeros((1, TILE), F32))
    share = 1.0 / total

    def weigh(index, carried):
        heads, delta = carried
        weights = s_ref[index] * share
        s_ref[index] = weights
        weights_b = weights.astype(BF)
        d_weights = nt(v_ref[head, rows_of(index), :], grad)
        p_ref[index] = d_weights
        dv_ref[head, rows_of(index), :] += nn(weights_b, grad)
        heads = heads + nn(vt_ref[dims, rows_of(index)], weights_b)
        return heads, delta + jnp.sum(weights * d_weights, axis=0, keepdims=True)

    heads, delta = fold(
        span, weigh, (jnp.zeros((HEAD_DIM, TILE), F32), jnp.zeros((1, TILE), F32))
    )
    ht_ref[dims, here] = heads

    def back(index, d_query):
        d_scores = (s_ref[index] * (p_ref[index] - delta)).astype(BF)
        dk_ref[head, rows_of(index), :] += nn(d_scores, query)
        return d_query + nn(kt_ref[dims, rows_of(index)], d_scores)

    dqt_ref[dims, here] = fold(span, back, jnp.zeros((HEAD_DIM, TILE), F32))

def attend(heads_n, length, refs):
    dk_ref, dv_ref = refs[-2:]
    dk_ref[...] = jnp.zeros(dk_ref.shape, F32)
    dv_ref[...] = jnp.zeros(dv_ref.shape, F32)
    blocks = length // TILE

    @pl.loop(0, heads_n)
    def _(head):
        if blocks <= 4:
            for block in range(blocks):
                attend_block(head, block, refs)
        else:
            @pl.loop(0, blocks)
            def _(block):
                attend_block(head, block, refs)

def attend_kernel(H, L, q, k, v, g, kt, vt, ht, dqt, dk, dv, s_ref, p_ref):
    attend(H, L, (q, k, v, g, kt, vt, s_ref, p_ref, ht, dqt, dk, dv))

def attention_call(q, k, v, g, kt, vt):
    H, L, _ = q.shape
    vm = pl.BlockSpec(memory_space=pltpu.VMEM)
    nb = L // TILE
    return pl.pallas_call(functools.partial(attend_kernel, H, L),
        out_shape=(jax.ShapeDtypeStruct((H*64, L), F32), jax.ShapeDtypeStruct((H*64, L), F32), jax.ShapeDtypeStruct((H, L, 128), F32), jax.ShapeDtypeStruct((H, L, 128), F32)),
        in_specs=[vm]*6, out_specs=[vm]*4,
        scratch_shapes=[pltpu.VMEM((nb, TILE, TILE), F32), pltpu.VMEM((nb, TILE, TILE), F32)],
        compiler_params=pltpu.CompilerParams(vmem_limit_bytes=56 * 2**20))(q, k, v, g, kt, vt)

def prep(queries, keys, values, d_heads, segments):
    seg = segments[:, None] == jnp.arange(64)[None, :]
    e = jnp.broadcast_to(seg.astype(BF)[None], queries.shape)
    f = jnp.broadcast_to(jnp.where(seg, 0.0, NEG).astype(BF)[None], queries.shape)
    lane = jnp.arange(64)
    f = jnp.where(lane < 4, f, 0).astype(BF)
    qa = jnp.concatenate([(queries.astype(F32) * 0.125).astype(BF), e], -1)
    ka = jnp.concatenate([keys, f], -1)
    z = jnp.zeros_like(values)
    va = jnp.concatenate([values, z], -1)
    ga = jnp.concatenate([d_heads, z], -1)
    kt = keys.transpose(0, 2, 1).reshape(-1, keys.shape[1])
    vt = values.transpose(0, 2, 1).reshape(-1, keys.shape[1])
    return qa, ka, va, ga, kt, vt

def attention(queries, keys, values, d_heads, segments):
    H, L, _ = queries.shape
    ht, dqt, dk, dv = attention_call(*prep(queries, keys, values, d_heads, segments))

    def back(t):
        return t.reshape(H, 64, L).transpose(0, 2, 1)

    return back(ht).astype(BF), (back(dqt) * 0.125).astype(BF), dk[..., :64].astype(BF), dv[..., :64].astype(BF)


def dot(a, b):
    return jnp.dot(a, b, preferred_element_type=F32)


def dot_t(a, b):
    return lax.dot_general(a, b, (((0,), (0,)), ((), ())), preferred_element_type=F32)


def dot_nt(a, b):
    return lax.dot_general(a, b, (((1,), (1,)), ((), ())), preferred_element_type=F32)


(
    OWN, XGO, DYGO, XFWD, DYFWD, HOTS, DYALL, VROWS, LN0, LN1, LN2, LN3, SWGO, SWIN, QKV0, QKV1,
    DH, GVC1, GVC2, GVC3, GVC4, GVC5, GMA1, GMA2, GMA3, GMA4, GMA5, GMB1, GMB2, GMB3, GMB4,
    GMB5, GPR1, GPR2, GPR3, GPR4, GPR5, GRA1, GRA2, GRA3, GRA4, GRA5, GRB1, GRB2, GRB3, GRB4,
    GRB5, GFA1, GFA2, GFA3, GFA4, GFA5, GFB1, GFB2, GFB3, GFB4, GFB5, RVC1, RVC2, RVC3, RVC4,
    RVC5, RMA1, RMA2, RMA3, RMA4, RMA5, RMB1, RMB2, RMB3, RMB4, RMB5, RPR1, RPR2, RPR3, RPR4,
    RPR5, RRA1, RRA2, RRA3, RRA4, RRA5, RRB1, RRB2, RRB3, RRB4, RRB5, RFA1, RFA2, RFA3, RFA4,
    RFA5, RFB1, RFB2, RFB3, RFB4, RFB5, AT00, AT02, AT03, AT10, AT12, AT13, AT20, AT22, AT23,
    AT30, AT32, AT33, POST0, POST1, GM0, GM1, GR0, GR1, GF0, GF1, GP, SBGO, SBIN, UP0, UP1, UP2,
    UP3, DN0, DN1, OP0, OP1, BK0, BK1, OM0, OM1, BM0, BM1, VP, BO, IG, SV, WV, VO, SMA, SMB,
    SPR, SRA, SRB, SFA, SFB, WMA, WMB, WPR, WRA, WRB, WFA, WFB,
) = range(154)

ORDER = (
    OWN, XGO, GVC1, GRB1, GRA1, GMA1, DYGO, GVC2, GPR1, GMB1, GRB2, GRA2, GVC3, GMA2, XFWD,
    GPR2, HOTS, GMB2, GRB3, GVC4, GRA3, GMA3, DYFWD, GPR3, DYALL, GMB3, GVC5, VROWS, LN0, GRB4,
    LN2, LN1, GRA4, LN3, GFB1, GMA4, GPR4, GFA1, GRB5, GMB4, GRA5, UP2, UP3, GMA5, GFB2, UP1,
    GPR5, SWGO, UP0, GMB5, GFA2, GF1, GF0, RFB1, RFA1, GFB3, QKV0, GFA3, QKV1, SWIN, RFB2, DH,
    RFA2, AT20, AT10, GFB4, AT00, GFA4, AT02, AT03, RFB3, AT30, AT12, RFA3, AT32, GFB5, AT33,
    GFA5, DN1, RFB4, DN0, GR1, RFA4, GR0, RRA1, RRB1, AT13, RFB5, SFB, AT22, AT23, RFA5, SFA,
    RRA2, POST1, RRB2, POST0, WFB, GP, SBGO, OP1, WFA, RRA3, GM0, OM1, GM1, RMA1, RRB3, RMB1,
    OP0, RRA4, BK1, SBIN, OM0, RPR1, RMA2, BK0, BM1, RRB4, RMB2, VP, RRA5, RVC1, BM0, RPR2,
    RMA3, SRA, BO, RRB5, SRB, RVC2, RMB3, RPR3, RMA4, RVC3, RMB4, RPR4, IG, RMA5, SMA, RVC4,
    WRA, RMB5, SMB, WRB, RVC5, SV, RPR5, SPR, WMA, WMB, WV, VO, WPR,
)
LANES = 128
HALF = LANES // 2
VEC_ROWS = 16
TURN = 32


def resident_fits(seq_size, dp_size, tok):
    return (
        D // dp_size == LANES
        and FF // dp_size // seq_size == LANES
        and HEADS // seq_size == 4
        and tok * seq_size <= TURN * TURN
        and tok % TILE == 0
    )


def rows_at(ref, index, count):
    return ref.at[pl.ds(pl.multiple_of(index * count, count), count)]


def columns_at(ref, index, count):
    return ref.at[:, pl.ds(pl.multiple_of(index * count, count), count)]


class Flat:
    def __init__(self, ref, count, stride=None, start=0):
        self.ref, self.count, self.start = ref, count, start
        self.stride = count if stride is None else stride

    @property
    def at(self):
        return self

    def __getitem__(self, index):
        first = pl.multiple_of(index * self.stride + self.start, self.count)
        return self.ref.at[pl.ds(first, self.count)]


class Stack:
    def __init__(self, ref, start, count):
        self.ref, self.start, self.count = ref, start, count

    @property
    def at(self):
        return self

    def __getitem__(self, index):
        return self.ref.at[index, pl.ds(self.start, self.count)]


def lanes_like(shape):
    return lax.broadcasted_iota(jnp.int32, shape, len(shape) - 1)


def head_part(values, start):
    tile = values[:, start // LANES * LANES : start // LANES * LANES + LANES]
    return tile if start % LANES == 0 else pltpu.roll(tile, HEAD_DIM, 1)


def spin(tile, cosine, sine):
    lane = lanes_like(tile.shape)
    partner = jnp.where(lane < ROT // 2, pltpu.roll(tile, LANES - ROT // 2, 1), pltpu.roll(tile, ROT // 2, 1))
    return tile * cosine + partner * sine


def attend_head(head, block, refs):
    q_ref, k_ref, v_ref, g_ref, kt_ref, vt_ref, s_ref, p_ref, ht_ref, dqt_ref, dk_ref, dv_ref = refs
    here = pl.ds(block * TILE, TILE)
    wide = pl.ds(head * LANES, LANES)
    dims = pl.ds(head * HEAD_DIM, HEAD_DIM)
    query = q_ref[here, wide]
    grad = g_ref[here, wide]
    span = block + 1
    top = jnp.full((1, TILE), 2 * NEG, F32)
    for index in range(span):
        tile = nt(k_ref[pl.ds(index * TILE, TILE), wide], query)
        if index == block:
            key = lax.broadcasted_iota(jnp.int32, (TILE, TILE), 0)
            place = lax.broadcasted_iota(jnp.int32, (TILE, TILE), 1)
            tile = jnp.where(key <= place, tile, NEG)
        s_ref[index] = tile
        top = jnp.maximum(top, jnp.max(tile, axis=0, keepdims=True))
    total = jnp.zeros((1, TILE), F32)
    for index in range(span):
        raised = jnp.exp(s_ref[index] - top)
        s_ref[index] = raised
        total = total + jnp.sum(raised, axis=0, keepdims=True)
    share = 1.0 / total
    delta = jnp.zeros((1, TILE), F32)
    heads = jnp.zeros((HEAD_DIM, TILE), F32)
    for index in range(span):
        there = pl.ds(index * TILE, TILE)
        weights = s_ref[index] * share
        s_ref[index] = weights
        weights_b = weights.astype(BF)
        d_weights = nt(v_ref[there, wide], grad)
        p_ref[index] = d_weights
        d_value = nn(weights_b, grad)
        dv_ref[head, there, :] = d_value if index == block else dv_ref[head, there, :] + d_value
        heads = heads + nn(vt_ref[dims, there], weights_b)
        delta = delta + jnp.sum(weights * d_weights, axis=0, keepdims=True)
    ht_ref[dims, here] = heads
    d_query = jnp.zeros((HEAD_DIM, TILE), F32)
    for index in range(span):
        there = pl.ds(index * TILE, TILE)
        d_scores = (s_ref[index] * (p_ref[index] - delta)).astype(BF)
        d_key = nn(d_scores, query)
        dk_ref[head, there, :] = d_key if index == block else dk_ref[head, there, :] + d_key
        d_query = d_query + nn(kt_ref[dims, there], d_scores)
    dqt_ref[dims, here] = d_query


class Refs(typing.NamedTuple):
    x_own: typing.Any
    dy_own: typing.Any
    w_mix_own: typing.Any
    w_proj_own: typing.Any
    w_rise_own: typing.Any
    w_fall_own: typing.Any
    gain1_own: typing.Any
    shift1_own: typing.Any
    gain2_own: typing.Any
    shift2_own: typing.Any
    b_proj_own: typing.Any
    b_fall_own: typing.Any
    b_mix_own: typing.Any
    b_rise_own: typing.Any
    seg_own: typing.Any
    pad_own: typing.Any
    turns: typing.Any
    block_out: typing.Any
    input_grad: typing.Any
    mix_fin: typing.Any
    proj_fin: typing.Any
    rise_fin: typing.Any
    fall_fin: typing.Any
    vec_result: typing.Any
    pad: typing.Any
    cos: typing.Any
    sin: typing.Any
    x: typing.Any
    dy: typing.Any
    hot: typing.Any
    segs: typing.Any
    w_mix: typing.Any
    w_proj_cols: typing.Any
    w_proj: typing.Any
    w_rise: typing.Any
    w_fall: typing.Any
    vec_all: typing.Any
    rows: typing.Any
    normed1: typing.Any
    normed2: typing.Any
    stat: typing.Any
    qk: typing.Any
    vg: typing.Any
    kt: typing.Any
    vt: typing.Any
    s: typing.Any
    p: typing.Any
    ht: typing.Any
    dqt: typing.Any
    dk: typing.Any
    dv: typing.Any
    attn: typing.Any
    d_mixed: typing.Any
    out_part: typing.Any
    back_part: typing.Any
    active: typing.Any
    d_up: typing.Any
    g_mix: typing.Any
    g_proj: typing.Any
    g_proj_cols: typing.Any
    g_rise: typing.Any
    g_fall: typing.Any
    c_mix: typing.Any
    c_proj: typing.Any
    c_rise: typing.Any
    c_fall: typing.Any
    out_cross: typing.Any
    out_came: typing.Any
    back_cross: typing.Any
    back_came: typing.Any
    sums: typing.Any
    vec_part: typing.Any
    vec_came: typing.Any
    vec_fin: typing.Any
    vec_out: typing.Any
    m_x: typing.Any
    m_dy: typing.Any
    m_hot: typing.Any
    m_vec: typing.Any
    m_mix: typing.Any
    m_proj: typing.Any
    m_rise: typing.Any
    m_fall: typing.Any
    m_swap: typing.Any
    m_own: typing.Any
    m_swap2: typing.Any
    m_rmix: typing.Any
    m_rproj: typing.Any
    m_rrise: typing.Any
    m_rfall: typing.Any
    m_out: typing.Any
    m_back: typing.Any
    m_vec2: typing.Any
    m_fmix: typing.Any
    m_fproj: typing.Any
    m_frise: typing.Any
    m_ffall: typing.Any
    m_fvec: typing.Any
    m_fin: typing.Any


def resident_kernel(seq_size, dp_size, *refs):
    r = Refs(*refs)
    place = Place(seq_size, dp_size)
    half = place.half
    tok = r.x_own.shape[0]
    length = r.x.shape[0]
    wide = r.w_proj.shape[0]
    mixed_wide = 3 * wide
    units = LANES
    each = dp_size // seq_size
    heads_n = wide // HEAD_DIM
    blocks = length // TILE

    place.greet_near()
    own = []

    def bring(src, dst):
        copy = pltpu.make_async_copy(src, dst, r.m_own.at[len(own)])
        copy.start()
        own.append(copy)

    bring(columns_at(r.w_mix_own, place.seq, mixed_wide), rows_at(r.w_mix, place.dp, LANES))
    bring(columns_at(r.w_proj_own, place.seq, wide), rows_at(r.w_proj_cols, place.dp, LANES))
    bring(r.x_own, rows_at(r.x, place.seq, tok))
    bring(r.dy_own, rows_at(r.dy, place.seq, tok))
    for index in range(dp_size):
        bring(
            columns_at(r.w_rise_own, index * seq_size + place.seq, units),
            rows_at(r.w_rise, place.dp, LANES).at[:, pl.ds(index * units, units)],
        )
    bring(rows_at(r.w_fall_own, place.seq, units), rows_at(r.w_fall, place.dp, units))
    bring(r.pad_own, r.pad)

    coarse_cos, coarse_sin, fine_cos, fine_sin = (
        r.turns.at[pl.ds(index * TURN, TURN)] for index in range(4)
    )

    @pl.loop(0, length // TURN)
    def _(step):
        here = pl.ds(pl.multiple_of(step * TURN, TURN), TURN)
        far_cos, far_sin = coarse_cos[pl.ds(step, 1), :], coarse_sin[pl.ds(step, 1), :]
        r.cos[here, :] = far_cos * fine_cos[...] - far_sin * fine_sin[...]
        r.sin[here, :] = far_sin * fine_cos[...] + far_cos * fine_sin[...]

    row = 0
    vectors = (r.gain1_own, r.shift1_own, r.gain2_own, r.shift2_own, r.b_proj_own, r.b_fall_own, r.b_mix_own, r.b_rise_own)
    for vector in vectors:
        count = vector.shape[0]
        r.vec_all[place.dp, row : row + count, :] = vector[...].astype(F32)
        row += count
    r.vec_all[place.dp, row:, :] = jnp.zeros((VEC_ROWS - row, LANES), F32)
    rows_at(r.segs, place.seq, 8)[...] = jnp.broadcast_to(r.seg_own[...], (8, tok)).astype(F32)

    def pair_of(ref, make):
        return [make(Flat(ref, HALF, LANES, start), index) for index, start in enumerate((0, HALF))]

    def gather_pair(ref, sems):
        return pair_of(ref, lambda part, index: RingGather(place, part, sems.at[index]))

    def reduce_pair(ref, came, sems):
        return pair_of(ref, lambda part, index: RingReduce(place, part, came.at[index], sems.at[index]))

    def final_pair(out_ref, sems, ref):
        return pair_of(
            ref,
            lambda part, index: SeqGather(
                place, Stack(out_ref, index * HALF, HALF), sems.at[index], part[place.dp]
            ),
        )

    gathers = [
        RingGather(place, r.vec_all, r.m_vec),
        *gather_pair(r.w_mix, r.m_mix),
        RingGather(place, Flat(r.w_proj_cols, LANES), r.m_proj),
        *gather_pair(r.w_rise, r.m_rise),
        *gather_pair(r.w_fall, r.m_fall),
    ]
    reduces = [
        RingReduce(place, r.vec_part, r.vec_came, r.m_vec2),
        *reduce_pair(r.g_mix, r.c_mix, r.m_rmix),
        RingReduce(place, Flat(r.g_proj_cols, LANES), r.c_proj, r.m_rproj),
        *reduce_pair(r.g_rise, r.c_rise, r.m_rrise),
        *reduce_pair(r.g_fall, r.c_fall, r.m_rfall),
    ]
    finals = [
        *final_pair(r.mix_fin, r.m_fmix, r.g_mix),
        SeqGather(place, r.proj_fin, r.m_fproj, rows_at(r.g_proj_cols, place.dp, LANES)),
        *final_pair(r.rise_fin, r.m_frise, r.g_rise),
        *final_pair(r.fall_fin, r.m_ffall, r.g_fall),
    ]
    f_vec = SeqGather(place, r.vec_fin, r.m_fvec)

    x_move = SeqGather(place, Flat(r.x, tok), r.m_x)
    dy_move = SeqGather(place, Flat(r.dy, tok), r.m_dy)
    seg_move = SeqGather(place, Flat(r.segs, 8), r.m_hot)
    out = SeqReduce(place, Flat(r.out_part, tok), r.out_cross, r.out_came, r.m_out)
    back = SeqReduce(place, Flat(r.back_part, tok), r.back_cross, r.back_came, r.m_back)

    leaving = []

    def leave(src, dst):
        copy = pltpu.make_async_copy(src, dst, r.m_fin.at[len(leaving)])
        copy.start()
        leaving.append(copy)

    pieces = {}

    def piece(name, *given):
        def note(run):
            pieces[name] = functools.partial(run, *given)
            return run

        return note

    def tile_rows(block):
        return pl.ds(pl.multiple_of(block * TILE, TILE), TILE)

    def gather(stream, step):
        gathers[stream].tick(step)

    def reduce(stream, step):
        reduces[stream].tick(step)

    for stream in range(len(gathers)):
        for step in range(1, half + 2):
            tick = stream * (half + 1) + step - 1
            piece(GVC1 + tick, stream, step)(gather)
            piece(RVC1 + tick, stream, step)(reduce)

    @piece(OWN)
    def _():
        for copy in own:
            copy.wait()

    @piece(XGO)
    def _():
        x_move.begin()
        seg_move.begin()

    piece(DYGO)(dy_move.begin)

    @piece(XFWD)
    def _():
        x_move.forward()
        seg_move.forward()

    piece(DYFWD)(dy_move.forward)

    @piece(HOTS)
    def _():
        for step in range(place.pairs):
            seg_move.across_arrived(step)
        kind = lax.broadcasted_iota(jnp.int32, (LANES, tok), 0) - HEAD_DIM
        for index in range(seq_size):
            segment = r.segs[index * 8 : index * 8 + 1, :].astype(jnp.int32)
            r.hot[index * tok : (index + 1) * tok, :] = jnp.where(segment == kind, 1.0, 0.0).T.astype(BF)

    @piece(DYALL)
    def _():
        for step in range(place.pairs):
            dy_move.across_arrived(step)

    @piece(VROWS)
    def _():
        for index in range(dp_size):
            at = slice(index * LANES, (index + 1) * LANES)
            for row in range(6):
                r.rows[row : row + 1, at] = r.vec_all[index, row : row + 1, :]
            r.rows[6:7, at] = r.vec_all[index, pl.ds(9 + place.seq, 1), :]
        for index in range(each):
            for row in range(3):
                start = (index * 3 + row) * LANES
                r.rows[7:8, start : start + LANES] = r.vec_all[place.seq * each + index, 6 + row : 7 + row, :]

    chunk = 64

    def normalize(block):
        @pl.loop(0, tok // chunk)
        def _(step):
            here = pl.ds(pl.multiple_of(block * tok + step * chunk, chunk), chunk)
            values = r.x[here, :].astype(F32)
            mean = jnp.sum(values, axis=-1, keepdims=True) * (1.0 / D)
            center = values - mean
            rstd = lax.rsqrt(jnp.sum(center * center, axis=-1, keepdims=True) * (1.0 / D) + EPS)
            n = center * rstd
            r.normed1[here, :] = (n * r.rows[0:1, :] + r.rows[1:2, :]).astype(BF)
            r.normed2[here, :] = (n * r.rows[2:3, :] + r.rows[3:4, :]).astype(BF)
            lane = lanes_like((chunk, LANES))
            r.stat[here, :] = jnp.where(lane < HEAD_DIM, mean, rstd)

    def unit_rows(here):
        stat = r.stat[here, :]
        return (r.x[here, :].astype(F32) - stat[:, 0:1]) * stat[:, HEAD_DIM : HEAD_DIM + 1]

    @piece(LN0)
    def _():
        normalize(place.seq)

    @piece(LN1)
    def _():
        x_move.across_arrived(0)
        normalize(place.sibling)

    @piece(LN2)
    def _():
        normalize(place.pair_peer(1))

    @piece(LN3)
    def _():
        x_move.across_arrived(1)
        normalize(place.across_source(1))

    def swap(step):
        peer = place.seq_peer(step)
        src, dst = rows_at(r.w_proj_cols, peer, wide), columns_at(r.w_proj, place.seq, wide)
        return send(src, dst, r.m_swap, step, {"seq": peer})

    def swap_arrival(step):
        source = place.seq_peer(-step)
        src, dst = rows_at(r.w_proj_cols, source, wide), columns_at(r.w_proj, source, wide)
        return send(src, dst, r.m_swap, step, {"seq": place.seq_peer(step)})

    @piece(SWGO)
    def _():
        for step in range(1, seq_size):
            swap(step).start()
        columns_at(r.w_proj, place.seq, wide)[...] = rows_at(r.w_proj_cols, place.seq, wide)[...]

    @piece(SWIN)
    def _():
        for step in range(1, seq_size):
            swap_arrival(step).wait_recv()

    def mix_columns(first, last):
        @pl.loop(first, last)
        def _(block):
            here = tile_rows(block)
            mixed = nn(r.normed1[here, :], r.w_mix[...]) + r.rows[7:8, 0:mixed_wide]
            cosine, sine = r.cos[here, :], r.sin[here, :]
            lane = lanes_like((TILE, LANES))
            hot = r.hot[here, :].astype(F32)
            cold = jnp.where((lane >= HEAD_DIM) & (lane < HEAD_DIM + 4), (1.0 - hot) * NEG, 0.0)
            for head in range(heads_n):
                start = head * 3 * HEAD_DIM
                query = spin(head_part(mixed, start), cosine, sine) * HEAD_DIM**-0.5
                key = spin(head_part(mixed, start + HEAD_DIM), cosine, sine)
                value = head_part(mixed, start + 2 * HEAD_DIM)
                at = pl.ds(head * LANES, LANES)
                at_more = pl.ds((heads_n + head) * LANES, LANES)
                dims = pl.ds(head * HEAD_DIM, HEAD_DIM)
                r.qk[here, at] = jnp.where(lane < HEAD_DIM, query, hot).astype(BF)
                r.qk[here, at_more] = jnp.where(lane < HEAD_DIM, key, cold).astype(BF)
                r.vg[here, at] = jnp.where(lane < HEAD_DIM, value, 0.0).astype(BF)
                r.kt[dims, here] = key.T[:HEAD_DIM, :].astype(BF)
                r.vt[dims, here] = value.T[:HEAD_DIM, :].astype(BF)

    middle = blocks // 2
    piece(QKV0, 0, middle)(mix_columns)
    piece(QKV1, middle, blocks)(mix_columns)
    @piece(DH)
    def _():
        @pl.loop(0, blocks)
        def _(block):
            here = tile_rows(block)
            place_in = lax.broadcasted_iota(jnp.int32, (TILE, wide), 0) + block * TILE
            d_heads = jnp.where(place_in < length - r.pad[0], nt(r.dy[here, :], r.w_proj[...]), 0.0)
            for head in range(heads_n):
                at_more = pl.ds((heads_n + head) * LANES, LANES)
                r.vg[here, at_more] = head_part(d_heads, head * HEAD_DIM).astype(BF)

    second = heads_n * LANES
    head_refs = (
        r.qk.at[:, pl.ds(0, second)],
        r.qk.at[:, pl.ds(second, second)],
        r.vg.at[:, pl.ds(0, second)],
        r.vg.at[:, pl.ds(second, second)],
        r.kt,
        r.vt,
        r.s,
        r.p,
        r.ht,
        r.dqt,
        r.dk,
        r.dv,
    )

    def attend_blocks(head, first, last):
        for block in range(first, last):
            if block == 0:
                attend_head(head, block, head_refs)
            elif block == 1:
                attend_head(head, block, head_refs)
            elif block == 2:
                attend_head(head, block, head_refs)
            else:
                attend_head(head, block, head_refs)

    for head in range(heads_n):
        first = AT00 + head * (middle + 1)
        piece(first, head, 0, middle)(attend_blocks)
        for block in range(middle, blocks):
            piece(first + block - middle + 1, head, block, block + 1)(attend_blocks)

    def heads_back(first, last):
        @pl.loop(first, last)
        def _(block):
            here = tile_rows(block)
            place_in = lax.broadcasted_iota(jnp.int32, (TILE, wide), 0) + block * TILE
            r.attn[here, :] = jnp.where(place_in < length - r.pad[0], r.ht[:, here].T, 0.0).astype(BF)
            d_query = r.dqt[:, here].T * HEAD_DIM**-0.5
            cosine, sine = r.cos[here, :], -r.sin[here, :]
            lane = lanes_like((TILE, LANES))
            parts = []
            for head in range(heads_n):
                parts.append(spin(head_part(d_query, head * HEAD_DIM), cosine, sine))
                parts.append(spin(r.dk[head, here, :], cosine, sine))
                parts.append(r.dv[head, here, :])
            for index in range(len(parts) // 2):
                tile = jnp.where(lane < HEAD_DIM, parts[2 * index], pltpu.roll(parts[2 * index + 1], HEAD_DIM, 1))
                at = slice(index * LANES, (index + 1) * LANES)
                tile = tile.astype(BF)
                r.d_mixed[here, at] = tile
                r.sums[6:7, at] += jnp.sum(tile.astype(F32), axis=0, keepdims=True)

    piece(POST0, 0, middle)(heads_back)
    piece(POST1, middle, blocks)(heads_back)
    big = 512

    def weight_grad(out_ref, left, right, index):
        at = pl.ds(index * big, big)
        out_ref[at, :] = tn(left[:, at], right[...]).astype(BF)

    for index in range(D // big):
        piece(GM0 + index, r.g_mix, r.normed1, r.d_mixed, index)(weight_grad)
        piece(GR0 + index, r.g_rise, r.normed2, r.d_up, index)(weight_grad)
        piece(GF0 + index, r.g_fall, r.active, r.dy, index)(weight_grad)

    @piece(GP)
    def _():
        r.g_proj[...] = tn(r.attn[...], r.dy[...]).astype(BF)

    def swap_back(step):
        peer = place.seq_peer(step)
        src, dst = columns_at(r.g_proj, peer, wide), rows_at(r.g_proj_cols, place.seq, wide)
        return send(src, dst, r.m_swap2, step, {"seq": peer})

    def swap_back_arrival(step):
        source = place.seq_peer(-step)
        src, dst = columns_at(r.g_proj, source, wide), rows_at(r.g_proj_cols, source, wide)
        return send(src, dst, r.m_swap2, step, {"seq": place.seq_peer(step)})

    @piece(SBGO)
    def _():
        for step in range(1, seq_size):
            swap_back(step).start()
        rows_at(r.g_proj_cols, place.seq, wide)[...] = columns_at(r.g_proj, place.seq, wide)[...]

    @piece(SBIN)
    def _():
        for step in range(1, seq_size):
            swap_back_arrival(step).wait_recv()

    def upward(block):
        here = tile_rows(block)
        up = nn(r.normed2[here, :], r.w_rise[...]) + r.rows[6:7, :]
        share = 0.5 + 0.5 * lax.erf(up * 0.5**0.5)
        r.active[here, :] = (up * share).astype(BF)
        bell = jnp.exp(-0.5 * up * up) * (2 * np.pi) ** -0.5
        r.d_up[here, :] = (share + up * bell).astype(BF)

    def downward(first, last):
        @pl.loop(first, last)
        def _(block):
            here = tile_rows(block)
            d_up = (r.d_up[here, :].astype(F32) * nt(r.dy[here, :], r.w_fall[...])).astype(BF)
            r.d_up[here, :] = d_up
            r.sums[5:6, :] += jnp.sum(d_up.astype(F32), axis=0, keepdims=True)

    for block in range(blocks):
        piece(UP0 + block, block)(upward)
    piece(DN0, 0, middle)(downward)
    piece(DN1, middle, blocks)(downward)

    def out_rows(step):
        first = ((place.pair + step) % place.pairs) * (2 * tok // TILE)
        @pl.loop(0, 2 * tok // TILE)
        def _(block):
            here = tile_rows(first + block)
            part = nn(r.attn[here, :], r.w_proj[...]) + nn(r.active[here, :], r.w_fall[...])
            r.out_part[here, :] = part.astype(BF)

        out.over_start(step)

    def back_rows(step):
        first = ((place.pair + step) % place.pairs) * (2 * tok // TILE)
        @pl.loop(0, 2 * tok // TILE)
        def _(block):
            here = tile_rows(first + block)
            d_one = nt(r.d_mixed[here, :], r.w_mix[...])
            d_two = nt(r.d_up[here, :], r.w_rise[...])
            r.back_part[here, :] = (r.rows[0:1, :] * d_one + r.rows[2:3, :] * d_two).astype(BF)
            n = unit_rows(here)
            r.sums[0:1, :] += jnp.sum(d_one * n, axis=0, keepdims=True)
            r.sums[1:2, :] += jnp.sum(d_one, axis=0, keepdims=True)
            r.sums[2:3, :] += jnp.sum(d_two * n, axis=0, keepdims=True)
            r.sums[3:4, :] += jnp.sum(d_two, axis=0, keepdims=True)
            r.sums[4:5, :] += jnp.sum(r.dy[here, :].astype(F32), axis=0, keepdims=True)

        back.over_start(step)

    for step in range(2):
        piece(OP0 + step, step)(out_rows)
        piece(BK0 + step, step)(back_rows)
        piece(OM0 + step, step)(out.over_add)
        piece(BM0 + step, step)(back.over_add)

    @piece(VP)
    def _():
        for index in range(dp_size):
            at = slice(index * LANES, (index + 1) * LANES)
            r.vec_part[index, 0:6, :] = r.sums[0:6, at]
            for row in range(mixed_wide // LANES):
                r.vec_part[index, 6 + row : 7 + row, :] = r.sums[6:7, row * LANES : (row + 1) * LANES]

    def settle(move):
        move.begin()
        leave(move.own, move.full.at[place.seq])

    for index, move in enumerate(finals):
        piece(SMA + index, move)(settle)
        piece(WMA + index)(move.forward)

    mine = pl.ds(pl.multiple_of(place.seq * tok, tok), tok)

    @piece(BO)
    def _():
        total = out.total()
        block_out = total + r.x[mine, :].astype(F32) + (r.rows[4:5, :] + r.rows[5:6, :])
        r.out_cross[0] = block_out.astype(BF)
        leave(r.out_cross.at[0], r.block_out)

    @piece(IG)
    def _():
        scaled = back.total()
        n = unit_rows(mine)
        rstd = r.stat[mine, HEAD_DIM : HEAD_DIM + 1]
        back_mean = jnp.sum(scaled, axis=-1, keepdims=True) * (1.0 / D)
        back_n = jnp.sum(scaled * n, axis=-1, keepdims=True) * (1.0 / D)
        input_grad = r.dy[mine, :].astype(F32) + rstd * (scaled - back_mean - n * back_n)
        r.back_cross[0] = input_grad.astype(BF)
        leave(r.back_cross.at[0], r.input_grad)

    @piece(SV)
    def _():
        r.vec_fin[place.seq] = r.vec_part[place.dp]
        f_vec.begin()

    piece(WV)(f_vec.forward)

    @piece(VO)
    def _():
        f_vec.finish()
        norm = r.vec_fin[0, 0:4, :]
        for index in range(1, seq_size):
            norm = norm + r.vec_fin[index, 0:4, :]
        r.vec_out[0:4, :] = norm
        r.vec_out[4:5, :] = r.vec_fin[0, 4:5, :]
        source = r.vec_fin[place.dp // each]
        pick = place.dp % each
        part = source[6:9, :]
        for index in range(1, each):
            part = jnp.where(pick == index, source[6 + 3 * index : 9 + 3 * index, :], part)
        r.vec_out[5:8, :] = part
        for index in range(seq_size):
            r.vec_out[8 + index : 9 + index, :] = r.vec_fin[index, 5:6, :]
        leave(r.vec_out, r.vec_result)

    place.met_near()
    r.sums[...] = jnp.zeros(r.sums.shape, F32)
    r.vec_part[...] = jnp.zeros(r.vec_part.shape, F32)
    assert sorted(ORDER) == sorted(pieces)
    for name in ORDER:
        pieces[name]()
    for move in finals:
        move.finish()
    for copy in leaving:
        copy.wait()
    for move in (*gathers, *reduces, out, back):
        move.finish()
    for move in (x_move, seg_move, dy_move):
        move.sent()
    for step in range(1, seq_size):
        swap(step).wait_send()
        swap_back(step).wait_send()


def resident_call(seq_size, dp_size, *args):
    tok = args[0].shape[0]
    length = tok * seq_size
    half, pairs = dp_size // 2, seq_size // 2
    wide = HEADS // seq_size * HEAD_DIM
    units_all = dp_size * LANES
    heads_n = wide // HEAD_DIM

    def half_vmem(*shape):
        return pltpu.VMEM(shape, BF)

    def full_vmem(*shape):
        return pltpu.VMEM(shape, F32)

    def ring(columns):
        return half_vmem(2, 2, half, HALF, columns)

    def pair_of_sems(count):
        return pltpu.SemaphoreType.DMA((2, 2, count))

    any_spec = pl.BlockSpec(memory_space=pl.ANY)
    vmem = pl.BlockSpec(memory_space=pltpu.VMEM)
    scratch = [
        pltpu.SMEM((1,), jnp.int32),
        full_vmem(length, LANES),
        full_vmem(length, LANES),
        half_vmem(length, D),
        half_vmem(length, D),
        half_vmem(length, LANES),
        full_vmem(seq_size * 8, tok),
        half_vmem(D, 3 * wide),
        half_vmem(D, wide),
        half_vmem(wide, D),
        half_vmem(D, units_all),
        half_vmem(units_all, D),
        full_vmem(dp_size, VEC_ROWS, LANES),
        full_vmem(8, D),
        half_vmem(length, D),
        half_vmem(length, D),
        full_vmem(length, LANES),
        half_vmem(length, units_all),
        half_vmem(length, units_all),
        half_vmem(wide, length),
        half_vmem(wide, length),
        full_vmem(length // TILE, TILE, TILE),
        full_vmem(length // TILE, TILE, TILE),
        full_vmem(wide, length),
        full_vmem(wide, length),
        full_vmem(heads_n, length, LANES),
        full_vmem(heads_n, length, LANES),
        half_vmem(length, wide),
        half_vmem(length, 3 * wide),
        half_vmem(length, D),
        half_vmem(length, D),
        half_vmem(length, units_all),
        half_vmem(length, units_all),
        half_vmem(D, 3 * wide),
        half_vmem(wide, D),
        half_vmem(D, wide),
        half_vmem(D, units_all),
        half_vmem(units_all, D),
        ring(3 * wide),
        half_vmem(2, half, LANES, wide),
        ring(units_all),
        ring(D),
        half_vmem(pairs, tok, D),
        half_vmem(pairs, tok, D),
        half_vmem(pairs, tok, D),
        half_vmem(pairs, tok, D),
        full_vmem(8, D),
        full_vmem(dp_size, VEC_ROWS, LANES),
        full_vmem(2, half, VEC_ROWS, LANES),
        full_vmem(seq_size, VEC_ROWS, LANES),
        full_vmem(16, LANES),
    ]
    scratch += [sems_of(2 * pairs)] * 3 + [sems_of(2 * half)]
    scratch += [pair_of_sems(2 * half), sems_of(2 * half), pair_of_sems(2 * half), pair_of_sems(2 * half)]
    scratch += [sems_of(seq_size), pltpu.SemaphoreType.DMA((dp_size + 6,)), sems_of(seq_size)]
    scratch += [pair_of_sems(2 * half), sems_of(2 * half), pair_of_sems(2 * half), pair_of_sems(2 * half)]
    scratch += [sems_of(2 * pairs)] * 2 + [sems_of(2 * half)]
    scratch += [pair_of_sems(2 * pairs), sems_of(2 * pairs), pair_of_sems(2 * pairs), pair_of_sems(2 * pairs)]
    scratch += [sems_of(2 * pairs)]
    scratch += [pltpu.SemaphoreType.DMA((12,))]
    return pl.pallas_call(
        functools.partial(resident_kernel, seq_size, dp_size),
        out_shape=(
            jax.ShapeDtypeStruct((tok, D), BF),
            jax.ShapeDtypeStruct((tok, D), BF),
            jax.ShapeDtypeStruct((seq_size, LANES, 3 * wide), BF),
            jax.ShapeDtypeStruct((seq_size, LANES, wide), BF),
            jax.ShapeDtypeStruct((seq_size, LANES, units_all), BF),
            jax.ShapeDtypeStruct((seq_size, LANES, D), BF),
            jax.ShapeDtypeStruct((16, LANES), F32),
        ),
        in_specs=[any_spec] * 6 + [vmem] * 9 + [any_spec, vmem],
        out_specs=[any_spec] * 7,
        scratch_shapes=scratch,
        compiler_params=pltpu.CompilerParams(
            collective_id=2, has_side_effects=True, vmem_limit_bytes=RESIDENT_VMEM
        ),
    )(*args)


RESIDENT_VMEM = 63 * 2**20


def finish_kernel(seq_size, dp_size, *refs):
    (block, grad, mix, proj, rise, fall, vec), refs = refs[:7], refs[7:]
    (block_out, grad_out, mix_out, proj_out, rise_out, fall_out), refs = refs[:6], refs[6:]
    vec_outs, refs = refs[:8], refs[8:]
    (block_in, grad_in, mix_in, proj_in, rise_in, fall_in, vec_in, mix_f, proj_f, rise_f, fall_f), refs = refs[:11], refs[11:]
    vec_fs, (in_sems, out_sems) = refs[:8], refs[8:]
    parts = [(fall.at[group], fall_in.at[group]) for group in range(seq_size)]
    parts += [(rise, rise_in), (mix, mix_in), (proj, proj_in), (block, block_in), (grad, grad_in), (vec, vec_in)]
    coming = []
    for src, dst in parts:
        copy = pltpu.make_async_copy(src, dst, in_sems.at[len(coming)])
        copy.start()
        coming.append(copy)
    *fall_copies, rise_copy, mix_copy, proj_copy, block_copy, grad_copy, vec_copy = coming
    leaving = []

    def leave(src, dst):
        copy = pltpu.make_async_copy(src, dst, out_sems.at[len(leaving)])
        copy.start()
        leaving.append(copy)

    for group in range(seq_size):
        fall_copies[group].wait()
        at = pl.ds(group * LANES, LANES)
        fall_f[at, :] = fall_in[group].astype(F32)
        leave(fall_f.at[at], fall_out.at[at])
    few = 32
    rise_copy.wait()
    for start in range(0, LANES, few):
        at = pl.ds(start, few)
        for group in range(seq_size):
            for index in range(dp_size):
                column = (index * seq_size + group) * LANES
                rise_f[at, column : column + LANES] = rise_in[group, at, index * LANES : (index + 1) * LANES].astype(F32)
        leave(rise_f.at[at], rise_out.at[at])
    mix_copy.wait()
    proj_copy.wait()
    for start in range(0, LANES, 2 * few):
        at = pl.ds(start, 2 * few)
        for held, full, out in ((mix_in, mix_f, mix_out), (proj_in, proj_f, proj_out)):
            columns = held.shape[2]
            for group in range(seq_size):
                full[at, group * columns : (group + 1) * columns] = held[group, at, :].astype(F32)
            leave(full.at[at], out.at[at])
    block_copy.wait()
    leave(block_in, block_out)
    grad_copy.wait()
    leave(grad_in, grad_out)
    vec_copy.wait()
    for held, out, row in zip(vec_fs, vec_outs, (0, 1, 2, 3, 4, 4, 5, 8), strict=True):
        for start in range(0, out.shape[0], LANES):
            held[start : start + LANES] = vec_in[row + start // LANES]
        leave(held, out)
    for copy in leaving:
        copy.wait()


def finish_call(seq_size, dp_size, block, grad, mix, proj, rise, fall, vec):
    tok = block.shape[0]
    vec_sizes = (LANES,) * 6 + (3 * LANES, seq_size * LANES)
    full_sizes = ((LANES, 3 * D), (LANES, D), (LANES, FF), (seq_size * LANES, D))
    any_spec = pl.BlockSpec(memory_space=pl.ANY)
    return pl.pallas_call(
        functools.partial(finish_kernel, seq_size, dp_size),
        out_shape=(jax.ShapeDtypeStruct((tok, D), BF),) * 2
        + tuple(jax.ShapeDtypeStruct(size, F32) for size in full_sizes)
        + tuple(jax.ShapeDtypeStruct((size,), F32) for size in vec_sizes),
        in_specs=[any_spec] * 7,
        out_specs=[any_spec] * 14,
        scratch_shapes=[pltpu.VMEM(array.shape, array.dtype) for array in (block, grad, mix, proj, rise, fall, vec)]
        + [pltpu.VMEM(size, F32) for size in full_sizes]
        + [pltpu.VMEM((size,), F32) for size in vec_sizes]
        + [pltpu.SemaphoreType.DMA((seq_size + 6,)), pltpu.SemaphoreType.DMA((24,))],
        compiler_params=pltpu.CompilerParams(vmem_limit_bytes=RESIDENT_VMEM),
    )(block, grad, mix, proj, rise, fall, vec)


def resident_tables():
    half = ROT // 2
    frequency = BASE ** (-np.arange(0, ROT, 2).astype(np.float32) / np.float32(ROT))
    lanes = np.zeros((LANES,), np.float64)
    lanes[:half] = lanes[half:ROT] = frequency.astype(np.float32)
    sign = np.where(np.arange(LANES) < half, -1.0, 1.0)
    steps = np.arange(TURN, dtype=np.float64)[:, None]
    tables = [f for scale in (TURN, 1) for f in (np.cos(steps * scale * lanes), sign * np.sin(steps * scale * lanes))]
    return jnp.asarray(np.concatenate(tables).astype(np.float32))


def resident_shards(
    tokens,
    cotangent,
    norm1_gain,
    norm1_bias,
    norm2_gain,
    norm2_bias,
    qkv_weight,
    qkv_bias,
    out_weight,
    out_bias,
    up_weight,
    up_bias,
    down_weight,
    down_bias,
    segment_ids,
    pad_length,
):
    seq_size, dp_size = lax.axis_size("seq"), lax.axis_size("dp")
    tok = tokens.shape[1]
    vectors = (norm1_gain, norm1_bias, norm2_gain, norm2_bias, out_bias, down_bias, qkv_bias, up_bias)
    parts = resident_call(
        seq_size,
        dp_size,
        tokens[0],
        cotangent[0],
        qkv_weight,
        out_weight,
        up_weight,
        down_weight,
        *(vector.reshape(-1, LANES) for vector in vectors),
        segment_ids,
        pad_length,
        resident_tables(),
    )
    done = finish_call(seq_size, dp_size, *parts)
    block_out, input_grad, g_mix, g_proj, g_rise, g_fall = done[:6]
    norm1_g, norm1_b, norm2_g, norm2_b, out_b, down_b, b_mix, b_rise = done[6:]
    return (
        block_out[None],
        input_grad[None],
        norm1_g,
        norm1_b,
        norm2_g,
        norm2_b,
        g_mix,
        b_mix,
        g_proj,
        out_b,
        g_rise,
        b_rise,
        g_fall,
        down_b,
    )


def streamed_shards(
    tokens,
    cotangent,
    norm1_gain,
    norm1_bias,
    norm2_gain,
    norm2_bias,
    qkv_weight,
    qkv_bias,
    out_weight,
    out_bias,
    up_weight,
    up_bias,
    down_weight,
    down_bias,
    segment_ids,
    pad_length,
):
    seq_size, dp_size = lax.axis_size("seq"), lax.axis_size("dp")
    seq = lax.axis_index("seq")
    dp = lax.axis_index("dp")
    tok = tokens.shape[1]
    length = tok * seq_size
    heads_n = HEADS // seq_size
    rows = D // dp_size
    wide = heads_n * HEAD_DIM
    units = FF // dp_size // seq_size

    mix = qkv_weight.reshape(rows, seq_size, heads_n, 3, HEAD_DIM)
    mix = lax.dynamic_index_in_dim(mix, seq, 1, keepdims=False)
    mix = mix.transpose(0, 2, 1, 3).reshape(rows, 3 * wide)
    proj = lax.dynamic_slice_in_dim(out_weight, seq * wide, wide, 1)
    rise = up_weight.reshape(rows, dp_size, seq_size, units)
    rise = lax.dynamic_index_in_dim(rise, seq, 2, keepdims=False).reshape(rows, dp_size * units)
    fall = lax.dynamic_slice_in_dim(down_weight, seq * units, units, 0)
    vec = jnp.concatenate(
        [norm1_gain, norm1_bias, norm2_gain, norm2_bias, out_bias, down_bias, qkv_bias, up_bias]
    )
    vec_len = vec.shape[0]
    vec = jnp.pad(vec, (0, 2048 - vec_len)).reshape(16, 128)
    seg = jnp.broadcast_to(segment_ids, (8, tok))
    x_all, dy_all, w_mix, _, w_rise, w_fall, vec_all, seg_all, w_proj = gather_all(
        seq_size, dp_size, tokens[0], cotangent[0], mix, proj, rise, fall, vec, seg
    )
    x = x_all.reshape(length, D).astype(F32)
    dy = dy_all.reshape(length, D)
    w_mix = w_mix.reshape(D, 3 * wide)
    w_rise = w_rise.reshape(D, dp_size * units)
    w_fall = w_fall.reshape(dp_size * units, D)
    w_proj = w_proj.reshape(seq_size, wide, wide).transpose(1, 0, 2).reshape(wide, D)
    segments = seg_all[:, 0, :].reshape(length)
    vec_all = vec_all.reshape(dp_size, 2048)[:, :vec_len].astype(F32)
    g1, s1, g2, s2, b_proj, b_fall = (
        vec_all[:, i * rows : (i + 1) * rows].reshape(D) for i in range(6)
    )
    b_mix = vec_all[:, 6 * rows : 9 * rows].reshape(seq_size, heads_n, 3, HEAD_DIM)
    b_mix = lax.dynamic_index_in_dim(b_mix, seq, 0, keepdims=False)
    b_mix = b_mix.transpose(1, 0, 2).reshape(3 * wide)
    b_rise = vec_all[:, 9 * rows :].reshape(dp_size, seq_size, units)
    b_rise = lax.dynamic_index_in_dim(b_rise, seq, 1, keepdims=False).reshape(dp_size * units)

    center = x - jnp.mean(x, axis=-1, keepdims=True)
    rstd = lax.rsqrt(jnp.mean(center * center, axis=-1, keepdims=True) + EPS)
    n = center * rstd
    normed1 = (n * g1 + s1).astype(BF)
    normed2 = (n * g2 + s2).astype(BF)
    valid = (jnp.arange(length, dtype=jnp.int32) < length - pad_length[0]).astype(F32)[:, None]
    cosine, sine = (jnp.asarray(t) for t in angle_tables(length))

    mixed = dot(normed1, w_mix) + b_mix
    mixed = mixed.reshape(length, 3, heads_n, HEAD_DIM).transpose(1, 2, 0, 3)
    queries = turn(mixed[0], cosine, sine, 1.0).astype(BF)
    keys = turn(mixed[1], cosine, sine, 1.0).astype(BF)
    values = mixed[2].astype(BF)
    d_heads = (dot_nt(dy, w_proj) * valid).astype(BF)
    d_heads = d_heads.reshape(length, heads_n, HEAD_DIM).transpose(1, 0, 2)
    heads, d_q, d_k, d_v = attention(queries, keys, values, d_heads, segments)
    attn_rows = (heads.transpose(1, 0, 2).reshape(length, wide).astype(F32) * valid).astype(BF)
    d_mixed = jnp.stack(
        [
            turn(d_q.astype(F32), cosine, sine, -1.0).astype(BF),
            turn(d_k.astype(F32), cosine, sine, -1.0).astype(BF),
            d_v,
        ]
    )
    d_mixed = d_mixed.transpose(2, 0, 1, 3).reshape(length, 3 * wide)

    upward = dot(normed2, w_rise) + b_rise
    active = jax.nn.gelu(upward, approximate=False).astype(BF)
    slope = 0.5 * (1 + lax.erf(upward * (0.5**0.5))) + upward * jnp.exp(
        -0.5 * upward * upward
    ) * ((2 * np.pi) ** -0.5)
    d_up = (slope * dot_nt(dy, w_fall)).astype(BF)
    out_part = (dot(attn_rows, w_proj) + dot(active, w_fall)).astype(BF)
    d_n1 = dot_nt(d_mixed, w_mix)
    d_n2 = dot_nt(d_up, w_rise)
    back_part = (g1 * d_n1 + g2 * d_n2).astype(BF)

    g_mix = dot_t(normed1, d_mixed).astype(BF).reshape(dp_size, rows, 3 * wide)
    g_proj = dot_t(attn_rows, dy).astype(BF).reshape(dp_size // seq_size, rows, seq_size, wide)
    g_proj = g_proj.transpose(2, 0, 1, 3)
    g_rise = dot_t(normed2, d_up).astype(BF).reshape(dp_size, rows, dp_size * units)
    g_fall = dot_t(active, dy).astype(BF).reshape(dp_size, units, D)
    dyf = dy.astype(F32)
    vec_part = jnp.concatenate(
        [
            t.reshape(dp_size, -1)
            for t in (
                jnp.sum(d_n1 * n, axis=0),
                jnp.sum(d_n1, axis=0),
                jnp.sum(d_n2 * n, axis=0),
                jnp.sum(d_n2, axis=0),
                jnp.sum(dyf, axis=0),
                jnp.sum(d_up.astype(F32), axis=0),
            )
        ]
        + [jnp.broadcast_to(jnp.sum(d_mixed.astype(F32), axis=0)[None], (dp_size, 3 * wide))],
        axis=1,
    )
    part_len = vec_part.shape[1]
    vec_part = jnp.pad(vec_part, ((0, 0), (0, 2048 - part_len))).reshape(dp_size, 16, 128)
    out_sum, back_sum, f_mix, f_proj, f_rise, f_fall, f_vec = reduce_all(
        seq_size,
        dp_size,
        out_part.reshape(seq_size, tok, D),
        back_part.reshape(seq_size, tok, D),
        g_mix,
        g_proj,
        g_rise,
        g_fall,
        vec_part,
    )
    own_x = tokens[0].astype(F32)
    block_output = (own_x + out_sum + b_proj + b_fall).astype(BF)
    own_center = own_x - jnp.mean(own_x, axis=-1, keepdims=True)
    own_rstd = lax.rsqrt(jnp.mean(own_center * own_center, axis=-1, keepdims=True) + EPS)
    own_n = own_center * own_rstd
    back = own_rstd * (
        back_sum
        - jnp.mean(back_sum, axis=-1, keepdims=True)
        - own_n * jnp.mean(back_sum * own_n, axis=-1, keepdims=True)
    )
    input_grad = (cotangent[0].astype(F32) + back).astype(BF)
    f_mix = f_mix.reshape(seq_size, rows, 3, heads_n, HEAD_DIM)
    f_mix = f_mix.transpose(1, 0, 3, 2, 4).reshape(rows, 3 * D).astype(F32)
    f_proj = f_proj.transpose(1, 0, 2).reshape(rows, D).astype(F32)
    f_rise = f_rise.reshape(seq_size, rows, dp_size, units)
    f_rise = f_rise.transpose(1, 2, 0, 3).reshape(rows, FF).astype(F32)
    f_fall = f_fall.reshape(seq_size * units, D).astype(F32)
    f_vec = f_vec.reshape(seq_size, 2048)[:, :part_len]
    norm_sums = jnp.sum(f_vec[:, : 4 * rows], axis=0)
    column = f_vec[0, 4 * rows : 5 * rows]
    f_b_rise = f_vec[:, 5 * rows : 5 * rows + units].reshape(seq_size * units)
    f_b_mix = f_vec[:, 5 * rows + units :].reshape(seq_size, 3, heads_n, HEAD_DIM)
    f_b_mix = f_b_mix.transpose(0, 2, 1, 3).reshape(dp_size, 3 * rows)
    f_b_mix = lax.dynamic_index_in_dim(f_b_mix, dp, 0, keepdims=False)
    return (
        block_output[None],
        input_grad[None],
        norm_sums[:rows],
        norm_sums[rows : 2 * rows],
        norm_sums[2 * rows : 3 * rows],
        norm_sums[3 * rows :],
        f_mix,
        f_b_mix,
        f_proj,
        column,
        f_rise,
        f_b_rise,
        f_fall,
        column,
    )


def shards(*args):
    seq_size, dp_size = lax.axis_size("seq"), lax.axis_size("dp")
    if resident_fits(seq_size, dp_size, args[0].shape[1]):
        return resident_shards(*args)
    return streamed_shards(*args)


def solution(mesh):
    rows = P("dp", "seq", None)
    weight = P("dp", None)
    vector = P("dp")
    return jax.shard_map(
        shards,
        mesh=mesh,
        in_specs=(rows, rows)
        + (vector,) * 4
        + (weight, vector) * 4
        + (P("dp", "seq"), vector),
        out_specs=(rows, rows) + (vector,) * 4 + (weight, vector) * 4,
        check_vma=False,
    )
```

```python
import functools
import typing

import jax
import jax.numpy as jnp
import numpy as np
from jax import lax
from jax.experimental import pallas as pl
from jax.experimental.pallas import tpu as pltpu
from jax.sharding import PartitionSpec as P

D = 1024
HEADS = 16
HEAD_DIM = 64
ROT = 16
FF = 4096
EPS = 1e-05
BASE = 10000.0
NEG = -1e30
MESH = pl.DeviceIdType.MESH
BF = jnp.bfloat16
F32 = jnp.float32


def ring_pos(dev, size):
    return (dev // 2) * (1 - dev % 2) + (size - 1 - dev // 2) * (dev % 2)


def ring_dev(pos, size):
    high = pos // (size // 2)
    return (1 - high) * 2 * pos + high * (2 * (size - 1 - pos) + 1)


class Place:
    def __init__(self, seq_size, dp_size):
        self.seq_size, self.dp_size = seq_size, dp_size
        self.seq = lax.axis_index("seq")
        self.dp = lax.axis_index("dp")
        self.pos = ring_pos(self.dp, dp_size)
        self.half = dp_size // 2
        self.pairs = seq_size // 2
        self.core = self.seq % 2
        self.pair = self.seq // 2
        self.sibling = self.pair * 2 + 1 - self.core

    def ring(self, offset):
        return ring_dev((self.pos + offset + self.dp_size) % self.dp_size, self.dp_size)

    def dp_peer(self, step):
        return (self.dp + step + self.dp_size) % self.dp_size

    def pair_peer(self, step):
        return ((self.pair + step + self.pairs) % self.pairs) * 2 + self.core

    def across_source(self, step):
        return ((self.pair - step + self.pairs) % self.pairs) * 2 + 1 - self.core

    def seq_peer(self, step):
        return (self.seq + step + self.seq_size) % self.seq_size

    def greet_near(self):
        barrier = pltpu.get_barrier_semaphore()
        for step in (1, -1):
            pl.semaphore_signal(barrier, inc=1, device_id={"dp": self.ring(step)}, device_id_type=MESH)
        for step in range(1, self.seq_size):
            pl.semaphore_signal(
                barrier, inc=1, device_id={"seq": self.seq_peer(step)}, device_id_type=MESH
            )

    def met_near(self):
        pl.semaphore_wait(pltpu.get_barrier_semaphore(), 2 + self.seq_size - 1)

    def greet(self):
        barrier = pltpu.get_barrier_semaphore()
        for step in range(1, self.dp_size):
            pl.semaphore_signal(
                barrier, inc=1, device_id={"dp": self.dp_peer(step)}, device_id_type=MESH
            )
        for step in range(1, self.seq_size):
            pl.semaphore_signal(
                barrier, inc=1, device_id={"seq": self.seq_peer(step)}, device_id_type=MESH
            )
        pl.semaphore_wait(barrier, self.dp_size - 1 + self.seq_size - 1)


def send(src, dst, sems, index, target):
    return pltpu.make_async_remote_copy(
        src_ref=src,
        dst_ref=dst,
        send_sem=sems.at[0, index],
        recv_sem=sems.at[1, index],
        device_id=target,
        device_id_type=MESH,
    )


def halves(ref):
    rows = ref.shape[0]
    columns = ref.shape[1]
    if rows % (32 if ref.dtype == BF else 16) == 0:
        return ref.at[pl.ds(0, rows // 2)], ref.at[pl.ds(rows // 2, rows // 2)]
    return ref.at[:, pl.ds(0, columns // 2)], ref.at[:, pl.ds(columns // 2, columns // 2)]


class RingGather:
    def __init__(self, place, full, sems):
        self.place, self.full, self.sems = place, full, sems

    def piece(self, offset, step, way):
        block = self.full.at[self.place.ring(offset)]
        return block if step < self.place.half else halves(block)[way]

    def copies(self, step):
        place = self.place
        right = self.piece(-(step - 1), step, 0)
        left = self.piece(step - 1, step, 1)
        index = 2 * (step - 1)
        return (
            send(right, right, self.sems, index, {"dp": place.ring(1)}),
            send(left, left, self.sems, index + 1, {"dp": place.ring(-1)}),
        )

    def arrivals(self, step):
        right = self.piece(-step, step, 0)
        left = self.piece(step, step, 1)
        index = 2 * (step - 1)
        return (
            send(right, right, self.sems, index, {"dp": self.place.ring(1)}),
            send(left, left, self.sems, index + 1, {"dp": self.place.ring(-1)}),
        )

    def tick(self, step):
        if step > 1:
            for copy in self.arrivals(step - 1):
                copy.wait_recv()
        if step <= self.place.half:
            for copy in self.copies(step):
                copy.start()

    def finish(self):
        for step in range(1, self.place.half + 1):
            for copy in self.copies(step):
                copy.wait_send()


class RingReduce:
    def __init__(self, place, parts, arrived, sems):
        self.place, self.parts, self.arrived, self.sems = place, parts, arrived, sems

    def piece(self, ref, step, way):
        return ref if step > 1 else halves(ref)[way]

    def copies(self, step):
        place = self.place
        away = place.half - step + 1
        index = 2 * (step - 1)
        out = []
        for way, (offset, target) in enumerate(((away, 1), (-away, -1))):
            src = self.piece(self.parts.at[place.ring(offset)], step, way)
            dst = self.piece(self.arrived.at[way, step - 1], step, way)
            out.append(send(src, dst, self.sems, index + way, {"dp": place.ring(target)}))
        return out

    def tick(self, step):
        place = self.place
        if step > 1:
            for way, copy in enumerate(self.copies(step - 1)):
                copy.wait_recv()
                away = (place.half - step + 1) * (1 - 2 * way)
                held = self.piece(self.parts.at[place.ring(away)], step - 1, way)
                came = self.piece(self.arrived.at[way, step - 2], step - 1, way)
                held[...] = (held[...].astype(F32) + came[...].astype(F32)).astype(held.dtype)
        if step <= place.half:
            for copy in self.copies(step):
                copy.start()

    def finish(self):
        for step in range(1, self.place.half + 1):
            for copy in self.copies(step):
                copy.wait_send()

    def own(self):
        return self.parts.at[self.place.dp]


class SeqGather:
    def __init__(self, place, full, sems, own=None):
        self.place, self.full, self.sems = place, full, sems
        self.own = full.at[place.seq] if own is None else own

    def direct(self, step):
        place = self.place
        target = {"seq": place.pair_peer(step)}
        return send(self.own, self.full.at[place.seq], self.sems, step, target)

    def arrival(self, step):
        place = self.place
        target = {"seq": place.pair_peer(step)}
        return send(self.own, self.full.at[place.pair_peer(-step)], self.sems, step, target)

    def across(self, step):
        place = self.place
        block = self.full.at[place.pair_peer(-step)]
        src = self.own if step == 0 else block
        return send(src, block, self.sems, place.pairs + step, {"seq": place.sibling})

    def across_arrival(self, step):
        place = self.place
        block = self.full.at[place.across_source(step)]
        return send(self.own, block, self.sems, place.pairs + step, {"seq": place.sibling})

    def begin(self):
        for step in range(1, self.place.pairs):
            self.direct(step).start()
        self.across(0).start()

    def forward(self):
        for step in range(1, self.place.pairs):
            self.arrival(step).wait_recv()
            self.across(step).start()

    def across_arrived(self, step):
        self.across_arrival(step).wait_recv()

    def sent(self):
        for step in range(1, self.place.pairs):
            self.direct(step).wait_send()
        for step in range(self.place.pairs):
            self.across(step).wait_send()

    def finish(self):
        for step in range(self.place.pairs):
            self.across_arrived(step)
        self.sent()


class SeqReduce:
    def __init__(self, place, parts, crossed, arrived, sems):
        self.place, self.parts, self.crossed, self.arrived = place, parts, crossed, arrived
        self.sems = sems

    def over(self, step):
        place = self.place
        index = (place.pair + step) % place.pairs
        src = self.parts.at[index * 2 + 1 - place.core]
        return send(src, self.crossed.at[index], self.sems, step, {"seq": place.sibling})

    def direct(self, step):
        place = self.place
        return send(
            self.parts.at[place.pair_peer(step)],
            self.arrived.at[step - 1],
            self.sems,
            place.pairs + step,
            {"seq": place.pair_peer(step)},
        )

    def over_start(self, step):
        self.over(step).start()

    def over_add(self, step):
        place = self.place
        index = (place.pair + step) % place.pairs
        self.over(step).wait_recv()
        held = self.parts.at[index * 2 + place.core]
        held[...] = (held[...].astype(F32) + self.crossed[index].astype(F32)).astype(held.dtype)
        if step > 0:
            self.direct(step).start()

    def begin(self):
        for step in range(self.place.pairs):
            self.over_start(step)

    def middle(self):
        for step in range(self.place.pairs):
            self.over_add(step)

    def total(self):
        place = self.place
        total = self.parts.at[place.seq][...].astype(F32)
        for step in range(1, place.pairs):
            self.direct(step).wait_recv()
            total = total + self.arrived[step - 1].astype(F32)
        return total

    def finish(self):
        for step in range(self.place.pairs):
            self.over(step).wait_send()
        for step in range(1, self.place.pairs):
            self.direct(step).wait_send()


class DpSpread:
    def __init__(self, place, src_of, full, sems):
        self.place, self.src_of, self.full, self.sems = place, src_of, full, sems

    def copy(self, step):
        place = self.place
        peer = place.dp_peer(step)
        return send(self.src_of(peer), self.full.at[place.dp], self.sems, step, {"dp": peer})

    def arrival(self, step):
        place = self.place
        source = place.dp_peer(-step)
        return send(
            self.src_of(source), self.full.at[source], self.sems, step, {"dp": place.dp_peer(step)}
        )

    def begin(self):
        for step in range(1, self.place.dp_size):
            self.copy(step).start()

    def finish(self):
        for step in range(1, self.place.dp_size):
            self.arrival(step).wait_recv()
        for step in range(1, self.place.dp_size):
            self.copy(step).wait_send()


def sems_of(count):
    return pltpu.SemaphoreType.DMA((2, count))


def gather_kernel(seq_size, dp_size, *refs):
    (x_ref, dy_ref, mix_ref, proj_ref, rise_ref, fall_ref, vec_ref, seg_ref) = refs[:8]
    (x_all, dy_all, mix_all, proj_cols, rise_all, fall_all, vec_all, seg_all, proj_all) = refs[8:17]
    (x_sems, dy_sems, mix_sems, proj_sems, rise_sems, fall_sems, vec_sems, seg_sems, swap_sems, own_sems) = refs[17:]
    place = Place(seq_size, dp_size)
    own = [
        pltpu.make_async_copy(src, dst, own_sems.at[i])
        for i, (src, dst) in enumerate(
            (
                (x_ref, x_all.at[place.seq]),
                (dy_ref, dy_all.at[place.seq]),
                (mix_ref, mix_all.at[place.dp]),
                (proj_ref, proj_cols.at[place.dp]),
                (rise_ref, rise_all.at[place.dp]),
                (fall_ref, fall_all.at[place.dp]),
                (vec_ref, vec_all.at[place.dp]),
                (seg_ref, seg_all.at[place.seq]),
            )
        )
    ]
    for copy in own:
        copy.start()
    place.greet()
    for copy in own:
        copy.wait()
    x_move = SeqGather(place, x_all, x_sems)
    dy_move = SeqGather(place, dy_all, dy_sems)
    seg_move = SeqGather(place, seg_all, seg_sems)
    vec_move = DpSpread(place, lambda peer: vec_ref, vec_all, vec_sems)
    mix_move = RingGather(place, mix_all, mix_sems)
    proj_move = RingGather(place, proj_cols, proj_sems)
    rise_move = RingGather(place, rise_all, rise_sems)
    fall_move = RingGather(place, fall_all, fall_sems)
    x_move.begin()
    seg_move.begin()
    vec_move.begin()
    half = place.half
    for step in range(1, half + 1):
        mix_move.tick(step)
        proj_move.tick(step)
    x_move.forward()
    seg_move.forward()
    dy_move.begin()
    mix_move.tick(half + 1)
    proj_move.tick(half + 1)
    rise_move.tick(1)
    fall_move.tick(1)
    rows = proj_cols.shape[0] * proj_cols.shape[1] // seq_size
    each = rows // proj_cols.shape[1]
    swaps = []
    for step in range(1, seq_size):
        peer = place.seq_peer(step)
        swaps.append(
            send(
                proj_cols.at[pl.ds(peer * each, each)],
                proj_all.at[place.seq],
                swap_sems,
                step,
                {"seq": peer},
            )
        )
    for copy in swaps:
        copy.start()
    mine = pltpu.make_async_copy(
        proj_cols.at[pl.ds(place.seq * each, each)], proj_all.at[place.seq], own_sems.at[0]
    )
    mine.start()
    for step in range(2, half + 2):
        rise_move.tick(step)
        fall_move.tick(step)
        if step == 3:
            dy_move.forward()
    mine.wait()
    for step in range(1, seq_size):
        source = place.seq_peer(-step)
        send(
            proj_cols.at[pl.ds(source * each, each)],
            proj_all.at[source],
            swap_sems,
            step,
            {"seq": place.seq_peer(step)},
        ).wait_recv()
    for copy in swaps:
        copy.wait_send()
    for move in (x_move, dy_move, seg_move, vec_move, mix_move, proj_move, rise_move, fall_move):
        move.finish()


def gather_all(seq_size, dp_size, x, dy, mix, proj, rise, fall, vec, seg):
    half = dp_size // 2
    pairs = seq_size // 2

    def lead(count, like):
        return jax.ShapeDtypeStruct((count,) + like.shape, like.dtype)

    each = dp_size // seq_size
    any_spec = pl.BlockSpec(memory_space=pl.ANY)
    return pl.pallas_call(
        functools.partial(gather_kernel, seq_size, dp_size),
        out_shape=(
            lead(seq_size, x),
            lead(seq_size, dy),
            lead(dp_size, mix),
            lead(dp_size, proj),
            lead(dp_size, rise),
            lead(dp_size, fall),
            lead(dp_size, vec),
            lead(seq_size, seg),
            jax.ShapeDtypeStruct((seq_size, each) + proj.shape, proj.dtype),
        ),
        in_specs=[any_spec] * 8,
        out_specs=[any_spec] * 9,
        scratch_shapes=[
            sems_of(2 * pairs),
            sems_of(2 * pairs),
            sems_of(2 * half),
            sems_of(2 * half),
            sems_of(2 * half),
            sems_of(2 * half),
            sems_of(dp_size),
            sems_of(2 * pairs),
            sems_of(seq_size),
            pltpu.SemaphoreType.DMA((8,)),
        ],
        compiler_params=pltpu.CompilerParams(collective_id=0, has_side_effects=True),
    )(x, dy, mix, proj, rise, fall, vec, seg)


def reduce_kernel(seq_size, dp_size, *refs):
    (out_ref, back_ref, mix_ref, proj_ref, rise_ref, fall_ref, vec_ref), refs = refs[:7], refs[7:]
    (out_sum, back_sum, mix_fin, proj_fin, rise_fin, fall_fin, vec_fin), refs = refs[:7], refs[7:]
    (
        out_cross,
        out_came,
        back_cross,
        back_came,
        proj_full,
        mix_came,
        proj_came,
        rise_came,
        fall_came,
        vec_came,
        out_sems,
        back_sems,
        swap_sems,
        mix_sems,
        proj_sems,
        rise_sems,
        fall_sems,
        vec_sems,
        mix_fs,
        proj_fs,
        rise_fs,
        fall_fs,
        vec_fs,
    ) = refs
    place = Place(seq_size, dp_size)
    each = dp_size // seq_size
    half = place.half
    place.greet()

    def mine(index):
        return proj_full.at[pl.ds(index * each, each)]

    def swap(step):
        peer = place.seq_peer(step)
        return send(proj_ref.at[peer], mine(place.seq), swap_sems, step, {"seq": peer})

    def swap_arrival(step):
        source = place.seq_peer(-step)
        target = {"seq": place.seq_peer(step)}
        return send(proj_ref.at[source], mine(source), swap_sems, step, target)

    for step in range(1, seq_size):
        swap(step).start()
    mine(place.seq)[...] = proj_ref[place.seq]
    mix = RingReduce(place, mix_ref, mix_came, mix_sems)
    proj = RingReduce(place, proj_full, proj_came, proj_sems)
    rise = RingReduce(place, rise_ref, rise_came, rise_sems)
    fall = RingReduce(place, fall_ref, fall_came, fall_sems)
    out = SeqReduce(place, out_ref, out_cross, out_came, out_sems)
    back = SeqReduce(place, back_ref, back_cross, back_came, back_sems)
    vec = DpSpread(place, lambda peer: vec_ref.at[peer], vec_came, vec_sems)
    mix.tick(1)
    rise.tick(1)
    out.begin()
    back.begin()
    vec.begin()
    for step in range(1, seq_size):
        swap_arrival(step).wait_recv()
    proj.tick(1)
    fall.tick(1)
    out.middle()
    back.middle()
    for step in range(2, half + 2):
        for move in (mix, rise, proj, fall):
            move.tick(step)
    finals = []
    for move, fin, fin_sems in (
        (mix, mix_fin, mix_fs),
        (rise, rise_fin, rise_fs),
        (proj, proj_fin, proj_fs),
        (fall, fall_fin, fall_fs),
    ):
        fin[place.seq] = move.parts[place.dp]
        gather = SeqGather(place, fin, fin_sems)
        gather.begin()
        finals.append(gather)
    vec_came[place.dp] = vec_ref[place.dp]
    vec.finish()
    vec_fin[place.seq] = jnp.sum(vec_came[...], axis=0)
    gather = SeqGather(place, vec_fin, vec_fs)
    gather.begin()
    finals.append(gather)
    out_sum[...] = out.total()
    back_sum[...] = back.total()
    for gather in finals:
        gather.forward()
    for gather in finals:
        gather.finish()
    for step in range(1, seq_size):
        swap(step).wait_send()
    for move in (mix, rise, proj, fall, out, back):
        move.finish()


def reduce_all(seq_size, dp_size, out, back, mix, proj, rise, fall, vec):
    half = dp_size // 2
    pairs = seq_size // 2
    each = dp_size // seq_size

    def fin(like):
        return jax.ShapeDtypeStruct((seq_size,) + like.shape[1:], like.dtype)

    def came(like):
        return pltpu.VMEM((2, half) + like.shape[1:], like.dtype)

    proj_blocks = jax.ShapeDtypeStruct((dp_size,) + proj.shape[2:], proj.dtype)
    vmem = pl.BlockSpec(memory_space=pltpu.VMEM)
    return pl.pallas_call(
        functools.partial(reduce_kernel, seq_size, dp_size),
        out_shape=(
            jax.ShapeDtypeStruct(out.shape[1:], F32),
            jax.ShapeDtypeStruct(back.shape[1:], F32),
            fin(mix),
            fin(proj_blocks),
            fin(rise),
            fin(fall),
            fin(vec),
        ),
        in_specs=[vmem] * 7,
        out_specs=[vmem] * 7,
        scratch_shapes=[
            pltpu.VMEM((pairs,) + out.shape[1:], BF),
            pltpu.VMEM((pairs,) + out.shape[1:], BF),
            pltpu.VMEM((pairs,) + back.shape[1:], BF),
            pltpu.VMEM((pairs,) + back.shape[1:], BF),
            pltpu.VMEM(proj_blocks.shape, BF),
            came(mix),
            came(proj_blocks),
            came(rise),
            came(fall),
            pltpu.VMEM(vec.shape, F32),
            sems_of(2 * pairs),
            sems_of(2 * pairs),
            sems_of(seq_size),
            sems_of(2 * half),
            sems_of(2 * half),
            sems_of(2 * half),
            sems_of(2 * half),
            sems_of(dp_size),
            sems_of(2 * pairs),
            sems_of(2 * pairs),
            sems_of(2 * pairs),
            sems_of(2 * pairs),
            sems_of(2 * pairs),
        ],
        compiler_params=pltpu.CompilerParams(
            collective_id=1, has_side_effects=True, vmem_limit_bytes=56 * 2**20
        ),
    )(out, back, mix, proj, rise, fall, vec)


def angle_tables(length):
    frequency = BASE ** (-np.arange(0, ROT, 2).astype(np.float32) / np.float32(ROT))
    angles = np.arange(length, dtype=np.float32)[:, None] * frequency.astype(np.float32)[None, :]
    return np.cos(angles).astype(np.float32), np.sin(angles).astype(np.float32)


def turn(piece, cosine, sine, sign):
    half = ROT // 2
    low, high = piece[..., :half], piece[..., half:ROT]
    return jnp.concatenate(
        [low * cosine - sign * high * sine, high * cosine + sign * low * sine, piece[..., ROT:]],
        axis=-1,
    )


TILE = 256

def mm(a, b, dims):
    return lax.dot_general(a, b, ((dims[0], dims[1]), ((), ())), preferred_element_type=F32)

def nn(a, b):
    return mm(a, b, ((1,), (0,)))

def nt(a, b):
    return mm(a, b, ((1,), (1,)))

def tn(a, b):
    return mm(a, b, ((0,), (0,)))

def fold(count, body, init):
    if isinstance(count, int):
        for index in range(count):
            init = body(index, init)
        return init
    return lax.fori_loop(0, count, body, init)

def rows_of(index):
    start = index * TILE
    return pl.ds(start if isinstance(start, int) else pl.multiple_of(start, TILE), TILE)

def attend_block(head, block, refs):
    q_ref, k_ref, v_ref, g_ref, kt_ref, vt_ref, s_ref, p_ref, ht_ref, dqt_ref, dk_ref, dv_ref = refs
    here = rows_of(block)
    span = block + 1
    dims = pl.ds(pl.multiple_of(head * HEAD_DIM, HEAD_DIM), HEAD_DIM)
    query = q_ref[head, here, :]
    grad = g_ref[head, here, :]

    def score(index, top):
        tile = nt(k_ref[head, rows_of(index), :], query)
        if isinstance(index, int) and isinstance(block, int) and index < block:
            keep = tile
        else:
            key = lax.broadcasted_iota(jnp.int32, (TILE, TILE), 0) + (index - block) * TILE
            place = lax.broadcasted_iota(jnp.int32, (TILE, TILE), 1)
            keep = jnp.where(key <= place, tile, NEG)
        s_ref[index] = keep
        return jnp.maximum(top, jnp.max(keep, axis=0, keepdims=True))

    top = fold(span, score, jnp.full((1, TILE), 2 * NEG, F32))

    def raise_(index, total):
        raised = jnp.exp(s_ref[index] - top)
        s_ref[index] = raised
        return total + jnp.sum(raised, axis=0, keepdims=True)

    total = fold(span, raise_, jnp.zeros((1, TILE), F32))
    share = 1.0 / total

    def weigh(index, carried):
        heads, delta = carried
        weights = s_ref[index] * share
        s_ref[index] = weights
        weights_b = weights.astype(BF)
        d_weights = nt(v_ref[head, rows_of(index), :], grad)
        p_ref[index] = d_weights
        dv_ref[head, rows_of(index), :] += nn(weights_b, grad)
        heads = heads + nn(vt_ref[dims, rows_of(index)], weights_b)
        return heads, delta + jnp.sum(weights * d_weights, axis=0, keepdims=True)

    heads, delta = fold(
        span, weigh, (jnp.zeros((HEAD_DIM, TILE), F32), jnp.zeros((1, TILE), F32))
    )
    ht_ref[dims, here] = heads

    def back(index, d_query):
        d_scores = (s_ref[index] * (p_ref[index] - delta)).astype(BF)
        dk_ref[head, rows_of(index), :] += nn(d_scores, query)
        return d_query + nn(kt_ref[dims, rows_of(index)], d_scores)

    dqt_ref[dims, here] = fold(span, back, jnp.zeros((HEAD_DIM, TILE), F32))

def attend(heads_n, length, refs):
    dk_ref, dv_ref = refs[-2:]
    dk_ref[...] = jnp.zeros(dk_ref.shape, F32)
    dv_ref[...] = jnp.zeros(dv_ref.shape, F32)
    blocks = length // TILE

    @pl.loop(0, heads_n)
    def _(head):
        if blocks <= 4:
            for block in range(blocks):
                attend_block(head, block, refs)
        else:
            @pl.loop(0, blocks)
            def _(block):
                attend_block(head, block, refs)

def attend_kernel(H, L, q, k, v, g, kt, vt, ht, dqt, dk, dv, s_ref, p_ref):
    attend(H, L, (q, k, v, g, kt, vt, s_ref, p_ref, ht, dqt, dk, dv))

def attention_call(q, k, v, g, kt, vt):
    H, L, _ = q.shape
    vm = pl.BlockSpec(memory_space=pltpu.VMEM)
    nb = L // TILE
    return pl.pallas_call(functools.partial(attend_kernel, H, L),
        out_shape=(jax.ShapeDtypeStruct((H*64, L), F32), jax.ShapeDtypeStruct((H*64, L), F32), jax.ShapeDtypeStruct((H, L, 128), F32), jax.ShapeDtypeStruct((H, L, 128), F32)),
        in_specs=[vm]*6, out_specs=[vm]*4,
        scratch_shapes=[pltpu.VMEM((nb, TILE, TILE), F32), pltpu.VMEM((nb, TILE, TILE), F32)],
        compiler_params=pltpu.CompilerParams(vmem_limit_bytes=56 * 2**20))(q, k, v, g, kt, vt)

def prep(queries, keys, values, d_heads, segments):
    seg = segments[:, None] == jnp.arange(64)[None, :]
    e = jnp.broadcast_to(seg.astype(BF)[None], queries.shape)
    f = jnp.broadcast_to(jnp.where(seg, 0.0, NEG).astype(BF)[None], queries.shape)
    lane = jnp.arange(64)
    f = jnp.where(lane < 4, f, 0).astype(BF)
    qa = jnp.concatenate([(queries.astype(F32) * 0.125).astype(BF), e], -1)
    ka = jnp.concatenate([keys, f], -1)
    z = jnp.zeros_like(values)
    va = jnp.concatenate([values, z], -1)
    ga = jnp.concatenate([d_heads, z], -1)
    kt = keys.transpose(0, 2, 1).reshape(-1, keys.shape[1])
    vt = values.transpose(0, 2, 1).reshape(-1, keys.shape[1])
    return qa, ka, va, ga, kt, vt

def attention(queries, keys, values, d_heads, segments):
    H, L, _ = queries.shape
    ht, dqt, dk, dv = attention_call(*prep(queries, keys, values, d_heads, segments))

    def back(t):
        return t.reshape(H, 64, L).transpose(0, 2, 1)

    return back(ht).astype(BF), (back(dqt) * 0.125).astype(BF), dk[..., :64].astype(BF), dv[..., :64].astype(BF)


def dot(a, b):
    return jnp.dot(a, b, preferred_element_type=F32)


def dot_t(a, b):
    return lax.dot_general(a, b, (((0,), (0,)), ((), ())), preferred_element_type=F32)


def dot_nt(a, b):
    return lax.dot_general(a, b, (((1,), (1,)), ((), ())), preferred_element_type=F32)


(
    OWN, XGO, DYGO, XFWD, DYFWD, HOTS, DYALL, VROWS, LN0, LN1, LN2, LN3, SWGO, SWIN, QKV0, QKV1,
    DH, GVC1, GVC2, GVC3, GVC4, GVC5, GMA1, GMA2, GMA3, GMA4, GMA5, GMB1, GMB2, GMB3, GMB4,
    GMB5, GPR1, GPR2, GPR3, GPR4, GPR5, GRA1, GRA2, GRA3, GRA4, GRA5, GRB1, GRB2, GRB3, GRB4,
    GRB5, GFA1, GFA2, GFA3, GFA4, GFA5, GFB1, GFB2, GFB3, GFB4, GFB5, RVC1, RVC2, RVC3, RVC4,
    RVC5, RMA1, RMA2, RMA3, RMA4, RMA5, RMB1, RMB2, RMB3, RMB4, RMB5, RPR1, RPR2, RPR3, RPR4,
    RPR5, RRA1, RRA2, RRA3, RRA4, RRA5, RRB1, RRB2, RRB3, RRB4, RRB5, RFA1, RFA2, RFA3, RFA4,
    RFA5, RFB1, RFB2, RFB3, RFB4, RFB5, AT00, AT02, AT03, AT10, AT12, AT13, AT20, AT22, AT23,
    AT30, AT32, AT33, POST0, POST1, GM0, GM1, GR0, GR1, GF0, GF1, GP, SBGO, SBIN, UP0, UP1, UP2,
    UP3, DN0, DN1, OP0, OP1, BK0, BK1, OM0, OM1, BM0, BM1, VP, BO, IG, SV, WV, VO, SMA, SMB,
    SPR, SRA, SRB, SFA, SFB, WMA, WMB, WPR, WRA, WRB, WFA, WFB, CMA, CMB, CPR, CRA, CRB, CFA,
    CFB,
) = range(161)

ORDER = (
    OWN, XGO, GPR1, GRA1, GVC1, GMB1, GPR2, GRB1, GRA2, DYGO, GPR3, GVC2, XFWD, GMB2, HOTS,
    GRA3, GPR4, GVC3, GRB2, GMB3, GPR5, SWGO, GRA4, DYFWD, GVC4, GMA1, DYALL, GRB3, GRA5, GVC5,
    VROWS, LN0, GMB4, LN1, SWIN, GMA2, DH, LN2, GRB4, LN3, GMB5, GFB1, GMA3, GRB5, UP2, GFA1,
    UP0, GFB2, UP1, GMA4, UP3, GFA2, GF0, GFB3, GF1, GMA5, QKV1, RFA1, RFB1, QKV0, GFB4, GFA3,
    AT30, AT32, RFA2, AT00, GFB5, AT02, RFB2, AT03, AT10, GFA4, AT12, RFA3, AT33, RFB3, AT20,
    GFA5, DN0, DN1, RFA4, GR1, RFB4, GR0, AT13, RRB1, AT22, RFA5, SFA, RRA1, AT23, RFB5, SFB,
    POST1, RRB2, POST0, RRA2, WFA, GP, SBGO, BK1, WFB, CFA, RRB3, OP1, CFB, BM1, RRA3, GM1, GM0,
    SBIN, RMA1, RMB1, OP0, RPR1, RRB4, BK0, RMA2, VP, RMB2, OM1, OM0, BM0, RRB5, RVC1, RPR2,
    RRA4, IG, RMA3, RMB3, RRA5, RVC2, RPR3, SRB, RMA4, SRA, RMB4, BO, RVC3, RPR4, WRB, RMA5,
    SMA, CRB, RMB5, SMB, RVC4, WRA, CRA, RPR5, SPR, WMA, RVC5, SV, CMA, WMB, CMB, WPR, WV, VO,
    CPR,
)
LANES = 128
HALF = LANES // 2
VEC_ROWS = 16
PROJ = 3
TURN = 32


def resident_fits(seq_size, dp_size, tok):
    return (
        D // dp_size == LANES
        and FF // dp_size // seq_size == LANES
        and HEADS // seq_size == 4
        and tok * seq_size <= TURN * TURN
        and tok % TILE == 0
    )


def rows_at(ref, index, count):
    return ref.at[pl.ds(pl.multiple_of(index * count, count), count)]


def columns_at(ref, index, count):
    return ref.at[:, pl.ds(pl.multiple_of(index * count, count), count)]


class Flat:
    def __init__(self, ref, count, stride=None, start=0):
        self.ref, self.count, self.start = ref, count, start
        self.stride = count if stride is None else stride

    @property
    def at(self):
        return self

    def __getitem__(self, index):
        first = pl.multiple_of(index * self.stride + self.start, self.count)
        return self.ref.at[pl.ds(first, self.count)]


class Stack:
    def __init__(self, ref, start, count):
        self.ref, self.start, self.count = ref, start, count

    @property
    def at(self):
        return self

    def __getitem__(self, index):
        return self.ref.at[index, pl.ds(self.start, self.count)]


def lanes_like(shape):
    return lax.broadcasted_iota(jnp.int32, shape, len(shape) - 1)


def head_part(values, start):
    tile = values[:, start // LANES * LANES : start // LANES * LANES + LANES]
    return tile if start % LANES == 0 else pltpu.roll(tile, HEAD_DIM, 1)


def spin(tile, cosine, sine):
    lane = lanes_like(tile.shape)
    partner = jnp.where(lane < ROT // 2, pltpu.roll(tile, LANES - ROT // 2, 1), pltpu.roll(tile, ROT // 2, 1))
    return tile * cosine + partner * sine


def attend_head(head, block, refs):
    q_ref, k_ref, v_ref, g_ref, kt_ref, vt_ref, s_ref, p_ref, ht_ref, dqt_ref, dk_ref, dv_ref = refs
    here = pl.ds(block * TILE, TILE)
    wide = pl.ds(head * LANES, LANES)
    dims = pl.ds(head * HEAD_DIM, HEAD_DIM)
    query = q_ref[here, wide]
    grad = g_ref[here, wide]
    span = block + 1
    top = jnp.full((1, TILE), 2 * NEG, F32)
    for index in range(span):
        tile = nt(k_ref[pl.ds(index * TILE, TILE), wide], query)
        if index == block:
            key = lax.broadcasted_iota(jnp.int32, (TILE, TILE), 0)
            place = lax.broadcasted_iota(jnp.int32, (TILE, TILE), 1)
            tile = jnp.where(key <= place, tile, NEG)
        s_ref[index] = tile
        top = jnp.maximum(top, jnp.max(tile, axis=0, keepdims=True))
    total = jnp.zeros((1, TILE), F32)
    for index in range(span):
        raised = jnp.exp(s_ref[index] - top)
        s_ref[index] = raised
        total = total + jnp.sum(raised, axis=0, keepdims=True)
    share = 1.0 / total
    delta = jnp.zeros((1, TILE), F32)
    heads = jnp.zeros((HEAD_DIM, TILE), F32)
    for index in range(span):
        there = pl.ds(index * TILE, TILE)
        weights = s_ref[index] * share
        s_ref[index] = weights
        weights_b = weights.astype(BF)
        d_weights = nt(v_ref[there, wide], grad)
        p_ref[index] = d_weights
        d_value = nn(weights_b, grad)
        dv_ref[head, there, :] = d_value if index == block else dv_ref[head, there, :] + d_value
        heads = heads + nn(vt_ref[dims, there], weights_b)
        delta = delta + jnp.sum(weights * d_weights, axis=0, keepdims=True)
    ht_ref[dims, here] = heads.astype(BF)
    d_query = jnp.zeros((HEAD_DIM, TILE), F32)
    for index in range(span):
        there = pl.ds(index * TILE, TILE)
        d_scores = (s_ref[index] * (p_ref[index] - delta)).astype(BF)
        d_key = nn(d_scores, query)
        dk_ref[head, there, :] = d_key if index == block else dk_ref[head, there, :] + d_key
        d_query = d_query + nn(kt_ref[dims, there], d_scores)
    dqt_ref[dims, here] = (d_query * HEAD_DIM**-0.5).astype(BF)


class Refs(typing.NamedTuple):
    x_own: typing.Any
    dy_own: typing.Any
    w_mix_own: typing.Any
    w_proj_own: typing.Any
    w_rise_own: typing.Any
    w_fall_own: typing.Any
    gain1_own: typing.Any
    shift1_own: typing.Any
    gain2_own: typing.Any
    shift2_own: typing.Any
    b_proj_own: typing.Any
    b_fall_own: typing.Any
    b_mix_own: typing.Any
    b_rise_own: typing.Any
    seg_own: typing.Any
    pad_own: typing.Any
    turns: typing.Any
    block_out: typing.Any
    input_grad: typing.Any
    mix_fin: typing.Any
    proj_fin: typing.Any
    rise_fin: typing.Any
    fall_fin: typing.Any
    vec_result: typing.Any
    pad: typing.Any
    cos: typing.Any
    sin: typing.Any
    x: typing.Any
    dy: typing.Any
    hot: typing.Any
    segs: typing.Any
    w_mix: typing.Any
    w_proj_cols: typing.Any
    w_proj: typing.Any
    w_rise: typing.Any
    w_fall: typing.Any
    vec_all: typing.Any
    rows: typing.Any
    normed1: typing.Any
    normed2: typing.Any
    stat: typing.Any
    qk: typing.Any
    vg: typing.Any
    kt: typing.Any
    vt: typing.Any
    s: typing.Any
    p: typing.Any
    ht: typing.Any
    dqt: typing.Any
    dk: typing.Any
    dv: typing.Any
    attn: typing.Any
    d_mixed: typing.Any
    out_part: typing.Any
    back_part: typing.Any
    active: typing.Any
    d_up: typing.Any
    g_mix: typing.Any
    g_proj_cols: typing.Any
    g_rise: typing.Any
    g_fall: typing.Any
    c_mix: typing.Any
    c_proj: typing.Any
    c_rise: typing.Any
    c_fall: typing.Any
    out_cross: typing.Any
    out_came: typing.Any
    back_cross: typing.Any
    back_came: typing.Any
    sums: typing.Any
    vec_part: typing.Any
    vec_came: typing.Any
    mix_got: typing.Any
    proj_got: typing.Any
    rise_got: typing.Any
    fall_got: typing.Any
    vec_fin: typing.Any
    vec_out: typing.Any
    m_x: typing.Any
    m_dy: typing.Any
    m_hot: typing.Any
    m_vec: typing.Any
    m_mix: typing.Any
    m_proj: typing.Any
    m_rise: typing.Any
    m_fall: typing.Any
    m_swap: typing.Any
    m_own: typing.Any
    m_swap2: typing.Any
    m_rmix: typing.Any
    m_rproj: typing.Any
    m_rrise: typing.Any
    m_rfall: typing.Any
    m_out: typing.Any
    m_back: typing.Any
    m_vec2: typing.Any
    m_fmix: typing.Any
    m_fproj: typing.Any
    m_frise: typing.Any
    m_ffall: typing.Any
    m_fvec: typing.Any
    m_fin: typing.Any


def resident_kernel(seq_size, dp_size, *refs):
    r = Refs(*refs)
    place = Place(seq_size, dp_size)
    half = place.half
    tok = r.x_own.shape[0]
    length = r.x.shape[0]
    wide = r.w_proj.shape[0]
    mixed_wide = 3 * wide
    units = LANES
    each = dp_size // seq_size
    heads_n = wide // HEAD_DIM
    blocks = length // TILE

    place.greet_near()
    own = []

    def bring(src, dst):
        copy = pltpu.make_async_copy(src, dst, r.m_own.at[len(own)])
        copy.start()
        own.append(copy)

    bring(columns_at(r.w_mix_own, place.seq, mixed_wide), rows_at(r.w_mix, place.dp, LANES))
    bring(columns_at(r.w_proj_own, place.seq, wide), rows_at(r.w_proj_cols, place.dp, LANES))
    bring(r.x_own, rows_at(r.x, place.seq, tok))
    bring(r.dy_own, rows_at(r.dy, place.seq, tok))
    for index in range(dp_size):
        bring(
            columns_at(r.w_rise_own, index * seq_size + place.seq, units),
            rows_at(r.w_rise, place.dp, LANES).at[:, pl.ds(index * units, units)],
        )
    bring(rows_at(r.w_fall_own, place.seq, units), rows_at(r.w_fall, place.dp, units))
    bring(r.pad_own, r.pad)

    coarse_cos, coarse_sin, fine_cos, fine_sin = (
        r.turns.at[pl.ds(index * TURN, TURN)] for index in range(4)
    )

    @pl.loop(0, length // TURN)
    def _(step):
        here = pl.ds(pl.multiple_of(step * TURN, TURN), TURN)
        far_cos, far_sin = coarse_cos[pl.ds(step, 1), :], coarse_sin[pl.ds(step, 1), :]
        r.cos[here, :] = far_cos * fine_cos[...] - far_sin * fine_sin[...]
        r.sin[here, :] = far_sin * fine_cos[...] + far_cos * fine_sin[...]

    row = 0
    vectors = (r.gain1_own, r.shift1_own, r.gain2_own, r.shift2_own, r.b_proj_own, r.b_fall_own, r.b_mix_own, r.b_rise_own)
    for vector in vectors:
        count = vector.shape[0]
        r.vec_all[place.dp, row : row + count, :] = vector[...].astype(F32)
        row += count
    r.vec_all[place.dp, row:, :] = jnp.zeros((VEC_ROWS - row, LANES), F32)
    rows_at(r.segs, place.seq, 8)[...] = jnp.broadcast_to(r.seg_own[...], (8, tok)).astype(F32)

    def pair_of(ref, make):
        return [make(Flat(ref, HALF, LANES, start), index) for index, start in enumerate((0, HALF))]

    def gather_pair(ref, sems):
        return pair_of(ref, lambda part, index: RingGather(place, part, sems.at[index]))

    def reduce_pair(ref, came, sems):
        return pair_of(ref, lambda part, index: RingReduce(place, part, came.at[index], sems.at[index]))

    def final_pair(out_ref, sems, ref):
        return pair_of(
            ref,
            lambda part, index: SeqGather(
                place, Stack(out_ref, index * HALF, HALF), sems.at[index], part[place.dp]
            ),
        )

    gathers = [
        RingGather(place, r.vec_all, r.m_vec),
        *gather_pair(r.w_mix, r.m_mix),
        RingGather(place, Flat(r.w_proj_cols, LANES), r.m_proj),
        *gather_pair(r.w_rise, r.m_rise),
        *gather_pair(r.w_fall, r.m_fall),
    ]
    reduces = [
        RingReduce(place, r.vec_part, r.vec_came, r.m_vec2),
        *reduce_pair(r.g_mix, r.c_mix, r.m_rmix),
        RingReduce(place, Flat(r.g_proj_cols, LANES), r.c_proj, r.m_rproj),
        *reduce_pair(r.g_rise, r.c_rise, r.m_rrise),
        *reduce_pair(r.g_fall, r.c_fall, r.m_rfall),
    ]
    finals = [
        *final_pair(r.mix_got, r.m_fmix, r.g_mix),
        SeqGather(place, r.proj_got, r.m_fproj, rows_at(r.g_proj_cols, place.dp, LANES)),
        *final_pair(r.rise_got, r.m_frise, r.g_rise),
        *final_pair(r.fall_got, r.m_ffall, r.g_fall),
    ]
    homes = [r.proj_fin]
    for out_ref in (r.rise_fin, r.fall_fin):
        homes += [Stack(out_ref, start, HALF) for start in (0, HALF)]
    homes = [Stack(r.mix_fin, start, HALF) for start in (0, HALF)] + homes
    f_vec = SeqGather(place, r.vec_fin, r.m_fvec)

    x_move = SeqGather(place, Flat(r.x, tok), r.m_x)
    dy_move = SeqGather(place, Flat(r.dy, tok), r.m_dy)
    seg_move = SeqGather(place, Flat(r.segs, 8), r.m_hot)
    out = SeqReduce(place, Flat(r.out_part, tok), r.out_cross, r.out_came, r.m_out)
    back = SeqReduce(place, Flat(r.back_part, tok), r.back_cross, r.back_came, r.m_back)

    leaving = []

    def leave(src, dst):
        copy = pltpu.make_async_copy(src, dst, r.m_fin.at[len(leaving)])
        copy.start()
        leaving.append(copy)

    pieces = {}

    def piece(name, *given):
        def note(run):
            pieces[name] = functools.partial(run, *given)
            return run

        return note

    def tile_rows(block):
        return pl.ds(pl.multiple_of(block * TILE, TILE), TILE)

    def gather(stream, step):
        gathers[stream].tick(step)

    def reduce(stream, step):
        reduces[stream].tick(step)

    for stream in range(len(gathers)):
        for step in range(1, half + 2):
            tick = stream * (half + 1) + step - 1
            piece(GVC1 + tick, stream, step)(gather)
            piece(RVC1 + tick, stream, step)(reduce)

    @piece(OWN)
    def _():
        for copy in own:
            copy.wait()

    @piece(XGO)
    def _():
        x_move.begin()
        seg_move.begin()

    piece(DYGO)(dy_move.begin)

    @piece(XFWD)
    def _():
        x_move.forward()
        seg_move.forward()

    piece(DYFWD)(dy_move.forward)

    @piece(HOTS)
    def _():
        for step in range(place.pairs):
            seg_move.across_arrived(step)
        kind = lax.broadcasted_iota(jnp.int32, (LANES, tok), 0) - HEAD_DIM
        for index in range(seq_size):
            segment = r.segs[index * 8 : index * 8 + 1, :].astype(jnp.int32)
            r.hot[index * tok : (index + 1) * tok, :] = jnp.where(segment == kind, 1.0, 0.0).T.astype(BF)

    @piece(DYALL)
    def _():
        for step in range(place.pairs):
            dy_move.across_arrived(step)

    @piece(VROWS)
    def _():
        for index in range(dp_size):
            at = slice(index * LANES, (index + 1) * LANES)
            for row in range(6):
                r.rows[row : row + 1, at] = r.vec_all[index, row : row + 1, :]
            r.rows[6:7, at] = r.vec_all[index, pl.ds(9 + place.seq, 1), :]
        for index in range(each):
            for row in range(3):
                start = (index * 3 + row) * LANES
                r.rows[7:8, start : start + LANES] = r.vec_all[place.seq * each + index, 6 + row : 7 + row, :]

    chunk = 64

    def normalize(block):
        @pl.loop(0, tok // chunk)
        def _(step):
            here = pl.ds(pl.multiple_of(block * tok + step * chunk, chunk), chunk)
            values = r.x[here, :].astype(F32)
            mean = jnp.sum(values, axis=-1, keepdims=True) * (1.0 / D)
            center = values - mean
            rstd = lax.rsqrt(jnp.sum(center * center, axis=-1, keepdims=True) * (1.0 / D) + EPS)
            n = center * rstd
            r.normed1[here, :] = (n * r.rows[0:1, :] + r.rows[1:2, :]).astype(BF)
            r.normed2[here, :] = (n * r.rows[2:3, :] + r.rows[3:4, :]).astype(BF)
            lane = lanes_like((chunk, LANES))
            r.stat[here, :] = jnp.where(lane < HEAD_DIM, mean, rstd)

    def unit_rows(here):
        stat = r.stat[here, :]
        return (r.x[here, :].astype(F32) - stat[:, 0:1]) * stat[:, HEAD_DIM : HEAD_DIM + 1]

    @piece(LN0)
    def _():
        normalize(place.seq)

    @piece(LN1)
    def _():
        x_move.across_arrived(0)
        normalize(place.sibling)

    @piece(LN2)
    def _():
        normalize(place.pair_peer(1))

    @piece(LN3)
    def _():
        x_move.across_arrived(1)
        normalize(place.across_source(1))

    def swap(step):
        peer = place.seq_peer(step)
        src, dst = rows_at(r.w_proj_cols, peer, wide), columns_at(r.w_proj, place.seq, wide)
        return send(src, dst, r.m_swap, step, {"seq": peer})

    def swap_arrival(step):
        source = place.seq_peer(-step)
        src, dst = rows_at(r.w_proj_cols, source, wide), columns_at(r.w_proj, source, wide)
        return send(src, dst, r.m_swap, step, {"seq": place.seq_peer(step)})

    @piece(SWGO)
    def _():
        for step in range(1, seq_size):
            swap(step).start()
        columns_at(r.w_proj, place.seq, wide)[...] = rows_at(r.w_proj_cols, place.seq, wide)[...]

    @piece(SWIN)
    def _():
        for step in range(1, seq_size):
            swap_arrival(step).wait_recv()

    def mix_columns(first, last):
        @pl.loop(first, last)
        def _(block):
            here = tile_rows(block)
            mixed = nn(r.normed1[here, :], r.w_mix[...]) + r.rows[7:8, 0:mixed_wide]
            cosine, sine = r.cos[here, :], r.sin[here, :]
            lane = lanes_like((TILE, LANES))
            hot = r.hot[here, :].astype(F32)
            cold = jnp.where((lane >= HEAD_DIM) & (lane < HEAD_DIM + 4), (1.0 - hot) * NEG, 0.0)
            for head in range(heads_n):
                start = head * 3 * HEAD_DIM
                query = spin(head_part(mixed, start), cosine, sine) * HEAD_DIM**-0.5
                key = spin(head_part(mixed, start + HEAD_DIM), cosine, sine)
                value = head_part(mixed, start + 2 * HEAD_DIM)
                at = pl.ds(head * LANES, LANES)
                at_more = pl.ds((heads_n + head) * LANES, LANES)
                dims = pl.ds(head * HEAD_DIM, HEAD_DIM)
                r.qk[here, at] = jnp.where(lane < HEAD_DIM, query, hot).astype(BF)
                r.qk[here, at_more] = jnp.where(lane < HEAD_DIM, key, cold).astype(BF)
                r.vg[here, at] = jnp.where(lane < HEAD_DIM, value, 0.0).astype(BF)
                r.kt[dims, here] = key.T[:HEAD_DIM, :].astype(BF)
                r.vt[dims, here] = value.T[:HEAD_DIM, :].astype(BF)

    middle = blocks // 2
    piece(QKV0, 0, middle)(mix_columns)
    piece(QKV1, middle, blocks)(mix_columns)
    @piece(DH)
    def _():
        @pl.loop(0, blocks)
        def _(block):
            here = tile_rows(block)
            place_in = lax.broadcasted_iota(jnp.int32, (TILE, wide), 0) + block * TILE
            d_heads = jnp.where(place_in < length - r.pad[0], nt(r.dy[here, :], r.w_proj[...]), 0.0)
            for head in range(heads_n):
                at_more = pl.ds((heads_n + head) * LANES, LANES)
                r.vg[here, at_more] = head_part(d_heads, head * HEAD_DIM).astype(BF)

    second = heads_n * LANES
    head_refs = (
        r.qk.at[:, pl.ds(0, second)],
        r.qk.at[:, pl.ds(second, second)],
        r.vg.at[:, pl.ds(0, second)],
        r.vg.at[:, pl.ds(second, second)],
        r.kt,
        r.vt,
        r.s,
        r.p,
        r.ht,
        r.dqt,
        r.dk,
        r.dv,
    )

    def attend_blocks(head, first, last):
        for block in range(first, last):
            if block == 0:
                attend_head(head, block, head_refs)
            elif block == 1:
                attend_head(head, block, head_refs)
            elif block == 2:
                attend_head(head, block, head_refs)
            else:
                attend_head(head, block, head_refs)

    for head in range(heads_n):
        first = AT00 + head * (middle + 1)
        piece(first, head, 0, middle)(attend_blocks)
        for block in range(middle, blocks):
            piece(first + block - middle + 1, head, block, block + 1)(attend_blocks)

    def heads_back(first, last):
        @pl.loop(first, last)
        def _(block):
            here = tile_rows(block)
            place_in = lax.broadcasted_iota(jnp.int32, (TILE, wide), 0) + block * TILE
            r.attn[here, :] = jnp.where(place_in < length - r.pad[0], r.ht[:, here].T.astype(F32), 0.0).astype(BF)
            d_query = r.dqt[:, here].T.astype(F32)
            cosine, sine = r.cos[here, :], -r.sin[here, :]
            lane = lanes_like((TILE, LANES))
            parts = []
            for head in range(heads_n):
                parts.append(spin(head_part(d_query, head * HEAD_DIM), cosine, sine))
                parts.append(spin(r.dk[head, here, :], cosine, sine))
                parts.append(r.dv[head, here, :])
            for index in range(len(parts) // 2):
                tile = jnp.where(lane < HEAD_DIM, parts[2 * index], pltpu.roll(parts[2 * index + 1], HEAD_DIM, 1))
                at = slice(index * LANES, (index + 1) * LANES)
                tile = tile.astype(BF)
                r.d_mixed[here, at] = tile
                r.sums[6:7, at] += jnp.sum(tile.astype(F32), axis=0, keepdims=True)

    piece(POST0, 0, middle)(heads_back)
    piece(POST1, middle, blocks)(heads_back)
    big = 512

    def weight_grad(out_ref, left, right, index):
        at = pl.ds(index * big, big)
        out_ref[at, :] = tn(left[:, at], right[...]).astype(BF)

    for index in range(D // big):
        piece(GM0 + index, r.g_mix, r.normed1, r.d_mixed, index)(weight_grad)
        piece(GR0 + index, r.g_rise, r.normed2, r.d_up, index)(weight_grad)
        piece(GF0 + index, r.g_fall, r.active, r.dy, index)(weight_grad)

    @piece(GP)
    def _():
        gathers[PROJ].finish()
        for step in range(1, seq_size):
            swap(step).wait_send()
        grad = tn(r.attn[...], r.dy[...]).astype(BF)
        for index in range(seq_size):
            r.w_proj_cols[index * wide : (index + 1) * wide, :] = grad[:, index * wide : (index + 1) * wide]

    def swap_back(step):
        peer = place.seq_peer(step)
        src, dst = rows_at(r.w_proj_cols, peer, wide), rows_at(r.g_proj_cols, place.seq, wide)
        return send(src, dst, r.m_swap2, step, {"seq": peer})

    def swap_back_arrival(step):
        source = place.seq_peer(-step)
        src, dst = rows_at(r.w_proj_cols, source, wide), rows_at(r.g_proj_cols, source, wide)
        return send(src, dst, r.m_swap2, step, {"seq": place.seq_peer(step)})

    @piece(SBGO)
    def _():
        for step in range(1, seq_size):
            swap_back(step).start()
        rows_at(r.g_proj_cols, place.seq, wide)[...] = rows_at(r.w_proj_cols, place.seq, wide)[...]

    @piece(SBIN)
    def _():
        for step in range(1, seq_size):
            swap_back_arrival(step).wait_recv()

    def upward(block):
        here = tile_rows(block)
        up = nn(r.normed2[here, :], r.w_rise[...]) + r.rows[6:7, :]
        share = 0.5 + 0.5 * lax.erf(up * 0.5**0.5)
        r.active[here, :] = (up * share).astype(BF)
        bell = jnp.exp(-0.5 * up * up) * (2 * np.pi) ** -0.5
        r.d_up[here, :] = (share + up * bell).astype(BF)

    def downward(first, last):
        @pl.loop(first, last)
        def _(block):
            here = tile_rows(block)
            d_up = (r.d_up[here, :].astype(F32) * nt(r.dy[here, :], r.w_fall[...])).astype(BF)
            r.d_up[here, :] = d_up
            r.sums[5:6, :] += jnp.sum(d_up.astype(F32), axis=0, keepdims=True)

    for block in range(blocks):
        piece(UP0 + block, block)(upward)
    piece(DN0, 0, middle)(downward)
    piece(DN1, middle, blocks)(downward)

    def out_rows(step):
        first = ((place.pair + step) % place.pairs) * (2 * tok // TILE)
        @pl.loop(0, 2 * tok // TILE)
        def _(block):
            here = tile_rows(first + block)
            part = nn(r.attn[here, :], r.w_proj[...]) + nn(r.active[here, :], r.w_fall[...])
            r.out_part[here, :] = part.astype(BF)

        out.over_start(step)

    def back_rows(step):
        first = ((place.pair + step) % place.pairs) * (2 * tok // TILE)
        @pl.loop(0, 2 * tok // TILE)
        def _(block):
            here = tile_rows(first + block)
            d_one = nt(r.d_mixed[here, :], r.w_mix[...])
            d_two = nt(r.d_up[here, :], r.w_rise[...])
            r.back_part[here, :] = (r.rows[0:1, :] * d_one + r.rows[2:3, :] * d_two).astype(BF)
            n = unit_rows(here)
            r.sums[0:1, :] += jnp.sum(d_one * n, axis=0, keepdims=True)
            r.sums[1:2, :] += jnp.sum(d_one, axis=0, keepdims=True)
            r.sums[2:3, :] += jnp.sum(d_two * n, axis=0, keepdims=True)
            r.sums[3:4, :] += jnp.sum(d_two, axis=0, keepdims=True)
            r.sums[4:5, :] += jnp.sum(r.dy[here, :].astype(F32), axis=0, keepdims=True)

        back.over_start(step)

    for step in range(2):
        piece(OP0 + step, step)(out_rows)
        piece(BK0 + step, step)(back_rows)
        piece(OM0 + step, step)(out.over_add)
        piece(BM0 + step, step)(back.over_add)

    @piece(VP)
    def _():
        for index in range(dp_size):
            at = slice(index * LANES, (index + 1) * LANES)
            r.vec_part[index, 0:6, :] = r.sums[0:6, at]
            for row in range(mixed_wide // LANES):
                r.vec_part[index, 6 + row : 7 + row, :] = r.sums[6:7, row * LANES : (row + 1) * LANES]

    def settle(move, home):
        move.begin()
        leave(move.own, home.at[place.seq])

    def pass_on(move, home):
        move.forward()
        for step in range(1, place.pairs):
            source = place.pair_peer(-step)
            leave(move.full.at[source], home.at[source])

    def complete(move, home):
        for step in range(place.pairs):
            move.across_arrived(step)
            source = place.across_source(step)
            leave(move.full.at[source], home.at[source])

    for index, (move, home) in enumerate(zip(finals, homes, strict=True)):
        piece(SMA + index, move, home)(settle)
        piece(WMA + index, move, home)(pass_on)
        piece(CMA + index, move, home)(complete)

    mine = pl.ds(pl.multiple_of(place.seq * tok, tok), tok)

    @piece(BO)
    def _():
        total = out.total()
        block_out = total + r.x[mine, :].astype(F32) + (r.rows[4:5, :] + r.rows[5:6, :])
        r.out_cross[0] = block_out.astype(BF)
        leave(r.out_cross.at[0], r.block_out)

    @piece(IG)
    def _():
        scaled = back.total()
        n = unit_rows(mine)
        rstd = r.stat[mine, HEAD_DIM : HEAD_DIM + 1]
        back_mean = jnp.sum(scaled, axis=-1, keepdims=True) * (1.0 / D)
        back_n = jnp.sum(scaled * n, axis=-1, keepdims=True) * (1.0 / D)
        input_grad = r.dy[mine, :].astype(F32) + rstd * (scaled - back_mean - n * back_n)
        r.back_cross[0] = input_grad.astype(BF)
        leave(r.back_cross.at[0], r.input_grad)

    @piece(SV)
    def _():
        r.vec_fin[place.seq] = r.vec_part[place.dp]
        f_vec.begin()

    piece(WV)(f_vec.forward)

    @piece(VO)
    def _():
        f_vec.finish()
        norm = r.vec_fin[0, 0:4, :]
        for index in range(1, seq_size):
            norm = norm + r.vec_fin[index, 0:4, :]
        r.vec_out[0:4, :] = norm
        r.vec_out[4:5, :] = r.vec_fin[0, 4:5, :]
        source = r.vec_fin[place.dp // each]
        pick = place.dp % each
        part = source[6:9, :]
        for index in range(1, each):
            part = jnp.where(pick == index, source[6 + 3 * index : 9 + 3 * index, :], part)
        r.vec_out[5:8, :] = part
        for index in range(seq_size):
            r.vec_out[8 + index : 9 + index, :] = r.vec_fin[index, 5:6, :]
        leave(r.vec_out, r.vec_result)

    place.met_near()
    r.sums[...] = jnp.zeros(r.sums.shape, F32)
    r.vec_part[...] = jnp.zeros(r.vec_part.shape, F32)
    assert sorted(ORDER) == sorted(pieces)
    for name in ORDER:
        pieces[name]()
    for move in finals:
        move.sent()
    for copy in leaving:
        copy.wait()
    for move in (*gathers[:PROJ], *gathers[PROJ + 1 :], *reduces, out, back):
        move.finish()
    for move in (x_move, seg_move, dy_move):
        move.sent()
    for step in range(1, seq_size):
        swap_back(step).wait_send()


def resident_call(seq_size, dp_size, *args):
    tok = args[0].shape[0]
    length = tok * seq_size
    half, pairs = dp_size // 2, seq_size // 2
    wide = HEADS // seq_size * HEAD_DIM
    units_all = dp_size * LANES
    heads_n = wide // HEAD_DIM

    def half_vmem(*shape):
        return pltpu.VMEM(shape, BF)

    def full_vmem(*shape):
        return pltpu.VMEM(shape, F32)

    def ring(columns):
        return half_vmem(2, 2, half, HALF, columns)

    def pair_of_sems(count):
        return pltpu.SemaphoreType.DMA((2, 2, count))

    any_spec = pl.BlockSpec(memory_space=pl.ANY)
    vmem = pl.BlockSpec(memory_space=pltpu.VMEM)
    scratch = [
        pltpu.SMEM((1,), jnp.int32),
        full_vmem(length, LANES),
        full_vmem(length, LANES),
        half_vmem(length, D),
        half_vmem(length, D),
        half_vmem(length, LANES),
        full_vmem(seq_size * 8, tok),
        half_vmem(D, 3 * wide),
        half_vmem(D, wide),
        half_vmem(wide, D),
        half_vmem(D, units_all),
        half_vmem(units_all, D),
        full_vmem(dp_size, VEC_ROWS, LANES),
        full_vmem(8, D),
        half_vmem(length, D),
        half_vmem(length, D),
        full_vmem(length, LANES),
        half_vmem(length, units_all),
        half_vmem(length, units_all),
        half_vmem(wide, length),
        half_vmem(wide, length),
        full_vmem(length // TILE, TILE, TILE),
        full_vmem(length // TILE, TILE, TILE),
        half_vmem(wide, length),
        half_vmem(wide, length),
        full_vmem(heads_n, length, LANES),
        full_vmem(heads_n, length, LANES),
        half_vmem(length, wide),
        half_vmem(length, 3 * wide),
        half_vmem(length, D),
        half_vmem(length, D),
        half_vmem(length, units_all),
        half_vmem(length, units_all),
        half_vmem(D, 3 * wide),
        half_vmem(D, wide),
        half_vmem(D, units_all),
        half_vmem(units_all, D),
        ring(3 * wide),
        half_vmem(2, half, LANES, wide),
        ring(units_all),
        ring(D),
        half_vmem(pairs, tok, D),
        half_vmem(pairs - 1, tok, D),
        half_vmem(pairs, tok, D),
        half_vmem(pairs - 1, tok, D),
        full_vmem(8, D),
        full_vmem(dp_size, VEC_ROWS, LANES),
        full_vmem(2, half, VEC_ROWS, LANES),
        half_vmem(seq_size, LANES, 3 * wide),
        half_vmem(seq_size, LANES, wide),
        half_vmem(seq_size, LANES, units_all),
        half_vmem(seq_size, LANES, D),
        full_vmem(seq_size, VEC_ROWS, LANES),
        full_vmem(16, LANES),
    ]
    scratch += [sems_of(2 * pairs)] * 3 + [sems_of(2 * half)]
    scratch += [pair_of_sems(2 * half), sems_of(2 * half), pair_of_sems(2 * half), pair_of_sems(2 * half)]
    scratch += [sems_of(seq_size), pltpu.SemaphoreType.DMA((dp_size + 6,)), sems_of(seq_size)]
    scratch += [pair_of_sems(2 * half), sems_of(2 * half), pair_of_sems(2 * half), pair_of_sems(2 * half)]
    scratch += [sems_of(2 * pairs)] * 2 + [sems_of(2 * half)]
    scratch += [pair_of_sems(2 * pairs), sems_of(2 * pairs), pair_of_sems(2 * pairs), pair_of_sems(2 * pairs)]
    scratch += [sems_of(2 * pairs)]
    scratch += [pltpu.SemaphoreType.DMA((32,))]
    return pl.pallas_call(
        functools.partial(resident_kernel, seq_size, dp_size),
        out_shape=(
            jax.ShapeDtypeStruct((tok, D), BF),
            jax.ShapeDtypeStruct((tok, D), BF),
            jax.ShapeDtypeStruct((seq_size, LANES, 3 * wide), BF),
            jax.ShapeDtypeStruct((seq_size, LANES, wide), BF),
            jax.ShapeDtypeStruct((seq_size, LANES, units_all), BF),
            jax.ShapeDtypeStruct((seq_size, LANES, D), BF),
            jax.ShapeDtypeStruct((16, LANES), F32),
        ),
        in_specs=[any_spec] * 6 + [vmem] * 9 + [any_spec, vmem],
        out_specs=[any_spec] * 7,
        scratch_shapes=scratch,
        compiler_params=pltpu.CompilerParams(
            collective_id=2, has_side_effects=True, vmem_limit_bytes=RESIDENT_VMEM
        ),
    )(*args)


RESIDENT_VMEM = 63 * 2**20


def finish_kernel(seq_size, dp_size, *refs):
    (block, grad, mix, proj, rise, fall, vec), refs = refs[:7], refs[7:]
    (block_out, grad_out, mix_out, proj_out, rise_out, fall_out), refs = refs[:6], refs[6:]
    vec_outs, refs = refs[:8], refs[8:]
    (block_in, grad_in, mix_in, proj_in, rise_in, fall_in, vec_in, mix_f, proj_f, rise_f, fall_f), refs = refs[:11], refs[11:]
    vec_fs, (in_sems, out_sems) = refs[:8], refs[8:]
    parts = [(fall.at[group], fall_in.at[group]) for group in range(seq_size)]
    parts += [(rise, rise_in), (mix, mix_in), (proj, proj_in), (block, block_in), (grad, grad_in), (vec, vec_in)]
    coming = []
    for src, dst in parts:
        copy = pltpu.make_async_copy(src, dst, in_sems.at[len(coming)])
        copy.start()
        coming.append(copy)
    *fall_copies, rise_copy, mix_copy, proj_copy, block_copy, grad_copy, vec_copy = coming
    leaving = []

    def leave(src, dst):
        copy = pltpu.make_async_copy(src, dst, out_sems.at[len(leaving)])
        copy.start()
        leaving.append(copy)

    for group in range(seq_size):
        fall_copies[group].wait()
        at = pl.ds(group * LANES, LANES)
        fall_f[at, :] = fall_in[group].astype(F32)
        leave(fall_f.at[at], fall_out.at[at])
    few = 32
    rise_copy.wait()
    for start in range(0, LANES, few):
        at = pl.ds(start, few)
        for group in range(seq_size):
            for index in range(dp_size):
                column = (index * seq_size + group) * LANES
                rise_f[at, column : column + LANES] = rise_in[group, at, index * LANES : (index + 1) * LANES].astype(F32)
        leave(rise_f.at[at], rise_out.at[at])
    mix_copy.wait()
    proj_copy.wait()
    for start in range(0, LANES, 2 * few):
        at = pl.ds(start, 2 * few)
        for held, full, out in ((mix_in, mix_f, mix_out), (proj_in, proj_f, proj_out)):
            columns = held.shape[2]
            for group in range(seq_size):
                full[at, group * columns : (group + 1) * columns] = held[group, at, :].astype(F32)
            leave(full.at[at], out.at[at])
    block_copy.wait()
    leave(block_in, block_out)
    grad_copy.wait()
    leave(grad_in, grad_out)
    vec_copy.wait()
    for held, out, row in zip(vec_fs, vec_outs, (0, 1, 2, 3, 4, 4, 5, 8), strict=True):
        for start in range(0, out.shape[0], LANES):
            held[start : start + LANES] = vec_in[row + start // LANES]
        leave(held, out)
    for copy in leaving:
        copy.wait()


def finish_call(seq_size, dp_size, block, grad, mix, proj, rise, fall, vec):
    tok = block.shape[0]
    vec_sizes = (LANES,) * 6 + (3 * LANES, seq_size * LANES)
    full_sizes = ((LANES, 3 * D), (LANES, D), (LANES, FF), (seq_size * LANES, D))
    any_spec = pl.BlockSpec(memory_space=pl.ANY)
    return pl.pallas_call(
        functools.partial(finish_kernel, seq_size, dp_size),
        out_shape=(jax.ShapeDtypeStruct((tok, D), BF),) * 2
        + tuple(jax.ShapeDtypeStruct(size, F32) for size in full_sizes)
        + tuple(jax.ShapeDtypeStruct((size,), F32) for size in vec_sizes),
        in_specs=[any_spec] * 7,
        out_specs=[any_spec] * 14,
        scratch_shapes=[pltpu.VMEM(array.shape, array.dtype) for array in (block, grad, mix, proj, rise, fall, vec)]
        + [pltpu.VMEM(size, F32) for size in full_sizes]
        + [pltpu.VMEM((size,), F32) for size in vec_sizes]
        + [pltpu.SemaphoreType.DMA((seq_size + 6,)), pltpu.SemaphoreType.DMA((24,))],
        compiler_params=pltpu.CompilerParams(vmem_limit_bytes=RESIDENT_VMEM),
    )(block, grad, mix, proj, rise, fall, vec)


def resident_tables():
    half = ROT // 2
    frequency = BASE ** (-np.arange(0, ROT, 2).astype(np.float32) / np.float32(ROT))
    lanes = np.zeros((LANES,), np.float64)
    lanes[:half] = lanes[half:ROT] = frequency.astype(np.float32)
    sign = np.where(np.arange(LANES) < half, -1.0, 1.0)
    steps = np.arange(TURN, dtype=np.float64)[:, None]
    tables = [f for scale in (TURN, 1) for f in (np.cos(steps * scale * lanes), sign * np.sin(steps * scale * lanes))]
    return jnp.asarray(np.concatenate(tables).astype(np.float32))


def resident_shards(
    tokens,
    cotangent,
    norm1_gain,
    norm1_bias,
    norm2_gain,
    norm2_bias,
    qkv_weight,
    qkv_bias,
    out_weight,
    out_bias,
    up_weight,
    up_bias,
    down_weight,
    down_bias,
    segment_ids,
    pad_length,
):
    seq_size, dp_size = lax.axis_size("seq"), lax.axis_size("dp")
    tok = tokens.shape[1]
    vectors = (norm1_gain, norm1_bias, norm2_gain, norm2_bias, out_bias, down_bias, qkv_bias, up_bias)
    parts = resident_call(
        seq_size,
        dp_size,
        tokens[0],
        cotangent[0],
        qkv_weight,
        out_weight,
        up_weight,
        down_weight,
        *(vector.reshape(-1, LANES) for vector in vectors),
        segment_ids,
        pad_length,
        resident_tables(),
    )
    done = finish_call(seq_size, dp_size, *parts)
    block_out, input_grad, g_mix, g_proj, g_rise, g_fall = done[:6]
    norm1_g, norm1_b, norm2_g, norm2_b, out_b, down_b, b_mix, b_rise = done[6:]
    return (
        block_out[None],
        input_grad[None],
        norm1_g,
        norm1_b,
        norm2_g,
        norm2_b,
        g_mix,
        b_mix,
        g_proj,
        out_b,
        g_rise,
        b_rise,
        g_fall,
        down_b,
    )


def streamed_shards(
    tokens,
    cotangent,
    norm1_gain,
    norm1_bias,
    norm2_gain,
    norm2_bias,
    qkv_weight,
    qkv_bias,
    out_weight,
    out_bias,
    up_weight,
    up_bias,
    down_weight,
    down_bias,
    segment_ids,
    pad_length,
):
    seq_size, dp_size = lax.axis_size("seq"), lax.axis_size("dp")
    seq = lax.axis_index("seq")
    dp = lax.axis_index("dp")
    tok = tokens.shape[1]
    length = tok * seq_size
    heads_n = HEADS // seq_size
    rows = D // dp_size
    wide = heads_n * HEAD_DIM
    units = FF // dp_size // seq_size

    mix = qkv_weight.reshape(rows, seq_size, heads_n, 3, HEAD_DIM)
    mix = lax.dynamic_index_in_dim(mix, seq, 1, keepdims=False)
    mix = mix.transpose(0, 2, 1, 3).reshape(rows, 3 * wide)
    proj = lax.dynamic_slice_in_dim(out_weight, seq * wide, wide, 1)
    rise = up_weight.reshape(rows, dp_size, seq_size, units)
    rise = lax.dynamic_index_in_dim(rise, seq, 2, keepdims=False).reshape(rows, dp_size * units)
    fall = lax.dynamic_slice_in_dim(down_weight, seq * units, units, 0)
    vec = jnp.concatenate(
        [norm1_gain, norm1_bias, norm2_gain, norm2_bias, out_bias, down_bias, qkv_bias, up_bias]
    )
    vec_len = vec.shape[0]
    vec = jnp.pad(vec, (0, 2048 - vec_len)).reshape(16, 128)
    seg = jnp.broadcast_to(segment_ids, (8, tok))
    x_all, dy_all, w_mix, _, w_rise, w_fall, vec_all, seg_all, w_proj = gather_all(
        seq_size, dp_size, tokens[0], cotangent[0], mix, proj, rise, fall, vec, seg
    )
    x = x_all.reshape(length, D).astype(F32)
    dy = dy_all.reshape(length, D)
    w_mix = w_mix.reshape(D, 3 * wide)
    w_rise = w_rise.reshape(D, dp_size * units)
    w_fall = w_fall.reshape(dp_size * units, D)
    w_proj = w_proj.reshape(seq_size, wide, wide).transpose(1, 0, 2).reshape(wide, D)
    segments = seg_all[:, 0, :].reshape(length)
    vec_all = vec_all.reshape(dp_size, 2048)[:, :vec_len].astype(F32)
    g1, s1, g2, s2, b_proj, b_fall = (
        vec_all[:, i * rows : (i + 1) * rows].reshape(D) for i in range(6)
    )
    b_mix = vec_all[:, 6 * rows : 9 * rows].reshape(seq_size, heads_n, 3, HEAD_DIM)
    b_mix = lax.dynamic_index_in_dim(b_mix, seq, 0, keepdims=False)
    b_mix = b_mix.transpose(1, 0, 2).reshape(3 * wide)
    b_rise = vec_all[:, 9 * rows :].reshape(dp_size, seq_size, units)
    b_rise = lax.dynamic_index_in_dim(b_rise, seq, 1, keepdims=False).reshape(dp_size * units)

    center = x - jnp.mean(x, axis=-1, keepdims=True)
    rstd = lax.rsqrt(jnp.mean(center * center, axis=-1, keepdims=True) + EPS)
    n = center * rstd
    normed1 = (n * g1 + s1).astype(BF)
    normed2 = (n * g2 + s2).astype(BF)
    valid = (jnp.arange(length, dtype=jnp.int32) < length - pad_length[0]).astype(F32)[:, None]
    cosine, sine = (jnp.asarray(t) for t in angle_tables(length))

    mixed = dot(normed1, w_mix) + b_mix
    mixed = mixed.reshape(length, 3, heads_n, HEAD_DIM).transpose(1, 2, 0, 3)
    queries = turn(mixed[0], cosine, sine, 1.0).astype(BF)
    keys = turn(mixed[1], cosine, sine, 1.0).astype(BF)
    values = mixed[2].astype(BF)
    d_heads = (dot_nt(dy, w_proj) * valid).astype(BF)
    d_heads = d_heads.reshape(length, heads_n, HEAD_DIM).transpose(1, 0, 2)
    heads, d_q, d_k, d_v = attention(queries, keys, values, d_heads, segments)
    attn_rows = (heads.transpose(1, 0, 2).reshape(length, wide).astype(F32) * valid).astype(BF)
    d_mixed = jnp.stack(
        [
            turn(d_q.astype(F32), cosine, sine, -1.0).astype(BF),
            turn(d_k.astype(F32), cosine, sine, -1.0).astype(BF),
            d_v,
        ]
    )
    d_mixed = d_mixed.transpose(2, 0, 1, 3).reshape(length, 3 * wide)

    upward = dot(normed2, w_rise) + b_rise
    active = jax.nn.gelu(upward, approximate=False).astype(BF)
    slope = 0.5 * (1 + lax.erf(upward * (0.5**0.5))) + upward * jnp.exp(
        -0.5 * upward * upward
    ) * ((2 * np.pi) ** -0.5)
    d_up = (slope * dot_nt(dy, w_fall)).astype(BF)
    out_part = (dot(attn_rows, w_proj) + dot(active, w_fall)).astype(BF)
    d_n1 = dot_nt(d_mixed, w_mix)
    d_n2 = dot_nt(d_up, w_rise)
    back_part = (g1 * d_n1 + g2 * d_n2).astype(BF)

    g_mix = dot_t(normed1, d_mixed).astype(BF).reshape(dp_size, rows, 3 * wide)
    g_proj = dot_t(attn_rows, dy).astype(BF).reshape(dp_size // seq_size, rows, seq_size, wide)
    g_proj = g_proj.transpose(2, 0, 1, 3)
    g_rise = dot_t(normed2, d_up).astype(BF).reshape(dp_size, rows, dp_size * units)
    g_fall = dot_t(active, dy).astype(BF).reshape(dp_size, units, D)
    dyf = dy.astype(F32)
    vec_part = jnp.concatenate(
        [
            t.reshape(dp_size, -1)
            for t in (
                jnp.sum(d_n1 * n, axis=0),
                jnp.sum(d_n1, axis=0),
                jnp.sum(d_n2 * n, axis=0),
                jnp.sum(d_n2, axis=0),
                jnp.sum(dyf, axis=0),
                jnp.sum(d_up.astype(F32), axis=0),
            )
        ]
        + [jnp.broadcast_to(jnp.sum(d_mixed.astype(F32), axis=0)[None], (dp_size, 3 * wide))],
        axis=1,
    )
    part_len = vec_part.shape[1]
    vec_part = jnp.pad(vec_part, ((0, 0), (0, 2048 - part_len))).reshape(dp_size, 16, 128)
    out_sum, back_sum, f_mix, f_proj, f_rise, f_fall, f_vec = reduce_all(
        seq_size,
        dp_size,
        out_part.reshape(seq_size, tok, D),
        back_part.reshape(seq_size, tok, D),
        g_mix,
        g_proj,
        g_rise,
        g_fall,
        vec_part,
    )
    own_x = tokens[0].astype(F32)
    block_output = (own_x + out_sum + b_proj + b_fall).astype(BF)
    own_center = own_x - jnp.mean(own_x, axis=-1, keepdims=True)
    own_rstd = lax.rsqrt(jnp.mean(own_center * own_center, axis=-1, keepdims=True) + EPS)
    own_n = own_center * own_rstd
    back = own_rstd * (
        back_sum
        - jnp.mean(back_sum, axis=-1, keepdims=True)
        - own_n * jnp.mean(back_sum * own_n, axis=-1, keepdims=True)
    )
    input_grad = (cotangent[0].astype(F32) + back).astype(BF)
    f_mix = f_mix.reshape(seq_size, rows, 3, heads_n, HEAD_DIM)
    f_mix = f_mix.transpose(1, 0, 3, 2, 4).reshape(rows, 3 * D).astype(F32)
    f_proj = f_proj.transpose(1, 0, 2).reshape(rows, D).astype(F32)
    f_rise = f_rise.reshape(seq_size, rows, dp_size, units)
    f_rise = f_rise.transpose(1, 2, 0, 3).reshape(rows, FF).astype(F32)
    f_fall = f_fall.reshape(seq_size * units, D).astype(F32)
    f_vec = f_vec.reshape(seq_size, 2048)[:, :part_len]
    norm_sums = jnp.sum(f_vec[:, : 4 * rows], axis=0)
    column = f_vec[0, 4 * rows : 5 * rows]
    f_b_rise = f_vec[:, 5 * rows : 5 * rows + units].reshape(seq_size * units)
    f_b_mix = f_vec[:, 5 * rows + units :].reshape(seq_size, 3, heads_n, HEAD_DIM)
    f_b_mix = f_b_mix.transpose(0, 2, 1, 3).reshape(dp_size, 3 * rows)
    f_b_mix = lax.dynamic_index_in_dim(f_b_mix, dp, 0, keepdims=False)
    return (
        block_output[None],
        input_grad[None],
        norm_sums[:rows],
        norm_sums[rows : 2 * rows],
        norm_sums[2 * rows : 3 * rows],
        norm_sums[3 * rows :],
        f_mix,
        f_b_mix,
        f_proj,
        column,
        f_rise,
        f_b_rise,
        f_fall,
        column,
    )


def shards(*args):
    seq_size, dp_size = lax.axis_size("seq"), lax.axis_size("dp")
    if resident_fits(seq_size, dp_size, args[0].shape[1]):
        return resident_shards(*args)
    return streamed_shards(*args)


def solution(mesh):
    rows = P("dp", "seq", None)
    weight = P("dp", None)
    vector = P("dp")
    return jax.shard_map(
        shards,
        mesh=mesh,
        in_specs=(rows, rows)
        + (vector,) * 4
        + (weight, vector) * 4
        + (P("dp", "seq"), vector),
        out_specs=(rows, rows) + (vector,) * 4 + (weight, vector) * 4,
        check_vma=False,
    )
```

```python
import functools
import typing

import jax
import jax.numpy as jnp
import numpy as np
from jax import lax
from jax.experimental import pallas as pl
from jax.experimental.pallas import tpu as pltpu
from jax.sharding import PartitionSpec as P

D = 1024
HEADS = 16
HEAD_DIM = 64
ROT = 16
FF = 4096
EPS = 1e-05
BASE = 10000.0
NEG = -1e30
MESH = pl.DeviceIdType.MESH
BF = jnp.bfloat16
F32 = jnp.float32


def ring_pos(dev, size):
    return (dev // 2) * (1 - dev % 2) + (size - 1 - dev // 2) * (dev % 2)


def ring_dev(pos, size):
    high = pos // (size // 2)
    return (1 - high) * 2 * pos + high * (2 * (size - 1 - pos) + 1)


class Place:
    def __init__(self, seq_size, dp_size):
        self.seq_size, self.dp_size = seq_size, dp_size
        self.seq = lax.axis_index("seq")
        self.dp = lax.axis_index("dp")
        self.pos = ring_pos(self.dp, dp_size)
        self.half = dp_size // 2
        self.pairs = seq_size // 2
        self.core = self.seq % 2
        self.pair = self.seq // 2
        self.sibling = self.pair * 2 + 1 - self.core

    def ring(self, offset):
        return ring_dev((self.pos + offset + self.dp_size) % self.dp_size, self.dp_size)

    def dp_peer(self, step):
        return (self.dp + step + self.dp_size) % self.dp_size

    def pair_peer(self, step):
        return ((self.pair + step + self.pairs) % self.pairs) * 2 + self.core

    def across_source(self, step):
        return ((self.pair - step + self.pairs) % self.pairs) * 2 + 1 - self.core

    def seq_peer(self, step):
        return (self.seq + step + self.seq_size) % self.seq_size

    def greet_near(self):
        barrier = pltpu.get_barrier_semaphore()
        for step in (1, -1):
            pl.semaphore_signal(barrier, inc=1, device_id={"dp": self.ring(step)}, device_id_type=MESH)
        for step in range(1, self.seq_size):
            pl.semaphore_signal(
                barrier, inc=1, device_id={"seq": self.seq_peer(step)}, device_id_type=MESH
            )

    def met_near(self):
        pl.semaphore_wait(pltpu.get_barrier_semaphore(), 2 + self.seq_size - 1)

    def greet(self):
        barrier = pltpu.get_barrier_semaphore()
        for step in range(1, self.dp_size):
            pl.semaphore_signal(
                barrier, inc=1, device_id={"dp": self.dp_peer(step)}, device_id_type=MESH
            )
        for step in range(1, self.seq_size):
            pl.semaphore_signal(
                barrier, inc=1, device_id={"seq": self.seq_peer(step)}, device_id_type=MESH
            )
        pl.semaphore_wait(barrier, self.dp_size - 1 + self.seq_size - 1)


def send(src, dst, sems, index, target):
    return pltpu.make_async_remote_copy(
        src_ref=src,
        dst_ref=dst,
        send_sem=sems.at[0, index],
        recv_sem=sems.at[1, index],
        device_id=target,
        device_id_type=MESH,
    )


def halves(ref):
    rows = ref.shape[0]
    columns = ref.shape[1]
    if rows % (32 if ref.dtype == BF else 16) == 0:
        return ref.at[pl.ds(0, rows // 2)], ref.at[pl.ds(rows // 2, rows // 2)]
    return ref.at[:, pl.ds(0, columns // 2)], ref.at[:, pl.ds(columns // 2, columns // 2)]


class RingGather:
    def __init__(self, place, full, sems):
        self.place, self.full, self.sems = place, full, sems

    def piece(self, offset, step, way):
        block = self.full.at[self.place.ring(offset)]
        return block if step < self.place.half else halves(block)[way]

    def copies(self, step):
        place = self.place
        right = self.piece(-(step - 1), step, 0)
        left = self.piece(step - 1, step, 1)
        index = 2 * (step - 1)
        return (
            send(right, right, self.sems, index, {"dp": place.ring(1)}),
            send(left, left, self.sems, index + 1, {"dp": place.ring(-1)}),
        )

    def arrivals(self, step):
        right = self.piece(-step, step, 0)
        left = self.piece(step, step, 1)
        index = 2 * (step - 1)
        return (
            send(right, right, self.sems, index, {"dp": self.place.ring(1)}),
            send(left, left, self.sems, index + 1, {"dp": self.place.ring(-1)}),
        )

    def tick(self, step):
        if step > 1:
            for copy in self.arrivals(step - 1):
                copy.wait_recv()
        if step <= self.place.half:
            for copy in self.copies(step):
                copy.start()

    def finish(self):
        for step in range(1, self.place.half + 1):
            for copy in self.copies(step):
                copy.wait_send()


class RingReduce:
    def __init__(self, place, parts, arrived, sems):
        self.place, self.parts, self.arrived, self.sems = place, parts, arrived, sems

    def piece(self, ref, step, way):
        return ref if step > 1 else halves(ref)[way]

    def copies(self, step):
        place = self.place
        away = place.half - step + 1
        index = 2 * (step - 1)
        out = []
        for way, (offset, target) in enumerate(((away, 1), (-away, -1))):
            src = self.piece(self.parts.at[place.ring(offset)], step, way)
            dst = self.piece(self.arrived.at[way, step - 1], step, way)
            out.append(send(src, dst, self.sems, index + way, {"dp": place.ring(target)}))
        return out

    def tick(self, step):
        place = self.place
        if step > 1:
            for way, copy in enumerate(self.copies(step - 1)):
                copy.wait_recv()
                away = (place.half - step + 1) * (1 - 2 * way)
                held = self.piece(self.parts.at[place.ring(away)], step - 1, way)
                came = self.piece(self.arrived.at[way, step - 2], step - 1, way)
                held[...] = (held[...].astype(F32) + came[...].astype(F32)).astype(held.dtype)
        if step <= place.half:
            for copy in self.copies(step):
                copy.start()

    def finish(self):
        for step in range(1, self.place.half + 1):
            for copy in self.copies(step):
                copy.wait_send()

    def own(self):
        return self.parts.at[self.place.dp]


class SeqGather:
    def __init__(self, place, full, sems, own=None):
        self.place, self.full, self.sems = place, full, sems
        self.own = full.at[place.seq] if own is None else own

    def direct(self, step):
        place = self.place
        target = {"seq": place.pair_peer(step)}
        return send(self.own, self.full.at[place.seq], self.sems, step, target)

    def arrival(self, step):
        place = self.place
        target = {"seq": place.pair_peer(step)}
        return send(self.own, self.full.at[place.pair_peer(-step)], self.sems, step, target)

    def across(self, step):
        place = self.place
        block = self.full.at[place.pair_peer(-step)]
        src = self.own if step == 0 else block
        return send(src, block, self.sems, place.pairs + step, {"seq": place.sibling})

    def across_arrival(self, step):
        place = self.place
        block = self.full.at[place.across_source(step)]
        return send(self.own, block, self.sems, place.pairs + step, {"seq": place.sibling})

    def begin(self):
        for step in range(1, self.place.pairs):
            self.direct(step).start()
        self.across(0).start()

    def forward(self):
        for step in range(1, self.place.pairs):
            self.arrival(step).wait_recv()
            self.across(step).start()

    def across_arrived(self, step):
        self.across_arrival(step).wait_recv()

    def sent(self):
        for step in range(1, self.place.pairs):
            self.direct(step).wait_send()
        for step in range(self.place.pairs):
            self.across(step).wait_send()

    def finish(self):
        for step in range(self.place.pairs):
            self.across_arrived(step)
        self.sent()


class SeqReduce:
    def __init__(self, place, parts, crossed, arrived, sems):
        self.place, self.parts, self.crossed, self.arrived = place, parts, crossed, arrived
        self.sems = sems

    def over(self, step):
        place = self.place
        index = (place.pair + step) % place.pairs
        src = self.parts.at[index * 2 + 1 - place.core]
        return send(src, self.crossed.at[index], self.sems, step, {"seq": place.sibling})

    def direct(self, step):
        place = self.place
        return send(
            self.parts.at[place.pair_peer(step)],
            self.arrived.at[step - 1],
            self.sems,
            place.pairs + step,
            {"seq": place.pair_peer(step)},
        )

    def over_start(self, step):
        self.over(step).start()

    def over_add(self, step):
        place = self.place
        index = (place.pair + step) % place.pairs
        self.over(step).wait_recv()
        held = self.parts.at[index * 2 + place.core]
        held[...] = (held[...].astype(F32) + self.crossed[index].astype(F32)).astype(held.dtype)
        if step > 0:
            self.direct(step).start()

    def begin(self):
        for step in range(self.place.pairs):
            self.over_start(step)

    def middle(self):
        for step in range(self.place.pairs):
            self.over_add(step)

    def total(self):
        place = self.place
        total = self.parts.at[place.seq][...].astype(F32)
        for step in range(1, place.pairs):
            self.direct(step).wait_recv()
            total = total + self.arrived[step - 1].astype(F32)
        return total

    def finish(self):
        for step in range(self.place.pairs):
            self.over(step).wait_send()
        for step in range(1, self.place.pairs):
            self.direct(step).wait_send()


class DpSpread:
    def __init__(self, place, src_of, full, sems):
        self.place, self.src_of, self.full, self.sems = place, src_of, full, sems

    def copy(self, step):
        place = self.place
        peer = place.dp_peer(step)
        return send(self.src_of(peer), self.full.at[place.dp], self.sems, step, {"dp": peer})

    def arrival(self, step):
        place = self.place
        source = place.dp_peer(-step)
        return send(
            self.src_of(source), self.full.at[source], self.sems, step, {"dp": place.dp_peer(step)}
        )

    def begin(self):
        for step in range(1, self.place.dp_size):
            self.copy(step).start()

    def finish(self):
        for step in range(1, self.place.dp_size):
            self.arrival(step).wait_recv()
        for step in range(1, self.place.dp_size):
            self.copy(step).wait_send()


def sems_of(count):
    return pltpu.SemaphoreType.DMA((2, count))


def gather_kernel(seq_size, dp_size, *refs):
    (x_ref, dy_ref, mix_ref, proj_ref, rise_ref, fall_ref, vec_ref, seg_ref) = refs[:8]
    (x_all, dy_all, mix_all, proj_cols, rise_all, fall_all, vec_all, seg_all, proj_all) = refs[8:17]
    (x_sems, dy_sems, mix_sems, proj_sems, rise_sems, fall_sems, vec_sems, seg_sems, swap_sems, own_sems) = refs[17:]
    place = Place(seq_size, dp_size)
    own = [
        pltpu.make_async_copy(src, dst, own_sems.at[i])
        for i, (src, dst) in enumerate(
            (
                (x_ref, x_all.at[place.seq]),
                (dy_ref, dy_all.at[place.seq]),
                (mix_ref, mix_all.at[place.dp]),
                (proj_ref, proj_cols.at[place.dp]),
                (rise_ref, rise_all.at[place.dp]),
                (fall_ref, fall_all.at[place.dp]),
                (vec_ref, vec_all.at[place.dp]),
                (seg_ref, seg_all.at[place.seq]),
            )
        )
    ]
    for copy in own:
        copy.start()
    place.greet()
    for copy in own:
        copy.wait()
    x_move = SeqGather(place, x_all, x_sems)
    dy_move = SeqGather(place, dy_all, dy_sems)
    seg_move = SeqGather(place, seg_all, seg_sems)
    vec_move = DpSpread(place, lambda peer: vec_ref, vec_all, vec_sems)
    mix_move = RingGather(place, mix_all, mix_sems)
    proj_move = RingGather(place, proj_cols, proj_sems)
    rise_move = RingGather(place, rise_all, rise_sems)
    fall_move = RingGather(place, fall_all, fall_sems)
    x_move.begin()
    seg_move.begin()
    vec_move.begin()
    half = place.half
    for step in range(1, half + 1):
        mix_move.tick(step)
        proj_move.tick(step)
    x_move.forward()
    seg_move.forward()
    dy_move.begin()
    mix_move.tick(half + 1)
    proj_move.tick(half + 1)
    rise_move.tick(1)
    fall_move.tick(1)
    rows = proj_cols.shape[0] * proj_cols.shape[1] // seq_size
    each = rows // proj_cols.shape[1]
    swaps = []
    for step in range(1, seq_size):
        peer = place.seq_peer(step)
        swaps.append(
            send(
                proj_cols.at[pl.ds(peer * each, each)],
                proj_all.at[place.seq],
                swap_sems,
                step,
                {"seq": peer},
            )
        )
    for copy in swaps:
        copy.start()
    mine = pltpu.make_async_copy(
        proj_cols.at[pl.ds(place.seq * each, each)], proj_all.at[place.seq], own_sems.at[0]
    )
    mine.start()
    for step in range(2, half + 2):
        rise_move.tick(step)
        fall_move.tick(step)
        if step == 3:
            dy_move.forward()
    mine.wait()
    for step in range(1, seq_size):
        source = place.seq_peer(-step)
        send(
            proj_cols.at[pl.ds(source * each, each)],
            proj_all.at[source],
            swap_sems,
            step,
            {"seq": place.seq_peer(step)},
        ).wait_recv()
    for copy in swaps:
        copy.wait_send()
    for move in (x_move, dy_move, seg_move, vec_move, mix_move, proj_move, rise_move, fall_move):
        move.finish()


def gather_all(seq_size, dp_size, x, dy, mix, proj, rise, fall, vec, seg):
    half = dp_size // 2
    pairs = seq_size // 2

    def lead(count, like):
        return jax.ShapeDtypeStruct((count,) + like.shape, like.dtype)

    each = dp_size // seq_size
    any_spec = pl.BlockSpec(memory_space=pl.ANY)
    return pl.pallas_call(
        functools.partial(gather_kernel, seq_size, dp_size),
        out_shape=(
            lead(seq_size, x),
            lead(seq_size, dy),
            lead(dp_size, mix),
            lead(dp_size, proj),
            lead(dp_size, rise),
            lead(dp_size, fall),
            lead(dp_size, vec),
            lead(seq_size, seg),
            jax.ShapeDtypeStruct((seq_size, each) + proj.shape, proj.dtype),
        ),
        in_specs=[any_spec] * 8,
        out_specs=[any_spec] * 9,
        scratch_shapes=[
            sems_of(2 * pairs),
            sems_of(2 * pairs),
            sems_of(2 * half),
            sems_of(2 * half),
            sems_of(2 * half),
            sems_of(2 * half),
            sems_of(dp_size),
            sems_of(2 * pairs),
            sems_of(seq_size),
            pltpu.SemaphoreType.DMA((8,)),
        ],
        compiler_params=pltpu.CompilerParams(collective_id=0, has_side_effects=True),
    )(x, dy, mix, proj, rise, fall, vec, seg)


def reduce_kernel(seq_size, dp_size, *refs):
    (out_ref, back_ref, mix_ref, proj_ref, rise_ref, fall_ref, vec_ref), refs = refs[:7], refs[7:]
    (out_sum, back_sum, mix_fin, proj_fin, rise_fin, fall_fin, vec_fin), refs = refs[:7], refs[7:]
    (
        out_cross,
        out_came,
        back_cross,
        back_came,
        proj_full,
        mix_came,
        proj_came,
        rise_came,
        fall_came,
        vec_came,
        out_sems,
        back_sems,
        swap_sems,
        mix_sems,
        proj_sems,
        rise_sems,
        fall_sems,
        vec_sems,
        mix_fs,
        proj_fs,
        rise_fs,
        fall_fs,
        vec_fs,
    ) = refs
    place = Place(seq_size, dp_size)
    each = dp_size // seq_size
    half = place.half
    place.greet()

    def mine(index):
        return proj_full.at[pl.ds(index * each, each)]

    def swap(step):
        peer = place.seq_peer(step)
        return send(proj_ref.at[peer], mine(place.seq), swap_sems, step, {"seq": peer})

    def swap_arrival(step):
        source = place.seq_peer(-step)
        target = {"seq": place.seq_peer(step)}
        return send(proj_ref.at[source], mine(source), swap_sems, step, target)

    for step in range(1, seq_size):
        swap(step).start()
    mine(place.seq)[...] = proj_ref[place.seq]
    mix = RingReduce(place, mix_ref, mix_came, mix_sems)
    proj = RingReduce(place, proj_full, proj_came, proj_sems)
    rise = RingReduce(place, rise_ref, rise_came, rise_sems)
    fall = RingReduce(place, fall_ref, fall_came, fall_sems)
    out = SeqReduce(place, out_ref, out_cross, out_came, out_sems)
    back = SeqReduce(place, back_ref, back_cross, back_came, back_sems)
    vec = DpSpread(place, lambda peer: vec_ref.at[peer], vec_came, vec_sems)
    mix.tick(1)
    rise.tick(1)
    out.begin()
    back.begin()
    vec.begin()
    for step in range(1, seq_size):
        swap_arrival(step).wait_recv()
    proj.tick(1)
    fall.tick(1)
    out.middle()
    back.middle()
    for step in range(2, half + 2):
        for move in (mix, rise, proj, fall):
            move.tick(step)
    finals = []
    for move, fin, fin_sems in (
        (mix, mix_fin, mix_fs),
        (rise, rise_fin, rise_fs),
        (proj, proj_fin, proj_fs),
        (fall, fall_fin, fall_fs),
    ):
        fin[place.seq] = move.parts[place.dp]
        gather = SeqGather(place, fin, fin_sems)
        gather.begin()
        finals.append(gather)
    vec_came[place.dp] = vec_ref[place.dp]
    vec.finish()
    vec_fin[place.seq] = jnp.sum(vec_came[...], axis=0)
    gather = SeqGather(place, vec_fin, vec_fs)
    gather.begin()
    finals.append(gather)
    out_sum[...] = out.total()
    back_sum[...] = back.total()
    for gather in finals:
        gather.forward()
    for gather in finals:
        gather.finish()
    for step in range(1, seq_size):
        swap(step).wait_send()
    for move in (mix, rise, proj, fall, out, back):
        move.finish()


def reduce_all(seq_size, dp_size, out, back, mix, proj, rise, fall, vec):
    half = dp_size // 2
    pairs = seq_size // 2
    each = dp_size // seq_size

    def fin(like):
        return jax.ShapeDtypeStruct((seq_size,) + like.shape[1:], like.dtype)

    def came(like):
        return pltpu.VMEM((2, half) + like.shape[1:], like.dtype)

    proj_blocks = jax.ShapeDtypeStruct((dp_size,) + proj.shape[2:], proj.dtype)
    vmem = pl.BlockSpec(memory_space=pltpu.VMEM)
    return pl.pallas_call(
        functools.partial(reduce_kernel, seq_size, dp_size),
        out_shape=(
            jax.ShapeDtypeStruct(out.shape[1:], F32),
            jax.ShapeDtypeStruct(back.shape[1:], F32),
            fin(mix),
            fin(proj_blocks),
            fin(rise),
            fin(fall),
            fin(vec),
        ),
        in_specs=[vmem] * 7,
        out_specs=[vmem] * 7,
        scratch_shapes=[
            pltpu.VMEM((pairs,) + out.shape[1:], BF),
            pltpu.VMEM((pairs,) + out.shape[1:], BF),
            pltpu.VMEM((pairs,) + back.shape[1:], BF),
            pltpu.VMEM((pairs,) + back.shape[1:], BF),
            pltpu.VMEM(proj_blocks.shape, BF),
            came(mix),
            came(proj_blocks),
            came(rise),
            came(fall),
            pltpu.VMEM(vec.shape, F32),
            sems_of(2 * pairs),
            sems_of(2 * pairs),
            sems_of(seq_size),
            sems_of(2 * half),
            sems_of(2 * half),
            sems_of(2 * half),
            sems_of(2 * half),
            sems_of(dp_size),
            sems_of(2 * pairs),
            sems_of(2 * pairs),
            sems_of(2 * pairs),
            sems_of(2 * pairs),
            sems_of(2 * pairs),
        ],
        compiler_params=pltpu.CompilerParams(
            collective_id=1, has_side_effects=True, vmem_limit_bytes=56 * 2**20
        ),
    )(out, back, mix, proj, rise, fall, vec)


def angle_tables(length):
    frequency = BASE ** (-np.arange(0, ROT, 2).astype(np.float32) / np.float32(ROT))
    angles = np.arange(length, dtype=np.float32)[:, None] * frequency.astype(np.float32)[None, :]
    return np.cos(angles).astype(np.float32), np.sin(angles).astype(np.float32)


def turn(piece, cosine, sine, sign):
    half = ROT // 2
    low, high = piece[..., :half], piece[..., half:ROT]
    return jnp.concatenate(
        [low * cosine - sign * high * sine, high * cosine + sign * low * sine, piece[..., ROT:]],
        axis=-1,
    )


TILE = 256

def mm(a, b, dims):
    return lax.dot_general(a, b, ((dims[0], dims[1]), ((), ())), preferred_element_type=F32)

def nn(a, b):
    return mm(a, b, ((1,), (0,)))

def nt(a, b):
    return mm(a, b, ((1,), (1,)))

def tn(a, b):
    return mm(a, b, ((0,), (0,)))

def fold(count, body, init):
    if isinstance(count, int):
        for index in range(count):
            init = body(index, init)
        return init
    return lax.fori_loop(0, count, body, init)

def rows_of(index):
    start = index * TILE
    return pl.ds(start if isinstance(start, int) else pl.multiple_of(start, TILE), TILE)

def attend_block(head, block, refs):
    q_ref, k_ref, v_ref, g_ref, kt_ref, vt_ref, s_ref, p_ref, ht_ref, dqt_ref, dk_ref, dv_ref = refs
    here = rows_of(block)
    span = block + 1
    dims = pl.ds(pl.multiple_of(head * HEAD_DIM, HEAD_DIM), HEAD_DIM)
    query = q_ref[head, here, :]
    grad = g_ref[head, here, :]

    def score(index, top):
        tile = nt(k_ref[head, rows_of(index), :], query)
        if isinstance(index, int) and isinstance(block, int) and index < block:
            keep = tile
        else:
            key = lax.broadcasted_iota(jnp.int32, (TILE, TILE), 0) + (index - block) * TILE
            place = lax.broadcasted_iota(jnp.int32, (TILE, TILE), 1)
            keep = jnp.where(key <= place, tile, NEG)
        s_ref[index] = keep
        return jnp.maximum(top, jnp.max(keep, axis=0, keepdims=True))

    top = fold(span, score, jnp.full((1, TILE), 2 * NEG, F32))

    def raise_(index, total):
        raised = jnp.exp(s_ref[index] - top)
        s_ref[index] = raised
        return total + jnp.sum(raised, axis=0, keepdims=True)

    total = fold(span, raise_, jnp.zeros((1, TILE), F32))
    share = 1.0 / total

    def weigh(index, carried):
        heads, delta = carried
        weights = s_ref[index] * share
        s_ref[index] = weights
        weights_b = weights.astype(BF)
        d_weights = nt(v_ref[head, rows_of(index), :], grad)
        p_ref[index] = d_weights
        dv_ref[head, rows_of(index), :] += nn(weights_b, grad)
        heads = heads + nn(vt_ref[dims, rows_of(index)], weights_b)
        return heads, delta + jnp.sum(weights * d_weights, axis=0, keepdims=True)

    heads, delta = fold(
        span, weigh, (jnp.zeros((HEAD_DIM, TILE), F32), jnp.zeros((1, TILE), F32))
    )
    ht_ref[dims, here] = heads

    def back(index, d_query):
        d_scores = (s_ref[index] * (p_ref[index] - delta)).astype(BF)
        dk_ref[head, rows_of(index), :] += nn(d_scores, query)
        return d_query + nn(kt_ref[dims, rows_of(index)], d_scores)

    dqt_ref[dims, here] = fold(span, back, jnp.zeros((HEAD_DIM, TILE), F32))

def attend(heads_n, length, refs):
    dk_ref, dv_ref = refs[-2:]
    dk_ref[...] = jnp.zeros(dk_ref.shape, F32)
    dv_ref[...] = jnp.zeros(dv_ref.shape, F32)
    blocks = length // TILE

    @pl.loop(0, heads_n)
    def _(head):
        if blocks <= 4:
            for block in range(blocks):
                attend_block(head, block, refs)
        else:
            @pl.loop(0, blocks)
            def _(block):
                attend_block(head, block, refs)

def attend_kernel(H, L, q, k, v, g, kt, vt, ht, dqt, dk, dv, s_ref, p_ref):
    attend(H, L, (q, k, v, g, kt, vt, s_ref, p_ref, ht, dqt, dk, dv))

def attention_call(q, k, v, g, kt, vt):
    H, L, _ = q.shape
    vm = pl.BlockSpec(memory_space=pltpu.VMEM)
    nb = L // TILE
    return pl.pallas_call(functools.partial(attend_kernel, H, L),
        out_shape=(jax.ShapeDtypeStruct((H*64, L), F32), jax.ShapeDtypeStruct((H*64, L), F32), jax.ShapeDtypeStruct((H, L, 128), F32), jax.ShapeDtypeStruct((H, L, 128), F32)),
        in_specs=[vm]*6, out_specs=[vm]*4,
        scratch_shapes=[pltpu.VMEM((nb, TILE, TILE), F32), pltpu.VMEM((nb, TILE, TILE), F32)],
        compiler_params=pltpu.CompilerParams(vmem_limit_bytes=56 * 2**20))(q, k, v, g, kt, vt)

def prep(queries, keys, values, d_heads, segments):
    seg = segments[:, None] == jnp.arange(64)[None, :]
    e = jnp.broadcast_to(seg.astype(BF)[None], queries.shape)
    f = jnp.broadcast_to(jnp.where(seg, 0.0, NEG).astype(BF)[None], queries.shape)
    lane = jnp.arange(64)
    f = jnp.where(lane < 4, f, 0).astype(BF)
    qa = jnp.concatenate([(queries.astype(F32) * 0.125).astype(BF), e], -1)
    ka = jnp.concatenate([keys, f], -1)
    z = jnp.zeros_like(values)
    va = jnp.concatenate([values, z], -1)
    ga = jnp.concatenate([d_heads, z], -1)
    kt = keys.transpose(0, 2, 1).reshape(-1, keys.shape[1])
    vt = values.transpose(0, 2, 1).reshape(-1, keys.shape[1])
    return qa, ka, va, ga, kt, vt

def attention(queries, keys, values, d_heads, segments):
    H, L, _ = queries.shape
    ht, dqt, dk, dv = attention_call(*prep(queries, keys, values, d_heads, segments))

    def back(t):
        return t.reshape(H, 64, L).transpose(0, 2, 1)

    return back(ht).astype(BF), (back(dqt) * 0.125).astype(BF), dk[..., :64].astype(BF), dv[..., :64].astype(BF)


def dot(a, b):
    return jnp.dot(a, b, preferred_element_type=F32)


def dot_t(a, b):
    return lax.dot_general(a, b, (((0,), (0,)), ((), ())), preferred_element_type=F32)


def dot_nt(a, b):
    return lax.dot_general(a, b, (((1,), (1,)), ((), ())), preferred_element_type=F32)


(
    OWN, XGO, DYGO, XFWD, DYFWD, HOTS, DYALL, VROWS, LN0, LN1, LN2, LN3, SWGO, SWIN, QKV0, QKV1,
    DH, GVC1, GVC2, GVC3, GVC4, GVC5, GMA1, GMA2, GMA3, GMA4, GMA5, GMB1, GMB2, GMB3, GMB4,
    GMB5, GPR1, GPR2, GPR3, GPR4, GPR5, GRA1, GRA2, GRA3, GRA4, GRA5, GRB1, GRB2, GRB3, GRB4,
    GRB5, GFA1, GFA2, GFA3, GFA4, GFA5, GFB1, GFB2, GFB3, GFB4, GFB5, RVC1, RVC2, RVC3, RVC4,
    RVC5, RMA1, RMA2, RMA3, RMA4, RMA5, RMB1, RMB2, RMB3, RMB4, RMB5, RPR1, RPR2, RPR3, RPR4,
    RPR5, RRA1, RRA2, RRA3, RRA4, RRA5, RRB1, RRB2, RRB3, RRB4, RRB5, RFA1, RFA2, RFA3, RFA4,
    RFA5, RFB1, RFB2, RFB3, RFB4, RFB5, AT00, AT02, AT03, AT10, AT12, AT13, AT20, AT22, AT23,
    AT30, AT32, AT33, POST, GM, GR, GF, GP, SBGO, SBIN, UP0, UP1, UP2, UP3, DN0, DN1, OP0, OP1,
    BK0, BK1, OM0, OM1, BM0, BM1, VP, BO, IG, SV, WV, VO, SMA, SMB, SPR, SRA, SRB, SFA, SFB,
    WMA, WMB, WPR, WRA, WRB, WFA, WFB, CMA, CMB, CPR, CRA, CRB, CFA, CFB,
) = range(157)

ORDER = (
    OWN, XGO, GPR1, GRA1, GVC1, GMB1, GPR2, GRB1, DYGO, GRA2, GPR3, GVC2, XFWD, GMB2, HOTS,
    GRA3, GPR4, GVC3, GRB2, GMB3, GPR5, SWGO, GRA4, DYFWD, GVC4, GMA1, DYALL, GRB3, GRA5, GVC5,
    VROWS, LN0, GMB4, LN1, SWIN, GMA2, LN2, DH, GRB4, LN3, GMB5, GFA1, GMA3, GRB5, UP2, GFB1,
    UP0, GFA2, UP1, GMA4, UP3, GFB2, GF, RFA1, GMA5, GFA3, QKV1, GFB3, QKV0, AT20, RFA2, AT22,
    AT23, GFA4, GFB4, AT30, RFB1, AT32, RFA3, AT33, GFA5, AT00, GFB5, AT02, RFB2, DN0, RFA4,
    DN1, AT03, RFB3, GR, RFA5, SFA, RRB1, RRA1, AT10, AT12, RFB4, AT13, RRB2, WFA, POST, CFA,
    RRA2, RFB5, SFB, GP, SBGO, OP1, RRB3, BK1, WFB, OM1, RRA3, GM, CFB, RMB1, RMA1, OP0, SBIN,
    RPR1, RRB4, BK0, OM0, RPR2, RMB2, VP, BM1, BM0, RVC1, RMA2, RRB5, RPR3, RRA4, BO, RMB3,
    RPR4, RVC2, RMA3, SRB, RRA5, RMB4, SRA, RPR5, RVC3, SPR, IG, RMA4, RMB5, SMB, RVC4, WRB,
    CRB, WRA, RMA5, SMA, RVC5, SV, CRA, WPR, CPR, WMB, CMB, WMA, WV, VO, CMA,
)
LANES = 128
HALF = LANES // 2
VEC_ROWS = 16
PROJ = 3
TURN = 32


def resident_fits(seq_size, dp_size, tok):
    return (
        D // dp_size == LANES
        and FF // dp_size // seq_size == LANES
        and HEADS // seq_size == 4
        and tok * seq_size <= TURN * TURN
        and tok % TILE == 0
    )


def rows_at(ref, index, count):
    return ref.at[pl.ds(pl.multiple_of(index * count, count), count)]


def columns_at(ref, index, count):
    return ref.at[:, pl.ds(pl.multiple_of(index * count, count), count)]


class Flat:
    def __init__(self, ref, count, stride=None, start=0):
        self.ref, self.count, self.start = ref, count, start
        self.stride = count if stride is None else stride

    @property
    def at(self):
        return self

    def __getitem__(self, index):
        first = pl.multiple_of(index * self.stride + self.start, self.count)
        return self.ref.at[pl.ds(first, self.count)]


class Stack:
    def __init__(self, ref, start, count):
        self.ref, self.start, self.count = ref, start, count

    @property
    def at(self):
        return self

    def __getitem__(self, index):
        return self.ref.at[index, pl.ds(self.start, self.count)]


def lanes_like(shape):
    return lax.broadcasted_iota(jnp.int32, shape, len(shape) - 1)


def head_part(values, start):
    tile = values[:, start // LANES * LANES : start // LANES * LANES + LANES]
    return tile if start % LANES == 0 else pltpu.roll(tile, HEAD_DIM, 1)


def spin(tile, cosine, sine):
    lane = lanes_like(tile.shape)
    partner = jnp.where(lane < ROT // 2, pltpu.roll(tile, LANES - ROT // 2, 1), pltpu.roll(tile, ROT // 2, 1))
    return tile * cosine + partner * sine


def attend_head(head, block, refs):
    q_ref, k_ref, v_ref, g_ref, kt_ref, vt_ref, s_ref, p_ref, ht_ref, dqt_ref, dk_ref, dv_ref = refs
    here = pl.ds(block * TILE, TILE)
    wide = pl.ds(head * LANES, LANES)
    dims = pl.ds(head * HEAD_DIM, HEAD_DIM)
    query = q_ref[here, wide]
    grad = g_ref[here, wide]
    span = block + 1
    top = jnp.full((1, TILE), 2 * NEG, F32)
    for index in range(span):
        tile = nt(k_ref[pl.ds(index * TILE, TILE), wide], query)
        if index == block:
            key = lax.broadcasted_iota(jnp.int32, (TILE, TILE), 0)
            place = lax.broadcasted_iota(jnp.int32, (TILE, TILE), 1)
            tile = jnp.where(key <= place, tile, NEG)
        s_ref[index] = tile
        top = jnp.maximum(top, jnp.max(tile, axis=0, keepdims=True))
    total = jnp.zeros((1, TILE), F32)
    for index in range(span):
        raised = jnp.exp(s_ref[index] - top)
        s_ref[index] = raised
        total = total + jnp.sum(raised, axis=0, keepdims=True)
    share = 1.0 / total
    delta = jnp.zeros((1, TILE), F32)
    heads = jnp.zeros((HEAD_DIM, TILE), F32)
    for index in range(span):
        there = pl.ds(index * TILE, TILE)
        weights = s_ref[index] * share
        s_ref[index] = weights
        weights_b = weights.astype(BF)
        d_weights = nt(v_ref[there, wide], grad)
        p_ref[index] = d_weights
        d_value = nn(weights_b, grad)
        dv_ref[head, there, :] = d_value if index == block else dv_ref[head, there, :] + d_value
        heads = heads + nn(vt_ref[dims, there], weights_b)
        delta = delta + jnp.sum(weights * d_weights, axis=0, keepdims=True)
    ht_ref[dims, here] = heads.astype(BF)
    d_query = jnp.zeros((HEAD_DIM, TILE), F32)
    for index in range(span):
        there = pl.ds(index * TILE, TILE)
        d_scores = (s_ref[index] * (p_ref[index] - delta)).astype(BF)
        d_key = nn(d_scores, query)
        dk_ref[head, there, :] = d_key if index == block else dk_ref[head, there, :] + d_key
        d_query = d_query + nn(kt_ref[dims, there], d_scores)
    dqt_ref[dims, here] = (d_query * HEAD_DIM**-0.5).astype(BF)


class Refs(typing.NamedTuple):
    x_own: typing.Any
    dy_own: typing.Any
    w_mix_own: typing.Any
    w_proj_own: typing.Any
    w_rise_own: typing.Any
    w_fall_own: typing.Any
    gain1_own: typing.Any
    shift1_own: typing.Any
    gain2_own: typing.Any
    shift2_own: typing.Any
    b_proj_own: typing.Any
    b_fall_own: typing.Any
    b_mix_own: typing.Any
    b_rise_own: typing.Any
    seg_own: typing.Any
    pad_own: typing.Any
    turns: typing.Any
    block_out: typing.Any
    input_grad: typing.Any
    mix_fin: typing.Any
    proj_fin: typing.Any
    rise_fin: typing.Any
    fall_fin: typing.Any
    vec_result: typing.Any
    pad: typing.Any
    cos: typing.Any
    sin: typing.Any
    x: typing.Any
    dy: typing.Any
    hot: typing.Any
    segs: typing.Any
    w_mix: typing.Any
    w_proj_cols: typing.Any
    w_proj: typing.Any
    w_rise: typing.Any
    w_fall: typing.Any
    vec_all: typing.Any
    rows: typing.Any
    normed1: typing.Any
    normed2: typing.Any
    stat: typing.Any
    qk: typing.Any
    vg: typing.Any
    kt: typing.Any
    vt: typing.Any
    s: typing.Any
    p: typing.Any
    ht: typing.Any
    dqt: typing.Any
    dk: typing.Any
    dv: typing.Any
    attn: typing.Any
    d_mixed: typing.Any
    out_part: typing.Any
    back_part: typing.Any
    active: typing.Any
    d_up: typing.Any
    g_mix: typing.Any
    g_proj_cols: typing.Any
    g_rise: typing.Any
    g_fall: typing.Any
    c_mix: typing.Any
    c_proj: typing.Any
    c_rise: typing.Any
    c_fall: typing.Any
    out_cross: typing.Any
    out_came: typing.Any
    back_cross: typing.Any
    back_came: typing.Any
    sums: typing.Any
    vec_part: typing.Any
    vec_came: typing.Any
    mix_got: typing.Any
    proj_got: typing.Any
    rise_got: typing.Any
    fall_got: typing.Any
    vec_fin: typing.Any
    vec_out: typing.Any
    m_x: typing.Any
    m_dy: typing.Any
    m_hot: typing.Any
    m_vec: typing.Any
    m_mix: typing.Any
    m_proj: typing.Any
    m_rise: typing.Any
    m_fall: typing.Any
    m_swap: typing.Any
    m_own: typing.Any
    m_swap2: typing.Any
    m_rmix: typing.Any
    m_rproj: typing.Any
    m_rrise: typing.Any
    m_rfall: typing.Any
    m_out: typing.Any
    m_back: typing.Any
    m_vec2: typing.Any
    m_fmix: typing.Any
    m_fproj: typing.Any
    m_frise: typing.Any
    m_ffall: typing.Any
    m_fvec: typing.Any
    m_fin: typing.Any


def resident_kernel(seq_size, dp_size, *refs):
    r = Refs(*refs)
    place = Place(seq_size, dp_size)
    half = place.half
    tok = r.x_own.shape[0]
    length = r.x.shape[0]
    wide = r.w_proj.shape[0]
    mixed_wide = 3 * wide
    units = LANES
    each = dp_size // seq_size
    heads_n = wide // HEAD_DIM
    blocks = length // TILE

    place.greet_near()
    own = []

    def bring(src, dst):
        copy = pltpu.make_async_copy(src, dst, r.m_own.at[len(own)])
        copy.start()
        own.append(copy)

    bring(columns_at(r.w_mix_own, place.seq, mixed_wide), rows_at(r.w_mix, place.dp, LANES))
    bring(columns_at(r.w_proj_own, place.seq, wide), rows_at(r.w_proj_cols, place.dp, LANES))
    bring(r.x_own, rows_at(r.x, place.seq, tok))
    bring(r.dy_own, rows_at(r.dy, place.seq, tok))
    for index in range(dp_size):
        bring(
            columns_at(r.w_rise_own, index * seq_size + place.seq, units),
            rows_at(r.w_rise, place.dp, LANES).at[:, pl.ds(index * units, units)],
        )
    bring(rows_at(r.w_fall_own, place.seq, units), rows_at(r.w_fall, place.dp, units))
    bring(r.pad_own, r.pad)

    coarse_cos, coarse_sin, fine_cos, fine_sin = (
        r.turns.at[pl.ds(index * TURN, TURN)] for index in range(4)
    )

    @pl.loop(0, length // TURN)
    def _(step):
        here = pl.ds(pl.multiple_of(step * TURN, TURN), TURN)
        far_cos, far_sin = coarse_cos[pl.ds(step, 1), :], coarse_sin[pl.ds(step, 1), :]
        r.cos[here, :] = far_cos * fine_cos[...] - far_sin * fine_sin[...]
        r.sin[here, :] = far_sin * fine_cos[...] + far_cos * fine_sin[...]

    row = 0
    vectors = (r.gain1_own, r.shift1_own, r.gain2_own, r.shift2_own, r.b_proj_own, r.b_fall_own, r.b_mix_own, r.b_rise_own)
    for vector in vectors:
        count = vector.shape[0]
        r.vec_all[place.dp, row : row + count, :] = vector[...].astype(F32)
        row += count
    r.vec_all[place.dp, row:, :] = jnp.zeros((VEC_ROWS - row, LANES), F32)
    rows_at(r.segs, place.seq, 8)[...] = jnp.broadcast_to(r.seg_own[...], (8, tok)).astype(F32)

    def pair_of(ref, make):
        return [make(Flat(ref, HALF, LANES, start), index) for index, start in enumerate((0, HALF))]

    def gather_pair(ref, sems):
        return pair_of(ref, lambda part, index: RingGather(place, part, sems.at[index]))

    def reduce_pair(ref, came, sems):
        return pair_of(ref, lambda part, index: RingReduce(place, part, came.at[index], sems.at[index]))

    def final_pair(out_ref, sems, ref):
        return pair_of(
            ref,
            lambda part, index: SeqGather(
                place, Stack(out_ref, index * HALF, HALF), sems.at[index], part[place.dp]
            ),
        )

    gathers = [
        RingGather(place, r.vec_all, r.m_vec),
        *gather_pair(r.w_mix, r.m_mix),
        RingGather(place, Flat(r.w_proj_cols, LANES), r.m_proj),
        *gather_pair(r.w_rise, r.m_rise),
        *gather_pair(r.w_fall, r.m_fall),
    ]
    reduces = [
        RingReduce(place, r.vec_part, r.vec_came, r.m_vec2),
        *reduce_pair(r.g_mix, r.c_mix, r.m_rmix),
        RingReduce(place, Flat(r.g_proj_cols, LANES), r.c_proj, r.m_rproj),
        *reduce_pair(r.g_rise, r.c_rise, r.m_rrise),
        *reduce_pair(r.g_fall, r.c_fall, r.m_rfall),
    ]
    finals = [
        *final_pair(r.mix_got, r.m_fmix, r.g_mix),
        SeqGather(place, r.proj_got, r.m_fproj, rows_at(r.g_proj_cols, place.dp, LANES)),
        *final_pair(r.rise_got, r.m_frise, r.g_rise),
        *final_pair(r.fall_got, r.m_ffall, r.g_fall),
    ]
    homes = [r.proj_fin]
    for out_ref in (r.rise_fin, r.fall_fin):
        homes += [Stack(out_ref, start, HALF) for start in (0, HALF)]
    homes = [Stack(r.mix_fin, start, HALF) for start in (0, HALF)] + homes
    f_vec = SeqGather(place, r.vec_fin, r.m_fvec)

    x_move = SeqGather(place, Flat(r.x, tok), r.m_x)
    dy_move = SeqGather(place, Flat(r.dy, tok), r.m_dy)
    seg_move = SeqGather(place, Flat(r.segs, 8), r.m_hot)
    out = SeqReduce(place, Flat(r.out_part, tok), r.out_cross, r.out_came, r.m_out)
    back = SeqReduce(place, Flat(r.back_part, tok), r.back_cross, r.back_came, r.m_back)

    leaving = []

    def leave(src, dst):
        copy = pltpu.make_async_copy(src, dst, r.m_fin.at[len(leaving)])
        copy.start()
        leaving.append(copy)

    pieces = {}

    def piece(name, *given):
        def note(run):
            pieces[name] = functools.partial(run, *given)
            return run

        return note

    def tile_rows(block):
        return pl.ds(pl.multiple_of(block * TILE, TILE), TILE)

    def gather(stream, step):
        gathers[stream].tick(step)

    def reduce(stream, step):
        reduces[stream].tick(step)

    for stream in range(len(gathers)):
        for step in range(1, half + 2):
            tick = stream * (half + 1) + step - 1
            piece(GVC1 + tick, stream, step)(gather)
            piece(RVC1 + tick, stream, step)(reduce)

    @piece(OWN)
    def _():
        for copy in own:
            copy.wait()

    @piece(XGO)
    def _():
        x_move.begin()
        seg_move.begin()

    piece(DYGO)(dy_move.begin)

    @piece(XFWD)
    def _():
        x_move.forward()
        seg_move.forward()

    piece(DYFWD)(dy_move.forward)

    @piece(HOTS)
    def _():
        for step in range(place.pairs):
            seg_move.across_arrived(step)
        kind = lax.broadcasted_iota(jnp.int32, (LANES, tok), 0) - HEAD_DIM
        for index in range(seq_size):
            segment = r.segs[index * 8 : index * 8 + 1, :].astype(jnp.int32)
            r.hot[index * tok : (index + 1) * tok, :] = jnp.where(segment == kind, 1.0, 0.0).T.astype(BF)

    @piece(DYALL)
    def _():
        for step in range(place.pairs):
            dy_move.across_arrived(step)

    @piece(VROWS)
    def _():
        for index in range(dp_size):
            at = slice(index * LANES, (index + 1) * LANES)
            for row in range(6):
                r.rows[row : row + 1, at] = r.vec_all[index, row : row + 1, :]
            r.rows[6:7, at] = r.vec_all[index, pl.ds(9 + place.seq, 1), :]
        for index in range(each):
            for row in range(3):
                start = (index * 3 + row) * LANES
                r.rows[7:8, start : start + LANES] = r.vec_all[place.seq * each + index, 6 + row : 7 + row, :]

    chunk = 64

    def normalize(block):
        @pl.loop(0, tok // chunk)
        def _(step):
            here = pl.ds(pl.multiple_of(block * tok + step * chunk, chunk), chunk)
            values = r.x[here, :].astype(F32)
            mean = jnp.sum(values, axis=-1, keepdims=True) * (1.0 / D)
            center = values - mean
            rstd = lax.rsqrt(jnp.sum(center * center, axis=-1, keepdims=True) * (1.0 / D) + EPS)
            n = center * rstd
            r.normed1[here, :] = (n * r.rows[0:1, :] + r.rows[1:2, :]).astype(BF)
            r.normed2[here, :] = (n * r.rows[2:3, :] + r.rows[3:4, :]).astype(BF)
            lane = lanes_like((chunk, LANES))
            r.stat[here, :] = jnp.where(lane < HEAD_DIM, mean, rstd)

    def unit_rows(here):
        stat = r.stat[here, :]
        return (r.x[here, :].astype(F32) - stat[:, 0:1]) * stat[:, HEAD_DIM : HEAD_DIM + 1]

    @piece(LN0)
    def _():
        normalize(place.seq)

    @piece(LN1)
    def _():
        x_move.across_arrived(0)
        normalize(place.sibling)

    @piece(LN2)
    def _():
        normalize(place.pair_peer(1))

    @piece(LN3)
    def _():
        x_move.across_arrived(1)
        normalize(place.across_source(1))

    def swap(step):
        peer = place.seq_peer(step)
        src, dst = rows_at(r.w_proj_cols, peer, wide), columns_at(r.w_proj, place.seq, wide)
        return send(src, dst, r.m_swap, step, {"seq": peer})

    def swap_arrival(step):
        source = place.seq_peer(-step)
        src, dst = rows_at(r.w_proj_cols, source, wide), columns_at(r.w_proj, source, wide)
        return send(src, dst, r.m_swap, step, {"seq": place.seq_peer(step)})

    @piece(SWGO)
    def _():
        for step in range(1, seq_size):
            swap(step).start()
        columns_at(r.w_proj, place.seq, wide)[...] = rows_at(r.w_proj_cols, place.seq, wide)[...]

    @piece(SWIN)
    def _():
        for step in range(1, seq_size):
            swap_arrival(step).wait_recv()

    def mix_columns(first, last):
        @pl.loop(first, last)
        def _(block):
            here = tile_rows(block)
            mixed = nn(r.normed1[here, :], r.w_mix[...]) + r.rows[7:8, 0:mixed_wide]
            cosine, sine = r.cos[here, :], r.sin[here, :]
            lane = lanes_like((TILE, LANES))
            hot = r.hot[here, :].astype(F32)
            cold = jnp.where((lane >= HEAD_DIM) & (lane < HEAD_DIM + 4), (1.0 - hot) * NEG, 0.0)
            for head in range(heads_n):
                start = head * 3 * HEAD_DIM
                query = spin(head_part(mixed, start), cosine, sine) * HEAD_DIM**-0.5
                key = spin(head_part(mixed, start + HEAD_DIM), cosine, sine)
                value = head_part(mixed, start + 2 * HEAD_DIM)
                at = pl.ds(head * LANES, LANES)
                at_more = pl.ds((heads_n + head) * LANES, LANES)
                dims = pl.ds(head * HEAD_DIM, HEAD_DIM)
                r.qk[here, at] = jnp.where(lane < HEAD_DIM, query, hot).astype(BF)
                r.qk[here, at_more] = jnp.where(lane < HEAD_DIM, key, cold).astype(BF)
                r.vg[here, at] = jnp.where(lane < HEAD_DIM, value, 0.0).astype(BF)
                r.kt[dims, here] = key.T[:HEAD_DIM, :].astype(BF)
                r.vt[dims, here] = value.T[:HEAD_DIM, :].astype(BF)

    middle = blocks // 2
    piece(QKV0, 0, middle)(mix_columns)
    piece(QKV1, middle, blocks)(mix_columns)
    @piece(DH)
    def _():
        @pl.loop(0, blocks)
        def _(block):
            here = tile_rows(block)
            place_in = lax.broadcasted_iota(jnp.int32, (TILE, wide), 0) + block * TILE
            d_heads = jnp.where(place_in < length - r.pad[0], nt(r.dy[here, :], r.w_proj[...]), 0.0)
            for head in range(heads_n):
                at_more = pl.ds((heads_n + head) * LANES, LANES)
                r.vg[here, at_more] = head_part(d_heads, head * HEAD_DIM).astype(BF)

    second = heads_n * LANES
    head_refs = (
        r.qk.at[:, pl.ds(0, second)],
        r.qk.at[:, pl.ds(second, second)],
        r.vg.at[:, pl.ds(0, second)],
        r.vg.at[:, pl.ds(second, second)],
        r.kt,
        r.vt,
        r.s,
        r.p,
        r.ht,
        r.dqt,
        r.dk,
        r.dv,
    )

    def attend_blocks(head, first, last):
        for block in range(first, last):
            if block == 0:
                attend_head(head, block, head_refs)
            elif block == 1:
                attend_head(head, block, head_refs)
            elif block == 2:
                attend_head(head, block, head_refs)
            else:
                attend_head(head, block, head_refs)

    for head in range(heads_n):
        first = AT00 + head * (middle + 1)
        piece(first, head, 0, middle)(attend_blocks)
        for block in range(middle, blocks):
            piece(first + block - middle + 1, head, block, block + 1)(attend_blocks)

    def heads_back():
        @pl.loop(0, blocks)
        def _(block):
            here = tile_rows(block)
            place_in = lax.broadcasted_iota(jnp.int32, (TILE, wide), 0) + block * TILE
            r.attn[here, :] = jnp.where(place_in < length - r.pad[0], r.ht[:, here].T.astype(F32), 0.0).astype(BF)
            d_query = r.dqt[:, here].T.astype(F32)
            cosine, sine = r.cos[here, :], -r.sin[here, :]
            lane = lanes_like((TILE, LANES))
            parts = []
            for head in range(heads_n):
                parts.append(spin(head_part(d_query, head * HEAD_DIM), cosine, sine))
                parts.append(spin(r.dk[head, here, :], cosine, sine))
                parts.append(r.dv[head, here, :])
            for index in range(len(parts) // 2):
                tile = jnp.where(lane < HEAD_DIM, parts[2 * index], pltpu.roll(parts[2 * index + 1], HEAD_DIM, 1))
                at = slice(index * LANES, (index + 1) * LANES)
                tile = tile.astype(BF)
                r.d_mixed[here, at] = tile
                r.sums[6:7, at] += jnp.sum(tile.astype(F32), axis=0, keepdims=True)

    piece(POST)(heads_back)
    big = 512

    def weight_grad(out_ref, left, right):
        @pl.loop(0, left.shape[1] // big)
        def _(index):
            at = pl.ds(pl.multiple_of(index * big, big), big)
            out_ref[at, :] = tn(left[:, at], right[...]).astype(BF)

    piece(GM, r.g_mix, r.normed1, r.d_mixed)(weight_grad)
    piece(GR, r.g_rise, r.normed2, r.d_up)(weight_grad)
    piece(GF, r.g_fall, r.active, r.dy)(weight_grad)

    @piece(GP)
    def _():
        gathers[PROJ].finish()
        for step in range(1, seq_size):
            swap(step).wait_send()
        grad = tn(r.attn[...], r.dy[...]).astype(BF)
        for index in range(seq_size):
            r.w_proj_cols[index * wide : (index + 1) * wide, :] = grad[:, index * wide : (index + 1) * wide]

    def swap_back(step):
        peer = place.seq_peer(step)
        src, dst = rows_at(r.w_proj_cols, peer, wide), rows_at(r.g_proj_cols, place.seq, wide)
        return send(src, dst, r.m_swap2, step, {"seq": peer})

    def swap_back_arrival(step):
        source = place.seq_peer(-step)
        src, dst = rows_at(r.w_proj_cols, source, wide), rows_at(r.g_proj_cols, source, wide)
        return send(src, dst, r.m_swap2, step, {"seq": place.seq_peer(step)})

    @piece(SBGO)
    def _():
        for step in range(1, seq_size):
            swap_back(step).start()
        rows_at(r.g_proj_cols, place.seq, wide)[...] = rows_at(r.w_proj_cols, place.seq, wide)[...]

    @piece(SBIN)
    def _():
        for step in range(1, seq_size):
            swap_back_arrival(step).wait_recv()

    def upward(block):
        here = tile_rows(block)
        up = nn(r.normed2[here, :], r.w_rise[...]) + r.rows[6:7, :]
        share = 0.5 + 0.5 * lax.erf(up * 0.5**0.5)
        r.active[here, :] = (up * share).astype(BF)
        bell = jnp.exp(-0.5 * up * up) * (2 * np.pi) ** -0.5
        r.d_up[here, :] = (share + up * bell).astype(BF)

    def downward(first, last):
        @pl.loop(first, last)
        def _(block):
            here = tile_rows(block)
            d_up = (r.d_up[here, :].astype(F32) * nt(r.dy[here, :], r.w_fall[...])).astype(BF)
            r.d_up[here, :] = d_up
            r.sums[5:6, :] += jnp.sum(d_up.astype(F32), axis=0, keepdims=True)

    for block in range(blocks):
        piece(UP0 + block, block)(upward)
    piece(DN0, 0, middle)(downward)
    piece(DN1, middle, blocks)(downward)

    def out_rows(step):
        first = ((place.pair + step) % place.pairs) * (2 * tok // TILE)
        @pl.loop(0, 2 * tok // TILE)
        def _(block):
            here = tile_rows(first + block)
            part = nn(r.attn[here, :], r.w_proj[...]) + nn(r.active[here, :], r.w_fall[...])
            r.out_part[here, :] = part.astype(BF)

        out.over_start(step)

    def back_rows(step):
        first = ((place.pair + step) % place.pairs) * (2 * tok // TILE)
        @pl.loop(0, 2 * tok // TILE)
        def _(block):
            here = tile_rows(first + block)
            d_one = nt(r.d_mixed[here, :], r.w_mix[...])
            d_two = nt(r.d_up[here, :], r.w_rise[...])
            r.back_part[here, :] = (r.rows[0:1, :] * d_one + r.rows[2:3, :] * d_two).astype(BF)
            n = unit_rows(here)
            r.sums[0:1, :] += jnp.sum(d_one * n, axis=0, keepdims=True)
            r.sums[1:2, :] += jnp.sum(d_one, axis=0, keepdims=True)
            r.sums[2:3, :] += jnp.sum(d_two * n, axis=0, keepdims=True)
            r.sums[3:4, :] += jnp.sum(d_two, axis=0, keepdims=True)
            r.sums[4:5, :] += jnp.sum(r.dy[here, :].astype(F32), axis=0, keepdims=True)

        back.over_start(step)

    for step in range(2):
        piece(OP0 + step, step)(out_rows)
        piece(BK0 + step, step)(back_rows)
        piece(OM0 + step, step)(out.over_add)
        piece(BM0 + step, step)(back.over_add)

    @piece(VP)
    def _():
        for index in range(dp_size):
            at = slice(index * LANES, (index + 1) * LANES)
            r.vec_part[index, 0:6, :] = r.sums[0:6, at]
            for row in range(mixed_wide // LANES):
                r.vec_part[index, 6 + row : 7 + row, :] = r.sums[6:7, row * LANES : (row + 1) * LANES]

    def settle(move, home):
        move.begin()
        leave(move.own, home.at[place.seq])

    def pass_on(move, home):
        move.forward()
        for step in range(1, place.pairs):
            source = place.pair_peer(-step)
            leave(move.full.at[source], home.at[source])

    def complete(move, home):
        for step in range(place.pairs):
            move.across_arrived(step)
            source = place.across_source(step)
            leave(move.full.at[source], home.at[source])

    for index, (move, home) in enumerate(zip(finals, homes, strict=True)):
        piece(SMA + index, move, home)(settle)
        piece(WMA + index, move, home)(pass_on)
        piece(CMA + index, move, home)(complete)

    mine = pl.ds(pl.multiple_of(place.seq * tok, tok), tok)

    @piece(BO)
    def _():
        total = out.total()
        block_out = total + r.x[mine, :].astype(F32) + (r.rows[4:5, :] + r.rows[5:6, :])
        r.out_cross[0] = block_out.astype(BF)
        leave(r.out_cross.at[0], r.block_out)

    @piece(IG)
    def _():
        scaled = back.total()
        n = unit_rows(mine)
        rstd = r.stat[mine, HEAD_DIM : HEAD_DIM + 1]
        back_mean = jnp.sum(scaled, axis=-1, keepdims=True) * (1.0 / D)
        back_n = jnp.sum(scaled * n, axis=-1, keepdims=True) * (1.0 / D)
        input_grad = r.dy[mine, :].astype(F32) + rstd * (scaled - back_mean - n * back_n)
        r.back_cross[0] = input_grad.astype(BF)
        leave(r.back_cross.at[0], r.input_grad)

    @piece(SV)
    def _():
        r.vec_fin[place.seq] = r.vec_part[place.dp]
        f_vec.begin()

    piece(WV)(f_vec.forward)

    @piece(VO)
    def _():
        f_vec.finish()
        norm = r.vec_fin[0, 0:4, :]
        for index in range(1, seq_size):
            norm = norm + r.vec_fin[index, 0:4, :]
        r.vec_out[0:4, :] = norm
        r.vec_out[4:5, :] = r.vec_fin[0, 4:5, :]
        source = r.vec_fin[place.dp // each]
        pick = place.dp % each
        part = source[6:9, :]
        for index in range(1, each):
            part = jnp.where(pick == index, source[6 + 3 * index : 9 + 3 * index, :], part)
        r.vec_out[5:8, :] = part
        for index in range(seq_size):
            r.vec_out[8 + index : 9 + index, :] = r.vec_fin[index, 5:6, :]
        leave(r.vec_out, r.vec_result)

    place.met_near()
    r.sums[...] = jnp.zeros(r.sums.shape, F32)
    r.vec_part[...] = jnp.zeros(r.vec_part.shape, F32)
    assert sorted(ORDER) == sorted(pieces)
    for name in ORDER:
        pieces[name]()
    for move in finals:
        move.sent()
    for copy in leaving:
        copy.wait()
    for move in (*gathers[:PROJ], *gathers[PROJ + 1 :], *reduces, out, back):
        move.finish()
    for move in (x_move, seg_move, dy_move):
        move.sent()
    for step in range(1, seq_size):
        swap_back(step).wait_send()


def resident_call(seq_size, dp_size, *args):
    tok = args[0].shape[0]
    length = tok * seq_size
    half, pairs = dp_size // 2, seq_size // 2
    wide = HEADS // seq_size * HEAD_DIM
    units_all = dp_size * LANES
    heads_n = wide // HEAD_DIM

    def half_vmem(*shape):
        return pltpu.VMEM(shape, BF)

    def full_vmem(*shape):
        return pltpu.VMEM(shape, F32)

    def ring(columns):
        return half_vmem(2, 2, half, HALF, columns)

    def pair_of_sems(count):
        return pltpu.SemaphoreType.DMA((2, 2, count))

    any_spec = pl.BlockSpec(memory_space=pl.ANY)
    vmem = pl.BlockSpec(memory_space=pltpu.VMEM)
    scratch = [
        pltpu.SMEM((1,), jnp.int32),
        full_vmem(length, LANES),
        full_vmem(length, LANES),
        half_vmem(length, D),
        half_vmem(length, D),
        half_vmem(length, LANES),
        full_vmem(seq_size * 8, tok),
        half_vmem(D, 3 * wide),
        half_vmem(D, wide),
        half_vmem(wide, D),
        half_vmem(D, units_all),
        half_vmem(units_all, D),
        full_vmem(dp_size, VEC_ROWS, LANES),
        full_vmem(8, D),
        half_vmem(length, D),
        half_vmem(length, D),
        full_vmem(length, LANES),
        half_vmem(length, units_all),
        half_vmem(length, units_all),
        half_vmem(wide, length),
        half_vmem(wide, length),
        full_vmem(length // TILE, TILE, TILE),
        full_vmem(length // TILE, TILE, TILE),
        half_vmem(wide, length),
        half_vmem(wide, length),
        full_vmem(heads_n, length, LANES),
        full_vmem(heads_n, length, LANES),
        half_vmem(length, wide),
        half_vmem(length, 3 * wide),
        half_vmem(length, D),
        half_vmem(length, D),
        half_vmem(length, units_all),
        half_vmem(length, units_all),
        half_vmem(D, 3 * wide),
        half_vmem(D, wide),
        half_vmem(D, units_all),
        half_vmem(units_all, D),
        ring(3 * wide),
        half_vmem(2, half, LANES, wide),
        ring(units_all),
        ring(D),
        half_vmem(pairs, tok, D),
        half_vmem(pairs - 1, tok, D),
        half_vmem(pairs, tok, D),
        half_vmem(pairs - 1, tok, D),
        full_vmem(8, D),
        full_vmem(dp_size, VEC_ROWS, LANES),
        full_vmem(2, half, VEC_ROWS, LANES),
        half_vmem(seq_size, LANES, 3 * wide),
        half_vmem(seq_size, LANES, wide),
        half_vmem(seq_size, LANES, units_all),
        half_vmem(seq_size, LANES, D),
        full_vmem(seq_size, VEC_ROWS, LANES),
        full_vmem(16, LANES),
    ]
    scratch += [sems_of(2 * pairs)] * 3 + [sems_of(2 * half)]
    scratch += [pair_of_sems(2 * half), sems_of(2 * half), pair_of_sems(2 * half), pair_of_sems(2 * half)]
    scratch += [sems_of(seq_size), pltpu.SemaphoreType.DMA((dp_size + 6,)), sems_of(seq_size)]
    scratch += [pair_of_sems(2 * half), sems_of(2 * half), pair_of_sems(2 * half), pair_of_sems(2 * half)]
    scratch += [sems_of(2 * pairs)] * 2 + [sems_of(2 * half)]
    scratch += [pair_of_sems(2 * pairs), sems_of(2 * pairs), pair_of_sems(2 * pairs), pair_of_sems(2 * pairs)]
    scratch += [sems_of(2 * pairs)]
    scratch += [pltpu.SemaphoreType.DMA((32,))]
    return pl.pallas_call(
        functools.partial(resident_kernel, seq_size, dp_size),
        out_shape=(
            jax.ShapeDtypeStruct((tok, D), BF),
            jax.ShapeDtypeStruct((tok, D), BF),
            jax.ShapeDtypeStruct((seq_size, LANES, 3 * wide), BF),
            jax.ShapeDtypeStruct((seq_size, LANES, wide), BF),
            jax.ShapeDtypeStruct((seq_size, LANES, units_all), BF),
            jax.ShapeDtypeStruct((seq_size, LANES, D), BF),
            jax.ShapeDtypeStruct((16, LANES), F32),
        ),
        in_specs=[any_spec] * 6 + [vmem] * 9 + [any_spec, vmem],
        out_specs=[any_spec] * 7,
        scratch_shapes=scratch,
        compiler_params=pltpu.CompilerParams(
            collective_id=2, has_side_effects=True, vmem_limit_bytes=RESIDENT_VMEM
        ),
    )(*args)


RESIDENT_VMEM = 63 * 2**20


def finish_kernel(seq_size, dp_size, *refs):
    (block, grad, mix, proj, rise, fall, vec), refs = refs[:7], refs[7:]
    (block_out, grad_out, mix_out, proj_out, rise_out, fall_out), refs = refs[:6], refs[6:]
    vec_outs, refs = refs[:8], refs[8:]
    (block_in, grad_in, mix_in, proj_in, rise_in, fall_in, vec_in, mix_f, proj_f, rise_f, fall_f), refs = refs[:11], refs[11:]
    vec_fs, (in_sems, out_sems) = refs[:8], refs[8:]
    parts = [(fall.at[group], fall_in.at[group]) for group in range(seq_size)]
    parts += [(rise, rise_in), (mix, mix_in), (proj, proj_in), (block, block_in), (grad, grad_in), (vec, vec_in)]
    coming = []
    for src, dst in parts:
        copy = pltpu.make_async_copy(src, dst, in_sems.at[len(coming)])
        copy.start()
        coming.append(copy)
    *fall_copies, rise_copy, mix_copy, proj_copy, block_copy, grad_copy, vec_copy = coming
    leaving = []

    def leave(src, dst):
        copy = pltpu.make_async_copy(src, dst, out_sems.at[len(leaving)])
        copy.start()
        leaving.append(copy)

    for group in range(seq_size):
        fall_copies[group].wait()
        at = pl.ds(group * LANES, LANES)
        fall_f[at, :] = fall_in[group].astype(F32)
        leave(fall_f.at[at], fall_out.at[at])
    few = 32
    rise_copy.wait()
    for start in range(0, LANES, few):
        at = pl.ds(start, few)
        for group in range(seq_size):
            for index in range(dp_size):
                column = (index * seq_size + group) * LANES
                rise_f[at, column : column + LANES] = rise_in[group, at, index * LANES : (index + 1) * LANES].astype(F32)
        leave(rise_f.at[at], rise_out.at[at])
    mix_copy.wait()
    proj_copy.wait()
    for start in range(0, LANES, 2 * few):
        at = pl.ds(start, 2 * few)
        for held, full, out in ((mix_in, mix_f, mix_out), (proj_in, proj_f, proj_out)):
            columns = held.shape[2]
            for group in range(seq_size):
                full[at, group * columns : (group + 1) * columns] = held[group, at, :].astype(F32)
            leave(full.at[at], out.at[at])
    block_copy.wait()
    leave(block_in, block_out)
    grad_copy.wait()
    leave(grad_in, grad_out)
    vec_copy.wait()
    for held, out, row in zip(vec_fs, vec_outs, (0, 1, 2, 3, 4, 4, 5, 8), strict=True):
        for start in range(0, out.shape[0], LANES):
            held[start : start + LANES] = vec_in[row + start // LANES]
        leave(held, out)
    for copy in leaving:
        copy.wait()


def finish_call(seq_size, dp_size, block, grad, mix, proj, rise, fall, vec):
    tok = block.shape[0]
    vec_sizes = (LANES,) * 6 + (3 * LANES, seq_size * LANES)
    full_sizes = ((LANES, 3 * D), (LANES, D), (LANES, FF), (seq_size * LANES, D))
    any_spec = pl.BlockSpec(memory_space=pl.ANY)
    return pl.pallas_call(
        functools.partial(finish_kernel, seq_size, dp_size),
        out_shape=(jax.ShapeDtypeStruct((tok, D), BF),) * 2
        + tuple(jax.ShapeDtypeStruct(size, F32) for size in full_sizes)
        + tuple(jax.ShapeDtypeStruct((size,), F32) for size in vec_sizes),
        in_specs=[any_spec] * 7,
        out_specs=[any_spec] * 14,
        scratch_shapes=[pltpu.VMEM(array.shape, array.dtype) for array in (block, grad, mix, proj, rise, fall, vec)]
        + [pltpu.VMEM(size, F32) for size in full_sizes]
        + [pltpu.VMEM((size,), F32) for size in vec_sizes]
        + [pltpu.SemaphoreType.DMA((seq_size + 6,)), pltpu.SemaphoreType.DMA((24,))],
        compiler_params=pltpu.CompilerParams(vmem_limit_bytes=RESIDENT_VMEM),
    )(block, grad, mix, proj, rise, fall, vec)


def resident_tables():
    half = ROT // 2
    frequency = BASE ** (-np.arange(0, ROT, 2).astype(np.float32) / np.float32(ROT))
    lanes = np.zeros((LANES,), np.float64)
    lanes[:half] = lanes[half:ROT] = frequency.astype(np.float32)
    sign = np.where(np.arange(LANES) < half, -1.0, 1.0)
    steps = np.arange(TURN, dtype=np.float64)[:, None]
    tables = [f for scale in (TURN, 1) for f in (np.cos(steps * scale * lanes), sign * np.sin(steps * scale * lanes))]
    return jnp.asarray(np.concatenate(tables).astype(np.float32))


def resident_shards(
    tokens,
    cotangent,
    norm1_gain,
    norm1_bias,
    norm2_gain,
    norm2_bias,
    qkv_weight,
    qkv_bias,
    out_weight,
    out_bias,
    up_weight,
    up_bias,
    down_weight,
    down_bias,
    segment_ids,
    pad_length,
):
    seq_size, dp_size = lax.axis_size("seq"), lax.axis_size("dp")
    tok = tokens.shape[1]
    vectors = (norm1_gain, norm1_bias, norm2_gain, norm2_bias, out_bias, down_bias, qkv_bias, up_bias)
    parts = resident_call(
        seq_size,
        dp_size,
        tokens[0],
        cotangent[0],
        qkv_weight,
        out_weight,
        up_weight,
        down_weight,
        *(vector.reshape(-1, LANES) for vector in vectors),
        segment_ids,
        pad_length,
        resident_tables(),
    )
    done = finish_call(seq_size, dp_size, *parts)
    block_out, input_grad, g_mix, g_proj, g_rise, g_fall = done[:6]
    norm1_g, norm1_b, norm2_g, norm2_b, out_b, down_b, b_mix, b_rise = done[6:]
    return (
        block_out[None],
        input_grad[None],
        norm1_g,
        norm1_b,
        norm2_g,
        norm2_b,
        g_mix,
        b_mix,
        g_proj,
        out_b,
        g_rise,
        b_rise,
        g_fall,
        down_b,
    )


def streamed_shards(
    tokens,
    cotangent,
    norm1_gain,
    norm1_bias,
    norm2_gain,
    norm2_bias,
    qkv_weight,
    qkv_bias,
    out_weight,
    out_bias,
    up_weight,
    up_bias,
    down_weight,
    down_bias,
    segment_ids,
    pad_length,
):
    seq_size, dp_size = lax.axis_size("seq"), lax.axis_size("dp")
    seq = lax.axis_index("seq")
    dp = lax.axis_index("dp")
    tok = tokens.shape[1]
    length = tok * seq_size
    heads_n = HEADS // seq_size
    rows = D // dp_size
    wide = heads_n * HEAD_DIM
    units = FF // dp_size // seq_size

    mix = qkv_weight.reshape(rows, seq_size, heads_n, 3, HEAD_DIM)
    mix = lax.dynamic_index_in_dim(mix, seq, 1, keepdims=False)
    mix = mix.transpose(0, 2, 1, 3).reshape(rows, 3 * wide)
    proj = lax.dynamic_slice_in_dim(out_weight, seq * wide, wide, 1)
    rise = up_weight.reshape(rows, dp_size, seq_size, units)
    rise = lax.dynamic_index_in_dim(rise, seq, 2, keepdims=False).reshape(rows, dp_size * units)
    fall = lax.dynamic_slice_in_dim(down_weight, seq * units, units, 0)
    vec = jnp.concatenate(
        [norm1_gain, norm1_bias, norm2_gain, norm2_bias, out_bias, down_bias, qkv_bias, up_bias]
    )
    vec_len = vec.shape[0]
    vec = jnp.pad(vec, (0, 2048 - vec_len)).reshape(16, 128)
    seg = jnp.broadcast_to(segment_ids, (8, tok))
    x_all, dy_all, w_mix, _, w_rise, w_fall, vec_all, seg_all, w_proj = gather_all(
        seq_size, dp_size, tokens[0], cotangent[0], mix, proj, rise, fall, vec, seg
    )
    x = x_all.reshape(length, D).astype(F32)
    dy = dy_all.reshape(length, D)
    w_mix = w_mix.reshape(D, 3 * wide)
    w_rise = w_rise.reshape(D, dp_size * units)
    w_fall = w_fall.reshape(dp_size * units, D)
    w_proj = w_proj.reshape(seq_size, wide, wide).transpose(1, 0, 2).reshape(wide, D)
    segments = seg_all[:, 0, :].reshape(length)
    vec_all = vec_all.reshape(dp_size, 2048)[:, :vec_len].astype(F32)
    g1, s1, g2, s2, b_proj, b_fall = (
        vec_all[:, i * rows : (i + 1) * rows].reshape(D) for i in range(6)
    )
    b_mix = vec_all[:, 6 * rows : 9 * rows].reshape(seq_size, heads_n, 3, HEAD_DIM)
    b_mix = lax.dynamic_index_in_dim(b_mix, seq, 0, keepdims=False)
    b_mix = b_mix.transpose(1, 0, 2).reshape(3 * wide)
    b_rise = vec_all[:, 9 * rows :].reshape(dp_size, seq_size, units)
    b_rise = lax.dynamic_index_in_dim(b_rise, seq, 1, keepdims=False).reshape(dp_size * units)

    center = x - jnp.mean(x, axis=-1, keepdims=True)
    rstd = lax.rsqrt(jnp.mean(center * center, axis=-1, keepdims=True) + EPS)
    n = center * rstd
    normed1 = (n * g1 + s1).astype(BF)
    normed2 = (n * g2 + s2).astype(BF)
    valid = (jnp.arange(length, dtype=jnp.int32) < length - pad_length[0]).astype(F32)[:, None]
    cosine, sine = (jnp.asarray(t) for t in angle_tables(length))

    mixed = dot(normed1, w_mix) + b_mix
    mixed = mixed.reshape(length, 3, heads_n, HEAD_DIM).transpose(1, 2, 0, 3)
    queries = turn(mixed[0], cosine, sine, 1.0).astype(BF)
    keys = turn(mixed[1], cosine, sine, 1.0).astype(BF)
    values = mixed[2].astype(BF)
    d_heads = (dot_nt(dy, w_proj) * valid).astype(BF)
    d_heads = d_heads.reshape(length, heads_n, HEAD_DIM).transpose(1, 0, 2)
    heads, d_q, d_k, d_v = attention(queries, keys, values, d_heads, segments)
    attn_rows = (heads.transpose(1, 0, 2).reshape(length, wide).astype(F32) * valid).astype(BF)
    d_mixed = jnp.stack(
        [
            turn(d_q.astype(F32), cosine, sine, -1.0).astype(BF),
            turn(d_k.astype(F32), cosine, sine, -1.0).astype(BF),
            d_v,
        ]
    )
    d_mixed = d_mixed.transpose(2, 0, 1, 3).reshape(length, 3 * wide)

    upward = dot(normed2, w_rise) + b_rise
    active = jax.nn.gelu(upward, approximate=False).astype(BF)
    slope = 0.5 * (1 + lax.erf(upward * (0.5**0.5))) + upward * jnp.exp(
        -0.5 * upward * upward
    ) * ((2 * np.pi) ** -0.5)
    d_up = (slope * dot_nt(dy, w_fall)).astype(BF)
    out_part = (dot(attn_rows, w_proj) + dot(active, w_fall)).astype(BF)
    d_n1 = dot_nt(d_mixed, w_mix)
    d_n2 = dot_nt(d_up, w_rise)
    back_part = (g1 * d_n1 + g2 * d_n2).astype(BF)

    g_mix = dot_t(normed1, d_mixed).astype(BF).reshape(dp_size, rows, 3 * wide)
    g_proj = dot_t(attn_rows, dy).astype(BF).reshape(dp_size // seq_size, rows, seq_size, wide)
    g_proj = g_proj.transpose(2, 0, 1, 3)
    g_rise = dot_t(normed2, d_up).astype(BF).reshape(dp_size, rows, dp_size * units)
    g_fall = dot_t(active, dy).astype(BF).reshape(dp_size, units, D)
    dyf = dy.astype(F32)
    vec_part = jnp.concatenate(
        [
            t.reshape(dp_size, -1)
            for t in (
                jnp.sum(d_n1 * n, axis=0),
                jnp.sum(d_n1, axis=0),
                jnp.sum(d_n2 * n, axis=0),
                jnp.sum(d_n2, axis=0),
                jnp.sum(dyf, axis=0),
                jnp.sum(d_up.astype(F32), axis=0),
            )
        ]
        + [jnp.broadcast_to(jnp.sum(d_mixed.astype(F32), axis=0)[None], (dp_size, 3 * wide))],
        axis=1,
    )
    part_len = vec_part.shape[1]
    vec_part = jnp.pad(vec_part, ((0, 0), (0, 2048 - part_len))).reshape(dp_size, 16, 128)
    out_sum, back_sum, f_mix, f_proj, f_rise, f_fall, f_vec = reduce_all(
        seq_size,
        dp_size,
        out_part.reshape(seq_size, tok, D),
        back_part.reshape(seq_size, tok, D),
        g_mix,
        g_proj,
        g_rise,
        g_fall,
        vec_part,
    )
    own_x = tokens[0].astype(F32)
    block_output = (own_x + out_sum + b_proj + b_fall).astype(BF)
    own_center = own_x - jnp.mean(own_x, axis=-1, keepdims=True)
    own_rstd = lax.rsqrt(jnp.mean(own_center * own_center, axis=-1, keepdims=True) + EPS)
    own_n = own_center * own_rstd
    back = own_rstd * (
        back_sum
        - jnp.mean(back_sum, axis=-1, keepdims=True)
        - own_n * jnp.mean(back_sum * own_n, axis=-1, keepdims=True)
    )
    input_grad = (cotangent[0].astype(F32) + back).astype(BF)
    f_mix = f_mix.reshape(seq_size, rows, 3, heads_n, HEAD_DIM)
    f_mix = f_mix.transpose(1, 0, 3, 2, 4).reshape(rows, 3 * D).astype(F32)
    f_proj = f_proj.transpose(1, 0, 2).reshape(rows, D).astype(F32)
    f_rise = f_rise.reshape(seq_size, rows, dp_size, units)
    f_rise = f_rise.transpose(1, 2, 0, 3).reshape(rows, FF).astype(F32)
    f_fall = f_fall.reshape(seq_size * units, D).astype(F32)
    f_vec = f_vec.reshape(seq_size, 2048)[:, :part_len]
    norm_sums = jnp.sum(f_vec[:, : 4 * rows], axis=0)
    column = f_vec[0, 4 * rows : 5 * rows]
    f_b_rise = f_vec[:, 5 * rows : 5 * rows + units].reshape(seq_size * units)
    f_b_mix = f_vec[:, 5 * rows + units :].reshape(seq_size, 3, heads_n, HEAD_DIM)
    f_b_mix = f_b_mix.transpose(0, 2, 1, 3).reshape(dp_size, 3 * rows)
    f_b_mix = lax.dynamic_index_in_dim(f_b_mix, dp, 0, keepdims=False)
    return (
        block_output[None],
        input_grad[None],
        norm_sums[:rows],
        norm_sums[rows : 2 * rows],
        norm_sums[2 * rows : 3 * rows],
        norm_sums[3 * rows :],
        f_mix,
        f_b_mix,
        f_proj,
        column,
        f_rise,
        f_b_rise,
        f_fall,
        column,
    )


def shards(*args):
    seq_size, dp_size = lax.axis_size("seq"), lax.axis_size("dp")
    if resident_fits(seq_size, dp_size, args[0].shape[1]):
        return resident_shards(*args)
    return streamed_shards(*args)


def solution(mesh):
    rows = P("dp", "seq", None)
    weight = P("dp", None)
    vector = P("dp")
    return jax.shard_map(
        shards,
        mesh=mesh,
        in_specs=(rows, rows)
        + (vector,) * 4
        + (weight, vector) * 4
        + (P("dp", "seq"), vector),
        out_specs=(rows, rows) + (vector,) * 4 + (weight, vector) * 4,
        check_vma=False,
    )
```

```python
import functools
import typing

import jax
import jax.numpy as jnp
import numpy as np
from jax import lax
from jax.experimental import pallas as pl
from jax.experimental.pallas import tpu as pltpu
from jax.sharding import PartitionSpec as P

D = 1024
HEADS = 16
HEAD_DIM = 64
ROT = 16
FF = 4096
EPS = 1e-05
BASE = 10000.0
NEG = -1e30
MESH = pl.DeviceIdType.MESH
BF = jnp.bfloat16
F32 = jnp.float32


def ring_pos(dev, size):
    return (dev // 2) * (1 - dev % 2) + (size - 1 - dev // 2) * (dev % 2)


def ring_dev(pos, size):
    high = pos // (size // 2)
    return (1 - high) * 2 * pos + high * (2 * (size - 1 - pos) + 1)


class Place:
    def __init__(self, seq_size, dp_size):
        self.seq_size, self.dp_size = seq_size, dp_size
        self.seq = lax.axis_index("seq")
        self.dp = lax.axis_index("dp")
        self.pos = ring_pos(self.dp, dp_size)
        self.half = dp_size // 2
        self.pairs = seq_size // 2
        self.core = self.seq % 2
        self.pair = self.seq // 2
        self.sibling = self.pair * 2 + 1 - self.core

    def ring(self, offset):
        return ring_dev((self.pos + offset + self.dp_size) % self.dp_size, self.dp_size)

    def dp_peer(self, step):
        return (self.dp + step + self.dp_size) % self.dp_size

    def pair_peer(self, step):
        return ((self.pair + step + self.pairs) % self.pairs) * 2 + self.core

    def across_source(self, step):
        return ((self.pair - step + self.pairs) % self.pairs) * 2 + 1 - self.core

    def seq_peer(self, step):
        return (self.seq + step + self.seq_size) % self.seq_size

    def greet_near(self):
        barrier = pltpu.get_barrier_semaphore()
        for step in (1, -1):
            pl.semaphore_signal(barrier, inc=1, device_id={"dp": self.ring(step)}, device_id_type=MESH)
        for step in range(1, self.seq_size):
            pl.semaphore_signal(
                barrier, inc=1, device_id={"seq": self.seq_peer(step)}, device_id_type=MESH
            )

    def met_near(self):
        pl.semaphore_wait(pltpu.get_barrier_semaphore(), 2 + self.seq_size - 1)

    def greet(self):
        barrier = pltpu.get_barrier_semaphore()
        for step in range(1, self.dp_size):
            pl.semaphore_signal(
                barrier, inc=1, device_id={"dp": self.dp_peer(step)}, device_id_type=MESH
            )
        for step in range(1, self.seq_size):
            pl.semaphore_signal(
                barrier, inc=1, device_id={"seq": self.seq_peer(step)}, device_id_type=MESH
            )
        pl.semaphore_wait(barrier, self.dp_size - 1 + self.seq_size - 1)


def send(src, dst, sems, index, target):
    return pltpu.make_async_remote_copy(
        src_ref=src,
        dst_ref=dst,
        send_sem=sems.at[0, index],
        recv_sem=sems.at[1, index],
        device_id=target,
        device_id_type=MESH,
    )


def halves(ref):
    rows = ref.shape[0]
    columns = ref.shape[1]
    if rows % (32 if ref.dtype == BF else 16) == 0:
        return ref.at[pl.ds(0, rows // 2)], ref.at[pl.ds(rows // 2, rows // 2)]
    return ref.at[:, pl.ds(0, columns // 2)], ref.at[:, pl.ds(columns // 2, columns // 2)]


class RingGather:
    def __init__(self, place, full, sems):
        self.place, self.full, self.sems = place, full, sems

    def piece(self, offset, step, way):
        block = self.full.at[self.place.ring(offset)]
        return block if step < self.place.half else halves(block)[way]

    def copies(self, step):
        place = self.place
        right = self.piece(-(step - 1), step, 0)
        left = self.piece(step - 1, step, 1)
        index = 2 * (step - 1)
        return (
            send(right, right, self.sems, index, {"dp": place.ring(1)}),
            send(left, left, self.sems, index + 1, {"dp": place.ring(-1)}),
        )

    def arrivals(self, step):
        right = self.piece(-step, step, 0)
        left = self.piece(step, step, 1)
        index = 2 * (step - 1)
        return (
            send(right, right, self.sems, index, {"dp": self.place.ring(1)}),
            send(left, left, self.sems, index + 1, {"dp": self.place.ring(-1)}),
        )

    def tick(self, step):
        if step > 1:
            for copy in self.arrivals(step - 1):
                copy.wait_recv()
        if step <= self.place.half:
            for copy in self.copies(step):
                copy.start()

    def finish(self):
        for step in range(1, self.place.half + 1):
            for copy in self.copies(step):
                copy.wait_send()


class RingReduce:
    def __init__(self, place, parts, arrived, sems):
        self.place, self.parts, self.arrived, self.sems = place, parts, arrived, sems

    def piece(self, ref, step, way):
        return ref if step > 1 else halves(ref)[way]

    def copies(self, step):
        place = self.place
        away = place.half - step + 1
        index = 2 * (step - 1)
        out = []
        for way, (offset, target) in enumerate(((away, 1), (-away, -1))):
            src = self.piece(self.parts.at[place.ring(offset)], step, way)
            dst = self.piece(self.arrived.at[way, step - 1], step, way)
            out.append(send(src, dst, self.sems, index + way, {"dp": place.ring(target)}))
        return out

    def tick(self, step):
        place = self.place
        if step > 1:
            for way, copy in enumerate(self.copies(step - 1)):
                copy.wait_recv()
                away = (place.half - step + 1) * (1 - 2 * way)
                held = self.piece(self.parts.at[place.ring(away)], step - 1, way)
                came = self.piece(self.arrived.at[way, step - 2], step - 1, way)
                held[...] = (held[...].astype(F32) + came[...].astype(F32)).astype(held.dtype)
        if step <= place.half:
            for copy in self.copies(step):
                copy.start()

    def finish(self):
        for step in range(1, self.place.half + 1):
            for copy in self.copies(step):
                copy.wait_send()

    def own(self):
        return self.parts.at[self.place.dp]


class SeqGather:
    def __init__(self, place, full, sems, own=None):
        self.place, self.full, self.sems = place, full, sems
        self.own = full.at[place.seq] if own is None else own

    def direct(self, step):
        place = self.place
        target = {"seq": place.pair_peer(step)}
        return send(self.own, self.full.at[place.seq], self.sems, step, target)

    def arrival(self, step):
        place = self.place
        target = {"seq": place.pair_peer(step)}
        return send(self.own, self.full.at[place.pair_peer(-step)], self.sems, step, target)

    def across(self, step):
        place = self.place
        block = self.full.at[place.pair_peer(-step)]
        src = self.own if step == 0 else block
        return send(src, block, self.sems, place.pairs + step, {"seq": place.sibling})

    def across_arrival(self, step):
        place = self.place
        block = self.full.at[place.across_source(step)]
        return send(self.own, block, self.sems, place.pairs + step, {"seq": place.sibling})

    def begin(self):
        for step in range(1, self.place.pairs):
            self.direct(step).start()
        self.across(0).start()

    def forward(self):
        for step in range(1, self.place.pairs):
            self.arrival(step).wait_recv()
            self.across(step).start()

    def across_arrived(self, step):
        self.across_arrival(step).wait_recv()

    def sent(self):
        for step in range(1, self.place.pairs):
            self.direct(step).wait_send()
        for step in range(self.place.pairs):
            self.across(step).wait_send()

    def finish(self):
        for step in range(self.place.pairs):
            self.across_arrived(step)
        self.sent()


class SeqReduce:
    def __init__(self, place, parts, crossed, arrived, sems):
        self.place, self.parts, self.crossed, self.arrived = place, parts, crossed, arrived
        self.sems = sems

    def over(self, step):
        place = self.place
        index = (place.pair + step) % place.pairs
        src = self.parts.at[index * 2 + 1 - place.core]
        return send(src, self.crossed.at[index], self.sems, step, {"seq": place.sibling})

    def direct(self, step):
        place = self.place
        return send(
            self.parts.at[place.pair_peer(step)],
            self.arrived.at[step - 1],
            self.sems,
            place.pairs + step,
            {"seq": place.pair_peer(step)},
        )

    def over_start(self, step):
        self.over(step).start()

    def over_add(self, step):
        place = self.place
        index = (place.pair + step) % place.pairs
        self.over(step).wait_recv()
        held = self.parts.at[index * 2 + place.core]
        held[...] = (held[...].astype(F32) + self.crossed[index].astype(F32)).astype(held.dtype)
        if step > 0:
            self.direct(step).start()

    def begin(self):
        for step in range(self.place.pairs):
            self.over_start(step)

    def middle(self):
        for step in range(self.place.pairs):
            self.over_add(step)

    def total(self):
        place = self.place
        total = self.parts.at[place.seq][...].astype(F32)
        for step in range(1, place.pairs):
            self.direct(step).wait_recv()
            total = total + self.arrived[step - 1].astype(F32)
        return total

    def finish(self):
        for step in range(self.place.pairs):
            self.over(step).wait_send()
        for step in range(1, self.place.pairs):
            self.direct(step).wait_send()


class DpSpread:
    def __init__(self, place, src_of, full, sems):
        self.place, self.src_of, self.full, self.sems = place, src_of, full, sems

    def copy(self, step):
        place = self.place
        peer = place.dp_peer(step)
        return send(self.src_of(peer), self.full.at[place.dp], self.sems, step, {"dp": peer})

    def arrival(self, step):
        place = self.place
        source = place.dp_peer(-step)
        return send(
            self.src_of(source), self.full.at[source], self.sems, step, {"dp": place.dp_peer(step)}
        )

    def begin(self):
        for step in range(1, self.place.dp_size):
            self.copy(step).start()

    def finish(self):
        for step in range(1, self.place.dp_size):
            self.arrival(step).wait_recv()
        for step in range(1, self.place.dp_size):
            self.copy(step).wait_send()


def sems_of(count):
    return pltpu.SemaphoreType.DMA((2, count))


def gather_kernel(seq_size, dp_size, *refs):
    (x_ref, dy_ref, mix_ref, proj_ref, rise_ref, fall_ref, vec_ref, seg_ref) = refs[:8]
    (x_all, dy_all, mix_all, proj_cols, rise_all, fall_all, vec_all, seg_all, proj_all) = refs[8:17]
    (x_sems, dy_sems, mix_sems, proj_sems, rise_sems, fall_sems, vec_sems, seg_sems, swap_sems, own_sems) = refs[17:]
    place = Place(seq_size, dp_size)
    own = [
        pltpu.make_async_copy(src, dst, own_sems.at[i])
        for i, (src, dst) in enumerate(
            (
                (x_ref, x_all.at[place.seq]),
                (dy_ref, dy_all.at[place.seq]),
                (mix_ref, mix_all.at[place.dp]),
                (proj_ref, proj_cols.at[place.dp]),
                (rise_ref, rise_all.at[place.dp]),
                (fall_ref, fall_all.at[place.dp]),
                (vec_ref, vec_all.at[place.dp]),
                (seg_ref, seg_all.at[place.seq]),
            )
        )
    ]
    for copy in own:
        copy.start()
    place.greet()
    for copy in own:
        copy.wait()
    x_move = SeqGather(place, x_all, x_sems)
    dy_move = SeqGather(place, dy_all, dy_sems)
    seg_move = SeqGather(place, seg_all, seg_sems)
    vec_move = DpSpread(place, lambda peer: vec_ref, vec_all, vec_sems)
    mix_move = RingGather(place, mix_all, mix_sems)
    proj_move = RingGather(place, proj_cols, proj_sems)
    rise_move = RingGather(place, rise_all, rise_sems)
    fall_move = RingGather(place, fall_all, fall_sems)
    x_move.begin()
    seg_move.begin()
    vec_move.begin()
    half = place.half
    for step in range(1, half + 1):
        mix_move.tick(step)
        proj_move.tick(step)
    x_move.forward()
    seg_move.forward()
    dy_move.begin()
    mix_move.tick(half + 1)
    proj_move.tick(half + 1)
    rise_move.tick(1)
    fall_move.tick(1)
    rows = proj_cols.shape[0] * proj_cols.shape[1] // seq_size
    each = rows // proj_cols.shape[1]
    swaps = []
    for step in range(1, seq_size):
        peer = place.seq_peer(step)
        swaps.append(
            send(
                proj_cols.at[pl.ds(peer * each, each)],
                proj_all.at[place.seq],
                swap_sems,
                step,
                {"seq": peer},
            )
        )
    for copy in swaps:
        copy.start()
    mine = pltpu.make_async_copy(
        proj_cols.at[pl.ds(place.seq * each, each)], proj_all.at[place.seq], own_sems.at[0]
    )
    mine.start()
    for step in range(2, half + 2):
        rise_move.tick(step)
        fall_move.tick(step)
        if step == 3:
            dy_move.forward()
    mine.wait()
    for step in range(1, seq_size):
        source = place.seq_peer(-step)
        send(
            proj_cols.at[pl.ds(source * each, each)],
            proj_all.at[source],
            swap_sems,
            step,
            {"seq": place.seq_peer(step)},
        ).wait_recv()
    for copy in swaps:
        copy.wait_send()
    for move in (x_move, dy_move, seg_move, vec_move, mix_move, proj_move, rise_move, fall_move):
        move.finish()


def gather_all(seq_size, dp_size, x, dy, mix, proj, rise, fall, vec, seg):
    half = dp_size // 2
    pairs = seq_size // 2

    def lead(count, like):
        return jax.ShapeDtypeStruct((count,) + like.shape, like.dtype)

    each = dp_size // seq_size
    any_spec = pl.BlockSpec(memory_space=pl.ANY)
    return pl.pallas_call(
        functools.partial(gather_kernel, seq_size, dp_size),
        out_shape=(
            lead(seq_size, x),
            lead(seq_size, dy),
            lead(dp_size, mix),
            lead(dp_size, proj),
            lead(dp_size, rise),
            lead(dp_size, fall),
            lead(dp_size, vec),
            lead(seq_size, seg),
            jax.ShapeDtypeStruct((seq_size, each) + proj.shape, proj.dtype),
        ),
        in_specs=[any_spec] * 8,
        out_specs=[any_spec] * 9,
        scratch_shapes=[
            sems_of(2 * pairs),
            sems_of(2 * pairs),
            sems_of(2 * half),
            sems_of(2 * half),
            sems_of(2 * half),
            sems_of(2 * half),
            sems_of(dp_size),
            sems_of(2 * pairs),
            sems_of(seq_size),
            pltpu.SemaphoreType.DMA((8,)),
        ],
        compiler_params=pltpu.CompilerParams(collective_id=0, has_side_effects=True),
    )(x, dy, mix, proj, rise, fall, vec, seg)


def reduce_kernel(seq_size, dp_size, *refs):
    (out_ref, back_ref, mix_ref, proj_ref, rise_ref, fall_ref, vec_ref), refs = refs[:7], refs[7:]
    (out_sum, back_sum, mix_fin, proj_fin, rise_fin, fall_fin, vec_fin), refs = refs[:7], refs[7:]
    (
        out_cross,
        out_came,
        back_cross,
        back_came,
        proj_full,
        mix_came,
        proj_came,
        rise_came,
        fall_came,
        vec_came,
        out_sems,
        back_sems,
        swap_sems,
        mix_sems,
        proj_sems,
        rise_sems,
        fall_sems,
        vec_sems,
        mix_fs,
        proj_fs,
        rise_fs,
        fall_fs,
        vec_fs,
    ) = refs
    place = Place(seq_size, dp_size)
    each = dp_size // seq_size
    half = place.half
    place.greet()

    def mine(index):
        return proj_full.at[pl.ds(index * each, each)]

    def swap(step):
        peer = place.seq_peer(step)
        return send(proj_ref.at[peer], mine(place.seq), swap_sems, step, {"seq": peer})

    def swap_arrival(step):
        source = place.seq_peer(-step)
        target = {"seq": place.seq_peer(step)}
        return send(proj_ref.at[source], mine(source), swap_sems, step, target)

    for step in range(1, seq_size):
        swap(step).start()
    mine(place.seq)[...] = proj_ref[place.seq]
    mix = RingReduce(place, mix_ref, mix_came, mix_sems)
    proj = RingReduce(place, proj_full, proj_came, proj_sems)
    rise = RingReduce(place, rise_ref, rise_came, rise_sems)
    fall = RingReduce(place, fall_ref, fall_came, fall_sems)
    out = SeqReduce(place, out_ref, out_cross, out_came, out_sems)
    back = SeqReduce(place, back_ref, back_cross, back_came, back_sems)
    vec = DpSpread(place, lambda peer: vec_ref.at[peer], vec_came, vec_sems)
    mix.tick(1)
    rise.tick(1)
    out.begin()
    back.begin()
    vec.begin()
    for step in range(1, seq_size):
        swap_arrival(step).wait_recv()
    proj.tick(1)
    fall.tick(1)
    out.middle()
    back.middle()
    for step in range(2, half + 2):
        for move in (mix, rise, proj, fall):
            move.tick(step)
    finals = []
    for move, fin, fin_sems in (
        (mix, mix_fin, mix_fs),
        (rise, rise_fin, rise_fs),
        (proj, proj_fin, proj_fs),
        (fall, fall_fin, fall_fs),
    ):
        fin[place.seq] = move.parts[place.dp]
        gather = SeqGather(place, fin, fin_sems)
        gather.begin()
        finals.append(gather)
    vec_came[place.dp] = vec_ref[place.dp]
    vec.finish()
    vec_fin[place.seq] = jnp.sum(vec_came[...], axis=0)
    gather = SeqGather(place, vec_fin, vec_fs)
    gather.begin()
    finals.append(gather)
    out_sum[...] = out.total()
    back_sum[...] = back.total()
    for gather in finals:
        gather.forward()
    for gather in finals:
        gather.finish()
    for step in range(1, seq_size):
        swap(step).wait_send()
    for move in (mix, rise, proj, fall, out, back):
        move.finish()


def reduce_all(seq_size, dp_size, out, back, mix, proj, rise, fall, vec):
    half = dp_size // 2
    pairs = seq_size // 2
    each = dp_size // seq_size

    def fin(like):
        return jax.ShapeDtypeStruct((seq_size,) + like.shape[1:], like.dtype)

    def came(like):
        return pltpu.VMEM((2, half) + like.shape[1:], like.dtype)

    proj_blocks = jax.ShapeDtypeStruct((dp_size,) + proj.shape[2:], proj.dtype)
    vmem = pl.BlockSpec(memory_space=pltpu.VMEM)
    return pl.pallas_call(
        functools.partial(reduce_kernel, seq_size, dp_size),
        out_shape=(
            jax.ShapeDtypeStruct(out.shape[1:], F32),
            jax.ShapeDtypeStruct(back.shape[1:], F32),
            fin(mix),
            fin(proj_blocks),
            fin(rise),
            fin(fall),
            fin(vec),
        ),
        in_specs=[vmem] * 7,
        out_specs=[vmem] * 7,
        scratch_shapes=[
            pltpu.VMEM((pairs,) + out.shape[1:], BF),
            pltpu.VMEM((pairs,) + out.shape[1:], BF),
            pltpu.VMEM((pairs,) + back.shape[1:], BF),
            pltpu.VMEM((pairs,) + back.shape[1:], BF),
            pltpu.VMEM(proj_blocks.shape, BF),
            came(mix),
            came(proj_blocks),
            came(rise),
            came(fall),
            pltpu.VMEM(vec.shape, F32),
            sems_of(2 * pairs),
            sems_of(2 * pairs),
            sems_of(seq_size),
            sems_of(2 * half),
            sems_of(2 * half),
            sems_of(2 * half),
            sems_of(2 * half),
            sems_of(dp_size),
            sems_of(2 * pairs),
            sems_of(2 * pairs),
            sems_of(2 * pairs),
            sems_of(2 * pairs),
            sems_of(2 * pairs),
        ],
        compiler_params=pltpu.CompilerParams(
            collective_id=1, has_side_effects=True, vmem_limit_bytes=56 * 2**20
        ),
    )(out, back, mix, proj, rise, fall, vec)


def angle_tables(length):
    frequency = BASE ** (-np.arange(0, ROT, 2).astype(np.float32) / np.float32(ROT))
    angles = np.arange(length, dtype=np.float32)[:, None] * frequency.astype(np.float32)[None, :]
    return np.cos(angles).astype(np.float32), np.sin(angles).astype(np.float32)


def turn(piece, cosine, sine, sign):
    half = ROT // 2
    low, high = piece[..., :half], piece[..., half:ROT]
    return jnp.concatenate(
        [low * cosine - sign * high * sine, high * cosine + sign * low * sine, piece[..., ROT:]],
        axis=-1,
    )


TILE = 256

def mm(a, b, dims):
    return lax.dot_general(a, b, ((dims[0], dims[1]), ((), ())), preferred_element_type=F32)

def nn(a, b):
    return mm(a, b, ((1,), (0,)))

def nt(a, b):
    return mm(a, b, ((1,), (1,)))

def tn(a, b):
    return mm(a, b, ((0,), (0,)))

def fold(count, body, init):
    if isinstance(count, int):
        for index in range(count):
            init = body(index, init)
        return init
    return lax.fori_loop(0, count, body, init)

def rows_of(index):
    start = index * TILE
    return pl.ds(start if isinstance(start, int) else pl.multiple_of(start, TILE), TILE)

def attend_block(head, block, refs):
    q_ref, k_ref, v_ref, g_ref, kt_ref, vt_ref, s_ref, p_ref, ht_ref, dqt_ref, dk_ref, dv_ref = refs
    here = rows_of(block)
    span = block + 1
    dims = pl.ds(pl.multiple_of(head * HEAD_DIM, HEAD_DIM), HEAD_DIM)
    query = q_ref[head, here, :]
    grad = g_ref[head, here, :]

    def score(index, top):
        tile = nt(k_ref[head, rows_of(index), :], query)
        if isinstance(index, int) and isinstance(block, int) and index < block:
            keep = tile
        else:
            key = lax.broadcasted_iota(jnp.int32, (TILE, TILE), 0) + (index - block) * TILE
            place = lax.broadcasted_iota(jnp.int32, (TILE, TILE), 1)
            keep = jnp.where(key <= place, tile, NEG)
        s_ref[index] = keep
        return jnp.maximum(top, jnp.max(keep, axis=0, keepdims=True))

    top = fold(span, score, jnp.full((1, TILE), 2 * NEG, F32))

    def raise_(index, total):
        raised = jnp.exp(s_ref[index] - top)
        s_ref[index] = raised
        return total + jnp.sum(raised, axis=0, keepdims=True)

    total = fold(span, raise_, jnp.zeros((1, TILE), F32))
    share = 1.0 / total

    def weigh(index, carried):
        heads, delta = carried
        weights = s_ref[index] * share
        s_ref[index] = weights
        weights_b = weights.astype(BF)
        d_weights = nt(v_ref[head, rows_of(index), :], grad)
        p_ref[index] = d_weights
        dv_ref[head, rows_of(index), :] += nn(weights_b, grad)
        heads = heads + nn(vt_ref[dims, rows_of(index)], weights_b)
        return heads, delta + jnp.sum(weights * d_weights, axis=0, keepdims=True)

    heads, delta = fold(
        span, weigh, (jnp.zeros((HEAD_DIM, TILE), F32), jnp.zeros((1, TILE), F32))
    )
    ht_ref[dims, here] = heads

    def back(index, d_query):
        d_scores = (s_ref[index] * (p_ref[index] - delta)).astype(BF)
        dk_ref[head, rows_of(index), :] += nn(d_scores, query)
        return d_query + nn(kt_ref[dims, rows_of(index)], d_scores)

    dqt_ref[dims, here] = fold(span, back, jnp.zeros((HEAD_DIM, TILE), F32))

def attend(heads_n, length, refs):
    dk_ref, dv_ref = refs[-2:]
    dk_ref[...] = jnp.zeros(dk_ref.shape, F32)
    dv_ref[...] = jnp.zeros(dv_ref.shape, F32)
    blocks = length // TILE

    @pl.loop(0, heads_n)
    def _(head):
        if blocks <= 4:
            for block in range(blocks):
                attend_block(head, block, refs)
        else:
            @pl.loop(0, blocks)
            def _(block):
                attend_block(head, block, refs)

def attend_kernel(H, L, q, k, v, g, kt, vt, ht, dqt, dk, dv, s_ref, p_ref):
    attend(H, L, (q, k, v, g, kt, vt, s_ref, p_ref, ht, dqt, dk, dv))

def attention_call(q, k, v, g, kt, vt):
    H, L, _ = q.shape
    vm = pl.BlockSpec(memory_space=pltpu.VMEM)
    nb = L // TILE
    return pl.pallas_call(functools.partial(attend_kernel, H, L),
        out_shape=(jax.ShapeDtypeStruct((H*64, L), F32), jax.ShapeDtypeStruct((H*64, L), F32), jax.ShapeDtypeStruct((H, L, 128), F32), jax.ShapeDtypeStruct((H, L, 128), F32)),
        in_specs=[vm]*6, out_specs=[vm]*4,
        scratch_shapes=[pltpu.VMEM((nb, TILE, TILE), F32), pltpu.VMEM((nb, TILE, TILE), F32)],
        compiler_params=pltpu.CompilerParams(vmem_limit_bytes=56 * 2**20))(q, k, v, g, kt, vt)

def prep(queries, keys, values, d_heads, segments):
    seg = segments[:, None] == jnp.arange(64)[None, :]
    e = jnp.broadcast_to(seg.astype(BF)[None], queries.shape)
    f = jnp.broadcast_to(jnp.where(seg, 0.0, NEG).astype(BF)[None], queries.shape)
    lane = jnp.arange(64)
    f = jnp.where(lane < 4, f, 0).astype(BF)
    qa = jnp.concatenate([(queries.astype(F32) * 0.125).astype(BF), e], -1)
    ka = jnp.concatenate([keys, f], -1)
    z = jnp.zeros_like(values)
    va = jnp.concatenate([values, z], -1)
    ga = jnp.concatenate([d_heads, z], -1)
    kt = keys.transpose(0, 2, 1).reshape(-1, keys.shape[1])
    vt = values.transpose(0, 2, 1).reshape(-1, keys.shape[1])
    return qa, ka, va, ga, kt, vt

def attention(queries, keys, values, d_heads, segments):
    H, L, _ = queries.shape
    ht, dqt, dk, dv = attention_call(*prep(queries, keys, values, d_heads, segments))

    def back(t):
        return t.reshape(H, 64, L).transpose(0, 2, 1)

    return back(ht).astype(BF), (back(dqt) * 0.125).astype(BF), dk[..., :64].astype(BF), dv[..., :64].astype(BF)


def dot(a, b):
    return jnp.dot(a, b, preferred_element_type=F32)


def dot_t(a, b):
    return lax.dot_general(a, b, (((0,), (0,)), ((), ())), preferred_element_type=F32)


def dot_nt(a, b):
    return lax.dot_general(a, b, (((1,), (1,)), ((), ())), preferred_element_type=F32)


(
    OWN, XGO, DYGO, XFWD, DYFWD, HOTS, DYALL, VROWS, LN0, LN1, LN2, LN3, SWGO, SWIN, QKV0, QKV1,
    DH, GVC1, GVC2, GVC3, GVC4, GVC5, GMA1, GMA2, GMA3, GMA4, GMA5, GMB1, GMB2, GMB3, GMB4,
    GMB5, GPR1, GPR2, GPR3, GPR4, GPR5, GRA1, GRA2, GRA3, GRA4, GRA5, GRB1, GRB2, GRB3, GRB4,
    GRB5, GFA1, GFA2, GFA3, GFA4, GFA5, GFB1, GFB2, GFB3, GFB4, GFB5, RVC1, RVC2, RVC3, RVC4,
    RVC5, RMA1, RMA2, RMA3, RMA4, RMA5, RMB1, RMB2, RMB3, RMB4, RMB5, RPR1, RPR2, RPR3, RPR4,
    RPR5, RRA1, RRA2, RRA3, RRA4, RRA5, RRB1, RRB2, RRB3, RRB4, RRB5, RFA1, RFA2, RFA3, RFA4,
    RFA5, RFB1, RFB2, RFB3, RFB4, RFB5, AT00, AT02, AT03, AT10, AT12, AT13, AT20, AT22, AT23,
    AT30, AT32, AT33, POST, GM, GR, GF, GP, SBGO, SBIN, UP0, UP1, UP2, UP3, DN0, DN1, OP0, OP1,
    BK0, BK1, OM0, OM1, BM0, BM1, VP, BO, IG, SV, WV, VO, SMA, SMB, SPR, SRA, SRB, SFA, SFB,
    WMA, WMB, WPR, WRA, WRB, WFA, WFB, CMA, CMB, CPR, CRA, CRB, CFA, CFB,
) = range(157)

ORDER = (
    OWN, GVC1, GPR1, XGO, GRA1, GVC2, GRB1, GPR2, GRA2, GVC3, GMB1, GRB2, GRA3, GPR3, DYGO,
    GVC4, GMA1, GMB2, GVC5, GRB3, GMA2, DYFWD, VROWS, GRA4, LN0, GPR4, DYALL, GRB4, XFWD, GMB3,
    LN1, GMA3, LN3, GRA5, GPR5, SWGO, LN2, GFA1, GRB5, HOTS, UP3, UP1, GFB1, UP2, UP0, GMA4,
    GMB4, GF, GFA2, SWIN, DH, GFB2, RFB1, GMA5, RFA1, GMB5, QKV0, AT20, AT00, GFA3, QKV1, AT22,
    RFB2, AT30, GFB3, RFA2, AT23, AT32, AT02, AT10, RFB3, AT33, AT12, AT03, GFB4, GFA4, AT13,
    RFA3, POST, GFB5, RFB4, GP, GM, RMB1, SBGO, RMA1, GFA5, RFA4, DN1, DN0, RMB2, OP1, RMA2, GR,
    RRA1, OM1, RRB1, SBIN, RMB3, BK1, RFA5, RRA2, RPR1, BK0, SFA, RRB2, OP0, RRA3, RPR2, VP,
    RVC1, BM1, RRB3, RFB5, RRA4, SFB, RPR3, RVC2, RRB4, RMA3, RVC3, RPR4, RRA5, SRA, RRB5, SRB,
    RMB4, RMA4, RPR5, SPR, WFA, RVC4, OM0, RMB5, SMB, RMA5, SMA, BM0, WRB, RVC5, WFB, CFA, SV,
    WPR, WRA, IG, CPR, BO, WMB, CMB, CRB, CRA, WMA, CFB, WV, CMA, VO,
)
LANES = 128
HALF = LANES // 2
VEC_ROWS = 16
PROJ = 3
TURN = 32


def resident_fits(seq_size, dp_size, tok):
    return (
        D // dp_size == LANES
        and FF // dp_size // seq_size == LANES
        and HEADS // seq_size == 4
        and tok * seq_size <= TURN * TURN
        and tok % TILE == 0
    )


def rows_at(ref, index, count):
    return ref.at[pl.ds(pl.multiple_of(index * count, count), count)]


def columns_at(ref, index, count):
    return ref.at[:, pl.ds(pl.multiple_of(index * count, count), count)]


class Flat:
    def __init__(self, ref, count, stride=None, start=0):
        self.ref, self.count, self.start = ref, count, start
        self.stride = count if stride is None else stride

    @property
    def at(self):
        return self

    def __getitem__(self, index):
        first = pl.multiple_of(index * self.stride + self.start, self.count)
        return self.ref.at[pl.ds(first, self.count)]


class Stack:
    def __init__(self, ref, start, count):
        self.ref, self.start, self.count = ref, start, count

    @property
    def at(self):
        return self

    def __getitem__(self, index):
        return self.ref.at[index, pl.ds(self.start, self.count)]


def lanes_like(shape):
    return lax.broadcasted_iota(jnp.int32, shape, len(shape) - 1)


def head_part(values, start):
    tile = values[:, start // LANES * LANES : start // LANES * LANES + LANES]
    return tile if start % LANES == 0 else pltpu.roll(tile, HEAD_DIM, 1)


def spin(tile, cosine, sine):
    lane = lanes_like(tile.shape)
    partner = jnp.where(lane < ROT // 2, pltpu.roll(tile, LANES - ROT // 2, 1), pltpu.roll(tile, ROT // 2, 1))
    return tile * cosine + partner * sine


def attend_head(head, block, refs):
    q_ref, k_ref, v_ref, g_ref, kt_ref, vt_ref, s_ref, p_ref, ht_ref, dqt_ref, dk_ref, dv_ref = refs
    here = pl.ds(block * TILE, TILE)
    wide = pl.ds(head * LANES, LANES)
    dims = pl.ds(head * HEAD_DIM, HEAD_DIM)
    query = q_ref[here, wide]
    grad = g_ref[here, wide]
    span = block + 1
    top = jnp.full((1, TILE), 2 * NEG, F32)
    for index in range(span):
        tile = nt(k_ref[pl.ds(index * TILE, TILE), wide], query)
        if index == block:
            key = lax.broadcasted_iota(jnp.int32, (TILE, TILE), 0)
            place = lax.broadcasted_iota(jnp.int32, (TILE, TILE), 1)
            tile = jnp.where(key <= place, tile, NEG)
        s_ref[index] = tile
        top = jnp.maximum(top, jnp.max(tile, axis=0, keepdims=True))
    total = jnp.zeros((1, TILE), F32)
    for index in range(span):
        raised = jnp.exp(s_ref[index] - top)
        s_ref[index] = raised
        total = total + jnp.sum(raised, axis=0, keepdims=True)
    share = 1.0 / total
    delta = jnp.zeros((1, TILE), F32)
    heads = jnp.zeros((HEAD_DIM, TILE), F32)
    for index in range(span):
        there = pl.ds(index * TILE, TILE)
        weights = s_ref[index] * share
        s_ref[index] = weights
        weights_b = weights.astype(BF)
        d_weights = nt(v_ref[there, wide], grad)
        p_ref[index] = d_weights
        d_value = nn(weights_b, grad)
        dv_ref[head, there, :] = d_value if index == block else dv_ref[head, there, :] + d_value
        heads = heads + nn(vt_ref[dims, there], weights_b)
        delta = delta + jnp.sum(weights * d_weights, axis=0, keepdims=True)
    ht_ref[dims, here] = heads.astype(BF)
    d_query = jnp.zeros((HEAD_DIM, TILE), F32)
    for index in range(span):
        there = pl.ds(index * TILE, TILE)
        d_scores = (s_ref[index] * (p_ref[index] - delta)).astype(BF)
        d_key = nn(d_scores, query)
        dk_ref[head, there, :] = d_key if index == block else dk_ref[head, there, :] + d_key
        d_query = d_query + nn(kt_ref[dims, there], d_scores)
    dqt_ref[dims, here] = (d_query * HEAD_DIM**-0.5).astype(BF)


class Refs(typing.NamedTuple):
    x_own: typing.Any
    dy_own: typing.Any
    w_mix_own: typing.Any
    w_proj_own: typing.Any
    w_rise_own: typing.Any
    w_fall_own: typing.Any
    gain1_own: typing.Any
    shift1_own: typing.Any
    gain2_own: typing.Any
    shift2_own: typing.Any
    b_proj_own: typing.Any
    b_fall_own: typing.Any
    b_mix_own: typing.Any
    b_rise_own: typing.Any
    seg_own: typing.Any
    pad_own: typing.Any
    turns: typing.Any
    block_out: typing.Any
    input_grad: typing.Any
    mix_fin: typing.Any
    proj_fin: typing.Any
    rise_fin: typing.Any
    fall_fin: typing.Any
    vec_result: typing.Any
    pad: typing.Any
    cos: typing.Any
    sin: typing.Any
    x: typing.Any
    dy: typing.Any
    hot: typing.Any
    segs: typing.Any
    w_mix: typing.Any
    w_proj_cols: typing.Any
    w_proj: typing.Any
    w_rise: typing.Any
    w_fall: typing.Any
    vec_all: typing.Any
    rows: typing.Any
    normed1: typing.Any
    normed2: typing.Any
    stat: typing.Any
    qk: typing.Any
    vg: typing.Any
    kt: typing.Any
    vt: typing.Any
    s: typing.Any
    p: typing.Any
    ht: typing.Any
    dqt: typing.Any
    dk: typing.Any
    dv: typing.Any
    attn: typing.Any
    d_mixed: typing.Any
    out_part: typing.Any
    back_part: typing.Any
    active: typing.Any
    d_up: typing.Any
    g_mix: typing.Any
    g_proj_cols: typing.Any
    g_rise: typing.Any
    g_fall: typing.Any
    c_mix: typing.Any
    c_proj: typing.Any
    c_rise: typing.Any
    c_fall: typing.Any
    out_cross: typing.Any
    out_came: typing.Any
    back_cross: typing.Any
    back_came: typing.Any
    sums: typing.Any
    vec_part: typing.Any
    vec_came: typing.Any
    mix_got: typing.Any
    proj_got: typing.Any
    rise_got: typing.Any
    fall_got: typing.Any
    vec_fin: typing.Any
    vec_out: typing.Any
    m_x: typing.Any
    m_dy: typing.Any
    m_hot: typing.Any
    m_vec: typing.Any
    m_mix: typing.Any
    m_proj: typing.Any
    m_rise: typing.Any
    m_fall: typing.Any
    m_swap: typing.Any
    m_own: typing.Any
    m_swap2: typing.Any
    m_rmix: typing.Any
    m_rproj: typing.Any
    m_rrise: typing.Any
    m_rfall: typing.Any
    m_out: typing.Any
    m_back: typing.Any
    m_vec2: typing.Any
    m_fmix: typing.Any
    m_fproj: typing.Any
    m_frise: typing.Any
    m_ffall: typing.Any
    m_fvec: typing.Any
    m_fin: typing.Any


def resident_kernel(seq_size, dp_size, *refs):
    r = Refs(*refs)
    place = Place(seq_size, dp_size)
    half = place.half
    tok = r.x_own.shape[0]
    length = r.x.shape[0]
    wide = r.w_proj.shape[0]
    mixed_wide = 3 * wide
    units = LANES
    each = dp_size // seq_size
    heads_n = wide // HEAD_DIM
    blocks = length // TILE

    place.greet_near()
    own = []

    def bring(src, dst):
        copy = pltpu.make_async_copy(src, dst, r.m_own.at[len(own)])
        copy.start()
        own.append(copy)

    bring(columns_at(r.w_mix_own, place.seq, mixed_wide), rows_at(r.w_mix, place.dp, LANES))
    bring(columns_at(r.w_proj_own, place.seq, wide), rows_at(r.w_proj_cols, place.dp, LANES))
    bring(r.x_own, rows_at(r.x, place.seq, tok))
    bring(r.dy_own, rows_at(r.dy, place.seq, tok))
    for index in range(dp_size):
        bring(
            columns_at(r.w_rise_own, index * seq_size + place.seq, units),
            rows_at(r.w_rise, place.dp, LANES).at[:, pl.ds(index * units, units)],
        )
    bring(rows_at(r.w_fall_own, place.seq, units), rows_at(r.w_fall, place.dp, units))
    bring(r.pad_own, r.pad)

    coarse_cos, coarse_sin, fine_cos, fine_sin = (
        r.turns.at[pl.ds(index * TURN, TURN)] for index in range(4)
    )

    @pl.loop(0, length // TURN)
    def _(step):
        here = pl.ds(pl.multiple_of(step * TURN, TURN), TURN)
        far_cos, far_sin = coarse_cos[pl.ds(step, 1), :], coarse_sin[pl.ds(step, 1), :]
        r.cos[here, :] = far_cos * fine_cos[...] - far_sin * fine_sin[...]
        r.sin[here, :] = far_sin * fine_cos[...] + far_cos * fine_sin[...]

    row = 0
    vectors = (r.gain1_own, r.shift1_own, r.gain2_own, r.shift2_own, r.b_proj_own, r.b_fall_own, r.b_mix_own, r.b_rise_own)
    for vector in vectors:
        count = vector.shape[0]
        r.vec_all[place.dp, row : row + count, :] = vector[...].astype(F32)
        row += count
    r.vec_all[place.dp, row:, :] = jnp.zeros((VEC_ROWS - row, LANES), F32)
    rows_at(r.segs, place.seq, 8)[...] = jnp.broadcast_to(r.seg_own[...], (8, tok)).astype(F32)

    def pair_of(ref, make):
        return [make(Flat(ref, HALF, LANES, start), index) for index, start in enumerate((0, HALF))]

    def gather_pair(ref, sems):
        return pair_of(ref, lambda part, index: RingGather(place, part, sems.at[index]))

    def reduce_pair(ref, came, sems):
        return pair_of(ref, lambda part, index: RingReduce(place, part, came.at[index], sems.at[index]))

    def final_pair(out_ref, sems, ref):
        return pair_of(
            ref,
            lambda part, index: SeqGather(
                place, Stack(out_ref, index * HALF, HALF), sems.at[index], part[place.dp]
            ),
        )

    gathers = [
        RingGather(place, r.vec_all, r.m_vec),
        *gather_pair(r.w_mix, r.m_mix),
        RingGather(place, Flat(r.w_proj_cols, LANES), r.m_proj),
        *gather_pair(r.w_rise, r.m_rise),
        *gather_pair(r.w_fall, r.m_fall),
    ]
    reduces = [
        RingReduce(place, r.vec_part, r.vec_came, r.m_vec2),
        *reduce_pair(r.g_mix, r.c_mix, r.m_rmix),
        RingReduce(place, Flat(r.g_proj_cols, LANES), r.c_proj, r.m_rproj),
        *reduce_pair(r.g_rise, r.c_rise, r.m_rrise),
        *reduce_pair(r.g_fall, r.c_fall, r.m_rfall),
    ]
    finals = [
        *final_pair(r.mix_got, r.m_fmix, r.g_mix),
        SeqGather(place, r.proj_got, r.m_fproj, rows_at(r.g_proj_cols, place.dp, LANES)),
        *final_pair(r.rise_got, r.m_frise, r.g_rise),
        *final_pair(r.fall_got, r.m_ffall, r.g_fall),
    ]
    homes = [r.proj_fin]
    for out_ref in (r.rise_fin, r.fall_fin):
        homes += [Stack(out_ref, start, HALF) for start in (0, HALF)]
    homes = [Stack(r.mix_fin, start, HALF) for start in (0, HALF)] + homes
    f_vec = SeqGather(place, r.vec_fin, r.m_fvec)

    x_move = SeqGather(place, Flat(r.x, tok), r.m_x)
    dy_move = SeqGather(place, Flat(r.dy, tok), r.m_dy)
    seg_move = SeqGather(place, Flat(r.segs, 8), r.m_hot)
    out = SeqReduce(place, Flat(r.out_part, tok), r.out_cross, r.out_came, r.m_out)
    back = SeqReduce(place, Flat(r.back_part, tok), r.back_cross, r.back_came, r.m_back)

    leaving = []

    def leave(src, dst):
        copy = pltpu.make_async_copy(src, dst, r.m_fin.at[len(leaving)])
        copy.start()
        leaving.append(copy)

    pieces = {}

    def piece(name, *given):
        def note(run):
            pieces[name] = functools.partial(run, *given)
            return run

        return note

    def tile_rows(block):
        return pl.ds(pl.multiple_of(block * TILE, TILE), TILE)

    def gather(stream, step):
        gathers[stream].tick(step)

    def reduce(stream, step):
        reduces[stream].tick(step)

    for stream in range(len(gathers)):
        for step in range(1, half + 2):
            tick = stream * (half + 1) + step - 1
            piece(GVC1 + tick, stream, step)(gather)
            piece(RVC1 + tick, stream, step)(reduce)

    @piece(OWN)
    def _():
        for copy in own:
            copy.wait()

    @piece(XGO)
    def _():
        x_move.begin()
        seg_move.begin()

    piece(DYGO)(dy_move.begin)

    @piece(XFWD)
    def _():
        x_move.forward()
        seg_move.forward()

    piece(DYFWD)(dy_move.forward)

    @piece(HOTS)
    def _():
        for step in range(place.pairs):
            seg_move.across_arrived(step)
        kind = lax.broadcasted_iota(jnp.int32, (LANES, tok), 0) - HEAD_DIM
        for index in range(seq_size):
            segment = r.segs[index * 8 : index * 8 + 1, :].astype(jnp.int32)
            r.hot[index * tok : (index + 1) * tok, :] = jnp.where(segment == kind, 1.0, 0.0).T.astype(BF)

    @piece(DYALL)
    def _():
        for step in range(place.pairs):
            dy_move.across_arrived(step)

    @piece(VROWS)
    def _():
        for index in range(dp_size):
            at = slice(index * LANES, (index + 1) * LANES)
            for row in range(6):
                r.rows[row : row + 1, at] = r.vec_all[index, row : row + 1, :]
            r.rows[6:7, at] = r.vec_all[index, pl.ds(9 + place.seq, 1), :]
        for index in range(each):
            for row in range(3):
                start = (index * 3 + row) * LANES
                r.rows[7:8, start : start + LANES] = r.vec_all[place.seq * each + index, 6 + row : 7 + row, :]

    chunk = 64

    def normalize(block):
        @pl.loop(0, tok // chunk)
        def _(step):
            here = pl.ds(pl.multiple_of(block * tok + step * chunk, chunk), chunk)
            values = r.x[here, :].astype(F32)
            mean = jnp.sum(values, axis=-1, keepdims=True) * (1.0 / D)
            center = values - mean
            rstd = lax.rsqrt(jnp.sum(center * center, axis=-1, keepdims=True) * (1.0 / D) + EPS)
            n = center * rstd
            r.normed1[here, :] = (n * r.rows[0:1, :] + r.rows[1:2, :]).astype(BF)
            r.normed2[here, :] = (n * r.rows[2:3, :] + r.rows[3:4, :]).astype(BF)
            lane = lanes_like((chunk, LANES))
            r.stat[here, :] = jnp.where(lane < HEAD_DIM, mean, rstd)

    def unit_rows(here):
        stat = r.stat[here, :]
        return (r.x[here, :].astype(F32) - stat[:, 0:1]) * stat[:, HEAD_DIM : HEAD_DIM + 1]

    @piece(LN0)
    def _():
        normalize(place.seq)

    @piece(LN1)
    def _():
        x_move.across_arrived(0)
        normalize(place.sibling)

    @piece(LN2)
    def _():
        normalize(place.pair_peer(1))

    @piece(LN3)
    def _():
        x_move.across_arrived(1)
        normalize(place.across_source(1))

    def swap(step):
        peer = place.seq_peer(step)
        src, dst = rows_at(r.w_proj_cols, peer, wide), columns_at(r.w_proj, place.seq, wide)
        return send(src, dst, r.m_swap, step, {"seq": peer})

    def swap_arrival(step):
        source = place.seq_peer(-step)
        src, dst = rows_at(r.w_proj_cols, source, wide), columns_at(r.w_proj, source, wide)
        return send(src, dst, r.m_swap, step, {"seq": place.seq_peer(step)})

    @piece(SWGO)
    def _():
        for step in range(1, seq_size):
            swap(step).start()
        columns_at(r.w_proj, place.seq, wide)[...] = rows_at(r.w_proj_cols, place.seq, wide)[...]

    @piece(SWIN)
    def _():
        for step in range(1, seq_size):
            swap_arrival(step).wait_recv()

    def mix_columns(first, last):
        @pl.loop(first, last)
        def _(block):
            here = tile_rows(block)
            mixed = nn(r.normed1[here, :], r.w_mix[...]) + r.rows[7:8, 0:mixed_wide]
            cosine, sine = r.cos[here, :], r.sin[here, :]
            lane = lanes_like((TILE, LANES))
            hot = r.hot[here, :].astype(F32)
            cold = jnp.where((lane >= HEAD_DIM) & (lane < HEAD_DIM + 4), (1.0 - hot) * NEG, 0.0)
            for head in range(heads_n):
                start = head * 3 * HEAD_DIM
                query = spin(head_part(mixed, start), cosine, sine) * HEAD_DIM**-0.5
                key = spin(head_part(mixed, start + HEAD_DIM), cosine, sine)
                value = head_part(mixed, start + 2 * HEAD_DIM)
                at = pl.ds(head * LANES, LANES)
                at_more = pl.ds((heads_n + head) * LANES, LANES)
                dims = pl.ds(head * HEAD_DIM, HEAD_DIM)
                r.qk[here, at] = jnp.where(lane < HEAD_DIM, query, hot).astype(BF)
                r.qk[here, at_more] = jnp.where(lane < HEAD_DIM, key, cold).astype(BF)
                r.vg[here, at] = jnp.where(lane < HEAD_DIM, value, 0.0).astype(BF)
                r.kt[dims, here] = key.T[:HEAD_DIM, :].astype(BF)
                r.vt[dims, here] = value.T[:HEAD_DIM, :].astype(BF)

    middle = blocks // 2
    piece(QKV0, 0, middle)(mix_columns)
    piece(QKV1, middle, blocks)(mix_columns)
    @piece(DH)
    def _():
        @pl.loop(0, blocks)
        def _(block):
            here = tile_rows(block)
            place_in = lax.broadcasted_iota(jnp.int32, (TILE, wide), 0) + block * TILE
            d_heads = jnp.where(place_in < length - r.pad[0], nt(r.dy[here, :], r.w_proj[...]), 0.0)
            for head in range(heads_n):
                at_more = pl.ds((heads_n + head) * LANES, LANES)
                r.vg[here, at_more] = head_part(d_heads, head * HEAD_DIM).astype(BF)

    second = heads_n * LANES
    head_refs = (
        r.qk.at[:, pl.ds(0, second)],
        r.qk.at[:, pl.ds(second, second)],
        r.vg.at[:, pl.ds(0, second)],
        r.vg.at[:, pl.ds(second, second)],
        r.kt,
        r.vt,
        r.s,
        r.p,
        r.ht,
        r.dqt,
        r.dk,
        r.dv,
    )

    def attend_blocks(head, first, last):
        for block in range(first, last):
            if block == 0:
                attend_head(head, block, head_refs)
            elif block == 1:
                attend_head(head, block, head_refs)
            elif block == 2:
                attend_head(head, block, head_refs)
            else:
                attend_head(head, block, head_refs)

    for head in range(heads_n):
        first = AT00 + head * (middle + 1)
        piece(first, head, 0, middle)(attend_blocks)
        for block in range(middle, blocks):
            piece(first + block - middle + 1, head, block, block + 1)(attend_blocks)

    def heads_back():
        @pl.loop(0, blocks)
        def _(block):
            here = tile_rows(block)
            place_in = lax.broadcasted_iota(jnp.int32, (TILE, wide), 0) + block * TILE
            r.attn[here, :] = jnp.where(place_in < length - r.pad[0], r.ht[:, here].T.astype(F32), 0.0).astype(BF)
            d_query = r.dqt[:, here].T.astype(F32)
            cosine, sine = r.cos[here, :], -r.sin[here, :]
            lane = lanes_like((TILE, LANES))
            parts = []
            for head in range(heads_n):
                parts.append(spin(head_part(d_query, head * HEAD_DIM), cosine, sine))
                parts.append(spin(r.dk[head, here, :], cosine, sine))
                parts.append(r.dv[head, here, :])
            for index in range(len(parts) // 2):
                tile = jnp.where(lane < HEAD_DIM, parts[2 * index], pltpu.roll(parts[2 * index + 1], HEAD_DIM, 1))
                at = slice(index * LANES, (index + 1) * LANES)
                tile = tile.astype(BF)
                r.d_mixed[here, at] = tile
                r.sums[6:7, at] += jnp.sum(tile.astype(F32), axis=0, keepdims=True)

    piece(POST)(heads_back)
    big = 512

    def weight_grad(out_ref, left, right):
        @pl.loop(0, left.shape[1] // big)
        def _(index):
            at = pl.ds(pl.multiple_of(index * big, big), big)
            out_ref[at, :] = tn(left[:, at], right[...]).astype(BF)

    piece(GM, r.g_mix, r.normed1, r.d_mixed)(weight_grad)
    piece(GR, r.g_rise, r.normed2, r.d_up)(weight_grad)
    piece(GF, r.g_fall, r.active, r.dy)(weight_grad)

    @piece(GP)
    def _():
        gathers[PROJ].finish()
        for step in range(1, seq_size):
            swap(step).wait_send()
        grad = tn(r.attn[...], r.dy[...]).astype(BF)
        for index in range(seq_size):
            r.w_proj_cols[index * wide : (index + 1) * wide, :] = grad[:, index * wide : (index + 1) * wide]

    def swap_back(step):
        peer = place.seq_peer(step)
        src, dst = rows_at(r.w_proj_cols, peer, wide), rows_at(r.g_proj_cols, place.seq, wide)
        return send(src, dst, r.m_swap2, step, {"seq": peer})

    def swap_back_arrival(step):
        source = place.seq_peer(-step)
        src, dst = rows_at(r.w_proj_cols, source, wide), rows_at(r.g_proj_cols, source, wide)
        return send(src, dst, r.m_swap2, step, {"seq": place.seq_peer(step)})

    @piece(SBGO)
    def _():
        for step in range(1, seq_size):
            swap_back(step).start()
        rows_at(r.g_proj_cols, place.seq, wide)[...] = rows_at(r.w_proj_cols, place.seq, wide)[...]

    @piece(SBIN)
    def _():
        for step in range(1, seq_size):
            swap_back_arrival(step).wait_recv()

    def upward(block):
        here = tile_rows(block)
        up = nn(r.normed2[here, :], r.w_rise[...]) + r.rows[6:7, :]
        share = 0.5 + 0.5 * lax.erf(up * 0.5**0.5)
        r.active[here, :] = (up * share).astype(BF)
        bell = jnp.exp(-0.5 * up * up) * (2 * np.pi) ** -0.5
        r.d_up[here, :] = (share + up * bell).astype(BF)

    def downward(first, last):
        @pl.loop(first, last)
        def _(block):
            here = tile_rows(block)
            d_up = (r.d_up[here, :].astype(F32) * nt(r.dy[here, :], r.w_fall[...])).astype(BF)
            r.d_up[here, :] = d_up
            r.sums[5:6, :] += jnp.sum(d_up.astype(F32), axis=0, keepdims=True)

    for block in range(blocks):
        piece(UP0 + block, block)(upward)
    piece(DN0, 0, middle)(downward)
    piece(DN1, middle, blocks)(downward)

    def out_rows(step):
        first = ((place.pair + step) % place.pairs) * (2 * tok // TILE)
        @pl.loop(0, 2 * tok // TILE)
        def _(block):
            here = tile_rows(first + block)
            part = nn(r.attn[here, :], r.w_proj[...]) + nn(r.active[here, :], r.w_fall[...])
            r.out_part[here, :] = part.astype(BF)

        out.over_start(step)

    def back_rows(step):
        first = ((place.pair + step) % place.pairs) * (2 * tok // TILE)
        @pl.loop(0, 2 * tok // TILE)
        def _(block):
            here = tile_rows(first + block)
            d_one = nt(r.d_mixed[here, :], r.w_mix[...])
            d_two = nt(r.d_up[here, :], r.w_rise[...])
            r.back_part[here, :] = (r.rows[0:1, :] * d_one + r.rows[2:3, :] * d_two).astype(BF)
            n = unit_rows(here)
            r.sums[0:1, :] += jnp.sum(d_one * n, axis=0, keepdims=True)
            r.sums[1:2, :] += jnp.sum(d_one, axis=0, keepdims=True)
            r.sums[2:3, :] += jnp.sum(d_two * n, axis=0, keepdims=True)
            r.sums[3:4, :] += jnp.sum(d_two, axis=0, keepdims=True)
            r.sums[4:5, :] += jnp.sum(r.dy[here, :].astype(F32), axis=0, keepdims=True)

        back.over_start(step)

    for step in range(2):
        piece(OP0 + step, step)(out_rows)
        piece(BK0 + step, step)(back_rows)
        piece(OM0 + step, step)(out.over_add)
        piece(BM0 + step, step)(back.over_add)

    @piece(VP)
    def _():
        for index in range(dp_size):
            at = slice(index * LANES, (index + 1) * LANES)
            r.vec_part[index, 0:6, :] = r.sums[0:6, at]
            for row in range(mixed_wide // LANES):
                r.vec_part[index, 6 + row : 7 + row, :] = r.sums[6:7, row * LANES : (row + 1) * LANES]

    def settle(move, home):
        move.begin()
        leave(move.own, home.at[place.seq])

    def pass_on(move, home):
        move.forward()
        for step in range(1, place.pairs):
            source = place.pair_peer(-step)
            leave(move.full.at[source], home.at[source])

    def complete(move, home):
        for step in range(place.pairs):
            move.across_arrived(step)
            source = place.across_source(step)
            leave(move.full.at[source], home.at[source])

    for index, (move, home) in enumerate(zip(finals, homes, strict=True)):
        piece(SMA + index, move, home)(settle)
        piece(WMA + index, move, home)(pass_on)
        piece(CMA + index, move, home)(complete)

    mine = pl.ds(pl.multiple_of(place.seq * tok, tok), tok)

    @piece(BO)
    def _():
        total = out.total()
        block_out = total + r.x[mine, :].astype(F32) + (r.rows[4:5, :] + r.rows[5:6, :])
        r.out_cross[0] = block_out.astype(BF)
        leave(r.out_cross.at[0], r.block_out)

    @piece(IG)
    def _():
        scaled = back.total()
        n = unit_rows(mine)
        rstd = r.stat[mine, HEAD_DIM : HEAD_DIM + 1]
        back_mean = jnp.sum(scaled, axis=-1, keepdims=True) * (1.0 / D)
        back_n = jnp.sum(scaled * n, axis=-1, keepdims=True) * (1.0 / D)
        input_grad = r.dy[mine, :].astype(F32) + rstd * (scaled - back_mean - n * back_n)
        r.back_cross[0] = input_grad.astype(BF)
        leave(r.back_cross.at[0], r.input_grad)

    @piece(SV)
    def _():
        r.vec_fin[place.seq] = r.vec_part[place.dp]
        f_vec.begin()

    piece(WV)(f_vec.forward)

    @piece(VO)
    def _():
        f_vec.finish()
        norm = r.vec_fin[0, 0:4, :]
        for index in range(1, seq_size):
            norm = norm + r.vec_fin[index, 0:4, :]
        r.vec_out[0:4, :] = norm
        r.vec_out[4:5, :] = r.vec_fin[0, 4:5, :]
        source = r.vec_fin[place.dp // each]
        pick = place.dp % each
        part = source[6:9, :]
        for index in range(1, each):
            part = jnp.where(pick == index, source[6 + 3 * index : 9 + 3 * index, :], part)
        r.vec_out[5:8, :] = part
        for index in range(seq_size):
            r.vec_out[8 + index : 9 + index, :] = r.vec_fin[index, 5:6, :]
        leave(r.vec_out, r.vec_result)

    place.met_near()
    r.sums[...] = jnp.zeros(r.sums.shape, F32)
    r.vec_part[...] = jnp.zeros(r.vec_part.shape, F32)
    assert sorted(ORDER) == sorted(pieces)
    for name in ORDER:
        pieces[name]()
    for move in finals:
        move.sent()
    for copy in leaving:
        copy.wait()
    for move in (*gathers[:PROJ], *gathers[PROJ + 1 :], *reduces, out, back):
        move.finish()
    for move in (x_move, seg_move, dy_move):
        move.sent()
    for step in range(1, seq_size):
        swap_back(step).wait_send()


def resident_call(seq_size, dp_size, *args):
    tok = args[0].shape[0]
    length = tok * seq_size
    half, pairs = dp_size // 2, seq_size // 2
    wide = HEADS // seq_size * HEAD_DIM
    units_all = dp_size * LANES
    heads_n = wide // HEAD_DIM

    def half_vmem(*shape):
        return pltpu.VMEM(shape, BF)

    def full_vmem(*shape):
        return pltpu.VMEM(shape, F32)

    def ring(columns):
        return half_vmem(2, 2, half, HALF, columns)

    def pair_of_sems(count):
        return pltpu.SemaphoreType.DMA((2, 2, count))

    any_spec = pl.BlockSpec(memory_space=pl.ANY)
    vmem = pl.BlockSpec(memory_space=pltpu.VMEM)
    scratch = [
        pltpu.SMEM((1,), jnp.int32),
        full_vmem(length, LANES),
        full_vmem(length, LANES),
        half_vmem(length, D),
        half_vmem(length, D),
        half_vmem(length, LANES),
        full_vmem(seq_size * 8, tok),
        half_vmem(D, 3 * wide),
        half_vmem(D, wide),
        half_vmem(wide, D),
        half_vmem(D, units_all),
        half_vmem(units_all, D),
        full_vmem(dp_size, VEC_ROWS, LANES),
        full_vmem(8, D),
        half_vmem(length, D),
        half_vmem(length, D),
        full_vmem(length, LANES),
        half_vmem(length, units_all),
        half_vmem(length, units_all),
        half_vmem(wide, length),
        half_vmem(wide, length),
        full_vmem(length // TILE, TILE, TILE),
        full_vmem(length // TILE, TILE, TILE),
        half_vmem(wide, length),
        half_vmem(wide, length),
        full_vmem(heads_n, length, LANES),
        full_vmem(heads_n, length, LANES),
        half_vmem(length, wide),
        half_vmem(length, 3 * wide),
        half_vmem(length, D),
        half_vmem(length, D),
        half_vmem(length, units_all),
        half_vmem(length, units_all),
        half_vmem(D, 3 * wide),
        half_vmem(D, wide),
        half_vmem(D, units_all),
        half_vmem(units_all, D),
        ring(3 * wide),
        half_vmem(2, half, LANES, wide),
        ring(units_all),
        ring(D),
        half_vmem(pairs, tok, D),
        half_vmem(pairs - 1, tok, D),
        half_vmem(pairs, tok, D),
        half_vmem(pairs - 1, tok, D),
        full_vmem(8, D),
        full_vmem(dp_size, VEC_ROWS, LANES),
        full_vmem(2, half, VEC_ROWS, LANES),
        half_vmem(seq_size, LANES, 3 * wide),
        half_vmem(seq_size, LANES, wide),
        half_vmem(seq_size, LANES, units_all),
        half_vmem(seq_size, LANES, D),
        full_vmem(seq_size, VEC_ROWS, LANES),
        full_vmem(16, LANES),
    ]
    scratch += [sems_of(2 * pairs)] * 3 + [sems_of(2 * half)]
    scratch += [pair_of_sems(2 * half), sems_of(2 * half), pair_of_sems(2 * half), pair_of_sems(2 * half)]
    scratch += [sems_of(seq_size), pltpu.SemaphoreType.DMA((dp_size + 6,)), sems_of(seq_size)]
    scratch += [pair_of_sems(2 * half), sems_of(2 * half), pair_of_sems(2 * half), pair_of_sems(2 * half)]
    scratch += [sems_of(2 * pairs)] * 2 + [sems_of(2 * half)]
    scratch += [pair_of_sems(2 * pairs), sems_of(2 * pairs), pair_of_sems(2 * pairs), pair_of_sems(2 * pairs)]
    scratch += [sems_of(2 * pairs)]
    scratch += [pltpu.SemaphoreType.DMA((32,))]
    return pl.pallas_call(
        functools.partial(resident_kernel, seq_size, dp_size),
        out_shape=(
            jax.ShapeDtypeStruct((tok, D), BF),
            jax.ShapeDtypeStruct((tok, D), BF),
            jax.ShapeDtypeStruct((seq_size, LANES, 3 * wide), BF),
            jax.ShapeDtypeStruct((seq_size, LANES, wide), BF),
            jax.ShapeDtypeStruct((seq_size, LANES, units_all), BF),
            jax.ShapeDtypeStruct((seq_size, LANES, D), BF),
            jax.ShapeDtypeStruct((16, LANES), F32),
        ),
        in_specs=[any_spec] * 6 + [vmem] * 9 + [any_spec, vmem],
        out_specs=[any_spec] * 7,
        scratch_shapes=scratch,
        compiler_params=pltpu.CompilerParams(
            collective_id=2, has_side_effects=True, vmem_limit_bytes=RESIDENT_VMEM
        ),
    )(*args)


RESIDENT_VMEM = 63 * 2**20


def finish_kernel(seq_size, dp_size, *refs):
    (block, grad, mix, proj, rise, fall, vec), refs = refs[:7], refs[7:]
    (block_out, grad_out, mix_out, proj_out, rise_out, fall_out), refs = refs[:6], refs[6:]
    vec_outs, refs = refs[:8], refs[8:]
    (block_in, grad_in, mix_in, proj_in, rise_in, fall_in, vec_in, mix_f, proj_f, rise_f, fall_f), refs = refs[:11], refs[11:]
    vec_fs, (in_sems, out_sems) = refs[:8], refs[8:]
    parts = [(fall.at[group], fall_in.at[group]) for group in range(seq_size)]
    parts += [(rise, rise_in), (mix, mix_in), (proj, proj_in), (block, block_in), (grad, grad_in), (vec, vec_in)]
    coming = []
    for src, dst in parts:
        copy = pltpu.make_async_copy(src, dst, in_sems.at[len(coming)])
        copy.start()
        coming.append(copy)
    *fall_copies, rise_copy, mix_copy, proj_copy, block_copy, grad_copy, vec_copy = coming
    leaving = []

    def leave(src, dst):
        copy = pltpu.make_async_copy(src, dst, out_sems.at[len(leaving)])
        copy.start()
        leaving.append(copy)

    for group in range(seq_size):
        fall_copies[group].wait()
        at = pl.ds(group * LANES, LANES)
        fall_f[at, :] = fall_in[group].astype(F32)
        leave(fall_f.at[at], fall_out.at[at])
    few = 32
    rise_copy.wait()
    for start in range(0, LANES, few):
        at = pl.ds(start, few)
        for group in range(seq_size):
            for index in range(dp_size):
                column = (index * seq_size + group) * LANES
                rise_f[at, column : column + LANES] = rise_in[group, at, index * LANES : (index + 1) * LANES].astype(F32)
        leave(rise_f.at[at], rise_out.at[at])
    mix_copy.wait()
    proj_copy.wait()
    for start in range(0, LANES, 2 * few):
        at = pl.ds(start, 2 * few)
        for held, full, out in ((mix_in, mix_f, mix_out), (proj_in, proj_f, proj_out)):
            columns = held.shape[2]
            for group in range(seq_size):
                full[at, group * columns : (group + 1) * columns] = held[group, at, :].astype(F32)
            leave(full.at[at], out.at[at])
    block_copy.wait()
    leave(block_in, block_out)
    grad_copy.wait()
    leave(grad_in, grad_out)
    vec_copy.wait()
    for held, out, row in zip(vec_fs, vec_outs, (0, 1, 2, 3, 4, 4, 5, 8), strict=True):
        for start in range(0, out.shape[0], LANES):
            held[start : start + LANES] = vec_in[row + start // LANES]
        leave(held, out)
    for copy in leaving:
        copy.wait()


def finish_call(seq_size, dp_size, block, grad, mix, proj, rise, fall, vec):
    tok = block.shape[0]
    vec_sizes = (LANES,) * 6 + (3 * LANES, seq_size * LANES)
    full_sizes = ((LANES, 3 * D), (LANES, D), (LANES, FF), (seq_size * LANES, D))
    any_spec = pl.BlockSpec(memory_space=pl.ANY)
    return pl.pallas_call(
        functools.partial(finish_kernel, seq_size, dp_size),
        out_shape=(jax.ShapeDtypeStruct((tok, D), BF),) * 2
        + tuple(jax.ShapeDtypeStruct(size, F32) for size in full_sizes)
        + tuple(jax.ShapeDtypeStruct((size,), F32) for size in vec_sizes),
        in_specs=[any_spec] * 7,
        out_specs=[any_spec] * 14,
        scratch_shapes=[pltpu.VMEM(array.shape, array.dtype) for array in (block, grad, mix, proj, rise, fall, vec)]
        + [pltpu.VMEM(size, F32) for size in full_sizes]
        + [pltpu.VMEM((size,), F32) for size in vec_sizes]
        + [pltpu.SemaphoreType.DMA((seq_size + 6,)), pltpu.SemaphoreType.DMA((24,))],
        compiler_params=pltpu.CompilerParams(vmem_limit_bytes=RESIDENT_VMEM),
    )(block, grad, mix, proj, rise, fall, vec)


def resident_tables():
    half = ROT // 2
    frequency = BASE ** (-np.arange(0, ROT, 2).astype(np.float32) / np.float32(ROT))
    lanes = np.zeros((LANES,), np.float64)
    lanes[:half] = lanes[half:ROT] = frequency.astype(np.float32)
    sign = np.where(np.arange(LANES) < half, -1.0, 1.0)
    steps = np.arange(TURN, dtype=np.float64)[:, None]
    tables = [f for scale in (TURN, 1) for f in (np.cos(steps * scale * lanes), sign * np.sin(steps * scale * lanes))]
    return jnp.asarray(np.concatenate(tables).astype(np.float32))


def resident_shards(
    tokens,
    cotangent,
    norm1_gain,
    norm1_bias,
    norm2_gain,
    norm2_bias,
    qkv_weight,
    qkv_bias,
    out_weight,
    out_bias,
    up_weight,
    up_bias,
    down_weight,
    down_bias,
    segment_ids,
    pad_length,
):
    seq_size, dp_size = lax.axis_size("seq"), lax.axis_size("dp")
    tok = tokens.shape[1]
    vectors = (norm1_gain, norm1_bias, norm2_gain, norm2_bias, out_bias, down_bias, qkv_bias, up_bias)
    parts = resident_call(
        seq_size,
        dp_size,
        tokens[0],
        cotangent[0],
        qkv_weight,
        out_weight,
        up_weight,
        down_weight,
        *(vector.reshape(-1, LANES) for vector in vectors),
        segment_ids,
        pad_length,
        resident_tables(),
    )
    done = finish_call(seq_size, dp_size, *parts)
    block_out, input_grad, g_mix, g_proj, g_rise, g_fall = done[:6]
    norm1_g, norm1_b, norm2_g, norm2_b, out_b, down_b, b_mix, b_rise = done[6:]
    return (
        block_out[None],
        input_grad[None],
        norm1_g,
        norm1_b,
        norm2_g,
        norm2_b,
        g_mix,
        b_mix,
        g_proj,
        out_b,
        g_rise,
        b_rise,
        g_fall,
        down_b,
    )


def streamed_shards(
    tokens,
    cotangent,
    norm1_gain,
    norm1_bias,
    norm2_gain,
    norm2_bias,
    qkv_weight,
    qkv_bias,
    out_weight,
    out_bias,
    up_weight,
    up_bias,
    down_weight,
    down_bias,
    segment_ids,
    pad_length,
):
    seq_size, dp_size = lax.axis_size("seq"), lax.axis_size("dp")
    seq = lax.axis_index("seq")
    dp = lax.axis_index("dp")
    tok = tokens.shape[1]
    length = tok * seq_size
    heads_n = HEADS // seq_size
    rows = D // dp_size
    wide = heads_n * HEAD_DIM
    units = FF // dp_size // seq_size

    mix = qkv_weight.reshape(rows, seq_size, heads_n, 3, HEAD_DIM)
    mix = lax.dynamic_index_in_dim(mix, seq, 1, keepdims=False)
    mix = mix.transpose(0, 2, 1, 3).reshape(rows, 3 * wide)
    proj = lax.dynamic_slice_in_dim(out_weight, seq * wide, wide, 1)
    rise = up_weight.reshape(rows, dp_size, seq_size, units)
    rise = lax.dynamic_index_in_dim(rise, seq, 2, keepdims=False).reshape(rows, dp_size * units)
    fall = lax.dynamic_slice_in_dim(down_weight, seq * units, units, 0)
    vec = jnp.concatenate(
        [norm1_gain, norm1_bias, norm2_gain, norm2_bias, out_bias, down_bias, qkv_bias, up_bias]
    )
    vec_len = vec.shape[0]
    vec = jnp.pad(vec, (0, 2048 - vec_len)).reshape(16, 128)
    seg = jnp.broadcast_to(segment_ids, (8, tok))
    x_all, dy_all, w_mix, _, w_rise, w_fall, vec_all, seg_all, w_proj = gather_all(
        seq_size, dp_size, tokens[0], cotangent[0], mix, proj, rise, fall, vec, seg
    )
    x = x_all.reshape(length, D).astype(F32)
    dy = dy_all.reshape(length, D)
    w_mix = w_mix.reshape(D, 3 * wide)
    w_rise = w_rise.reshape(D, dp_size * units)
    w_fall = w_fall.reshape(dp_size * units, D)
    w_proj = w_proj.reshape(seq_size, wide, wide).transpose(1, 0, 2).reshape(wide, D)
    segments = seg_all[:, 0, :].reshape(length)
    vec_all = vec_all.reshape(dp_size, 2048)[:, :vec_len].astype(F32)
    g1, s1, g2, s2, b_proj, b_fall = (
        vec_all[:, i * rows : (i + 1) * rows].reshape(D) for i in range(6)
    )
    b_mix = vec_all[:, 6 * rows : 9 * rows].reshape(seq_size, heads_n, 3, HEAD_DIM)
    b_mix = lax.dynamic_index_in_dim(b_mix, seq, 0, keepdims=False)
    b_mix = b_mix.transpose(1, 0, 2).reshape(3 * wide)
    b_rise = vec_all[:, 9 * rows :].reshape(dp_size, seq_size, units)
    b_rise = lax.dynamic_index_in_dim(b_rise, seq, 1, keepdims=False).reshape(dp_size * units)

    center = x - jnp.mean(x, axis=-1, keepdims=True)
    rstd = lax.rsqrt(jnp.mean(center * center, axis=-1, keepdims=True) + EPS)
    n = center * rstd
    normed1 = (n * g1 + s1).astype(BF)
    normed2 = (n * g2 + s2).astype(BF)
    valid = (jnp.arange(length, dtype=jnp.int32) < length - pad_length[0]).astype(F32)[:, None]
    cosine, sine = (jnp.asarray(t) for t in angle_tables(length))

    mixed = dot(normed1, w_mix) + b_mix
    mixed = mixed.reshape(length, 3, heads_n, HEAD_DIM).transpose(1, 2, 0, 3)
    queries = turn(mixed[0], cosine, sine, 1.0).astype(BF)
    keys = turn(mixed[1], cosine, sine, 1.0).astype(BF)
    values = mixed[2].astype(BF)
    d_heads = (dot_nt(dy, w_proj) * valid).astype(BF)
    d_heads = d_heads.reshape(length, heads_n, HEAD_DIM).transpose(1, 0, 2)
    heads, d_q, d_k, d_v = attention(queries, keys, values, d_heads, segments)
    attn_rows = (heads.transpose(1, 0, 2).reshape(length, wide).astype(F32) * valid).astype(BF)
    d_mixed = jnp.stack(
        [
            turn(d_q.astype(F32), cosine, sine, -1.0).astype(BF),
            turn(d_k.astype(F32), cosine, sine, -1.0).astype(BF),
            d_v,
        ]
    )
    d_mixed = d_mixed.transpose(2, 0, 1, 3).reshape(length, 3 * wide)

    upward = dot(normed2, w_rise) + b_rise
    active = jax.nn.gelu(upward, approximate=False).astype(BF)
    slope = 0.5 * (1 + lax.erf(upward * (0.5**0.5))) + upward * jnp.exp(
        -0.5 * upward * upward
    ) * ((2 * np.pi) ** -0.5)
    d_up = (slope * dot_nt(dy, w_fall)).astype(BF)
    out_part = (dot(attn_rows, w_proj) + dot(active, w_fall)).astype(BF)
    d_n1 = dot_nt(d_mixed, w_mix)
    d_n2 = dot_nt(d_up, w_rise)
    back_part = (g1 * d_n1 + g2 * d_n2).astype(BF)

    g_mix = dot_t(normed1, d_mixed).astype(BF).reshape(dp_size, rows, 3 * wide)
    g_proj = dot_t(attn_rows, dy).astype(BF).reshape(dp_size // seq_size, rows, seq_size, wide)
    g_proj = g_proj.transpose(2, 0, 1, 3)
    g_rise = dot_t(normed2, d_up).astype(BF).reshape(dp_size, rows, dp_size * units)
    g_fall = dot_t(active, dy).astype(BF).reshape(dp_size, units, D)
    dyf = dy.astype(F32)
    vec_part = jnp.concatenate(
        [
            t.reshape(dp_size, -1)
            for t in (
                jnp.sum(d_n1 * n, axis=0),
                jnp.sum(d_n1, axis=0),
                jnp.sum(d_n2 * n, axis=0),
                jnp.sum(d_n2, axis=0),
                jnp.sum(dyf, axis=0),
                jnp.sum(d_up.astype(F32), axis=0),
            )
        ]
        + [jnp.broadcast_to(jnp.sum(d_mixed.astype(F32), axis=0)[None], (dp_size, 3 * wide))],
        axis=1,
    )
    part_len = vec_part.shape[1]
    vec_part = jnp.pad(vec_part, ((0, 0), (0, 2048 - part_len))).reshape(dp_size, 16, 128)
    out_sum, back_sum, f_mix, f_proj, f_rise, f_fall, f_vec = reduce_all(
        seq_size,
        dp_size,
        out_part.reshape(seq_size, tok, D),
        back_part.reshape(seq_size, tok, D),
        g_mix,
        g_proj,
        g_rise,
        g_fall,
        vec_part,
    )
    own_x = tokens[0].astype(F32)
    block_output = (own_x + out_sum + b_proj + b_fall).astype(BF)
    own_center = own_x - jnp.mean(own_x, axis=-1, keepdims=True)
    own_rstd = lax.rsqrt(jnp.mean(own_center * own_center, axis=-1, keepdims=True) + EPS)
    own_n = own_center * own_rstd
    back = own_rstd * (
        back_sum
        - jnp.mean(back_sum, axis=-1, keepdims=True)
        - own_n * jnp.mean(back_sum * own_n, axis=-1, keepdims=True)
    )
    input_grad = (cotangent[0].astype(F32) + back).astype(BF)
    f_mix = f_mix.reshape(seq_size, rows, 3, heads_n, HEAD_DIM)
    f_mix = f_mix.transpose(1, 0, 3, 2, 4).reshape(rows, 3 * D).astype(F32)
    f_proj = f_proj.transpose(1, 0, 2).reshape(rows, D).astype(F32)
    f_rise = f_rise.reshape(seq_size, rows, dp_size, units)
    f_rise = f_rise.transpose(1, 2, 0, 3).reshape(rows, FF).astype(F32)
    f_fall = f_fall.reshape(seq_size * units, D).astype(F32)
    f_vec = f_vec.reshape(seq_size, 2048)[:, :part_len]
    norm_sums = jnp.sum(f_vec[:, : 4 * rows], axis=0)
    column = f_vec[0, 4 * rows : 5 * rows]
    f_b_rise = f_vec[:, 5 * rows : 5 * rows + units].reshape(seq_size * units)
    f_b_mix = f_vec[:, 5 * rows + units :].reshape(seq_size, 3, heads_n, HEAD_DIM)
    f_b_mix = f_b_mix.transpose(0, 2, 1, 3).reshape(dp_size, 3 * rows)
    f_b_mix = lax.dynamic_index_in_dim(f_b_mix, dp, 0, keepdims=False)
    return (
        block_output[None],
        input_grad[None],
        norm_sums[:rows],
        norm_sums[rows : 2 * rows],
        norm_sums[2 * rows : 3 * rows],
        norm_sums[3 * rows :],
        f_mix,
        f_b_mix,
        f_proj,
        column,
        f_rise,
        f_b_rise,
        f_fall,
        column,
    )


def shards(*args):
    seq_size, dp_size = lax.axis_size("seq"), lax.axis_size("dp")
    if resident_fits(seq_size, dp_size, args[0].shape[1]):
        return resident_shards(*args)
    return streamed_shards(*args)


def solution(mesh):
    rows = P("dp", "seq", None)
    weight = P("dp", None)
    vector = P("dp")
    return jax.shard_map(
        shards,
        mesh=mesh,
        in_specs=(rows, rows)
        + (vector,) * 4
        + (weight, vector) * 4
        + (P("dp", "seq"), vector),
        out_specs=(rows, rows) + (vector,) * 4 + (weight, vector) * 4,
        check_vma=False,
    )
```

```python
import functools
import typing

import jax
import jax.numpy as jnp
import numpy as np
from jax import lax
from jax.experimental import pallas as pl
from jax.experimental.pallas import tpu as pltpu
from jax.sharding import PartitionSpec as P

D = 1024
HEADS = 16
HEAD_DIM = 64
ROT = 16
FF = 4096
EPS = 1e-05
BASE = 10000.0
NEG = -1e30
MESH = pl.DeviceIdType.MESH
BF = jnp.bfloat16
F32 = jnp.float32


def ring_pos(dev, size):
    return (dev // 2) * (1 - dev % 2) + (size - 1 - dev // 2) * (dev % 2)


def ring_dev(pos, size):
    high = pos // (size // 2)
    return (1 - high) * 2 * pos + high * (2 * (size - 1 - pos) + 1)


class Place:
    def __init__(self, seq_size, dp_size):
        self.seq_size, self.dp_size = seq_size, dp_size
        self.seq = lax.axis_index("seq")
        self.dp = lax.axis_index("dp")
        self.pos = ring_pos(self.dp, dp_size)
        self.half = dp_size // 2
        self.pairs = seq_size // 2
        self.core = self.seq % 2
        self.pair = self.seq // 2
        self.sibling = self.pair * 2 + 1 - self.core

    def ring(self, offset):
        return ring_dev((self.pos + offset + self.dp_size) % self.dp_size, self.dp_size)

    def dp_peer(self, step):
        return (self.dp + step + self.dp_size) % self.dp_size

    def pair_peer(self, step):
        return ((self.pair + step + self.pairs) % self.pairs) * 2 + self.core

    def across_source(self, step):
        return ((self.pair - step + self.pairs) % self.pairs) * 2 + 1 - self.core

    def seq_peer(self, step):
        return (self.seq + step + self.seq_size) % self.seq_size

    def greet_near(self):
        barrier = pltpu.get_barrier_semaphore()
        for step in (1, -1):
            pl.semaphore_signal(barrier, inc=1, device_id={"dp": self.ring(step)}, device_id_type=MESH)
        for step in range(1, self.seq_size):
            pl.semaphore_signal(
                barrier, inc=1, device_id={"seq": self.seq_peer(step)}, device_id_type=MESH
            )

    def met_near(self):
        pl.semaphore_wait(pltpu.get_barrier_semaphore(), 2 + self.seq_size - 1)

    def greet(self):
        barrier = pltpu.get_barrier_semaphore()
        for step in range(1, self.dp_size):
            pl.semaphore_signal(
                barrier, inc=1, device_id={"dp": self.dp_peer(step)}, device_id_type=MESH
            )
        for step in range(1, self.seq_size):
            pl.semaphore_signal(
                barrier, inc=1, device_id={"seq": self.seq_peer(step)}, device_id_type=MESH
            )
        pl.semaphore_wait(barrier, self.dp_size - 1 + self.seq_size - 1)


def send(src, dst, sems, index, target):
    return pltpu.make_async_remote_copy(
        src_ref=src,
        dst_ref=dst,
        send_sem=sems.at[0, index],
        recv_sem=sems.at[1, index],
        device_id=target,
        device_id_type=MESH,
    )


def halves(ref):
    rows = ref.shape[0]
    columns = ref.shape[1]
    if rows % (32 if ref.dtype == BF else 16) == 0:
        return ref.at[pl.ds(0, rows // 2)], ref.at[pl.ds(rows // 2, rows // 2)]
    return ref.at[:, pl.ds(0, columns // 2)], ref.at[:, pl.ds(columns // 2, columns // 2)]


class RingGather:
    def __init__(self, place, full, sems):
        self.place, self.full, self.sems = place, full, sems

    def piece(self, offset, step, way):
        block = self.full.at[self.place.ring(offset)]
        return block if step < self.place.half else halves(block)[way]

    def copies(self, step):
        place = self.place
        right = self.piece(-(step - 1), step, 0)
        left = self.piece(step - 1, step, 1)
        index = 2 * (step - 1)
        return (
            send(right, right, self.sems, index, {"dp": place.ring(1)}),
            send(left, left, self.sems, index + 1, {"dp": place.ring(-1)}),
        )

    def arrivals(self, step):
        right = self.piece(-step, step, 0)
        left = self.piece(step, step, 1)
        index = 2 * (step - 1)
        return (
            send(right, right, self.sems, index, {"dp": self.place.ring(1)}),
            send(left, left, self.sems, index + 1, {"dp": self.place.ring(-1)}),
        )

    def tick(self, step):
        if step > 1:
            for copy in self.arrivals(step - 1):
                copy.wait_recv()
        if step <= self.place.half:
            for copy in self.copies(step):
                copy.start()

    def finish(self):
        for step in range(1, self.place.half + 1):
            for copy in self.copies(step):
                copy.wait_send()


class RingReduce:
    def __init__(self, place, parts, arrived, sems):
        self.place, self.parts, self.arrived, self.sems = place, parts, arrived, sems

    def piece(self, ref, step, way):
        return ref if step > 1 else halves(ref)[way]

    def copies(self, step):
        place = self.place
        away = place.half - step + 1
        index = 2 * (step - 1)
        out = []
        for way, (offset, target) in enumerate(((away, 1), (-away, -1))):
            src = self.piece(self.parts.at[place.ring(offset)], step, way)
            dst = self.piece(self.arrived.at[way, step - 1], step, way)
            out.append(send(src, dst, self.sems, index + way, {"dp": place.ring(target)}))
        return out

    def tick(self, step):
        place = self.place
        if step > 1:
            for way, copy in enumerate(self.copies(step - 1)):
                copy.wait_recv()
                away = (place.half - step + 1) * (1 - 2 * way)
                held = self.piece(self.parts.at[place.ring(away)], step - 1, way)
                came = self.piece(self.arrived.at[way, step - 2], step - 1, way)
                held[...] = (held[...].astype(F32) + came[...].astype(F32)).astype(held.dtype)
        if step <= place.half:
            for copy in self.copies(step):
                copy.start()

    def finish(self):
        for step in range(1, self.place.half + 1):
            for copy in self.copies(step):
                copy.wait_send()

    def own(self):
        return self.parts.at[self.place.dp]


class SeqGather:
    def __init__(self, place, full, sems, own=None):
        self.place, self.full, self.sems = place, full, sems
        self.own = full.at[place.seq] if own is None else own

    def direct(self, step):
        place = self.place
        target = {"seq": place.pair_peer(step)}
        return send(self.own, self.full.at[place.seq], self.sems, step, target)

    def arrival(self, step):
        place = self.place
        target = {"seq": place.pair_peer(step)}
        return send(self.own, self.full.at[place.pair_peer(-step)], self.sems, step, target)

    def across(self, step):
        place = self.place
        block = self.full.at[place.pair_peer(-step)]
        src = self.own if step == 0 else block
        return send(src, block, self.sems, place.pairs + step, {"seq": place.sibling})

    def across_arrival(self, step):
        place = self.place
        block = self.full.at[place.across_source(step)]
        return send(self.own, block, self.sems, place.pairs + step, {"seq": place.sibling})

    def begin(self):
        for step in range(1, self.place.pairs):
            self.direct(step).start()
        self.across(0).start()

    def forward(self):
        for step in range(1, self.place.pairs):
            self.arrival(step).wait_recv()
            self.across(step).start()

    def across_arrived(self, step):
        self.across_arrival(step).wait_recv()

    def sent(self):
        for step in range(1, self.place.pairs):
            self.direct(step).wait_send()
        for step in range(self.place.pairs):
            self.across(step).wait_send()

    def finish(self):
        for step in range(self.place.pairs):
            self.across_arrived(step)
        self.sent()


class SeqReduce:
    def __init__(self, place, parts, crossed, arrived, sems):
        self.place, self.parts, self.crossed, self.arrived = place, parts, crossed, arrived
        self.sems = sems

    def over(self, step):
        place = self.place
        index = (place.pair + step) % place.pairs
        src = self.parts.at[index * 2 + 1 - place.core]
        return send(src, self.crossed.at[index], self.sems, step, {"seq": place.sibling})

    def direct(self, step):
        place = self.place
        return send(
            self.parts.at[place.pair_peer(step)],
            self.arrived.at[step - 1],
            self.sems,
            place.pairs + step,
            {"seq": place.pair_peer(step)},
        )

    def over_start(self, step):
        self.over(step).start()

    def over_add(self, step):
        place = self.place
        index = (place.pair + step) % place.pairs
        self.over(step).wait_recv()
        held = self.parts.at[index * 2 + place.core]
        held[...] = (held[...].astype(F32) + self.crossed[index].astype(F32)).astype(held.dtype)
        if step > 0:
            self.direct(step).start()

    def begin(self):
        for step in range(self.place.pairs):
            self.over_start(step)

    def middle(self):
        for step in range(self.place.pairs):
            self.over_add(step)

    def total(self):
        place = self.place
        total = self.parts.at[place.seq][...].astype(F32)
        for step in range(1, place.pairs):
            self.direct(step).wait_recv()
            total = total + self.arrived[step - 1].astype(F32)
        return total

    def finish(self):
        for step in range(self.place.pairs):
            self.over(step).wait_send()
        for step in range(1, self.place.pairs):
            self.direct(step).wait_send()


class DpSpread:
    def __init__(self, place, src_of, full, sems):
        self.place, self.src_of, self.full, self.sems = place, src_of, full, sems

    def copy(self, step):
        place = self.place
        peer = place.dp_peer(step)
        return send(self.src_of(peer), self.full.at[place.dp], self.sems, step, {"dp": peer})

    def arrival(self, step):
        place = self.place
        source = place.dp_peer(-step)
        return send(
            self.src_of(source), self.full.at[source], self.sems, step, {"dp": place.dp_peer(step)}
        )

    def begin(self):
        for step in range(1, self.place.dp_size):
            self.copy(step).start()

    def finish(self):
        for step in range(1, self.place.dp_size):
            self.arrival(step).wait_recv()
        for step in range(1, self.place.dp_size):
            self.copy(step).wait_send()


def sems_of(count):
    return pltpu.SemaphoreType.DMA((2, count))


def gather_kernel(seq_size, dp_size, *refs):
    (x_ref, dy_ref, mix_ref, proj_ref, rise_ref, fall_ref, vec_ref, seg_ref) = refs[:8]
    (x_all, dy_all, mix_all, proj_cols, rise_all, fall_all, vec_all, seg_all, proj_all) = refs[8:17]
    (x_sems, dy_sems, mix_sems, proj_sems, rise_sems, fall_sems, vec_sems, seg_sems, swap_sems, own_sems) = refs[17:]
    place = Place(seq_size, dp_size)
    own = [
        pltpu.make_async_copy(src, dst, own_sems.at[i])
        for i, (src, dst) in enumerate(
            (
                (x_ref, x_all.at[place.seq]),
                (dy_ref, dy_all.at[place.seq]),
                (mix_ref, mix_all.at[place.dp]),
                (proj_ref, proj_cols.at[place.dp]),
                (rise_ref, rise_all.at[place.dp]),
                (fall_ref, fall_all.at[place.dp]),
                (vec_ref, vec_all.at[place.dp]),
                (seg_ref, seg_all.at[place.seq]),
            )
        )
    ]
    for copy in own:
        copy.start()
    place.greet()
    for copy in own:
        copy.wait()
    x_move = SeqGather(place, x_all, x_sems)
    dy_move = SeqGather(place, dy_all, dy_sems)
    seg_move = SeqGather(place, seg_all, seg_sems)
    vec_move = DpSpread(place, lambda peer: vec_ref, vec_all, vec_sems)
    mix_move = RingGather(place, mix_all, mix_sems)
    proj_move = RingGather(place, proj_cols, proj_sems)
    rise_move = RingGather(place, rise_all, rise_sems)
    fall_move = RingGather(place, fall_all, fall_sems)
    x_move.begin()
    seg_move.begin()
    vec_move.begin()
    half = place.half
    for step in range(1, half + 1):
        mix_move.tick(step)
        proj_move.tick(step)
    x_move.forward()
    seg_move.forward()
    dy_move.begin()
    mix_move.tick(half + 1)
    proj_move.tick(half + 1)
    rise_move.tick(1)
    fall_move.tick(1)
    rows = proj_cols.shape[0] * proj_cols.shape[1] // seq_size
    each = rows // proj_cols.shape[1]
    swaps = []
    for step in range(1, seq_size):
        peer = place.seq_peer(step)
        swaps.append(
            send(
                proj_cols.at[pl.ds(peer * each, each)],
                proj_all.at[place.seq],
                swap_sems,
                step,
                {"seq": peer},
            )
        )
    for copy in swaps:
        copy.start()
    mine = pltpu.make_async_copy(
        proj_cols.at[pl.ds(place.seq * each, each)], proj_all.at[place.seq], own_sems.at[0]
    )
    mine.start()
    for step in range(2, half + 2):
        rise_move.tick(step)
        fall_move.tick(step)
        if step == 3:
            dy_move.forward()
    mine.wait()
    for step in range(1, seq_size):
        source = place.seq_peer(-step)
        send(
            proj_cols.at[pl.ds(source * each, each)],
            proj_all.at[source],
            swap_sems,
            step,
            {"seq": place.seq_peer(step)},
        ).wait_recv()
    for copy in swaps:
        copy.wait_send()
    for move in (x_move, dy_move, seg_move, vec_move, mix_move, proj_move, rise_move, fall_move):
        move.finish()


def gather_all(seq_size, dp_size, x, dy, mix, proj, rise, fall, vec, seg):
    half = dp_size // 2
    pairs = seq_size // 2

    def lead(count, like):
        return jax.ShapeDtypeStruct((count,) + like.shape, like.dtype)

    each = dp_size // seq_size
    any_spec = pl.BlockSpec(memory_space=pl.ANY)
    return pl.pallas_call(
        functools.partial(gather_kernel, seq_size, dp_size),
        out_shape=(
            lead(seq_size, x),
            lead(seq_size, dy),
            lead(dp_size, mix),
            lead(dp_size, proj),
            lead(dp_size, rise),
            lead(dp_size, fall),
            lead(dp_size, vec),
            lead(seq_size, seg),
            jax.ShapeDtypeStruct((seq_size, each) + proj.shape, proj.dtype),
        ),
        in_specs=[any_spec] * 8,
        out_specs=[any_spec] * 9,
        scratch_shapes=[
            sems_of(2 * pairs),
            sems_of(2 * pairs),
            sems_of(2 * half),
            sems_of(2 * half),
            sems_of(2 * half),
            sems_of(2 * half),
            sems_of(dp_size),
            sems_of(2 * pairs),
            sems_of(seq_size),
            pltpu.SemaphoreType.DMA((8,)),
        ],
        compiler_params=pltpu.CompilerParams(collective_id=0, has_side_effects=True),
    )(x, dy, mix, proj, rise, fall, vec, seg)


def reduce_kernel(seq_size, dp_size, *refs):
    (out_ref, back_ref, mix_ref, proj_ref, rise_ref, fall_ref, vec_ref), refs = refs[:7], refs[7:]
    (out_sum, back_sum, mix_fin, proj_fin, rise_fin, fall_fin, vec_fin), refs = refs[:7], refs[7:]
    (
        out_cross,
        out_came,
        back_cross,
        back_came,
        proj_full,
        mix_came,
        proj_came,
        rise_came,
        fall_came,
        vec_came,
        out_sems,
        back_sems,
        swap_sems,
        mix_sems,
        proj_sems,
        rise_sems,
        fall_sems,
        vec_sems,
        mix_fs,
        proj_fs,
        rise_fs,
        fall_fs,
        vec_fs,
    ) = refs
    place = Place(seq_size, dp_size)
    each = dp_size // seq_size
    half = place.half
    place.greet()

    def mine(index):
        return proj_full.at[pl.ds(index * each, each)]

    def swap(step):
        peer = place.seq_peer(step)
        return send(proj_ref.at[peer], mine(place.seq), swap_sems, step, {"seq": peer})

    def swap_arrival(step):
        source = place.seq_peer(-step)
        target = {"seq": place.seq_peer(step)}
        return send(proj_ref.at[source], mine(source), swap_sems, step, target)

    for step in range(1, seq_size):
        swap(step).start()
    mine(place.seq)[...] = proj_ref[place.seq]
    mix = RingReduce(place, mix_ref, mix_came, mix_sems)
    proj = RingReduce(place, proj_full, proj_came, proj_sems)
    rise = RingReduce(place, rise_ref, rise_came, rise_sems)
    fall = RingReduce(place, fall_ref, fall_came, fall_sems)
    out = SeqReduce(place, out_ref, out_cross, out_came, out_sems)
    back = SeqReduce(place, back_ref, back_cross, back_came, back_sems)
    vec = DpSpread(place, lambda peer: vec_ref.at[peer], vec_came, vec_sems)
    mix.tick(1)
    rise.tick(1)
    out.begin()
    back.begin()
    vec.begin()
    for step in range(1, seq_size):
        swap_arrival(step).wait_recv()
    proj.tick(1)
    fall.tick(1)
    out.middle()
    back.middle()
    for step in range(2, half + 2):
        for move in (mix, rise, proj, fall):
            move.tick(step)
    finals = []
    for move, fin, fin_sems in (
        (mix, mix_fin, mix_fs),
        (rise, rise_fin, rise_fs),
        (proj, proj_fin, proj_fs),
        (fall, fall_fin, fall_fs),
    ):
        fin[place.seq] = move.parts[place.dp]
        gather = SeqGather(place, fin, fin_sems)
        gather.begin()
        finals.append(gather)
    vec_came[place.dp] = vec_ref[place.dp]
    vec.finish()
    vec_fin[place.seq] = jnp.sum(vec_came[...], axis=0)
    gather = SeqGather(place, vec_fin, vec_fs)
    gather.begin()
    finals.append(gather)
    out_sum[...] = out.total()
    back_sum[...] = back.total()
    for gather in finals:
        gather.forward()
    for gather in finals:
        gather.finish()
    for step in range(1, seq_size):
        swap(step).wait_send()
    for move in (mix, rise, proj, fall, out, back):
        move.finish()


def reduce_all(seq_size, dp_size, out, back, mix, proj, rise, fall, vec):
    half = dp_size // 2
    pairs = seq_size // 2
    each = dp_size // seq_size

    def fin(like):
        return jax.ShapeDtypeStruct((seq_size,) + like.shape[1:], like.dtype)

    def came(like):
        return pltpu.VMEM((2, half) + like.shape[1:], like.dtype)

    proj_blocks = jax.ShapeDtypeStruct((dp_size,) + proj.shape[2:], proj.dtype)
    vmem = pl.BlockSpec(memory_space=pltpu.VMEM)
    return pl.pallas_call(
        functools.partial(reduce_kernel, seq_size, dp_size),
        out_shape=(
            jax.ShapeDtypeStruct(out.shape[1:], F32),
            jax.ShapeDtypeStruct(back.shape[1:], F32),
            fin(mix),
            fin(proj_blocks),
            fin(rise),
            fin(fall),
            fin(vec),
        ),
        in_specs=[vmem] * 7,
        out_specs=[vmem] * 7,
        scratch_shapes=[
            pltpu.VMEM((pairs,) + out.shape[1:], BF),
            pltpu.VMEM((pairs,) + out.shape[1:], BF),
            pltpu.VMEM((pairs,) + back.shape[1:], BF),
            pltpu.VMEM((pairs,) + back.shape[1:], BF),
            pltpu.VMEM(proj_blocks.shape, BF),
            came(mix),
            came(proj_blocks),
            came(rise),
            came(fall),
            pltpu.VMEM(vec.shape, F32),
            sems_of(2 * pairs),
            sems_of(2 * pairs),
            sems_of(seq_size),
            sems_of(2 * half),
            sems_of(2 * half),
            sems_of(2 * half),
            sems_of(2 * half),
            sems_of(dp_size),
            sems_of(2 * pairs),
            sems_of(2 * pairs),
            sems_of(2 * pairs),
            sems_of(2 * pairs),
            sems_of(2 * pairs),
        ],
        compiler_params=pltpu.CompilerParams(
            collective_id=1, has_side_effects=True, vmem_limit_bytes=56 * 2**20
        ),
    )(out, back, mix, proj, rise, fall, vec)


def angle_tables(length):
    frequency = BASE ** (-np.arange(0, ROT, 2).astype(np.float32) / np.float32(ROT))
    angles = np.arange(length, dtype=np.float32)[:, None] * frequency.astype(np.float32)[None, :]
    return np.cos(angles).astype(np.float32), np.sin(angles).astype(np.float32)


def turn(piece, cosine, sine, sign):
    half = ROT // 2
    low, high = piece[..., :half], piece[..., half:ROT]
    return jnp.concatenate(
        [low * cosine - sign * high * sine, high * cosine + sign * low * sine, piece[..., ROT:]],
        axis=-1,
    )


TILE = 256

def mm(a, b, dims):
    return lax.dot_general(a, b, ((dims[0], dims[1]), ((), ())), preferred_element_type=F32)

def nn(a, b):
    return mm(a, b, ((1,), (0,)))

def nt(a, b):
    return mm(a, b, ((1,), (1,)))

def tn(a, b):
    return mm(a, b, ((0,), (0,)))

def fold(count, body, init):
    if isinstance(count, int):
        for index in range(count):
            init = body(index, init)
        return init
    return lax.fori_loop(0, count, body, init)

def rows_of(index):
    start = index * TILE
    return pl.ds(start if isinstance(start, int) else pl.multiple_of(start, TILE), TILE)

def attend_block(head, block, refs):
    q_ref, k_ref, v_ref, g_ref, kt_ref, vt_ref, s_ref, p_ref, ht_ref, dqt_ref, dk_ref, dv_ref = refs
    here = rows_of(block)
    span = block + 1
    dims = pl.ds(pl.multiple_of(head * HEAD_DIM, HEAD_DIM), HEAD_DIM)
    query = q_ref[head, here, :]
    grad = g_ref[head, here, :]

    def score(index, top):
        tile = nt(k_ref[head, rows_of(index), :], query)
        if isinstance(index, int) and isinstance(block, int) and index < block:
            keep = tile
        else:
            key = lax.broadcasted_iota(jnp.int32, (TILE, TILE), 0) + (index - block) * TILE
            place = lax.broadcasted_iota(jnp.int32, (TILE, TILE), 1)
            keep = jnp.where(key <= place, tile, NEG)
        s_ref[index] = keep
        return jnp.maximum(top, jnp.max(keep, axis=0, keepdims=True))

    top = fold(span, score, jnp.full((1, TILE), 2 * NEG, F32))

    def raise_(index, total):
        raised = jnp.exp(s_ref[index] - top)
        s_ref[index] = raised
        return total + jnp.sum(raised, axis=0, keepdims=True)

    total = fold(span, raise_, jnp.zeros((1, TILE), F32))
    share = 1.0 / total

    def weigh(index, carried):
        heads, delta = carried
        weights = s_ref[index] * share
        s_ref[index] = weights
        weights_b = weights.astype(BF)
        d_weights = nt(v_ref[head, rows_of(index), :], grad)
        p_ref[index] = d_weights
        dv_ref[head, rows_of(index), :] += nn(weights_b, grad)
        heads = heads + nn(vt_ref[dims, rows_of(index)], weights_b)
        return heads, delta + jnp.sum(weights * d_weights, axis=0, keepdims=True)

    heads, delta = fold(
        span, weigh, (jnp.zeros((HEAD_DIM, TILE), F32), jnp.zeros((1, TILE), F32))
    )
    ht_ref[dims, here] = heads

    def back(index, d_query):
        d_scores = (s_ref[index] * (p_ref[index] - delta)).astype(BF)
        dk_ref[head, rows_of(index), :] += nn(d_scores, query)
        return d_query + nn(kt_ref[dims, rows_of(index)], d_scores)

    dqt_ref[dims, here] = fold(span, back, jnp.zeros((HEAD_DIM, TILE), F32))

def attend(heads_n, length, refs):
    dk_ref, dv_ref = refs[-2:]
    dk_ref[...] = jnp.zeros(dk_ref.shape, F32)
    dv_ref[...] = jnp.zeros(dv_ref.shape, F32)
    blocks = length // TILE

    @pl.loop(0, heads_n)
    def _(head):
        if blocks <= 4:
            for block in range(blocks):
                attend_block(head, block, refs)
        else:
            @pl.loop(0, blocks)
            def _(block):
                attend_block(head, block, refs)

def attend_kernel(H, L, q, k, v, g, kt, vt, ht, dqt, dk, dv, s_ref, p_ref):
    attend(H, L, (q, k, v, g, kt, vt, s_ref, p_ref, ht, dqt, dk, dv))

def attention_call(q, k, v, g, kt, vt):
    H, L, _ = q.shape
    vm = pl.BlockSpec(memory_space=pltpu.VMEM)
    nb = L // TILE
    return pl.pallas_call(functools.partial(attend_kernel, H, L),
        out_shape=(jax.ShapeDtypeStruct((H*64, L), F32), jax.ShapeDtypeStruct((H*64, L), F32), jax.ShapeDtypeStruct((H, L, 128), F32), jax.ShapeDtypeStruct((H, L, 128), F32)),
        in_specs=[vm]*6, out_specs=[vm]*4,
        scratch_shapes=[pltpu.VMEM((nb, TILE, TILE), F32), pltpu.VMEM((nb, TILE, TILE), F32)],
        compiler_params=pltpu.CompilerParams(vmem_limit_bytes=56 * 2**20))(q, k, v, g, kt, vt)

def prep(queries, keys, values, d_heads, segments):
    seg = segments[:, None] == jnp.arange(64)[None, :]
    e = jnp.broadcast_to(seg.astype(BF)[None], queries.shape)
    f = jnp.broadcast_to(jnp.where(seg, 0.0, NEG).astype(BF)[None], queries.shape)
    lane = jnp.arange(64)
    f = jnp.where(lane < 4, f, 0).astype(BF)
    qa = jnp.concatenate([(queries.astype(F32) * 0.125).astype(BF), e], -1)
    ka = jnp.concatenate([keys, f], -1)
    z = jnp.zeros_like(values)
    va = jnp.concatenate([values, z], -1)
    ga = jnp.concatenate([d_heads, z], -1)
    kt = keys.transpose(0, 2, 1).reshape(-1, keys.shape[1])
    vt = values.transpose(0, 2, 1).reshape(-1, keys.shape[1])
    return qa, ka, va, ga, kt, vt

def attention(queries, keys, values, d_heads, segments):
    H, L, _ = queries.shape
    ht, dqt, dk, dv = attention_call(*prep(queries, keys, values, d_heads, segments))

    def back(t):
        return t.reshape(H, 64, L).transpose(0, 2, 1)

    return back(ht).astype(BF), (back(dqt) * 0.125).astype(BF), dk[..., :64].astype(BF), dv[..., :64].astype(BF)


def dot(a, b):
    return jnp.dot(a, b, preferred_element_type=F32)


def dot_t(a, b):
    return lax.dot_general(a, b, (((0,), (0,)), ((), ())), preferred_element_type=F32)


def dot_nt(a, b):
    return lax.dot_general(a, b, (((1,), (1,)), ((), ())), preferred_element_type=F32)


(
    OWN, XGO, DYGO, XFWD, DYFWD, HOTS, DYALL, VROWS, LN0, LN1, LN2, LN3, SWGO, SWIN, QKV0, QKV1,
    DH, GVC1, GVC2, GVC3, GVC4, GVC5, GMA1, GMA2, GMA3, GMA4, GMA5, GMB1, GMB2, GMB3, GMB4,
    GMB5, GPR1, GPR2, GPR3, GPR4, GPR5, GRA1, GRA2, GRA3, GRA4, GRA5, GRB1, GRB2, GRB3, GRB4,
    GRB5, GFA1, GFA2, GFA3, GFA4, GFA5, GFB1, GFB2, GFB3, GFB4, GFB5, RVC1, RVC2, RVC3, RVC4,
    RVC5, RMA1, RMA2, RMA3, RMA4, RMA5, RMB1, RMB2, RMB3, RMB4, RMB5, RPR1, RPR2, RPR3, RPR4,
    RPR5, RRA1, RRA2, RRA3, RRA4, RRA5, RRB1, RRB2, RRB3, RRB4, RRB5, RFA1, RFA2, RFA3, RFA4,
    RFA5, RFB1, RFB2, RFB3, RFB4, RFB5, AT00, AT02, AT03, AT10, AT12, AT13, AT20, AT22, AT23,
    AT30, AT32, AT33, POST, GM, GR, GF, GP, SBGO, SBIN, UP0, UP1, UP2, UP3, DN0, DN1, OP0, OP1,
    BK0, BK1, OM0, OM1, BM0, BM1, VP, BO, IG, SV, WV, VO, SMA, SMB, SPR, SRA, SRB, SFA, SFB,
    WMA, WMB, WPR, WRA, WRB, WFA, WFB, CMA, CMB, CPR, CRA, CRB, CFA, CFB,
) = range(157)

ORDER = (
    OWN, GPR1, GVC1, XGO, GMB1, GRA1, GVC2, GPR2, GRB1, GRA2, DYGO, GVC3, GPR3, GRB2, GRA3,
    GVC4, GPR4, GMA1, GRB3, DYFWD, GVC5, XFWD, GMB2, GPR5, VROWS, GMA2, GRA4, SWGO, LN1, GRB4,
    GMB3, LN0, LN2, GMA3, GFB1, HOTS, GRA5, LN3, GRB5, UP0, UP2, SWIN, UP3, GMB4, DYALL, UP1,
    GMA4, GFA1, GF, RFB1, DH, GMA5, GMB5, GFB2, QKV0, RFA1, AT20, GFA2, QKV1, RFB2, AT10, GFB3,
    AT22, RFA2, AT23, AT30, AT00, AT12, GFA3, AT02, AT13, GFB4, RFB3, AT32, AT33, AT03, RFA3,
    GFA4, POST, RFB4, GM, GFB5, RMB1, GP, SBGO, GFA5, RFA4, RMA1, DN0, DN1, RMB2, GR, RRB1,
    RFB5, RRA1, RMA2, SBIN, RFA5, SFB, OP1, RPR1, SFA, RMB3, OM1, RRA2, BK1, RRB2, BK0, VP,
    RVC1, RPR2, RRA3, WFA, BM1, RVC2, RRB3, RPR3, BM0, OP0, RRA4, RVC3, RRB4, RMA3, RVC4, RRA5,
    WFB, RPR4, SRA, RRB5, SRB, CFA, RMB4, RMA4, OM0, RPR5, RVC5, SV, SPR, WRA, RMB5, SMB, CFB,
    IG, WRB, RMA5, SMA, WPR, WMB, WV, CRA, CPR, WMA, CMB, CRB, BO, VO, CMA,
)
LANES = 128
HALF = LANES // 2
VEC_ROWS = 16
PROJ = 3
TURN = 32


def resident_fits(seq_size, dp_size, tok):
    return (
        D // dp_size == LANES
        and FF // dp_size // seq_size == LANES
        and HEADS // seq_size == 4
        and tok * seq_size <= TURN * TURN
        and tok % TILE == 0
    )


def rows_at(ref, index, count):
    return ref.at[pl.ds(pl.multiple_of(index * count, count), count)]


def columns_at(ref, index, count):
    return ref.at[:, pl.ds(pl.multiple_of(index * count, count), count)]


class Flat:
    def __init__(self, ref, count, stride=None, start=0):
        self.ref, self.count, self.start = ref, count, start
        self.stride = count if stride is None else stride

    @property
    def at(self):
        return self

    def __getitem__(self, index):
        first = pl.multiple_of(index * self.stride + self.start, self.count)
        return self.ref.at[pl.ds(first, self.count)]


class Stack:
    def __init__(self, ref, start, count):
        self.ref, self.start, self.count = ref, start, count

    @property
    def at(self):
        return self

    def __getitem__(self, index):
        return self.ref.at[index, pl.ds(self.start, self.count)]


def lanes_like(shape):
    return lax.broadcasted_iota(jnp.int32, shape, len(shape) - 1)


def head_part(values, start):
    tile = values[:, start // LANES * LANES : start // LANES * LANES + LANES]
    return tile if start % LANES == 0 else pltpu.roll(tile, HEAD_DIM, 1)


def spin(tile, cosine, sine):
    lane = lanes_like(tile.shape)
    partner = jnp.where(lane < ROT // 2, pltpu.roll(tile, LANES - ROT // 2, 1), pltpu.roll(tile, ROT // 2, 1))
    return tile * cosine + partner * sine


def attend_head(head, block, refs):
    q_ref, k_ref, v_ref, g_ref, kt_ref, vt_ref, s_ref, p_ref, ht_ref, dqt_ref, dk_ref, dv_ref = refs
    here = pl.ds(block * TILE, TILE)
    wide = pl.ds(head * LANES, LANES)
    dims = pl.ds(head * HEAD_DIM, HEAD_DIM)
    query = q_ref[here, wide]
    grad = g_ref[here, wide]
    span = block + 1
    top = jnp.full((1, TILE), 2 * NEG, F32)
    for index in range(span):
        tile = nt(k_ref[pl.ds(index * TILE, TILE), wide], query)
        if index == block:
            key = lax.broadcasted_iota(jnp.int32, (TILE, TILE), 0)
            place = lax.broadcasted_iota(jnp.int32, (TILE, TILE), 1)
            tile = jnp.where(key <= place, tile, NEG)
        s_ref[index] = tile
        top = jnp.maximum(top, jnp.max(tile, axis=0, keepdims=True))
    total = jnp.zeros((1, TILE), F32)
    for index in range(span):
        raised = jnp.exp(s_ref[index] - top)
        s_ref[index] = raised
        total = total + jnp.sum(raised, axis=0, keepdims=True)
    share = 1.0 / total
    delta = jnp.zeros((1, TILE), F32)
    heads = jnp.zeros((HEAD_DIM, TILE), F32)
    for index in range(span):
        there = pl.ds(index * TILE, TILE)
        weights = s_ref[index] * share
        s_ref[index] = weights
        weights_b = weights.astype(BF)
        d_weights = nt(v_ref[there, wide], grad)
        p_ref[index] = d_weights
        d_value = nn(weights_b, grad)
        dv_ref[head, there, :] = d_value if index == block else dv_ref[head, there, :] + d_value
        heads = heads + nn(vt_ref[dims, there], weights_b)
        delta = delta + jnp.sum(weights * d_weights, axis=0, keepdims=True)
    ht_ref[dims, here] = heads.astype(BF)
    d_query = jnp.zeros((HEAD_DIM, TILE), F32)
    for index in range(span):
        there = pl.ds(index * TILE, TILE)
        d_scores = (s_ref[index] * (p_ref[index] - delta)).astype(BF)
        d_key = nn(d_scores, query)
        dk_ref[head, there, :] = d_key if index == block else dk_ref[head, there, :] + d_key
        d_query = d_query + nn(kt_ref[dims, there], d_scores)
    dqt_ref[dims, here] = (d_query * HEAD_DIM**-0.5).astype(BF)


class Refs(typing.NamedTuple):
    x_own: typing.Any
    dy_own: typing.Any
    w_mix_own: typing.Any
    w_proj_own: typing.Any
    w_rise_own: typing.Any
    w_fall_own: typing.Any
    gain1_own: typing.Any
    shift1_own: typing.Any
    gain2_own: typing.Any
    shift2_own: typing.Any
    b_proj_own: typing.Any
    b_fall_own: typing.Any
    b_mix_own: typing.Any
    b_rise_own: typing.Any
    seg_own: typing.Any
    pad_own: typing.Any
    turns: typing.Any
    block_out: typing.Any
    input_grad: typing.Any
    mix_fin: typing.Any
    proj_fin: typing.Any
    rise_fin: typing.Any
    fall_fin: typing.Any
    vec_result: typing.Any
    pad: typing.Any
    cos: typing.Any
    sin: typing.Any
    x: typing.Any
    dy: typing.Any
    hot: typing.Any
    segs: typing.Any
    w_mix: typing.Any
    w_proj_cols: typing.Any
    w_proj: typing.Any
    w_rise: typing.Any
    w_fall: typing.Any
    vec_all: typing.Any
    rows: typing.Any
    normed1: typing.Any
    normed2: typing.Any
    stat: typing.Any
    qk: typing.Any
    vg: typing.Any
    kt: typing.Any
    vt: typing.Any
    s: typing.Any
    p: typing.Any
    ht: typing.Any
    dqt: typing.Any
    dk: typing.Any
    dv: typing.Any
    attn: typing.Any
    d_mixed: typing.Any
    out_part: typing.Any
    back_part: typing.Any
    active: typing.Any
    d_up: typing.Any
    g_mix: typing.Any
    g_proj_cols: typing.Any
    g_rise: typing.Any
    g_fall: typing.Any
    c_mix: typing.Any
    c_proj: typing.Any
    c_rise: typing.Any
    c_fall: typing.Any
    out_cross: typing.Any
    out_came: typing.Any
    back_cross: typing.Any
    back_came: typing.Any
    sums: typing.Any
    vec_part: typing.Any
    vec_came: typing.Any
    mix_got: typing.Any
    proj_got: typing.Any
    rise_got: typing.Any
    fall_got: typing.Any
    vec_fin: typing.Any
    vec_out: typing.Any
    m_x: typing.Any
    m_dy: typing.Any
    m_hot: typing.Any
    m_vec: typing.Any
    m_mix: typing.Any
    m_proj: typing.Any
    m_rise: typing.Any
    m_fall: typing.Any
    m_swap: typing.Any
    m_own: typing.Any
    m_swap2: typing.Any
    m_rmix: typing.Any
    m_rproj: typing.Any
    m_rrise: typing.Any
    m_rfall: typing.Any
    m_out: typing.Any
    m_back: typing.Any
    m_vec2: typing.Any
    m_fmix: typing.Any
    m_fproj: typing.Any
    m_frise: typing.Any
    m_ffall: typing.Any
    m_fvec: typing.Any
    m_fin: typing.Any


def resident_kernel(seq_size, dp_size, *refs):
    r = Refs(*refs)
    place = Place(seq_size, dp_size)
    half = place.half
    tok = r.x_own.shape[0]
    length = r.x.shape[0]
    wide = r.w_proj.shape[0]
    mixed_wide = 3 * wide
    units = LANES
    each = dp_size // seq_size
    heads_n = wide // HEAD_DIM
    blocks = length // TILE

    place.greet_near()
    own = []

    def bring(src, dst):
        copy = pltpu.make_async_copy(src, dst, r.m_own.at[len(own)])
        copy.start()
        own.append(copy)

    bring(columns_at(r.w_mix_own, place.seq, mixed_wide), rows_at(r.w_mix, place.dp, LANES))
    bring(columns_at(r.w_proj_own, place.seq, wide), rows_at(r.w_proj_cols, place.dp, LANES))
    bring(r.x_own, rows_at(r.x, place.seq, tok))
    bring(r.dy_own, rows_at(r.dy, place.seq, tok))
    for index in range(dp_size):
        bring(
            columns_at(r.w_rise_own, index * seq_size + place.seq, units),
            rows_at(r.w_rise, place.dp, LANES).at[:, pl.ds(index * units, units)],
        )
    bring(rows_at(r.w_fall_own, place.seq, units), rows_at(r.w_fall, place.dp, units))
    bring(r.pad_own, r.pad)

    coarse_cos, coarse_sin, fine_cos, fine_sin = (
        r.turns.at[pl.ds(index * TURN, TURN)] for index in range(4)
    )

    @pl.loop(0, length // TURN)
    def _(step):
        here = pl.ds(pl.multiple_of(step * TURN, TURN), TURN)
        far_cos, far_sin = coarse_cos[pl.ds(step, 1), :], coarse_sin[pl.ds(step, 1), :]
        r.cos[here, :] = far_cos * fine_cos[...] - far_sin * fine_sin[...]
        r.sin[here, :] = far_sin * fine_cos[...] + far_cos * fine_sin[...]

    row = 0
    vectors = (r.gain1_own, r.shift1_own, r.gain2_own, r.shift2_own, r.b_proj_own, r.b_fall_own, r.b_mix_own, r.b_rise_own)
    for vector in vectors:
        count = vector.shape[0]
        r.vec_all[place.dp, row : row + count, :] = vector[...].astype(F32)
        row += count
    r.vec_all[place.dp, row:, :] = jnp.zeros((VEC_ROWS - row, LANES), F32)
    rows_at(r.segs, place.seq, 8)[...] = jnp.broadcast_to(r.seg_own[...], (8, tok)).astype(F32)

    def pair_of(ref, make):
        return [make(Flat(ref, HALF, LANES, start), index) for index, start in enumerate((0, HALF))]

    def gather_pair(ref, sems):
        return pair_of(ref, lambda part, index: RingGather(place, part, sems.at[index]))

    def reduce_pair(ref, came, sems):
        return pair_of(ref, lambda part, index: RingReduce(place, part, came.at[index], sems.at[index]))

    def final_pair(out_ref, sems, ref):
        return pair_of(
            ref,
            lambda part, index: SeqGather(
                place, Stack(out_ref, index * HALF, HALF), sems.at[index], part[place.dp]
            ),
        )

    gathers = [
        RingGather(place, r.vec_all, r.m_vec),
        *gather_pair(r.w_mix, r.m_mix),
        RingGather(place, Flat(r.w_proj_cols, LANES), r.m_proj),
        *gather_pair(r.w_rise, r.m_rise),
        *gather_pair(r.w_fall, r.m_fall),
    ]
    reduces = [
        RingReduce(place, r.vec_part, r.vec_came, r.m_vec2),
        *reduce_pair(r.g_mix, r.c_mix, r.m_rmix),
        RingReduce(place, Flat(r.g_proj_cols, LANES), r.c_proj, r.m_rproj),
        *reduce_pair(r.g_rise, r.c_rise, r.m_rrise),
        *reduce_pair(r.g_fall, r.c_fall, r.m_rfall),
    ]
    finals = [
        *final_pair(r.mix_got, r.m_fmix, r.g_mix),
        SeqGather(place, r.proj_got, r.m_fproj, rows_at(r.g_proj_cols, place.dp, LANES)),
        *final_pair(r.rise_got, r.m_frise, r.g_rise),
        *final_pair(r.fall_got, r.m_ffall, r.g_fall),
    ]
    homes = [r.proj_fin]
    for out_ref in (r.rise_fin, r.fall_fin):
        homes += [Stack(out_ref, start, HALF) for start in (0, HALF)]
    homes = [Stack(r.mix_fin, start, HALF) for start in (0, HALF)] + homes
    f_vec = SeqGather(place, r.vec_fin, r.m_fvec)

    x_move = SeqGather(place, Flat(r.x, tok), r.m_x)
    dy_move = SeqGather(place, Flat(r.dy, tok), r.m_dy)
    seg_move = SeqGather(place, Flat(r.segs, 8), r.m_hot)
    out = SeqReduce(place, Flat(r.out_part, tok), r.out_cross, r.out_came, r.m_out)
    back = SeqReduce(place, Flat(r.back_part, tok), r.back_cross, r.back_came, r.m_back)

    leaving = []

    def leave(src, dst):
        copy = pltpu.make_async_copy(src, dst, r.m_fin.at[len(leaving)])
        copy.start()
        leaving.append(copy)

    pieces = {}

    def piece(name, *given):
        def note(run):
            pieces[name] = functools.partial(run, *given)
            return run

        return note

    def tile_rows(block):
        return pl.ds(pl.multiple_of(block * TILE, TILE), TILE)

    def gather(stream, step):
        gathers[stream].tick(step)

    def reduce(stream, step):
        reduces[stream].tick(step)

    for stream in range(len(gathers)):
        for step in range(1, half + 2):
            tick = stream * (half + 1) + step - 1
            piece(GVC1 + tick, stream, step)(gather)
            piece(RVC1 + tick, stream, step)(reduce)

    @piece(OWN)
    def _():
        for copy in own:
            copy.wait()

    @piece(XGO)
    def _():
        x_move.begin()
        seg_move.begin()

    piece(DYGO)(dy_move.begin)

    @piece(XFWD)
    def _():
        x_move.forward()
        seg_move.forward()

    piece(DYFWD)(dy_move.forward)

    @piece(HOTS)
    def _():
        for step in range(place.pairs):
            seg_move.across_arrived(step)
        kind = lax.broadcasted_iota(jnp.int32, (LANES, tok), 0) - HEAD_DIM
        for index in range(seq_size):
            segment = r.segs[index * 8 : index * 8 + 1, :].astype(jnp.int32)
            r.hot[index * tok : (index + 1) * tok, :] = jnp.where(segment == kind, 1.0, 0.0).T.astype(BF)

    @piece(DYALL)
    def _():
        for step in range(place.pairs):
            dy_move.across_arrived(step)

    @piece(VROWS)
    def _():
        for index in range(dp_size):
            at = slice(index * LANES, (index + 1) * LANES)
            for row in range(6):
                r.rows[row : row + 1, at] = r.vec_all[index, row : row + 1, :]
            r.rows[6:7, at] = r.vec_all[index, pl.ds(9 + place.seq, 1), :]
        for index in range(each):
            for row in range(3):
                start = (index * 3 + row) * LANES
                r.rows[7:8, start : start + LANES] = r.vec_all[place.seq * each + index, 6 + row : 7 + row, :]

    chunk = 64

    def normalize(block):
        @pl.loop(0, tok // chunk)
        def _(step):
            here = pl.ds(pl.multiple_of(block * tok + step * chunk, chunk), chunk)
            values = r.x[here, :].astype(F32)
            mean = jnp.sum(values, axis=-1, keepdims=True) * (1.0 / D)
            center = values - mean
            rstd = lax.rsqrt(jnp.sum(center * center, axis=-1, keepdims=True) * (1.0 / D) + EPS)
            n = center * rstd
            r.normed1[here, :] = (n * r.rows[0:1, :] + r.rows[1:2, :]).astype(BF)
            r.normed2[here, :] = (n * r.rows[2:3, :] + r.rows[3:4, :]).astype(BF)
            lane = lanes_like((chunk, LANES))
            r.stat[here, :] = jnp.where(lane < HEAD_DIM, mean, rstd)

    def unit_rows(here):
        stat = r.stat[here, :]
        return (r.x[here, :].astype(F32) - stat[:, 0:1]) * stat[:, HEAD_DIM : HEAD_DIM + 1]

    @piece(LN0)
    def _():
        normalize(place.seq)

    @piece(LN1)
    def _():
        x_move.across_arrived(0)
        normalize(place.sibling)

    @piece(LN2)
    def _():
        normalize(place.pair_peer(1))

    @piece(LN3)
    def _():
        x_move.across_arrived(1)
        normalize(place.across_source(1))

    def swap(step):
        peer = place.seq_peer(step)
        src, dst = rows_at(r.w_proj_cols, peer, wide), columns_at(r.w_proj, place.seq, wide)
        return send(src, dst, r.m_swap, step, {"seq": peer})

    def swap_arrival(step):
        source = place.seq_peer(-step)
        src, dst = rows_at(r.w_proj_cols, source, wide), columns_at(r.w_proj, source, wide)
        return send(src, dst, r.m_swap, step, {"seq": place.seq_peer(step)})

    @piece(SWGO)
    def _():
        for step in range(1, seq_size):
            swap(step).start()
        columns_at(r.w_proj, place.seq, wide)[...] = rows_at(r.w_proj_cols, place.seq, wide)[...]

    @piece(SWIN)
    def _():
        for step in range(1, seq_size):
            swap_arrival(step).wait_recv()

    def mix_columns(first, last):
        @pl.loop(first, last)
        def _(block):
            here = tile_rows(block)
            mixed = nn(r.normed1[here, :], r.w_mix[...]) + r.rows[7:8, 0:mixed_wide]
            cosine, sine = r.cos[here, :], r.sin[here, :]
            lane = lanes_like((TILE, LANES))
            hot = r.hot[here, :].astype(F32)
            cold = jnp.where((lane >= HEAD_DIM) & (lane < HEAD_DIM + 4), (1.0 - hot) * NEG, 0.0)
            for head in range(heads_n):
                start = head * 3 * HEAD_DIM
                query = spin(head_part(mixed, start), cosine, sine) * HEAD_DIM**-0.5
                key = spin(head_part(mixed, start + HEAD_DIM), cosine, sine)
                value = head_part(mixed, start + 2 * HEAD_DIM)
                at = pl.ds(head * LANES, LANES)
                at_more = pl.ds((heads_n + head) * LANES, LANES)
                dims = pl.ds(head * HEAD_DIM, HEAD_DIM)
                r.qk[here, at] = jnp.where(lane < HEAD_DIM, query, hot).astype(BF)
                r.qk[here, at_more] = jnp.where(lane < HEAD_DIM, key, cold).astype(BF)
                r.vg[here, at] = jnp.where(lane < HEAD_DIM, value, 0.0).astype(BF)
                r.kt[dims, here] = key.T[:HEAD_DIM, :].astype(BF)
                r.vt[dims, here] = value.T[:HEAD_DIM, :].astype(BF)

    middle = blocks // 2
    piece(QKV0, 0, middle)(mix_columns)
    piece(QKV1, middle, blocks)(mix_columns)
    @piece(DH)
    def _():
        @pl.loop(0, blocks)
        def _(block):
            here = tile_rows(block)
            place_in = lax.broadcasted_iota(jnp.int32, (TILE, wide), 0) + block * TILE
            d_heads = jnp.where(place_in < length - r.pad[0], nt(r.dy[here, :], r.w_proj[...]), 0.0)
            for head in range(heads_n):
                at_more = pl.ds((heads_n + head) * LANES, LANES)
                r.vg[here, at_more] = head_part(d_heads, head * HEAD_DIM).astype(BF)

    second = heads_n * LANES
    head_refs = (
        r.qk.at[:, pl.ds(0, second)],
        r.qk.at[:, pl.ds(second, second)],
        r.vg.at[:, pl.ds(0, second)],
        r.vg.at[:, pl.ds(second, second)],
        r.kt,
        r.vt,
        r.s,
        r.p,
        r.ht,
        r.dqt,
        r.dk,
        r.dv,
    )

    def attend_blocks(head, first, last):
        for block in range(first, last):
            if block == 0:
                attend_head(head, block, head_refs)
            elif block == 1:
                attend_head(head, block, head_refs)
            elif block == 2:
                attend_head(head, block, head_refs)
            else:
                attend_head(head, block, head_refs)

    for head in range(heads_n):
        first = AT00 + head * (middle + 1)
        piece(first, head, 0, middle)(attend_blocks)
        for block in range(middle, blocks):
            piece(first + block - middle + 1, head, block, block + 1)(attend_blocks)

    def heads_back():
        @pl.loop(0, blocks)
        def _(block):
            here = tile_rows(block)
            place_in = lax.broadcasted_iota(jnp.int32, (TILE, wide), 0) + block * TILE
            r.attn[here, :] = jnp.where(place_in < length - r.pad[0], r.ht[:, here].T.astype(F32), 0.0).astype(BF)
            d_query = r.dqt[:, here].T.astype(F32)
            cosine, sine = r.cos[here, :], -r.sin[here, :]
            lane = lanes_like((TILE, LANES))
            parts = []
            for head in range(heads_n):
                parts.append(spin(head_part(d_query, head * HEAD_DIM), cosine, sine))
                parts.append(spin(r.dk[head, here, :], cosine, sine))
                parts.append(r.dv[head, here, :])
            for index in range(len(parts) // 2):
                tile = jnp.where(lane < HEAD_DIM, parts[2 * index], pltpu.roll(parts[2 * index + 1], HEAD_DIM, 1))
                at = slice(index * LANES, (index + 1) * LANES)
                tile = tile.astype(BF)
                r.d_mixed[here, at] = tile
                r.sums[6:7, at] += jnp.sum(tile.astype(F32), axis=0, keepdims=True)

    piece(POST)(heads_back)
    big = 512

    def weight_grad(out_ref, left, right):
        @pl.loop(0, left.shape[1] // big)
        def _(index):
            at = pl.ds(pl.multiple_of(index * big, big), big)
            out_ref[at, :] = tn(left[:, at], right[...]).astype(BF)

    piece(GM, r.g_mix, r.normed1, r.d_mixed)(weight_grad)
    piece(GR, r.g_rise, r.normed2, r.d_up)(weight_grad)
    piece(GF, r.g_fall, r.active, r.dy)(weight_grad)

    @piece(GP)
    def _():
        gathers[PROJ].finish()
        for step in range(1, seq_size):
            swap(step).wait_send()
        grad = tn(r.attn[...], r.dy[...]).astype(BF)
        for index in range(seq_size):
            r.w_proj_cols[index * wide : (index + 1) * wide, :] = grad[:, index * wide : (index + 1) * wide]

    def swap_back(step):
        peer = place.seq_peer(step)
        src, dst = rows_at(r.w_proj_cols, peer, wide), rows_at(r.g_proj_cols, place.seq, wide)
        return send(src, dst, r.m_swap2, step, {"seq": peer})

    def swap_back_arrival(step):
        source = place.seq_peer(-step)
        src, dst = rows_at(r.w_proj_cols, source, wide), rows_at(r.g_proj_cols, source, wide)
        return send(src, dst, r.m_swap2, step, {"seq": place.seq_peer(step)})

    @piece(SBGO)
    def _():
        for step in range(1, seq_size):
            swap_back(step).start()
        rows_at(r.g_proj_cols, place.seq, wide)[...] = rows_at(r.w_proj_cols, place.seq, wide)[...]

    @piece(SBIN)
    def _():
        for step in range(1, seq_size):
            swap_back_arrival(step).wait_recv()

    def upward(block):
        here = tile_rows(block)
        up = nn(r.normed2[here, :], r.w_rise[...]) + r.rows[6:7, :]
        share = 0.5 + 0.5 * lax.erf(up * 0.5**0.5)
        r.active[here, :] = (up * share).astype(BF)
        bell = jnp.exp(-0.5 * up * up) * (2 * np.pi) ** -0.5
        r.d_up[here, :] = (share + up * bell).astype(BF)

    def downward(first, last):
        @pl.loop(first, last)
        def _(block):
            here = tile_rows(block)
            d_up = (r.d_up[here, :].astype(F32) * nt(r.dy[here, :], r.w_fall[...])).astype(BF)
            r.d_up[here, :] = d_up
            r.sums[5:6, :] += jnp.sum(d_up.astype(F32), axis=0, keepdims=True)

    for block in range(blocks):
        piece(UP0 + block, block)(upward)
    piece(DN0, 0, middle)(downward)
    piece(DN1, middle, blocks)(downward)

    def out_rows(step):
        first = ((place.pair + step) % place.pairs) * (2 * tok // TILE)
        @pl.loop(0, 2 * tok // TILE)
        def _(block):
            here = tile_rows(first + block)
            part = nn(r.attn[here, :], r.w_proj[...]) + nn(r.active[here, :], r.w_fall[...])
            r.out_part[here, :] = part.astype(BF)

        out.over_start(step)

    def back_rows(step):
        first = ((place.pair + step) % place.pairs) * (2 * tok // TILE)
        @pl.loop(0, 2 * tok // TILE)
        def _(block):
            here = tile_rows(first + block)
            d_one = nt(r.d_mixed[here, :], r.w_mix[...])
            d_two = nt(r.d_up[here, :], r.w_rise[...])
            r.back_part[here, :] = (r.rows[0:1, :] * d_one + r.rows[2:3, :] * d_two).astype(BF)
            n = unit_rows(here)
            r.sums[0:1, :] += jnp.sum(d_one * n, axis=0, keepdims=True)
            r.sums[1:2, :] += jnp.sum(d_one, axis=0, keepdims=True)
            r.sums[2:3, :] += jnp.sum(d_two * n, axis=0, keepdims=True)
            r.sums[3:4, :] += jnp.sum(d_two, axis=0, keepdims=True)
            r.sums[4:5, :] += jnp.sum(r.dy[here, :].astype(F32), axis=0, keepdims=True)

        back.over_start(step)

    for step in range(2):
        piece(OP0 + step, step)(out_rows)
        piece(BK0 + step, step)(back_rows)
        piece(OM0 + step, step)(out.over_add)
        piece(BM0 + step, step)(back.over_add)

    @piece(VP)
    def _():
        for index in range(dp_size):
            at = slice(index * LANES, (index + 1) * LANES)
            r.vec_part[index, 0:6, :] = r.sums[0:6, at]
            for row in range(mixed_wide // LANES):
                r.vec_part[index, 6 + row : 7 + row, :] = r.sums[6:7, row * LANES : (row + 1) * LANES]

    def settle(move, home):
        move.begin()
        leave(move.own, home.at[place.seq])

    def pass_on(move, home):
        move.forward()
        for step in range(1, place.pairs):
            source = place.pair_peer(-step)
            leave(move.full.at[source], home.at[source])

    def complete(move, home):
        for step in range(place.pairs):
            move.across_arrived(step)
            source = place.across_source(step)
            leave(move.full.at[source], home.at[source])

    for index, (move, home) in enumerate(zip(finals, homes, strict=True)):
        piece(SMA + index, move, home)(settle)
        piece(WMA + index, move, home)(pass_on)
        piece(CMA + index, move, home)(complete)

    mine = pl.ds(pl.multiple_of(place.seq * tok, tok), tok)

    @piece(BO)
    def _():
        total = out.total()
        block_out = total + r.x[mine, :].astype(F32) + (r.rows[4:5, :] + r.rows[5:6, :])
        r.out_cross[0] = block_out.astype(BF)
        leave(r.out_cross.at[0], r.block_out)

    @piece(IG)
    def _():
        scaled = back.total()
        n = unit_rows(mine)
        rstd = r.stat[mine, HEAD_DIM : HEAD_DIM + 1]
        back_mean = jnp.sum(scaled, axis=-1, keepdims=True) * (1.0 / D)
        back_n = jnp.sum(scaled * n, axis=-1, keepdims=True) * (1.0 / D)
        input_grad = r.dy[mine, :].astype(F32) + rstd * (scaled - back_mean - n * back_n)
        r.back_cross[0] = input_grad.astype(BF)
        leave(r.back_cross.at[0], r.input_grad)

    @piece(SV)
    def _():
        r.vec_fin[place.seq] = r.vec_part[place.dp]
        f_vec.begin()

    piece(WV)(f_vec.forward)

    @piece(VO)
    def _():
        f_vec.finish()
        norm = r.vec_fin[0, 0:4, :]
        for index in range(1, seq_size):
            norm = norm + r.vec_fin[index, 0:4, :]
        r.vec_out[0:4, :] = norm
        r.vec_out[4:5, :] = r.vec_fin[0, 4:5, :]
        source = r.vec_fin[place.dp // each]
        pick = place.dp % each
        part = source[6:9, :]
        for index in range(1, each):
            part = jnp.where(pick == index, source[6 + 3 * index : 9 + 3 * index, :], part)
        r.vec_out[5:8, :] = part
        for index in range(seq_size):
            r.vec_out[8 + index : 9 + index, :] = r.vec_fin[index, 5:6, :]
        leave(r.vec_out, r.vec_result)

    place.met_near()
    r.sums[...] = jnp.zeros(r.sums.shape, F32)
    r.vec_part[...] = jnp.zeros(r.vec_part.shape, F32)
    assert sorted(ORDER) == sorted(pieces)
    for name in ORDER:
        pieces[name]()
    for move in finals:
        move.sent()
    for copy in leaving:
        copy.wait()
    for move in (*gathers[:PROJ], *gathers[PROJ + 1 :], *reduces, out, back):
        move.finish()
    for move in (x_move, seg_move, dy_move):
        move.sent()
    for step in range(1, seq_size):
        swap_back(step).wait_send()


def resident_call(seq_size, dp_size, *args):
    tok = args[0].shape[0]
    length = tok * seq_size
    half, pairs = dp_size // 2, seq_size // 2
    wide = HEADS // seq_size * HEAD_DIM
    units_all = dp_size * LANES
    heads_n = wide // HEAD_DIM

    def half_vmem(*shape):
        return pltpu.VMEM(shape, BF)

    def full_vmem(*shape):
        return pltpu.VMEM(shape, F32)

    def ring(columns):
        return half_vmem(2, 2, half, HALF, columns)

    def pair_of_sems(count):
        return pltpu.SemaphoreType.DMA((2, 2, count))

    any_spec = pl.BlockSpec(memory_space=pl.ANY)
    vmem = pl.BlockSpec(memory_space=pltpu.VMEM)
    scratch = [
        pltpu.SMEM((1,), jnp.int32),
        full_vmem(length, LANES),
        full_vmem(length, LANES),
        half_vmem(length, D),
        half_vmem(length, D),
        half_vmem(length, LANES),
        full_vmem(seq_size * 8, tok),
        half_vmem(D, 3 * wide),
        half_vmem(D, wide),
        half_vmem(wide, D),
        half_vmem(D, units_all),
        half_vmem(units_all, D),
        full_vmem(dp_size, VEC_ROWS, LANES),
        full_vmem(8, D),
        half_vmem(length, D),
        half_vmem(length, D),
        full_vmem(length, LANES),
        half_vmem(length, units_all),
        half_vmem(length, units_all),
        half_vmem(wide, length),
        half_vmem(wide, length),
        full_vmem(length // TILE, TILE, TILE),
        full_vmem(length // TILE, TILE, TILE),
        half_vmem(wide, length),
        half_vmem(wide, length),
        full_vmem(heads_n, length, LANES),
        full_vmem(heads_n, length, LANES),
        half_vmem(length, wide),
        half_vmem(length, 3 * wide),
        half_vmem(length, D),
        half_vmem(length, D),
        half_vmem(length, units_all),
        half_vmem(length, units_all),
        half_vmem(D, 3 * wide),
        half_vmem(D, wide),
        half_vmem(D, units_all),
        half_vmem(units_all, D),
        ring(3 * wide),
        half_vmem(2, half, LANES, wide),
        ring(units_all),
        ring(D),
        half_vmem(pairs, tok, D),
        half_vmem(pairs - 1, tok, D),
        half_vmem(pairs, tok, D),
        half_vmem(pairs - 1, tok, D),
        full_vmem(8, D),
        full_vmem(dp_size, VEC_ROWS, LANES),
        full_vmem(2, half, VEC_ROWS, LANES),
        half_vmem(seq_size, LANES, 3 * wide),
        half_vmem(seq_size, LANES, wide),
        half_vmem(seq_size, LANES, units_all),
        half_vmem(seq_size, LANES, D),
        full_vmem(seq_size, VEC_ROWS, LANES),
        full_vmem(16, LANES),
    ]
    scratch += [sems_of(2 * pairs)] * 3 + [sems_of(2 * half)]
    scratch += [pair_of_sems(2 * half), sems_of(2 * half), pair_of_sems(2 * half), pair_of_sems(2 * half)]
    scratch += [sems_of(seq_size), pltpu.SemaphoreType.DMA((dp_size + 6,)), sems_of(seq_size)]
    scratch += [pair_of_sems(2 * half), sems_of(2 * half), pair_of_sems(2 * half), pair_of_sems(2 * half)]
    scratch += [sems_of(2 * pairs)] * 2 + [sems_of(2 * half)]
    scratch += [pair_of_sems(2 * pairs), sems_of(2 * pairs), pair_of_sems(2 * pairs), pair_of_sems(2 * pairs)]
    scratch += [sems_of(2 * pairs)]
    scratch += [pltpu.SemaphoreType.DMA((32,))]
    return pl.pallas_call(
        functools.partial(resident_kernel, seq_size, dp_size),
        out_shape=(
            jax.ShapeDtypeStruct((tok, D), BF),
            jax.ShapeDtypeStruct((tok, D), BF),
            jax.ShapeDtypeStruct((seq_size, LANES, 3 * wide), BF),
            jax.ShapeDtypeStruct((seq_size, LANES, wide), BF),
            jax.ShapeDtypeStruct((seq_size, LANES, units_all), BF),
            jax.ShapeDtypeStruct((seq_size, LANES, D), BF),
            jax.ShapeDtypeStruct((16, LANES), F32),
        ),
        in_specs=[any_spec] * 6 + [vmem] * 9 + [any_spec, vmem],
        out_specs=[any_spec] * 7,
        scratch_shapes=scratch,
        compiler_params=pltpu.CompilerParams(
            collective_id=2, has_side_effects=True, vmem_limit_bytes=RESIDENT_VMEM
        ),
    )(*args)


RESIDENT_VMEM = 63 * 2**20


def finish_kernel(seq_size, dp_size, *refs):
    (block, grad, mix, proj, rise, fall, vec), refs = refs[:7], refs[7:]
    (block_out, grad_out, mix_out, proj_out, rise_out, fall_out), refs = refs[:6], refs[6:]
    vec_outs, refs = refs[:8], refs[8:]
    (block_in, grad_in, mix_in, proj_in, rise_in, fall_in, vec_in, mix_f, proj_f, rise_f, fall_f), refs = refs[:11], refs[11:]
    vec_fs, (in_sems, out_sems) = refs[:8], refs[8:]
    parts = [(fall.at[group], fall_in.at[group]) for group in range(seq_size)]
    parts += [(rise, rise_in), (mix, mix_in), (proj, proj_in), (block, block_in), (grad, grad_in), (vec, vec_in)]
    coming = []
    for src, dst in parts:
        copy = pltpu.make_async_copy(src, dst, in_sems.at[len(coming)])
        copy.start()
        coming.append(copy)
    *fall_copies, rise_copy, mix_copy, proj_copy, block_copy, grad_copy, vec_copy = coming
    leaving = []

    def leave(src, dst):
        copy = pltpu.make_async_copy(src, dst, out_sems.at[len(leaving)])
        copy.start()
        leaving.append(copy)

    for group in range(seq_size):
        fall_copies[group].wait()
        at = pl.ds(group * LANES, LANES)
        fall_f[at, :] = fall_in[group].astype(F32)
        leave(fall_f.at[at], fall_out.at[at])
    few = 32
    rise_copy.wait()
    for start in range(0, LANES, few):
        at = pl.ds(start, few)
        for group in range(seq_size):
            for index in range(dp_size):
                column = (index * seq_size + group) * LANES
                rise_f[at, column : column + LANES] = rise_in[group, at, index * LANES : (index + 1) * LANES].astype(F32)
        leave(rise_f.at[at], rise_out.at[at])
    mix_copy.wait()
    proj_copy.wait()
    for start in range(0, LANES, 2 * few):
        at = pl.ds(start, 2 * few)
        for held, full, out in ((mix_in, mix_f, mix_out), (proj_in, proj_f, proj_out)):
            columns = held.shape[2]
            for group in range(seq_size):
                full[at, group * columns : (group + 1) * columns] = held[group, at, :].astype(F32)
            leave(full.at[at], out.at[at])
    block_copy.wait()
    leave(block_in, block_out)
    grad_copy.wait()
    leave(grad_in, grad_out)
    vec_copy.wait()
    for held, out, row in zip(vec_fs, vec_outs, (0, 1, 2, 3, 4, 4, 5, 8), strict=True):
        for start in range(0, out.shape[0], LANES):
            held[start : start + LANES] = vec_in[row + start // LANES]
        leave(held, out)
    for copy in leaving:
        copy.wait()


def finish_call(seq_size, dp_size, block, grad, mix, proj, rise, fall, vec):
    tok = block.shape[0]
    vec_sizes = (LANES,) * 6 + (3 * LANES, seq_size * LANES)
    full_sizes = ((LANES, 3 * D), (LANES, D), (LANES, FF), (seq_size * LANES, D))
    any_spec = pl.BlockSpec(memory_space=pl.ANY)
    return pl.pallas_call(
        functools.partial(finish_kernel, seq_size, dp_size),
        out_shape=(jax.ShapeDtypeStruct((tok, D), BF),) * 2
        + tuple(jax.ShapeDtypeStruct(size, F32) for size in full_sizes)
        + tuple(jax.ShapeDtypeStruct((size,), F32) for size in vec_sizes),
        in_specs=[any_spec] * 7,
        out_specs=[any_spec] * 14,
        scratch_shapes=[pltpu.VMEM(array.shape, array.dtype) for array in (block, grad, mix, proj, rise, fall, vec)]
        + [pltpu.VMEM(size, F32) for size in full_sizes]
        + [pltpu.VMEM((size,), F32) for size in vec_sizes]
        + [pltpu.SemaphoreType.DMA((seq_size + 6,)), pltpu.SemaphoreType.DMA((24,))],
        compiler_params=pltpu.CompilerParams(vmem_limit_bytes=RESIDENT_VMEM),
    )(block, grad, mix, proj, rise, fall, vec)


def resident_tables():
    half = ROT // 2
    frequency = BASE ** (-np.arange(0, ROT, 2).astype(np.float32) / np.float32(ROT))
    lanes = np.zeros((LANES,), np.float64)
    lanes[:half] = lanes[half:ROT] = frequency.astype(np.float32)
    sign = np.where(np.arange(LANES) < half, -1.0, 1.0)
    steps = np.arange(TURN, dtype=np.float64)[:, None]
    tables = [f for scale in (TURN, 1) for f in (np.cos(steps * scale * lanes), sign * np.sin(steps * scale * lanes))]
    return jnp.asarray(np.concatenate(tables).astype(np.float32))


def resident_shards(
    tokens,
    cotangent,
    norm1_gain,
    norm1_bias,
    norm2_gain,
    norm2_bias,
    qkv_weight,
    qkv_bias,
    out_weight,
    out_bias,
    up_weight,
    up_bias,
    down_weight,
    down_bias,
    segment_ids,
    pad_length,
):
    seq_size, dp_size = lax.axis_size("seq"), lax.axis_size("dp")
    tok = tokens.shape[1]
    vectors = (norm1_gain, norm1_bias, norm2_gain, norm2_bias, out_bias, down_bias, qkv_bias, up_bias)
    parts = resident_call(
        seq_size,
        dp_size,
        tokens[0],
        cotangent[0],
        qkv_weight,
        out_weight,
        up_weight,
        down_weight,
        *(vector.reshape(-1, LANES) for vector in vectors),
        segment_ids,
        pad_length,
        resident_tables(),
    )
    done = finish_call(seq_size, dp_size, *parts)
    block_out, input_grad, g_mix, g_proj, g_rise, g_fall = done[:6]
    norm1_g, norm1_b, norm2_g, norm2_b, out_b, down_b, b_mix, b_rise = done[6:]
    return (
        block_out[None],
        input_grad[None],
        norm1_g,
        norm1_b,
        norm2_g,
        norm2_b,
        g_mix,
        b_mix,
        g_proj,
        out_b,
        g_rise,
        b_rise,
        g_fall,
        down_b,
    )


def streamed_shards(
    tokens,
    cotangent,
    norm1_gain,
    norm1_bias,
    norm2_gain,
    norm2_bias,
    qkv_weight,
    qkv_bias,
    out_weight,
    out_bias,
    up_weight,
    up_bias,
    down_weight,
    down_bias,
    segment_ids,
    pad_length,
):
    seq_size, dp_size = lax.axis_size("seq"), lax.axis_size("dp")
    seq = lax.axis_index("seq")
    dp = lax.axis_index("dp")
    tok = tokens.shape[1]
    length = tok * seq_size
    heads_n = HEADS // seq_size
    rows = D // dp_size
    wide = heads_n * HEAD_DIM
    units = FF // dp_size // seq_size

    mix = qkv_weight.reshape(rows, seq_size, heads_n, 3, HEAD_DIM)
    mix = lax.dynamic_index_in_dim(mix, seq, 1, keepdims=False)
    mix = mix.transpose(0, 2, 1, 3).reshape(rows, 3 * wide)
    proj = lax.dynamic_slice_in_dim(out_weight, seq * wide, wide, 1)
    rise = up_weight.reshape(rows, dp_size, seq_size, units)
    rise = lax.dynamic_index_in_dim(rise, seq, 2, keepdims=False).reshape(rows, dp_size * units)
    fall = lax.dynamic_slice_in_dim(down_weight, seq * units, units, 0)
    vec = jnp.concatenate(
        [norm1_gain, norm1_bias, norm2_gain, norm2_bias, out_bias, down_bias, qkv_bias, up_bias]
    )
    vec_len = vec.shape[0]
    vec = jnp.pad(vec, (0, 2048 - vec_len)).reshape(16, 128)
    seg = jnp.broadcast_to(segment_ids, (8, tok))
    x_all, dy_all, w_mix, _, w_rise, w_fall, vec_all, seg_all, w_proj = gather_all(
        seq_size, dp_size, tokens[0], cotangent[0], mix, proj, rise, fall, vec, seg
    )
    x = x_all.reshape(length, D).astype(F32)
    dy = dy_all.reshape(length, D)
    w_mix = w_mix.reshape(D, 3 * wide)
    w_rise = w_rise.reshape(D, dp_size * units)
    w_fall = w_fall.reshape(dp_size * units, D)
    w_proj = w_proj.reshape(seq_size, wide, wide).transpose(1, 0, 2).reshape(wide, D)
    segments = seg_all[:, 0, :].reshape(length)
    vec_all = vec_all.reshape(dp_size, 2048)[:, :vec_len].astype(F32)
    g1, s1, g2, s2, b_proj, b_fall = (
        vec_all[:, i * rows : (i + 1) * rows].reshape(D) for i in range(6)
    )
    b_mix = vec_all[:, 6 * rows : 9 * rows].reshape(seq_size, heads_n, 3, HEAD_DIM)
    b_mix = lax.dynamic_index_in_dim(b_mix, seq, 0, keepdims=False)
    b_mix = b_mix.transpose(1, 0, 2).reshape(3 * wide)
    b_rise = vec_all[:, 9 * rows :].reshape(dp_size, seq_size, units)
    b_rise = lax.dynamic_index_in_dim(b_rise, seq, 1, keepdims=False).reshape(dp_size * units)

    center = x - jnp.mean(x, axis=-1, keepdims=True)
    rstd = lax.rsqrt(jnp.mean(center * center, axis=-1, keepdims=True) + EPS)
    n = center * rstd
    normed1 = (n * g1 + s1).astype(BF)
    normed2 = (n * g2 + s2).astype(BF)
    valid = (jnp.arange(length, dtype=jnp.int32) < length - pad_length[0]).astype(F32)[:, None]
    cosine, sine = (jnp.asarray(t) for t in angle_tables(length))

    mixed = dot(normed1, w_mix) + b_mix
    mixed = mixed.reshape(length, 3, heads_n, HEAD_DIM).transpose(1, 2, 0, 3)
    queries = turn(mixed[0], cosine, sine, 1.0).astype(BF)
    keys = turn(mixed[1], cosine, sine, 1.0).astype(BF)
    values = mixed[2].astype(BF)
    d_heads = (dot_nt(dy, w_proj) * valid).astype(BF)
    d_heads = d_heads.reshape(length, heads_n, HEAD_DIM).transpose(1, 0, 2)
    heads, d_q, d_k, d_v = attention(queries, keys, values, d_heads, segments)
    attn_rows = (heads.transpose(1, 0, 2).reshape(length, wide).astype(F32) * valid).astype(BF)
    d_mixed = jnp.stack(
        [
            turn(d_q.astype(F32), cosine, sine, -1.0).astype(BF),
            turn(d_k.astype(F32), cosine, sine, -1.0).astype(BF),
            d_v,
        ]
    )
    d_mixed = d_mixed.transpose(2, 0, 1, 3).reshape(length, 3 * wide)

    upward = dot(normed2, w_rise) + b_rise
    active = jax.nn.gelu(upward, approximate=False).astype(BF)
    slope = 0.5 * (1 + lax.erf(upward * (0.5**0.5))) + upward * jnp.exp(
        -0.5 * upward * upward
    ) * ((2 * np.pi) ** -0.5)
    d_up = (slope * dot_nt(dy, w_fall)).astype(BF)
    out_part = (dot(attn_rows, w_proj) + dot(active, w_fall)).astype(BF)
    d_n1 = dot_nt(d_mixed, w_mix)
    d_n2 = dot_nt(d_up, w_rise)
    back_part = (g1 * d_n1 + g2 * d_n2).astype(BF)

    g_mix = dot_t(normed1, d_mixed).astype(BF).reshape(dp_size, rows, 3 * wide)
    g_proj = dot_t(attn_rows, dy).astype(BF).reshape(dp_size // seq_size, rows, seq_size, wide)
    g_proj = g_proj.transpose(2, 0, 1, 3)
    g_rise = dot_t(normed2, d_up).astype(BF).reshape(dp_size, rows, dp_size * units)
    g_fall = dot_t(active, dy).astype(BF).reshape(dp_size, units, D)
    dyf = dy.astype(F32)
    vec_part = jnp.concatenate(
        [
            t.reshape(dp_size, -1)
            for t in (
                jnp.sum(d_n1 * n, axis=0),
                jnp.sum(d_n1, axis=0),
                jnp.sum(d_n2 * n, axis=0),
                jnp.sum(d_n2, axis=0),
                jnp.sum(dyf, axis=0),
                jnp.sum(d_up.astype(F32), axis=0),
            )
        ]
        + [jnp.broadcast_to(jnp.sum(d_mixed.astype(F32), axis=0)[None], (dp_size, 3 * wide))],
        axis=1,
    )
    part_len = vec_part.shape[1]
    vec_part = jnp.pad(vec_part, ((0, 0), (0, 2048 - part_len))).reshape(dp_size, 16, 128)
    out_sum, back_sum, f_mix, f_proj, f_rise, f_fall, f_vec = reduce_all(
        seq_size,
        dp_size,
        out_part.reshape(seq_size, tok, D),
        back_part.reshape(seq_size, tok, D),
        g_mix,
        g_proj,
        g_rise,
        g_fall,
        vec_part,
    )
    own_x = tokens[0].astype(F32)
    block_output = (own_x + out_sum + b_proj + b_fall).astype(BF)
    own_center = own_x - jnp.mean(own_x, axis=-1, keepdims=True)
    own_rstd = lax.rsqrt(jnp.mean(own_center * own_center, axis=-1, keepdims=True) + EPS)
    own_n = own_center * own_rstd
    back = own_rstd * (
        back_sum
        - jnp.mean(back_sum, axis=-1, keepdims=True)
        - own_n * jnp.mean(back_sum * own_n, axis=-1, keepdims=True)
    )
    input_grad = (cotangent[0].astype(F32) + back).astype(BF)
    f_mix = f_mix.reshape(seq_size, rows, 3, heads_n, HEAD_DIM)
    f_mix = f_mix.transpose(1, 0, 3, 2, 4).reshape(rows, 3 * D).astype(F32)
    f_proj = f_proj.transpose(1, 0, 2).reshape(rows, D).astype(F32)
    f_rise = f_rise.reshape(seq_size, rows, dp_size, units)
    f_rise = f_rise.transpose(1, 2, 0, 3).reshape(rows, FF).astype(F32)
    f_fall = f_fall.reshape(seq_size * units, D).astype(F32)
    f_vec = f_vec.reshape(seq_size, 2048)[:, :part_len]
    norm_sums = jnp.sum(f_vec[:, : 4 * rows], axis=0)
    column = f_vec[0, 4 * rows : 5 * rows]
    f_b_rise = f_vec[:, 5 * rows : 5 * rows + units].reshape(seq_size * units)
    f_b_mix = f_vec[:, 5 * rows + units :].reshape(seq_size, 3, heads_n, HEAD_DIM)
    f_b_mix = f_b_mix.transpose(0, 2, 1, 3).reshape(dp_size, 3 * rows)
    f_b_mix = lax.dynamic_index_in_dim(f_b_mix, dp, 0, keepdims=False)
    return (
        block_output[None],
        input_grad[None],
        norm_sums[:rows],
        norm_sums[rows : 2 * rows],
        norm_sums[2 * rows : 3 * rows],
        norm_sums[3 * rows :],
        f_mix,
        f_b_mix,
        f_proj,
        column,
        f_rise,
        f_b_rise,
        f_fall,
        column,
    )


def shards(*args):
    seq_size, dp_size = lax.axis_size("seq"), lax.axis_size("dp")
    if resident_fits(seq_size, dp_size, args[0].shape[1]):
        return resident_shards(*args)
    return streamed_shards(*args)


def solution(mesh):
    rows = P("dp", "seq", None)
    weight = P("dp", None)
    vector = P("dp")
    return jax.shard_map(
        shards,
        mesh=mesh,
        in_specs=(rows, rows)
        + (vector,) * 4
        + (weight, vector) * 4
        + (P("dp", "seq"), vector),
        out_specs=(rows, rows) + (vector,) * 4 + (weight, vector) * 4,
        check_vma=False,
    )
```
